32 devices in a mesh: batch: 8 (over y, x, core), blk: 4 (over z).
Axes of the slice: x: 2, y: 2, z: 4, core: 2. Of those that a mesh axis runs over, the one named last changes fastest.
Arguments:
- hidden_in: bfloat16 [8, 512, 768], P('batch', 'blk'), may hold values from -6 to 6
- w_query: bfloat16 [768, 768], replicated, may hold values from -0.21875 to 0.21875
- b_query: bfloat16 [768], replicated, may hold values from -3 to 3
- w_key: bfloat16 [768, 768], replicated, may hold values from -0.21875 to 0.21875
- w_value: bfloat16 [768, 768], replicated, may hold values from -0.21875 to 0.21875
- b_value: bfloat16 [768], replicated, may hold values from -3 to 3
- w_output: bfloat16 [768, 768], replicated, may hold values from -1.25 to 1.25
- b_output: bfloat16 [768], replicated, may hold values from -3 to 3
- attn_gain: bfloat16 [768], replicated, may hold values from 0.5 to 1.5
- attn_shift: bfloat16 [768], replicated, may hold values from -3 to 3
- w_inner: bfloat16 [768, 3072], replicated, may hold values from -0.21875 to 0.21875
- b_inner: bfloat16 [3072], replicated, may hold values from -3 to 3
- w_outer: bfloat16 [3072, 768], replicated, may hold values from -0.109375 to 0.109375
- b_outer: bfloat16 [768], replicated, may hold values from -3 to 3
- ffn_gain: bfloat16 [768], replicated, may hold values from 0.5 to 1.5
- ffn_shift: bfloat16 [768], replicated, may hold values from -3 to 3
- text_lengths: int32 [8, 4], P('batch'), may hold values from 1 to 64, as said below
- region_lengths: int32 [8, 4], P('batch'), may hold values from 1 to 505
- out_grad: bfloat16 [8, 512, 768], P('batch', 'blk'), may hold values from -6 to 6
Outputs:
- layer_out: bfloat16 [8, 512, 768], P('batch', 'blk')
- grad_in: bfloat16 [8, 512, 768], P('batch', 'blk')
- grad_w_query: float32 [768, 768], P('batch', 'blk')
- grad_b_query: float32 [768], replicated
- grad_w_key: float32 [768, 768], P('batch', 'blk')
- grad_w_value: float32 [768, 768], P('batch', 'blk')
- grad_b_value: float32 [768], replicated
- grad_w_output: float32 [768, 768], P('batch', 'blk')
- grad_b_output: float32 [768], replicated
- grad_attn_gain: float32 [768], replicated
- grad_attn_shift: float32 [768], replicated
- grad_w_inner: float32 [768, 3072], P('batch', 'blk')
- grad_b_inner: float32 [3072], replicated
- grad_w_outer: float32 [3072, 768], P('batch', 'blk')
- grad_b_outer: float32 [768], replicated
- grad_ffn_gain: float32 [768], replicated
- grad_ffn_shift: float32 [768], replicated
The draws below stay inside these ranges and needn't reach their ends.
Inputs may be any that keep to these rules, and one draw needn't show every extreme that they name: `text_lengths`: in each row the pairs lie end to end from its first position; text and region tokens of all pairs add up to at most 512, and the positions after them are pad.
All inputs are finite; a program needn't handle non-finite values.
Results may differ from the reference program's by a relative error of at most 0.02.
Values may be sent and summed in bfloat16 or wider, within the bound.
No kernel may reach another device: no remote copies, remote signals or barrier semaphores. Data moves between devices by JAX's collectives and lax.ppermute only.
A program may use at most 128 MiB of HBM per device.

```python
import math
import jax
import jax.numpy as jnp
from jax import lax

D = 768
HEADS = 12
HEAD_DIM = 64
FF = 3072
SEQ = 512
PAIRS = 4
ROWS = 8
SPAN = 128


def pair_lengths(key):
    keys_all = jax.random.split(key, 6)
    grid_shape = (ROWS, PAIRS)
    short_cap = max(1, SPAN // 8)
    text_short = jax.random.randint(keys_all[0], grid_shape, 1, short_cap + 1, dtype=jnp.int32)
    region_short = jax.random.randint(keys_all[1], grid_shape, 1, short_cap + 1, dtype=jnp.int32)
    long_pick = jax.random.randint(keys_all[2], (ROWS, 1), 0, PAIRS, dtype=jnp.int32)
    is_long = jnp.arange(PAIRS, dtype=jnp.int32)[None, :] == long_pick
    long_text = jax.random.randint(keys_all[3], (ROWS, 1), 1, max(1, SEQ // 8) + 1, dtype=jnp.int32)
    pad_slots = jax.random.randint(keys_all[4], (ROWS, 1), 0, max(1, SEQ // 16) + 1, dtype=jnp.int32)
    tight_row = jax.random.randint(keys_all[5], (), 0, ROWS, dtype=jnp.int32)
    row_ids = jnp.arange(ROWS, dtype=jnp.int32)[:, None]
    is_tight = row_ids == tight_row
    is_widest = row_ids == (tight_row + 1) % ROWS
    text_short = jnp.where(is_tight, 1, text_short)
    region_short = jnp.where(is_tight, 1, region_short)
    pad_slots = jnp.where(is_tight, 0, pad_slots)
    long_text = jnp.where(is_tight, 1, long_text)
    long_text = jnp.where(is_widest, max(1, SEQ // 8), long_text)
    short_total = jnp.sum(jnp.where(is_long, 0, text_short + region_short), axis=1, keepdims=True).astype(jnp.int32)
    long_region = SEQ - pad_slots - short_total - long_text
    text_vals = jnp.where(is_long, long_text, text_short)
    region_vals = jnp.where(is_long, long_region, region_short)
    return (text_vals.astype(jnp.int32), region_vals.astype(jnp.int32))


def draw_text_lengths(key, part):
    return pair_lengths(key)[0]


def draw_region_lengths(key, part):
    return pair_lengths(key)[1]


def level_of(own_key, dims, shards, low, largest):
    def one(axis_at, parts):
        draws = jax.random.uniform(jax.random.fold_in(jax.random.fold_in(own_key, 6), axis_at), (parts,), jnp.float32, low / len(shards), largest / len(shards))
        return jnp.repeat(jnp.exp(draws), dims[axis_at] // parts).reshape((-1,) + (1,) * (len(dims) - axis_at - 1))

    level = one(*shards[0])
    for cut in shards[1:]:
        level = level * one(*cut)
    return level


def bell_draw(stream_key, extent, spread, limit, cuts=(), held_as=jnp.bfloat16):
    level = level_of(stream_key, extent, cuts, -0.22, 0.18) if cuts else 1.0
    array = jax.random.normal(stream_key, extent, jnp.float32) * spread * level
    return jnp.minimum(jnp.maximum(array, -limit), limit).astype(held_as)


def setup_inputs(seed: int = 0) -> dict:
    seeds = jax.random.split(jax.random.key(seed), 20)
    return {
        "hidden_in": bell_draw(seeds[0], (ROWS, SEQ, D), 1.0, 6.0, ((0, 8), (1, 4))),
        "w_query": bell_draw(seeds[1], (D, D), D ** -0.5, 0.21875),
        "b_query": bell_draw(seeds[2], (D,), 0.5, 3.0),
        "w_key": bell_draw(seeds[3], (D, D), D ** -0.5, 0.21875),
        "w_value": bell_draw(seeds[4], (D, D), D ** -0.5, 0.21875),
        "b_value": bell_draw(seeds[5], (D,), 0.5, 3.0),
        "w_output": bell_draw(seeds[6], (D, D), (D // 32) ** -0.5, 1.25),
        "b_output": bell_draw(seeds[7], (D,), 0.5, 3.0),
        "attn_gain": jnp.clip(1.0 + 0.1 * jax.random.normal(seeds[8], (D,), jnp.float32), 0.5, 1.5).astype(jnp.bfloat16),
        "attn_shift": bell_draw(seeds[9], (D,), 0.5, 3.0),
        "w_inner": bell_draw(seeds[10], (D, FF), D ** -0.5, 0.21875),
        "b_inner": bell_draw(seeds[11], (FF,), 0.5, 3.0),
        "w_outer": bell_draw(seeds[12], (FF, D), FF ** -0.5, 0.109375),
        "b_outer": bell_draw(seeds[13], (D,), 0.5, 3.0),
        "ffn_gain": jnp.clip(1.0 + 0.1 * jax.random.normal(seeds[14], (D,), jnp.float32), 0.5, 1.5).astype(jnp.bfloat16),
        "ffn_shift": bell_draw(seeds[15], (D,), 0.5, 3.0),
        "text_lengths": draw_text_lengths(jax.random.fold_in(seeds[19], 71), 0),
        "region_lengths": draw_region_lengths(jax.random.fold_in(seeds[19], 71), 0),
        "out_grad": bell_draw(seeds[18], (ROWS, SEQ, D), 1.0, 6.0, ((0, 8), (1, 4))),
    }


HIGH = lax.Precision.HIGHEST
NORM_EPS = 1e-05
MASKED_SCORE = -1e+30

@jax.custom_vjp
def low(v):
    return lax.optimization_barrier(v.astype(jnp.bfloat16)).astype(jnp.float32)

@jax.custom_vjp
def low_back(v):
    return v

def low_keep(v):
    return (low(v), None)

def low_pass(kept, grad):
    return (grad,)

def back_keep(v):
    return (v, None)

def back_low(kept, grad):
    return (low(grad),)
low.defvjp(low_keep, low_pass)
low_back.defvjp(back_keep, back_low)

def matmul_high(left_side, right_side):
    return jnp.dot(left_side, right_side, precision=HIGH)

def layer_norm(values_in, norm_gain, norm_shift):
    row_mean = lax.optimization_barrier(jnp.mean(values_in, axis=-1, keepdims=True))
    centred = values_in - row_mean
    row_var = lax.optimization_barrier(jnp.mean(centred * centred, axis=-1, keepdims=True))
    return centred * lax.rsqrt(row_var + NORM_EPS) * norm_gain + norm_shift

def segments(text_lengths, region_lengths):
    pair_ends = jnp.cumsum(text_lengths + region_lengths, axis=-1).astype(jnp.int32)
    positions = jnp.arange(SEQ, dtype=jnp.int32)
    above = (positions[None, :, None] >= pair_ends[:, None, :]).astype(jnp.int32)
    return lax.optimization_barrier(jnp.sum(above, axis=-1)).astype(jnp.int32)

def block_forward(params, block_in, block_seg):
    w_query, b_query, w_key, w_value, b_value, w_output, b_output, attn_gain, attn_shift, w_inner, b_inner, w_outer, b_outer, ffn_gain, ffn_shift = params
    group_rows = block_in.shape[0]
    flat_in = block_in.reshape(group_rows * SEQ, D)
    head_shape = (group_rows, SEQ, HEADS, HEAD_DIM)
    query_rows = low_back(low(matmul_high(flat_in, w_query) + b_query)).reshape(head_shape)
    key_rows = low_back(low(matmul_high(flat_in, w_key))).reshape(head_shape)
    value_rows = low_back(low(matmul_high(flat_in, w_value) + b_value)).reshape(head_shape)
    scores = jnp.einsum('gqhd,gkhd->ghqk', query_rows, key_rows, precision=HIGH) * HEAD_DIM ** (-0.5)
    same_seg = block_seg[:, :, None] == block_seg[:, None, :]
    diagonal = jnp.arange(SEQ)[:, None] == jnp.arange(SEQ)[None, :]
    allowed = same_seg & ((block_seg[:, None, :] < PAIRS) | diagonal[None])
    scores = low_back(jnp.where(allowed[:, None], scores, MASKED_SCORE))
    attn_probs = low(jax.nn.softmax(scores, axis=-1))
    context = jnp.einsum('ghqk,gkhd->gqhd', attn_probs, value_rows, precision=HIGH)
    context = low_back(low(context.reshape(group_rows * SEQ, D)))
    branch_out = low_back(matmul_high(context, w_output) + b_output)
    attn_norm = layer_norm(flat_in + branch_out, attn_gain, attn_shift)
    pre_act = low_back(matmul_high(low(attn_norm), w_inner) + b_inner)
    activated = low(jax.nn.gelu(pre_act, approximate=False))
    outer = low_back(matmul_high(activated, w_outer) + b_outer)
    return layer_norm(attn_norm + outer, ffn_gain, ffn_shift).reshape(group_rows, SEQ, D)

def reference(hidden_in, w_query, b_query, w_key, w_value, b_value, w_output, b_output, attn_gain, attn_shift, w_inner, b_inner, w_outer, b_outer, ffn_gain, ffn_shift, text_lengths, region_lengths, out_grad):
    params = tuple((weight_arg.astype(jnp.float32) for weight_arg in (w_query, b_query, w_key, w_value, b_value, w_output, b_output, attn_gain, attn_shift, w_inner, b_inner, w_outer, b_outer, ffn_gain, ffn_shift)))
    group_rows = math.gcd(ROWS, max(1, 4096 // SEQ))
    group_count = ROWS // group_rows
    block_seg = segments(text_lengths, region_lengths).reshape(group_count, group_rows, SEQ)
    grouped_in = hidden_in.astype(jnp.float32).reshape(group_count, group_rows, SEQ, D)
    step_fn = jax.checkpoint(block_forward)

    def forward_all(inputs_all, params_all):
        return lax.map(lambda pair_item: step_fn(params_all, pair_item[0], pair_item[1]), (inputs_all, block_seg))
    forward_out, pull_back = jax.vjp(forward_all, grouped_in, params)
    grad_inputs, grad_params = pull_back(out_grad.astype(jnp.float32).reshape(grouped_in.shape))
    return (forward_out.reshape(ROWS, SEQ, D).astype(jnp.bfloat16), grad_inputs.reshape(ROWS, SEQ, D).astype(jnp.bfloat16), grad_params[0], grad_params[1], grad_params[2], grad_params[3], grad_params[4], grad_params[5], grad_params[6], grad_params[7], grad_params[8], grad_params[9], grad_params[10], grad_params[11], grad_params[12], grad_params[13], grad_params[14])
```

```python
import jax
import jax.numpy as jnp
from jax import lax
from jax.sharding import PartitionSpec as P

HEADS = 12
HEAD_DIM = 64
PAIRS = 4


NORM_EPS = 1e-05
MASKED_SCORE = -1e30
INV_ROOT_TWO = 0.7071067811865476
INV_ROOT_TWO_PI = 0.3989422804014327


def segment_ids(text_lengths, region_lengths, row_len):
    pair_ends = jnp.cumsum(text_lengths + region_lengths, axis=1)
    positions = jnp.arange(row_len, dtype=jnp.int32)
    above = (positions[None, :, None] >= pair_ends[:, None, :]).astype(jnp.int32)
    return jnp.sum(above, axis=2)


def norm_parts(values_in, norm_gain, norm_shift):
    row_mean = jnp.mean(values_in, axis=-1, keepdims=True)
    centred = values_in - row_mean
    inv_dev = lax.rsqrt(jnp.mean(centred * centred, axis=-1, keepdims=True) + NORM_EPS)
    normed = centred * inv_dev
    return (
        normed * norm_gain.astype(jnp.float32) + norm_shift.astype(jnp.float32),
        normed,
        inv_dev,
    )


def norm_back(grad_out, norm_gain, normed, inv_dev):
    scaled = grad_out * norm_gain.astype(jnp.float32)
    centre_term = jnp.mean(scaled, axis=-1, keepdims=True)
    slope_term = jnp.mean(scaled * normed, axis=-1, keepdims=True)
    return inv_dev * (scaled - centre_term - normed * slope_term)


def gelu_slope(values_in):
    normal_cdf = 0.5 * (1.0 + lax.erf(values_in * INV_ROOT_TWO))
    density = jnp.exp(-0.5 * values_in * values_in) * INV_ROOT_TWO_PI
    return normal_cdf + values_in * density


def local(
    hidden_in,
    w_query,
    b_query,
    w_key,
    w_value,
    b_value,
    w_output,
    b_output,
    attn_gain,
    attn_shift,
    w_inner,
    b_inner,
    w_outer,
    b_outer,
    ffn_gain,
    ffn_shift,
    text_lengths,
    region_lengths,
    out_grad,
):
    row_count, block_len, model_width = hidden_in.shape
    row_len = block_len * lax.axis_size("blk")
    first_pos = lax.axis_index("blk") * block_len
    score_scale = HEAD_DIM ** (-0.5)
    token_count = row_count * block_len
    f32 = jnp.float32
    bf16 = jnp.bfloat16
    seg_all = segment_ids(text_lengths, region_lengths, row_len)
    query_seg = lax.dynamic_slice_in_dim(seg_all, first_pos, block_len, 1)
    query_pos = first_pos + jnp.arange(block_len, dtype=jnp.int32)

    def allowed_mask(key_count):
        key_pos = jnp.arange(key_count, dtype=jnp.int32)
        same_seg = query_seg[:, :, None] == seg_all[:, None, :]
        diagonal = query_pos[:, None] == key_pos[None, :]
        live_key = (seg_all[:, None, :] < PAIRS) | diagonal[None]
        return (same_seg & live_key)[:, None]

    flat_in = hidden_in.reshape(token_count, model_width)
    query_rows = (
        jnp.dot(flat_in, w_query, preferred_element_type=f32) + b_query.astype(f32)
    ).astype(bf16)
    key_rows = jnp.dot(flat_in, w_key, preferred_element_type=f32).astype(bf16)
    value_rows = (
        jnp.dot(flat_in, w_value, preferred_element_type=f32) + b_value.astype(f32)
    ).astype(bf16)
    query_heads = query_rows.reshape(row_count, block_len, HEADS, HEAD_DIM)
    key_local = key_rows.reshape(row_count, block_len, model_width)
    value_local = value_rows.reshape(row_count, block_len, model_width)
    both_all = lax.all_gather(
        jnp.stack((key_local, value_local), axis=0), "blk", axis=2, tiled=True
    )
    pieces = (both_all[0], both_all[1])
    run_max = jnp.full((row_count, HEADS, block_len), MASKED_SCORE, f32)
    key_count = pieces[0].shape[1]
    key_heads = pieces[0].reshape(row_count, key_count, HEADS, HEAD_DIM)
    value_heads = pieces[1].reshape(row_count, key_count, HEADS, HEAD_DIM)
    allowed = allowed_mask(key_count)
    scores = (
        jnp.einsum("rqhd,rkhd->rhqk", query_heads, key_heads, preferred_element_type=f32)
        * score_scale
    )
    scores = jnp.where(allowed, scores, MASKED_SCORE)
    new_max = jnp.maximum(run_max, jnp.max(scores, axis=-1))
    weights = jnp.where(allowed, jnp.exp(scores - new_max[..., None]), 0.0)
    run_sum = jnp.sum(weights, axis=-1)
    added = jnp.einsum(
        "rhqk,rkhd->rhqd", weights.astype(bf16), value_heads, preferred_element_type=f32
    )
    run_acc = added
    run_max, run_sum, run_acc = (new_max, run_sum, run_acc)
    context_heads = run_acc / run_sum[..., None]
    log_total = run_max + jnp.log(run_sum)
    context_full = context_heads.transpose(0, 2, 1, 3).reshape(token_count, model_width)
    context_low = context_full.astype(bf16)
    attn_out = jnp.dot(context_low, w_output, preferred_element_type=f32) + b_output.astype(f32)
    mixed = flat_in.astype(f32) + attn_out
    attn_norm, attn_hat, attn_inv = norm_parts(mixed, attn_gain, attn_shift)
    inner_in = attn_norm.astype(bf16)
    pre_act = jnp.dot(inner_in, w_inner, preferred_element_type=f32) + b_inner.astype(f32)
    activated = jax.nn.gelu(pre_act, approximate=False).astype(bf16)
    outer = jnp.dot(activated, w_outer, preferred_element_type=f32) + b_outer.astype(f32)
    summed = attn_norm + outer
    final_out, final_hat, final_inv = norm_parts(summed, ffn_gain, ffn_shift)
    layer_out = final_out.astype(bf16).reshape(row_count, block_len, model_width)
    upstream = out_grad.reshape(token_count, model_width).astype(f32)
    grad_ffn_gain = jnp.sum(upstream * final_hat, axis=0)
    grad_ffn_shift = jnp.sum(upstream, axis=0)
    grad_summed = norm_back(upstream, ffn_gain, final_hat, final_inv)
    outer_low = grad_summed.astype(bf16)
    grad_w_outer = jnp.einsum("nf,nd->fd", activated, outer_low, preferred_element_type=f32)
    grad_b_outer = jnp.sum(outer_low.astype(f32), axis=0)
    grad_act = jnp.einsum("nd,fd->nf", outer_low, w_outer, preferred_element_type=f32)
    pre_low = (grad_act * gelu_slope(pre_act)).astype(bf16)
    grad_w_inner = jnp.einsum("nd,nf->df", inner_in, pre_low, preferred_element_type=f32)
    grad_b_inner = jnp.sum(pre_low.astype(f32), axis=0)
    grad_norm = jnp.einsum("nf,df->nd", pre_low, w_inner, preferred_element_type=f32) + grad_summed
    grad_attn_gain = jnp.sum(grad_norm * attn_hat, axis=0)
    grad_attn_shift = jnp.sum(grad_norm, axis=0)
    grad_mixed = norm_back(grad_norm, attn_gain, attn_hat, attn_inv)
    mixed_low = grad_mixed.astype(bf16)
    grad_w_output = jnp.einsum("nc,nd->cd", context_low, mixed_low, preferred_element_type=f32)
    grad_b_output = jnp.sum(mixed_low.astype(f32), axis=0)
    context_grad = jnp.einsum("nd,cd->nc", mixed_low, w_output, preferred_element_type=f32).astype(
        bf16
    )
    context_grad_heads = context_grad.reshape(row_count, block_len, HEADS, HEAD_DIM)
    row_delta = jnp.einsum("rqhd,rhqd->rhq", context_grad_heads.astype(f32), context_heads)
    key_count = pieces[0].shape[1]
    key_heads = pieces[0].reshape(row_count, key_count, HEADS, HEAD_DIM)
    value_heads = pieces[1].reshape(row_count, key_count, HEADS, HEAD_DIM)
    allowed = allowed_mask(key_count)
    scores = (
        jnp.einsum("rqhd,rkhd->rhqk", query_heads, key_heads, preferred_element_type=f32)
        * score_scale
    )
    attn_probs = jnp.where(allowed, jnp.exp(scores - log_total[..., None]), 0.0)
    value_part = jnp.einsum(
        "rhqk,rqhd->rkhd", attn_probs.astype(bf16), context_grad_heads, preferred_element_type=f32
    )
    grad_probs = jnp.einsum(
        "rqhd,rkhd->rhqk", context_grad_heads, value_heads, preferred_element_type=f32
    )
    score_grad = (attn_probs * (grad_probs - row_delta[..., None])).astype(bf16)
    grad_query = (
        jnp.einsum("rhqk,rkhd->rqhd", score_grad, key_heads, preferred_element_type=f32)
        * score_scale
    )
    key_part = (
        jnp.einsum("rhqk,rqhd->rkhd", score_grad, query_heads, preferred_element_type=f32)
        * score_scale
    )
    key_grads = key_part.reshape(row_count, key_count, model_width)
    value_grads = value_part.reshape(row_count, key_count, model_width)
    grad_query, key_grads, value_grads = (grad_query, key_grads, value_grads)
    both_sum = lax.psum_scatter(
        jnp.stack((key_grads, value_grads), axis=0).astype(bf16),
        "blk",
        scatter_dimension=2,
        tiled=True,
    )
    key_sum, value_sum = (both_sum[0], both_sum[1])
    query_low = grad_query.reshape(token_count, model_width).astype(bf16)
    key_low = key_sum.reshape(token_count, model_width).astype(bf16)
    value_low = value_sum.reshape(token_count, model_width).astype(bf16)
    grad_w_query = jnp.einsum("nd,ne->de", flat_in, query_low, preferred_element_type=f32)
    grad_b_query = jnp.sum(query_low.astype(f32), axis=0)
    grad_w_key = jnp.einsum("nd,ne->de", flat_in, key_low, preferred_element_type=f32)
    grad_w_value = jnp.einsum("nd,ne->de", flat_in, value_low, preferred_element_type=f32)
    grad_b_value = jnp.sum(value_low.astype(f32), axis=0)
    grad_input = jnp.einsum("ne,de->nd", query_low, w_query, preferred_element_type=f32)
    grad_input = grad_input + jnp.einsum("ne,de->nd", key_low, w_key, preferred_element_type=f32)
    grad_input = grad_input + jnp.einsum(
        "ne,de->nd", value_low, w_value, preferred_element_type=f32
    )
    grad_in = (grad_input + grad_mixed).astype(bf16).reshape(row_count, block_len, model_width)
    batch_size = lax.axis_size("batch")
    blk_size = lax.axis_size("blk")

    def pack(grads):
        flat = []
        for grad in grads:
            rows, cols = grad.shape
            tiles = grad.astype(bf16).reshape(
                batch_size, rows // batch_size, blk_size, cols // blk_size
            )
            flat.append(tiles.transpose(0, 2, 1, 3).reshape(batch_size, blk_size, -1))
        return jnp.concatenate(flat, axis=2).reshape(-1, model_width)

    def scatter(packed):
        kept = lax.psum_scatter(packed, "batch", scatter_dimension=0, tiled=True)
        return lax.psum_scatter(kept, "blk", scatter_dimension=0, tiled=True).reshape(-1)

    def unpack(total, grads):
        outs = []
        start = 0
        for grad in grads:
            rows, cols = grad.shape[0] // batch_size, grad.shape[1] // blk_size
            outs.append(total[start : start + rows * cols].reshape(rows, cols).astype(f32))
            start += rows * cols
        return outs

    early = (grad_w_output, grad_w_inner, grad_w_outer)
    late = (grad_w_query, grad_w_key, grad_w_value)
    early_sum = scatter(pack(early))
    late_sum = scatter(pack(late))
    mats = unpack(late_sum, late) + unpack(early_sum, early)
    vec_list = (
        grad_b_query,
        grad_b_value,
        grad_b_output,
        grad_attn_gain,
        grad_attn_shift,
        grad_b_inner,
        grad_b_outer,
        grad_ffn_gain,
        grad_ffn_shift,
    )
    vec_sum = lax.psum(jnp.concatenate(vec_list), ("batch", "blk"))
    vecs = []
    start = 0
    for vec in vec_list:
        vecs.append(vec_sum[start : start + vec.shape[0]])
        start += vec.shape[0]
    return (
        layer_out,
        grad_in,
        mats[0],
        vecs[0],
        mats[1],
        mats[2],
        vecs[1],
        mats[3],
        vecs[2],
        vecs[3],
        vecs[4],
        mats[4],
        vecs[5],
        mats[5],
        vecs[6],
        vecs[7],
        vecs[8],
    )


def solution(mesh):
    placed = (
        P("batch", "blk", None),
        P(),
        P(),
        P(),
        P(),
        P(),
        P(),
        P(),
        P(),
        P(),
        P(),
        P(),
        P(),
        P(),
        P(),
        P(),
        P("batch", None),
        P("batch", None),
        P("batch", "blk", None),
    )
    return jax.shard_map(
        local,
        mesh=mesh,
        in_specs=placed,
        out_specs=(
            P("batch", "blk", None),
            P("batch", "blk", None),
            P("batch", "blk"),
            P(),
            P("batch", "blk"),
            P("batch", "blk"),
            P(),
            P("batch", "blk"),
            P(),
            P(),
            P(),
            P("batch", "blk"),
            P(),
            P("batch", "blk"),
            P(),
            P(),
            P(),
        ),
        check_vma=False,
    )
```

```python
import jax
import jax.numpy as jnp
from jax import lax
from jax.sharding import PartitionSpec as P

HEADS = 12
HEAD_DIM = 64
PAIRS = 4


NORM_EPS = 1e-05
MASKED_SCORE = -1e30
INV_ROOT_TWO = 0.7071067811865476
INV_ROOT_TWO_PI = 0.3989422804014327

f32 = jnp.float32
bf16 = jnp.bfloat16


def mm(left, right):
    return jnp.dot(left, right, preferred_element_type=f32)


def mm_nt(left, right):
    return lax.dot_general(left, right, (((1,), (1,)), ((), ())), preferred_element_type=f32)


def norm_parts(values_in, norm_gain, norm_shift):
    row_mean = jnp.mean(values_in, axis=-1, keepdims=True)
    centred = values_in - row_mean
    inv_dev = lax.rsqrt(jnp.mean(centred * centred, axis=-1, keepdims=True) + NORM_EPS)
    normed = centred * inv_dev
    return (
        normed * norm_gain.astype(f32) + norm_shift.astype(f32),
        normed,
        inv_dev,
    )


def norm_back(grad_out, norm_gain, normed, inv_dev):
    scaled = grad_out * norm_gain.astype(f32)
    centre_term = jnp.mean(scaled, axis=-1, keepdims=True)
    slope_term = jnp.mean(scaled * normed, axis=-1, keepdims=True)
    return inv_dev * (scaled - centre_term - normed * slope_term)


def gelu_slope(values_in):
    normal_cdf = 0.5 * (1.0 + lax.erf(values_in * INV_ROOT_TWO))
    density = jnp.exp(-0.5 * values_in * values_in) * INV_ROOT_TWO_PI
    return normal_cdf + values_in * density


def blk_shift(values, step):
    size = lax.axis_size("blk")
    return lax.ppermute(values, "blk", [(i, (i + step) % size) for i in range(size)])


def batch_swap(values, bit):
    size = lax.axis_size("batch")
    return lax.ppermute(values, "batch", [(i, i ^ (1 << bit)) for i in range(size)])


def split_bit(values, dim, bit):
    own = (lax.axis_index("batch") >> bit) & 1
    send = lax.dynamic_index_in_dim(values, 1 - own, dim, keepdims=False)
    keep = lax.dynamic_index_in_dim(values, own, dim, keepdims=False)
    return send, keep


def bits_of_batch():
    return lax.axis_size("batch").bit_length() - 1


def by_bits(values):
    size = lax.axis_size("batch")
    return values.reshape((2,) * bits_of_batch() + (values.shape[0] // size,) + values.shape[1:])


def take_bits(total, bits, remaining):
    remaining = list(remaining)
    for bit in bits:
        dim = remaining.index(bit)
        send, keep = split_bit(total, dim, bit)
        total = keep + batch_swap(send.astype(bf16), bit).astype(f32)
        remaining.remove(bit)
    return total


def pair_tokens(left_t, right):
    send, keep = split_bit(by_bits(left_t), bits_of_batch() - 1, 0)
    left_both = jnp.concatenate((keep, batch_swap(send, 0)), axis=-1)
    right_both = jnp.concatenate((right, batch_swap(right, 0)), axis=0)
    return left_both, right_both


def weight_rows(left_both, right_both, order):
    remaining = list(range(bits_of_batch() - 1, 0, -1))
    first = order[0]
    depth = left_both.shape[-1]
    send_l, keep_l = split_bit(left_both, remaining.index(first), first)
    send = mm(send_l.reshape(-1, depth), right_both).astype(bf16)
    keep = mm(keep_l.reshape(-1, depth), right_both)
    total = keep + batch_swap(send, first).astype(f32)
    remaining.remove(first)
    total = total.reshape((2,) * len(remaining) + (-1, right_both.shape[1]))
    return take_bits(total, order[1:], remaining)


def blk_scatter(total):
    size = lax.axis_size("blk")
    me = lax.axis_index("blk")
    width = total.shape[1] // size

    def block(step):
        return lax.dynamic_slice_in_dim(total, ((me + step) % size) * width, width, 1)

    out = block(0)
    for step in range(1, size):
        out = out + blk_shift(block(step).astype(bf16), step).astype(f32)
    return out


def blk_sum(values):
    out = values
    for step in range(1, lax.axis_size("blk")):
        out = out + blk_shift(values, step)
    return out


def batch_sum(values):
    for bit in range(bits_of_batch()):
        values = values + batch_swap(values, bit)
    return values


def local(
    hidden_in,
    w_query,
    b_query,
    w_key,
    w_value,
    b_value,
    w_output,
    b_output,
    attn_gain,
    attn_shift,
    w_inner,
    b_inner,
    w_outer,
    b_outer,
    ffn_gain,
    ffn_shift,
    text_lengths,
    region_lengths,
    out_grad,
):
    _, block_len, model_width = hidden_in.shape
    blk_size = lax.axis_size("blk")
    me = lax.axis_index("blk")
    row_len = block_len * blk_size
    own_heads = HEADS // blk_size
    own_width = own_heads * HEAD_DIM
    score_scale = HEAD_DIM ** (-0.5)
    flat_in = hidden_in[0]
    x_all = jnp.concatenate(
        [flat_in] + [blk_shift(flat_in, step) for step in range(1, blk_size)], axis=0
    )
    positions = jnp.concatenate(
        [
            ((me - step) % blk_size) * block_len + jnp.arange(block_len, dtype=jnp.int32)
            for step in range(blk_size)
        ]
    )
    pair_ends = jnp.cumsum(text_lengths[0] + region_lengths[0])
    seg = jnp.sum((positions[:, None] >= pair_ends[None, :]).astype(jnp.int32), axis=1)
    same_seg = seg[:, None] == seg[None, :]
    diagonal = positions[:, None] == positions[None, :]
    allowed = (same_seg & ((seg[None, :] < PAIRS) | diagonal))[None]

    def own_cols(weight):
        return lax.dynamic_slice_in_dim(weight, me * own_width, own_width, weight.ndim - 1)

    w_qkv = jnp.concatenate((own_cols(w_query), own_cols(w_key), own_cols(w_value)), axis=1)
    b_qkv = jnp.concatenate(
        (own_cols(b_query), jnp.zeros((own_width,), bf16), own_cols(b_value))
    )
    qkv = (mm(x_all, w_qkv) + b_qkv.astype(f32)).astype(bf16)
    by_head = qkv.reshape(row_len, 3, own_heads, HEAD_DIM).transpose(1, 2, 0, 3)
    query_heads, key_heads, value_heads = by_head[0], by_head[1], by_head[2]
    scores = (
        jnp.einsum("hqd,hkd->hqk", query_heads, key_heads, preferred_element_type=f32)
        * score_scale
    )
    scores = jnp.where(allowed, scores, MASKED_SCORE)
    row_max = jnp.max(scores, axis=-1, keepdims=True)
    weights = jnp.exp(scores - row_max)
    row_sum = jnp.sum(weights, axis=-1, keepdims=True)
    probs = weights / row_sum
    probs_low = probs.astype(bf16)
    context_heads = jnp.einsum("hqk,hkd->hqd", probs_low, value_heads, preferred_element_type=f32)
    context_own = context_heads.transpose(1, 0, 2).reshape(row_len, own_width).astype(bf16)
    parts = [context_own[:block_len]]
    for step in range(1, blk_size):
        rows = context_own[step * block_len : (step + 1) * block_len]
        parts.append(blk_shift(rows, blk_size - step))
    context_low = jnp.roll(jnp.stack(parts, 0), me, 0).transpose(1, 0, 2)
    context_low = context_low.reshape(block_len, model_width)
    attn_out = mm(context_low, w_output) + b_output.astype(f32)
    mixed = flat_in.astype(f32) + attn_out
    attn_norm, attn_hat, attn_inv = norm_parts(mixed, attn_gain, attn_shift)
    inner_in = attn_norm.astype(bf16)
    pre_act = mm(inner_in, w_inner) + b_inner.astype(f32)
    activated = jax.nn.gelu(pre_act, approximate=False).astype(bf16)
    outer = mm(activated, w_outer) + b_outer.astype(f32)
    summed = attn_norm + outer
    final_out, final_hat, final_inv = norm_parts(summed, ffn_gain, ffn_shift)
    layer_out = final_out.astype(bf16)[None]
    upstream = out_grad[0].astype(f32)
    grad_ffn_gain = jnp.sum(upstream * final_hat, axis=0)
    grad_ffn_shift = jnp.sum(upstream, axis=0)
    grad_summed = norm_back(upstream, ffn_gain, final_hat, final_inv)
    outer_low = grad_summed.astype(bf16)
    grad_b_outer = jnp.sum(outer_low.astype(f32), axis=0)
    grad_act = mm_nt(outer_low, w_outer)
    pre_low = (grad_act * gelu_slope(pre_act)).astype(bf16)
    grad_b_inner = jnp.sum(pre_low.astype(f32), axis=0)
    grad_norm = mm_nt(pre_low, w_inner) + grad_summed
    grad_attn_gain = jnp.sum(grad_norm * attn_hat, axis=0)
    grad_attn_shift = jnp.sum(grad_norm, axis=0)
    grad_mixed = norm_back(grad_norm, attn_gain, attn_hat, attn_inv)
    mixed_low = grad_mixed.astype(bf16)
    grad_b_output = jnp.sum(mixed_low.astype(f32), axis=0)
    context_grad = mm_nt(mixed_low, w_output).astype(bf16)

    def head_group(values, step):
        return lax.dynamic_slice_in_dim(
            values, ((me + step) % blk_size) * own_width, own_width, 1
        )

    context_grad_all = jnp.concatenate(
        [head_group(context_grad, 0)]
        + [blk_shift(head_group(context_grad, step), step) for step in range(1, blk_size)],
        axis=0,
    )

    up = list(range(1, bits_of_batch()))
    down = up[::-1]
    grad_outer = weight_rows(*pair_tokens(activated.T, outer_low), up)
    grad_inner = weight_rows(*pair_tokens(inner_in.T, pre_low), down)
    grad_output = weight_rows(*pair_tokens(context_low.T, mixed_low), up)
    grad_w_outer = blk_scatter(grad_outer)
    grad_w_inner = blk_scatter(grad_inner)
    grad_w_output = blk_scatter(grad_output)

    context_grad_heads = context_grad_all.reshape(row_len, own_heads, HEAD_DIM).transpose(1, 0, 2)
    row_delta = jnp.sum(context_grad_heads.astype(f32) * context_heads, axis=-1, keepdims=True)
    value_grad = jnp.einsum(
        "hqk,hqd->khd", probs_low, context_grad_heads, preferred_element_type=f32
    )
    grad_probs = jnp.einsum(
        "hqd,hkd->hqk", context_grad_heads, value_heads, preferred_element_type=f32
    )
    score_grad = (probs * (grad_probs - row_delta)).astype(bf16)
    query_grad = (
        jnp.einsum("hqk,hkd->qhd", score_grad, key_heads, preferred_element_type=f32)
        * score_scale
    )
    key_grad = (
        jnp.einsum("hqk,hqd->khd", score_grad, query_heads, preferred_element_type=f32)
        * score_scale
    )
    qkv_grad = jnp.concatenate(
        [
            part.reshape(row_len, own_width).astype(bf16)
            for part in (query_grad, key_grad, value_grad)
        ],
        axis=1,
    )
    grad_qkv = mm(x_all.T, qkv_grad)
    every = list(range(bits_of_batch()))
    grad_qkv = take_bits(by_bits(grad_qkv), every, every[::-1])
    grad_input = grad_mixed

    def rows_of(step):
        group = (me + step) % blk_size
        cols = [
            lax.dynamic_slice_in_dim(weight, group * own_width, own_width, 1)
            for weight in (w_query, w_key, w_value)
        ]
        return jnp.concatenate(cols, axis=1)

    for step in range(blk_size):
        part = qkv_grad[step * block_len : (step + 1) * block_len]
        if step:
            part = blk_shift(part, blk_size - step)
        grad_input = grad_input + mm_nt(part, rows_of(step))
    grad_in = grad_input.astype(bf16)[None]

    early = (
        grad_b_output,
        grad_attn_gain,
        grad_attn_shift,
        grad_b_inner,
        grad_b_outer,
        grad_ffn_gain,
        grad_ffn_shift,
    )
    early_sum = batch_sum(blk_sum(jnp.concatenate(early)))
    vecs = []
    start = 0
    for vec in early:
        vecs.append(early_sum[start : start + vec.shape[0]])
        start += vec.shape[0]
    late = batch_sum(jnp.sum(qkv_grad.astype(f32), axis=0).reshape(3, own_width))
    late_parts = [late] + [blk_shift(late, step) for step in range(1, blk_size)]
    late_all = jnp.roll(jnp.stack(late_parts[::-1], 0), me + 1, 0)
    late_all = late_all.transpose(1, 0, 2).reshape(3, model_width)
    return (
        layer_out,
        grad_in,
        grad_qkv[:, :own_width],
        late_all[0],
        grad_qkv[:, own_width : 2 * own_width],
        grad_qkv[:, 2 * own_width :],
        late_all[2],
        grad_w_output,
        vecs[0],
        vecs[1],
        vecs[2],
        grad_w_inner,
        vecs[3],
        grad_w_outer,
        vecs[4],
        vecs[5],
        vecs[6],
    )


def solution(mesh):
    rows = P("batch", "blk", None)
    tile = P("batch", "blk")
    return jax.shard_map(
        local,
        mesh=mesh,
        in_specs=(rows,) + (P(),) * 15 + (P("batch", None), P("batch", None), rows),
        out_specs=(
            rows,
            rows,
            tile,
            P(),
            tile,
            tile,
            P(),
            tile,
            P(),
            P(),
            P(),
            tile,
            P(),
            tile,
            P(),
            P(),
            P(),
        ),
        check_vma=False,
    )
```

```python
import jax
import jax.numpy as jnp
from jax import lax
from jax.experimental import pallas as pl
from jax.experimental.pallas import tpu as pltpu
from jax.sharding import PartitionSpec as P

HEADS = 12
HEAD_DIM = 64
PAIRS = 4

NORM_EPS = 1e-05
MASKED_SCORE = -1e30
INV_ROOT_TWO = 0.7071067811865476
INV_ROOT_TWO_PI = 0.3989422804014327
MIB = 1024 * 1024

B_OUTER, FFN_GAIN, FFN_SHIFT, ATTN_GAIN, ATTN_SHIFT, B_OUTPUT, B_QUERY, B_VALUE, B_INNER = range(9)

f32 = jnp.float32
bf16 = jnp.bfloat16


def mm(left, right):
    return jnp.dot(left, right, preferred_element_type=f32)


def mm_nt(left, right):
    return lax.dot_general(left, right, (((1,), (1,)), ((), ())), preferred_element_type=f32)


def norm_stats(values_in):
    row_mean = jnp.mean(values_in, axis=-1, keepdims=True)
    centred = values_in - row_mean
    inv_dev = lax.rsqrt(jnp.mean(centred * centred, axis=-1, keepdims=True) + NORM_EPS)
    return centred * inv_dev, inv_dev


def norm_back(scaled, normed, inv_dev):
    centre_term = jnp.mean(scaled, axis=-1, keepdims=True)
    slope_term = jnp.mean(scaled * normed, axis=-1, keepdims=True)
    return inv_dev * (scaled - centre_term - normed * slope_term)


def sum_rows(values):
    return jnp.sum(values, axis=0, keepdims=True)


def as_row(ref):
    return ref[...].astype(f32).reshape(1, -1)


def ahead(me, step, size):
    return lax.rem(me + step, size)


def behind(me, group, size):
    return lax.rem(group - me + size, size)


def attention_kernel(
    text, region, x0, x1, x2, x3, w_q, w_k, w_v, b_query, b_value, *outs_and_scratch
):
    xs = (x0, x1, x2, x3)
    size = len(xs)
    context_refs = outs_and_scratch[:size]
    probs_ref, q_t_ref, k_t_ref, v_t_ref, context_ref, x_all, mask = outs_and_scratch[size:]
    me = lax.axis_index("blk")
    span = x0.shape[0]
    row_len = span * size
    width = w_q.shape[1]
    for s in range(size):
        x_all[s * span : (s + 1) * span] = xs[s][...]

    def own(ref):
        row = as_row(ref)
        out = jnp.zeros((1, width), f32)
        for g in range(size):
            out = jnp.where(me == g, row[:, g * width : (g + 1) * width], out)
        return out

    ends = []
    total = jnp.int32(0)
    for k in range(PAIRS):
        total = total + text[0, k] + region[0, k]
        ends.append(total)

    def segments(dim):
        shape = [1, 1]
        shape[dim] = span
        parts = []
        for s in range(size):
            start = lax.rem(me - s + size, size) * span
            pos = lax.broadcasted_iota(jnp.int32, tuple(shape), dim) + start
            seg = jnp.zeros(tuple(shape), jnp.int32)
            for end in ends:
                seg = seg + (pos >= end).astype(jnp.int32)
            parts.append(seg)
        return jnp.concatenate(parts, axis=dim)

    seg_q = segments(0)
    seg_k = segments(1)
    diagonal = lax.broadcasted_iota(jnp.int32, (row_len, row_len), 0) == lax.broadcasted_iota(
        jnp.int32, (row_len, row_len), 1
    )
    allowed = (seg_q == seg_k) & ((seg_k < PAIRS) | diagonal)
    mask[...] = jnp.where(allowed, 0.0, MASKED_SCORE)
    rows = x_all[...]
    query = ((mm(rows, w_q[...]) + own(b_query)).astype(bf16) * HEAD_DIM ** (-0.5)).astype(bf16)
    key = mm(rows, w_k[...]).astype(bf16)
    value = (mm(rows, w_v[...]) + own(b_value)).astype(bf16)
    q_t_ref[...] = query.T
    k_t_ref[...] = key.T
    v_t_ref[...] = value.T
    heads = width // HEAD_DIM
    for h in range(heads):
        cols = slice(h * HEAD_DIM, (h + 1) * HEAD_DIM)
        for s in range(size):
            part = slice(s * span, (s + 1) * span)
            scores = mm_nt(query[part, cols], key[:, cols]) + mask[part]
            weights = jnp.exp(scores - jnp.max(scores, axis=-1, keepdims=True))
            probs = (weights / jnp.sum(weights, axis=-1, keepdims=True)).astype(bf16)
            probs_ref[h, part] = probs
            context_ref[part, cols] = mm(probs, value[:, cols])
    for s in range(size):
        context_refs[s][...] = context_ref[s * span : (s + 1) * span].astype(bf16).T


def mixed_kernel(
    x_ref,
    c0,
    c1,
    c2,
    c3,
    w_output,
    b_output,
    attn_gain,
    attn_shift,
    inner_t_ref,
    hat_ref,
    inv_ref,
    context_t_ref,
    groups,
):
    me = lax.axis_index("blk")
    slots = (c0, c1, c2, c3)
    size = len(slots)
    for s in range(size):
        groups[ahead(me, s, size)] = slots[s][...]
    context_t = jnp.concatenate([groups[g] for g in range(size)], axis=0)
    context_t_ref[...] = context_t
    mixed = x_ref[...].astype(f32) + mm(context_t.T, w_output[...]) + as_row(b_output)
    hat, inv = norm_stats(mixed)
    hat_ref[...] = hat
    inv_ref[...] = inv
    inner_in = (hat * as_row(attn_gain) + as_row(attn_shift)).astype(bf16)
    inner_t_ref[...] = inner_in.T


def forward_kernel(blocks):
    def body(
        hat_ref,
        context_t_ref,
        w_inner,
        w_outer,
        attn_gain,
        attn_shift,
        b_inner,
        b_outer,
        ffn_gain,
        ffn_shift,
        grad_ref,
        out_ref,
        left_ref,
        outer_low_ref,
        slope_ref,
        grad_summed_ref,
        sums_ref,
        wi,
        wu,
        sems,
    ):
        width, hidden = wi.shape
        count = sems.shape[0] // 2
        step = hidden // count
        ff_rows = hidden // blocks
        block = left_ref.shape[0] // blocks
        copies = []
        for k in range(count):
            part = pl.ds(k * step, step)
            copies.append(pltpu.make_async_copy(w_inner.at[:, part], wi.at[:, part], sems.at[2 * k]))
            copies.append(pltpu.make_async_copy(w_outer.at[part], wu.at[part], sems.at[2 * k + 1]))
        for copy in copies:
            copy.start()
        attn_norm = hat_ref[...] * as_row(attn_gain) + as_row(attn_shift)
        inner_in = attn_norm.astype(bf16)
        outer = jnp.zeros(attn_norm.shape, f32)
        for k in range(count):
            part = slice(k * step, (k + 1) * step)
            copies[2 * k].wait()
            pre = mm(inner_in, wi[:, part]) + b_inner[part].astype(f32).reshape(1, -1)
            cdf = 0.5 + 0.5 * lax.erf(pre * INV_ROOT_TWO)
            act = (pre * cdf).astype(bf16)
            slope_ref[:, part] = cdf + pre * (jnp.exp(-0.5 * pre * pre) * INV_ROOT_TWO_PI)
            copies[2 * k + 1].wait()
            outer += mm(act, wu[part])
            act_t = act.T
            for j in range(step // ff_rows):
                at = (k * step // ff_rows + j) * block
                left_ref[at : at + ff_rows] = act_t[j * ff_rows : (j + 1) * ff_rows]
        out_rows = width // blocks
        padded = block - ff_rows
        if padded == out_rows:
            for b in range(blocks):
                at = b * block + ff_rows
                left_ref[at : at + padded] = context_t_ref[b * out_rows : (b + 1) * out_rows]
        else:
            for b in range(blocks):
                at = b * block + ff_rows
                row = lax.broadcasted_iota(jnp.int32, (padded, width), 0)
                col = lax.broadcasted_iota(jnp.int32, (padded, width), 1)
                pick = ((row < out_rows) & (col == row + b * out_rows)).astype(f32).astype(bf16)
                left_ref[at : at + padded] = mm(pick, context_t_ref[...]).astype(bf16)
        summed = attn_norm + outer + as_row(b_outer)
        final_hat, final_inv = norm_stats(summed)
        gain = as_row(ffn_gain)
        out_ref[...] = (final_hat * gain + as_row(ffn_shift)).astype(bf16)
        upstream = grad_ref[...].astype(f32)
        grad_summed = norm_back(upstream * gain, final_hat, final_inv)
        grad_summed_ref[...] = grad_summed
        outer_low = grad_summed.astype(bf16)
        outer_low_ref[...] = outer_low
        sums_ref[...] = jnp.zeros(sums_ref.shape, f32)
        sums_ref[B_OUTER : B_OUTER + 1] = sum_rows(outer_low.astype(f32))
        sums_ref[FFN_GAIN : FFN_GAIN + 1] = sum_rows(upstream * final_hat)
        sums_ref[FFN_SHIFT : FFN_SHIFT + 1] = sum_rows(upstream)

    return body


def backward_kernel(
    outer_low_ref,
    slope_ref,
    grad_summed_ref,
    hat_ref,
    inv_ref,
    sums_in,
    w_output,
    w_inner,
    w_outer,
    attn_gain,
    pair_ref,
    grad_mixed_ref,
    sums_ref,
    p0,
    p1,
    p2,
    p3,
    wo,
    wi,
    wu,
    groups,
    sems,
):
    width, hidden = wi.shape
    piece_refs = (p0, p1, p2, p3)
    size = len(piece_refs)
    me = lax.axis_index("blk")
    step = hidden // size
    rows = width // size
    span = outer_low_ref.shape[0]
    copies = []
    parts = []
    for s in range(size):
        g = ahead(me, s, size)
        part = pl.ds(pl.multiple_of(g * step, 128), step)
        parts.append((g, part))
        copies.append(pltpu.make_async_copy(w_outer.at[part], wu.at[part], sems.at[2 * s]))
        copies.append(
            pltpu.make_async_copy(w_inner.at[:, part], wi.at[:, part], sems.at[2 * s + 1])
        )
    copies.append(pltpu.make_async_copy(w_output, wo, sems.at[2 * size]))
    for copy in copies:
        copy.start()
    sums_ref[...] = sums_in[...]
    outer_low = outer_low_ref[...]
    grad_norm = grad_summed_ref[...]
    for s in range(size):
        g, part = parts[s]
        copies[2 * s].wait()
        pre_low = (mm_nt(outer_low, wu[part]) * slope_ref[:, part]).astype(bf16)
        piece_refs[s][rows:] = pre_low.T
        bias = sum_rows(pre_low.astype(f32))
        for k in range(step // width):
            sums_ref[pl.ds(B_INNER + g * (step // width) + k, 1)] = bias[:, k * width : (k + 1) * width]
        copies[2 * s + 1].wait()
        grad_norm += mm_nt(pre_low, wi[:, part])
    hat = hat_ref[...]
    grad_mixed = norm_back(grad_norm * as_row(attn_gain), hat, inv_ref[...])
    grad_mixed_ref[...] = grad_mixed
    mixed_low = grad_mixed.astype(bf16)
    pair_ref[:span] = outer_low
    pair_ref[span:] = mixed_low
    copies[2 * size].wait()
    context_grad_t = mm_nt(wo[...], mixed_low).astype(bf16)
    for g in range(size):
        groups[behind(me, g, size)] = context_grad_t[g * rows : (g + 1) * rows]
    for s in range(size):
        piece_refs[s][:rows] = groups[s]
    sums_ref[ATTN_GAIN : ATTN_GAIN + 1] = sum_rows(grad_norm * hat)
    sums_ref[ATTN_SHIFT : ATTN_SHIFT + 1] = sum_rows(grad_norm)
    sums_ref[B_OUTPUT : B_OUTPUT + 1] = sum_rows(mixed_low.astype(f32))


def first_products_kernel(blocks, ff_rows):
    def body(left, left_pair, own, pair, *order_and_outs):
        send_ref, keep_ref = order_and_outs[-2:]
        span = own.shape[0] // 2
        me = lax.axis_index("batch")
        core = me & 1
        near = (me >> 1) & 1
        block = left.shape[0] // blocks
        outer_both = jnp.concatenate((own[:span], pair[:span]), axis=0)
        mixed_both = jnp.concatenate((own[span:], pair[span:]), axis=0)
        for ref, side in ((send_ref, 1 - near), (keep_ref, near)):
            for j in range(ref.shape[0]):
                start = (j * 4 + side * 2 + core) * block

                def rows(at, count):
                    part = pl.ds(pl.multiple_of(start + at, 16), count)
                    return jnp.concatenate((left[part], left_pair[part]), axis=1)

                ref[j, :ff_rows] = mm(rows(0, ff_rows), outer_both).astype(bf16)
                ref[j, ff_rows:] = mm(rows(ff_rows, block - ff_rows), mixed_both).astype(bf16)

    return body


def attention_back_kernel(
    probs_ref,
    q_t_ref,
    k_t_ref,
    v_t_ref,
    context_ref,
    sums_in,
    d0,
    d1,
    d2,
    d3,
    order_after,
    e0,
    e1,
    e2,
    e3,
    sums_ref,
    score_grad,
    out_t,
):
    del order_after
    slots = (d0, d1, d2, d3)
    outs = (e0, e1, e2, e3)
    size = len(slots)
    me = lax.axis_index("blk")
    width, row_len = q_t_ref.shape
    span = row_len // size
    grad_t = jnp.concatenate([slot[:width] for slot in slots], axis=1)
    grad = grad_t.T
    for h in range(width // HEAD_DIM):
        cols = slice(h * HEAD_DIM, (h + 1) * HEAD_DIM)
        for s in range(size):
            part = slice(s * span, (s + 1) * span)
            grad_part = grad[part, cols]
            delta = jnp.sum(
                grad_part.astype(f32) * context_ref[part, cols], axis=-1, keepdims=True
            )
            grad_probs = mm(grad_part, v_t_ref[cols])
            score_grad[part] = (probs_ref[h, part].astype(f32) * (grad_probs - delta)).astype(bf16)
        out_t[cols] = (mm_nt(k_t_ref[cols], score_grad[...]) * HEAD_DIM ** (-0.5)).astype(bf16)
        out_t[width + h * HEAD_DIM : width + (h + 1) * HEAD_DIM] = mm(
            q_t_ref[cols], score_grad[...]
        ).astype(bf16)
        out_t[2 * width + h * HEAD_DIM : 2 * width + (h + 1) * HEAD_DIM] = mm(
            grad_t[cols], probs_ref[h]
        ).astype(bf16)
    for s in range(size):
        outs[s][...] = out_t[:, s * span : (s + 1) * span]
    token_sums = mm_nt(jnp.ones((8, row_len), bf16), out_t[...])[0:1]
    sums_ref[...] = sums_in[...]
    for g in range(size):
        cols = slice(g * width, (g + 1) * width)
        sums_ref[B_QUERY : B_QUERY + 1, cols] = jnp.where(me == g, token_sums[:, :width], 0.0)
        sums_ref[B_VALUE : B_VALUE + 1, cols] = jnp.where(me == g, token_sums[:, 2 * width :], 0.0)


def second_products_kernel(
    x0,
    x1,
    x2,
    x3,
    e0,
    e1,
    e2,
    e3,
    i0,
    i1,
    i2,
    i3,
    p0,
    p1,
    p2,
    p3,
    order_after,
    send_ref,
    keep_ref,
    total,
):
    del order_after
    core = lax.axis_index("batch") & 1
    own = e0.shape[0] // 3
    pre_t = jnp.concatenate([ref[own:] for ref in (p0, p1, p2, p3)], axis=1)
    inner_t = jnp.concatenate([ref[...] for ref in (i0, i1, i2, i3)], axis=1)
    x_t = jnp.concatenate([ref[...].T for ref in (x0, x1, x2, x3)], axis=1)
    heads_t = jnp.concatenate([ref[...] for ref in (e0, e1, e2, e3)], axis=1)
    wide = pre_t.shape[0]
    total[:, :wide] = mm_nt(inner_t, pre_t)
    total[:, wide:] = mm_nt(x_t, heads_t)
    pairs, rows, _ = send_ref.shape
    for own, refs in ((0, (keep_ref, send_ref)), (1, (send_ref, keep_ref))):

        @pl.when(core == own)
        def _():
            for b in range(2 * pairs):
                refs[b & 1][b >> 1] = total[b * rows : (b + 1) * rows].astype(bf16)


def grad_in_kernel(
    e0, e1, e2, e3, grad_mixed, w_query, w_key, w_value, out_ref, groups
):
    slots = (e0, e1, e2, e3)
    size = len(slots)
    me = lax.axis_index("blk")
    for s in range(size):
        groups[ahead(me, s, size)] = slots[s][...]
    total = grad_mixed[...]
    own = e0.shape[0] // 3
    for k, weight in enumerate((w_query, w_key, w_value)):
        rows = [groups[g, k * own : (k + 1) * own] for g in range(size)]
        total += mm_nt(jnp.concatenate(rows, axis=0).T, weight[...])
    out_ref[...] = total.astype(bf16)


def split_columns_kernel(keep, got, own_ref, s1, s2, s3, groups):
    outs = (s1, s2, s3)
    size = len(outs) + 1
    me = lax.axis_index("blk")
    total = keep[...].astype(f32) + got[...].astype(f32)
    half = total.shape[0] // 2
    width = total.shape[1] // size
    for g in range(size):
        cols = slice(g * width, (g + 1) * width)
        groups[behind(me, g, size)] = jnp.concatenate((total[:half, cols], total[half:, cols]), axis=1)
    own_ref[...] = groups[0]
    for s in range(1, size):
        outs[s - 1][...] = groups[s].astype(bf16)


def join_rows_kernel(own, r1, r2, r3, first_ref, second_ref, rows):
    total = own[...] + r1[...].astype(f32) + r2[...].astype(f32) + r3[...].astype(f32)
    half, width = total.shape[0], total.shape[1] // 2
    rows[:half] = total[:, :width]
    rows[half:] = total[:, width:]
    ff_rows = first_ref.shape[0]
    first_ref[...] = rows[:ff_rows]
    second_ref[...] = rows[ff_rows : ff_rows + second_ref.shape[0]]


def run_kernel(body, operands, outs, scratch=(), in_hbm=(), in_smem=(), limit=32):
    vmem = pl.BlockSpec(memory_space=pltpu.VMEM)

    def place(k):
        if k in in_hbm:
            return pl.BlockSpec(memory_space=pl.ANY)
        if k in in_smem:
            return pl.BlockSpec(memory_space=pltpu.SMEM)
        return vmem

    return pl.pallas_call(
        body,
        out_shape=[jax.ShapeDtypeStruct(shape, dtype) for shape, dtype in outs],
        in_specs=[place(k) for k in range(len(operands))],
        out_specs=[vmem] * len(outs),
        scratch_shapes=list(scratch),
        compiler_params=pltpu.CompilerParams(vmem_limit_bytes=limit * MIB),
        cost_estimate=pl.CostEstimate(flops=1, bytes_accessed=1, transcendentals=0),
    )(*operands)


def blk_shift(values, step):
    size = lax.axis_size("blk")
    return lax.ppermute(values, "blk", [(i, (i + step) % size) for i in range(size)])


def batch_swap(values, bit):
    size = lax.axis_size("batch")
    return lax.ppermute(values, "batch", [(i, i ^ (1 << bit)) for i in range(size)])


def split_bit(values, dim, bit):
    own = (lax.axis_index("batch") >> bit) & 1
    send = lax.dynamic_index_in_dim(values, 1 - own, dim, keepdims=False)
    keep = lax.dynamic_index_in_dim(values, own, dim, keepdims=False)
    return send, keep


def next_half(keep, got, bit, remaining):
    dim = remaining.index(bit)
    shape = (2,) * len(remaining) + keep.shape[-2:]
    keep_send, keep = split_bit(keep.reshape(shape), dim, bit)
    got_send, got = split_bit(got.reshape(shape), dim, bit)
    send = (keep_send.astype(f32) + got_send.astype(f32)).astype(bf16)
    return send, keep.astype(f32) + got.astype(f32)


def take_bits(keep, got, bits, remaining):
    remaining = list(remaining)
    for bit in bits:
        send, keep = next_half(keep, got, bit, remaining)
        got = batch_swap(send, bit)
        remaining.remove(bit)
    return keep, got


def spread_sum(values):
    for bit in range(lax.axis_size("batch").bit_length() - 1):
        values = values + batch_swap(values, bit)
    out = values
    for step in range(1, lax.axis_size("blk")):
        out = out + blk_shift(values, step)
    return out


def local(
    hidden_in,
    w_query,
    b_query,
    w_key,
    w_value,
    b_value,
    w_output,
    b_output,
    attn_gain,
    attn_shift,
    w_inner,
    b_inner,
    w_outer,
    b_outer,
    ffn_gain,
    ffn_shift,
    text_lengths,
    region_lengths,
    out_grad,
):
    _, span, width = hidden_in.shape
    hidden = w_inner.shape[1]
    size = lax.axis_size("blk")
    blocks = lax.axis_size("batch")
    bits = blocks.bit_length() - 1
    me = lax.axis_index("blk")
    row_len = span * size
    own_heads = HEADS // size
    own_width = own_heads * HEAD_DIM
    steps = range(1, size)
    tokens_f32 = ((span, width), f32)
    tokens_bf16 = ((span, width), bf16)
    sums_shape = ((16, width), f32)

    flat_in = hidden_in[0]
    x_slots = [flat_in] + [blk_shift(flat_in, step) for step in steps]
    own_weights = [
        lax.dynamic_slice_in_dim(weight, me * own_width, own_width, 1)
        for weight in (w_query, w_key, w_value)
    ]
    heads_shape = ((own_width, row_len), bf16)
    *context_slots, probs, q_t, k_t, v_t, context_own = run_kernel(
        attention_kernel,
        [text_lengths, region_lengths] + x_slots + own_weights + [b_query, b_value],
        [((own_width, span), bf16)] * size
        + [((own_heads, row_len, row_len), bf16)]
        + [heads_shape] * 3
        + [((row_len, own_width), f32)],
        [pltpu.VMEM((row_len, width), bf16), pltpu.VMEM((row_len, row_len), f32)],
        in_smem=(0, 1),
    )
    context_slots = context_slots[:1] + [
        blk_shift(context_slots[step], size - step) for step in steps
    ]
    inner_t, attn_hat, attn_inv, context_t = run_kernel(
        mixed_kernel,
        [flat_in] + context_slots + [w_output, b_output, attn_gain, attn_shift],
        [((width, span), bf16), tokens_f32, ((span, 1), f32), ((width, span), bf16)],
        [pltpu.VMEM((size, own_width, span), bf16)],
    )
    inner_slots = [inner_t] + [blk_shift(inner_t, step) for step in steps]
    ff_rows = hidden // blocks
    out_rows = -(-(width // blocks) // 16) * 16
    block = ff_rows + out_rows
    layer_out, left, outer_low, slope, grad_summed, sums = run_kernel(
        forward_kernel(blocks),
        [
            attn_hat,
            context_t,
            w_inner,
            w_outer,
            attn_gain,
            attn_shift,
            b_inner,
            b_outer,
            ffn_gain,
            ffn_shift,
            out_grad[0],
        ],
        [
            tokens_bf16,
            ((blocks * block, span), bf16),
            tokens_bf16,
            ((span, hidden), f32),
            tokens_f32,
            sums_shape,
        ],
        [
            pltpu.VMEM((width, hidden), bf16),
            pltpu.VMEM((hidden, width), bf16),
            pltpu.SemaphoreType.DMA((2 * size,)),
        ],
        in_hbm=(2, 3),
    )
    left_pair = batch_swap(left, 0)
    pair_rows, grad_mixed, sums, *pieces = run_kernel(
        backward_kernel,
        [
            outer_low,
            slope,
            grad_summed,
            attn_hat,
            attn_inv,
            sums,
            w_output,
            w_inner,
            w_outer,
            attn_gain,
        ],
        [((2 * span, width), bf16), tokens_f32, sums_shape]
        + [((own_width + hidden // size, span), bf16)] * size,
        [
            pltpu.VMEM((width, width), bf16),
            pltpu.VMEM((width, hidden), bf16),
            pltpu.VMEM((hidden, width), bf16),
            pltpu.VMEM((size, own_width, span), bf16),
            pltpu.SemaphoreType.DMA((2 * size + 1,)),
        ],
        in_hbm=(6, 7, 8),
    )
    piece_slots = pieces[:1] + [blk_shift(pieces[step], step) for step in steps]
    send, keep = run_kernel(
        first_products_kernel(blocks, ff_rows),
        [left, left_pair, pair_rows, batch_swap(pair_rows, 0)] + inner_slots,
        [((blocks // 4, block, width), bf16)] * 2,
        in_hbm=range(4, 4 + size),
    )
    first_got = batch_swap(send, 1)
    *head_grads, sums = run_kernel(
        attention_back_kernel,
        [probs, q_t, k_t, v_t, context_own, sums] + piece_slots + [send],
        [((3 * own_width, span), bf16)] * size + [sums_shape],
        [pltpu.VMEM((row_len, row_len), bf16), pltpu.VMEM((3 * own_width, row_len), bf16)],
        in_hbm=(6 + size,),
    )
    head_slots = head_grads[:1] + [blk_shift(head_grads[step], size - step) for step in steps]
    remaining = list(range(bits - 1, 1, -1))
    send, keep = next_half(keep, first_got, 2, remaining)
    wide = hidden // size + 3 * own_width
    inner_send, inner_keep = run_kernel(
        second_products_kernel,
        x_slots + head_grads + inner_slots + piece_slots + [send],
        [((blocks // 2, width // blocks, wide), bf16)] * 2,
        [pltpu.VMEM((width, wide), f32)],
        in_hbm=(4 * size,),
    )
    grad_in = run_kernel(
        grad_in_kernel,
        head_slots + [grad_mixed, w_query, w_key, w_value],
        [tokens_bf16],
        [pltpu.VMEM((size, 3 * own_width, span), bf16)],
    )[0]

    remaining.remove(2)
    first_keep, first_got = take_bits(keep, batch_swap(send, 2), range(3, bits), remaining)
    half = (block // 2, 2 * own_width)
    own_part, *sends = run_kernel(
        split_columns_kernel,
        [first_keep.reshape(block, width), first_got.reshape(block, width)],
        [(half, f32)] + [(half, bf16)] * (size - 1),
        [pltpu.VMEM((size,) + half, f32)],
    )
    grad_w_outer, grad_w_output = run_kernel(
        join_rows_kernel,
        [own_part] + [blk_shift(sends[step - 1], step) for step in steps],
        [((ff_rows, own_width), f32), ((width // blocks, own_width), f32)],
        [pltpu.VMEM((block, own_width), f32)],
    )
    order = list(range(bits - 1, 0, -1))
    inner_got = batch_swap(inner_send, 0)
    inner_keep, inner_got = take_bits(inner_keep, inner_got, order[::-1], order)
    inner_sum = inner_keep.astype(f32) + inner_got.astype(f32)
    cuts = [hidden // size + k * own_width for k in range(3)]
    grad_qkv = [inner_sum[:, cut : cut + own_width] for cut in cuts]
    sums = spread_sum(sums)
    return (
        layer_out[None],
        grad_in[None],
        grad_qkv[0],
        sums[B_QUERY],
        grad_qkv[1],
        grad_qkv[2],
        sums[B_VALUE],
        grad_w_output,
        sums[B_OUTPUT],
        sums[ATTN_GAIN],
        sums[ATTN_SHIFT],
        inner_sum[:, : cuts[0]],
        sums[B_INNER : B_INNER + hidden // width].reshape(hidden),
        grad_w_outer,
        sums[B_OUTER],
        sums[FFN_GAIN],
        sums[FFN_SHIFT],
    )


def solution(mesh):
    rows = P("batch", "blk", None)
    tile = P("batch", "blk")
    return jax.shard_map(
        local,
        mesh=mesh,
        in_specs=(rows,) + (P(),) * 15 + (P("batch", None), P("batch", None), rows),
        out_specs=(
            rows,
            rows,
            tile,
            P(),
            tile,
            tile,
            P(),
            tile,
            P(),
            P(),
            P(),
            tile,
            P(),
            tile,
            P(),
            P(),
            P(),
        ),
        check_vma=False,
    )
```

```python
import jax
import jax.numpy as jnp
from jax import lax
from jax.experimental import pallas as pl
from jax.experimental.pallas import tpu as pltpu
from jax.sharding import PartitionSpec as P

HEADS = 12
HEAD_DIM = 64
PAIRS = 4

NORM_EPS = 1e-05
MASKED_SCORE = -1e30
INV_ROOT_TWO = 0.7071067811865476
INV_ROOT_TWO_PI = 0.3989422804014327
MIB = 1024 * 1024

B_OUTER, FFN_GAIN, FFN_SHIFT, ATTN_GAIN, ATTN_SHIFT, B_OUTPUT, B_QUERY, B_VALUE, B_INNER = range(9)

EXTRA = 16

f32 = jnp.float32
bf16 = jnp.bfloat16


def mm(left, right):
    return jnp.dot(left, right, preferred_element_type=f32)


def mm_nt(left, right):
    return lax.dot_general(left, right, (((1,), (1,)), ((), ())), preferred_element_type=f32)


def norm_stats(values_in):
    row_mean = jnp.mean(values_in, axis=-1, keepdims=True)
    centred = values_in - row_mean
    inv_dev = lax.rsqrt(jnp.mean(centred * centred, axis=-1, keepdims=True) + NORM_EPS)
    return centred * inv_dev, inv_dev


def norm_back(scaled, normed, inv_dev):
    centre_term = jnp.mean(scaled, axis=-1, keepdims=True)
    slope_term = jnp.mean(scaled * normed, axis=-1, keepdims=True)
    return inv_dev * (scaled - centre_term - normed * slope_term)


def sum_rows(values):
    return jnp.sum(values, axis=0, keepdims=True)


def as_row(ref):
    return ref[...].astype(f32).reshape(1, -1)


def ahead(me, step, size):
    return lax.rem(me + step, size)


def behind(me, group, size):
    return lax.rem(group - me + size, size)


def lane_window(me, width):
    return pl.multiple_of((me * width) // 128 * 128, 128)


def prep_kernel(
    text,
    region,
    x_ref,
    grad_ref,
    b_query,
    b_value,
    b_output,
    attn_gain,
    attn_shift,
    b_outer,
    ffn_gain,
    ffn_shift,
    b_inner,
    w_query,
    w_key,
    w_value,
    own_weights,
    own_bias,
    mask,
    vecs,
    x_out,
    grad_out,
    windows,
    sems,
):
    me = lax.axis_index("blk")
    row_len = mask.shape[0]
    span = x_ref.shape[0]
    size = row_len // span
    width = own_weights.shape[1] // 3
    model_width = x_ref.shape[1]
    start = lane_window(me, width)
    copies = []
    for k, weight in enumerate((w_query, w_key, w_value)):
        part = weight.at[:, pl.ds(start, windows.shape[2])]
        copies.append(pltpu.make_async_copy(part, windows.at[k], sems.at[k]))
    for copy in copies:
        copy.start()
    x_out[...] = x_ref[...]
    grad_out[...] = grad_ref[...]
    vecs[...] = jnp.zeros(vecs.shape, f32)
    for k, ref in (
        (B_OUTER, b_outer),
        (FFN_GAIN, ffn_gain),
        (FFN_SHIFT, ffn_shift),
        (ATTN_GAIN, attn_gain),
        (ATTN_SHIFT, attn_shift),
        (B_OUTPUT, b_output),
    ):
        vecs[k : k + 1] = as_row(ref)
    hidden_row = as_row(b_inner)
    for k in range(hidden_row.shape[1] // model_width):
        part = slice(k * model_width, (k + 1) * model_width)
        vecs[B_INNER + k : B_INNER + k + 1] = hidden_row[:, part]
    own_bias[...] = jnp.zeros(own_bias.shape, f32)
    for at, ref in ((0, b_query), (2, b_value)):
        row = as_row(ref)
        out = jnp.zeros((1, width), f32)
        for g in range(size):
            out = jnp.where(me == g, row[:, g * width : (g + 1) * width], out)
        own_bias[0:1, at * width : (at + 1) * width] = out

    ends = []
    total = jnp.zeros((1, 1), jnp.int32)
    for k in range(PAIRS):
        total = total + text[:, k : k + 1] + region[:, k : k + 1]
        ends.append(total)

    def segments(dim):
        shape = [1, 1]
        shape[dim] = span
        parts = []
        for s in range(size):
            first = lax.rem(me - s + size, size) * span
            pos = lax.broadcasted_iota(jnp.int32, tuple(shape), dim) + first
            seg = jnp.zeros(tuple(shape), jnp.int32)
            for end in ends:
                seg = seg + (pos >= end).astype(jnp.int32)
            parts.append(seg)
        return jnp.concatenate(parts, axis=dim)

    seg_q = segments(0)
    seg_k = segments(1)
    diagonal = lax.broadcasted_iota(jnp.int32, (row_len, row_len), 0) == lax.broadcasted_iota(
        jnp.int32, (row_len, row_len), 1
    )
    allowed = (seg_q == seg_k) & ((seg_k < PAIRS) | diagonal)
    mask[...] = jnp.where(allowed, 0.0, MASKED_SCORE)
    off = windows.shape[2] - width
    for k in range(3):
        copies[k].wait()
        window = windows[k]
        own_weights[:, k * width : (k + 1) * width] = jnp.where(
            (me * width) % 128 == 0, window[:, :width], window[:, off:]
        )


def attention_kernel(
    x0, x1, x2, x3, own_weights, own_bias, mask, c0, c1, c2, c3, probs_ref, q_t_ref, k_t_ref, v_t_ref, context_ref, x_all
):
    xs = (x0, x1, x2, x3)
    context_refs = (c0, c1, c2, c3)
    size = len(xs)
    span = x0.shape[0]
    width = own_weights.shape[1] // 3
    for s in range(size):
        x_all[s * span : (s + 1) * span] = xs[s][...]
    qkv = (mm(x_all[...], own_weights[...]) + own_bias[0:1]).astype(bf16)
    query = (qkv[:, :width] * HEAD_DIM ** (-0.5)).astype(bf16)
    key = qkv[:, width : 2 * width]
    value = qkv[:, 2 * width :]
    q_t_ref[...] = query.T
    k_t_ref[...] = key.T
    v_t_ref[...] = value.T
    for h in range(width // HEAD_DIM):
        cols = slice(h * HEAD_DIM, (h + 1) * HEAD_DIM)
        for s in range(size):
            part = slice(s * span, (s + 1) * span)
            scores = mm_nt(query[part, cols], key[:, cols]) + mask[part]
            weights = jnp.exp(scores - jnp.max(scores, axis=-1, keepdims=True))
            probs = (weights / jnp.sum(weights, axis=-1, keepdims=True)).astype(bf16)
            probs_ref[h, part] = probs
            context_ref[part, cols] = mm(probs, value[:, cols])
    for s in range(size):
        context_refs[s][...] = context_ref[s * span : (s + 1) * span].astype(bf16).T


def forward_kernel(blocks):
    def body(
        x_ref,
        c0,
        c1,
        c2,
        c3,
        vecs,
        grad_ref,
        w_output,
        w_inner,
        w_outer,
        out_ref,
        left_ref,
        inner_t_ref,
        outer_low_ref,
        slope_t_ref,
        grad_summed_ref,
        hat_ref,
        inv_ref,
        sums_ref,
        wo,
        wi,
        wu,
        groups,
        sems,
    ):
        me = lax.axis_index("blk")
        slots = (c0, c1, c2, c3)
        size = len(slots)
        width, hidden = wi.shape
        step = width
        count = hidden // step
        ff_rows = hidden // blocks
        block = left_ref.shape[0] // blocks
        copies = [pltpu.make_async_copy(w_output, wo, sems.at[2 * count])]
        for k in range(count):
            part = pl.ds(k * step, step)
            copies.append(pltpu.make_async_copy(w_inner.at[:, part], wi.at[:, part], sems.at[2 * k]))
            copies.append(pltpu.make_async_copy(w_outer.at[part], wu.at[part], sems.at[2 * k + 1]))
        for copy in copies:
            copy.start()

        def vec(k):
            return vecs[k : k + 1]

        for s in range(size):
            groups[ahead(me, s, size)] = slots[s][...]
        context_t = jnp.concatenate([groups[g] for g in range(size)], axis=0)
        context = context_t.T
        copies[0].wait()
        mixed = x_ref[...].astype(f32) + mm(context, wo[...]) + vec(B_OUTPUT)
        hat, inv = norm_stats(mixed)
        hat_ref[...] = hat
        inv_ref[...] = inv
        attn_norm = hat * vec(ATTN_GAIN) + vec(ATTN_SHIFT)
        inner_in = attn_norm.astype(bf16)
        outer = jnp.zeros(attn_norm.shape, f32)
        for k in range(count):
            part = slice(k * step, (k + 1) * step)
            copies[1 + 2 * k].wait()
            pre = mm(inner_in, wi[:, part]) + vec(B_INNER + k)
            cdf = 0.5 + 0.5 * lax.erf(pre * INV_ROOT_TWO)
            act = (pre * cdf).astype(bf16)
            slope = cdf + pre * (jnp.exp(-0.5 * pre * pre) * INV_ROOT_TWO_PI)
            copies[2 + 2 * k].wait()
            outer += mm(act, wu[part])
            slope_t_ref[part] = slope.astype(bf16).T
            act_t = act.T
            for j in range(step // ff_rows):
                at = (k * step // ff_rows + j) * block
                left_ref[at : at + ff_rows] = act_t[j * ff_rows : (j + 1) * ff_rows]
        summed = attn_norm + outer + vec(B_OUTER)
        final_hat, final_inv = norm_stats(summed)
        gain = vec(FFN_GAIN)
        upstream = grad_ref[...].astype(f32)
        grad_summed = norm_back(upstream * gain, final_hat, final_inv)
        grad_summed_ref[...] = grad_summed
        outer_low = grad_summed.astype(bf16)
        outer_low_ref[...] = outer_low
        out_ref[...] = (final_hat * gain + vec(FFN_SHIFT)).astype(bf16)
        sums_ref[...] = jnp.zeros(sums_ref.shape, f32)
        sums_ref[B_OUTER : B_OUTER + 1] = sum_rows(outer_low.astype(f32))
        sums_ref[FFN_GAIN : FFN_GAIN + 1] = sum_rows(upstream * final_hat)
        sums_ref[FFN_SHIFT : FFN_SHIFT + 1] = sum_rows(upstream)
        inner_t_ref[...] = inner_in.T
        out_rows = width // blocks
        padded = block - ff_rows
        for b in range(blocks):
            at = b * block + ff_rows
            if padded == out_rows:
                left_ref[at : at + padded] = context_t[b * out_rows : (b + 1) * out_rows]
            else:
                row = lax.broadcasted_iota(jnp.int32, (padded, width), 0)
                col = lax.broadcasted_iota(jnp.int32, (padded, width), 1)
                pick = ((row < out_rows) & (col == row + b * out_rows)).astype(f32).astype(bf16)
                left_ref[at : at + padded] = mm(pick, context_t).astype(bf16)

    return body


def backward_kernel(
    outer_low_ref,
    slope_t_ref,
    grad_summed_ref,
    hat_ref,
    inv_ref,
    inner_t_ref,
    vecs,
    sums_in,
    w_output,
    w_inner,
    w_outer,
    pair_ref,
    grad_mixed_ref,
    g0,
    g1,
    g2,
    g3,
    p0,
    p1,
    p2,
    p3,
    wo,
    wi,
    wu,
    groups,
    sums,
    sems,
):
    width, hidden = wi.shape
    group_refs = (g0, g1, g2, g3)
    piece_refs = (p0, p1, p2, p3)
    size = len(piece_refs)
    me = lax.axis_index("blk")
    step = hidden // size
    rows = width // size
    span = outer_low_ref.shape[0]
    copies = []
    parts = []
    for s in range(size):
        g = ahead(me, s, size)
        part = pl.ds(pl.multiple_of(g * step, 128), step)
        parts.append((g, part))
        copies.append(pltpu.make_async_copy(w_outer.at[part], wu.at[part], sems.at[2 * s]))
        copies.append(
            pltpu.make_async_copy(w_inner.at[:, part], wi.at[:, part], sems.at[2 * s + 1])
        )
    copies.append(pltpu.make_async_copy(w_output, wo, sems.at[2 * size]))
    for copy in copies:
        copy.start()
    sums[...] = sums_in[...]
    outer_low = outer_low_ref[...]
    ones = jnp.ones((8, span), bf16)
    grad_norm_t = jnp.zeros((width, span), f32)
    for s in range(size):
        g, part = parts[s]
        copies[2 * s].wait()
        pre_t = (mm_nt(wu[part], outer_low) * slope_t_ref[part].astype(f32)).astype(bf16)
        piece_refs[s][:step] = pre_t
        sums[pl.ds(B_INNER + g, 1)] = mm_nt(ones, pre_t)[0:1]
        copies[2 * s + 1].wait()
        grad_norm_t += mm(wi[:, part], pre_t)
        piece_refs[s][step:] = inner_t_ref[...]
    grad_norm = grad_norm_t.T + grad_summed_ref[...]
    hat = hat_ref[...]
    grad_mixed = norm_back(grad_norm * vecs[ATTN_GAIN : ATTN_GAIN + 1], hat, inv_ref[...])
    grad_mixed_ref[...] = grad_mixed
    mixed_low = grad_mixed.astype(bf16)
    pair_ref[:span] = outer_low
    pair_ref[span : 2 * span] = mixed_low
    copies[2 * size].wait()
    context_grad_t = mm_nt(wo[...], mixed_low).astype(bf16)
    for g in range(size):
        groups[behind(me, g, size)] = context_grad_t[g * rows : (g + 1) * rows]
    for s in range(size):
        group_refs[s][...] = groups[s]
    sums[ATTN_GAIN : ATTN_GAIN + 1] = sum_rows(grad_norm * hat)
    sums[ATTN_SHIFT : ATTN_SHIFT + 1] = sum_rows(grad_norm)
    sums[B_OUTPUT : B_OUTPUT + 1] = sum_rows(mixed_low.astype(f32))
    pair_ref[2 * span :] = sums[...].astype(bf16)


def first_products_kernel(blocks, ff_rows):
    def body(left, left_pair, own, pair, send_ref, keep_ref):
        span = (own.shape[0] - EXTRA) // 2
        me = lax.axis_index("batch")
        core = me & 1
        near = (me >> 1) & 1
        block = left.shape[0] // blocks
        outer_both = jnp.concatenate((own[:span], pair[:span]), axis=0)
        mixed_both = jnp.concatenate((own[span : 2 * span], pair[span : 2 * span]), axis=0)
        sums = (own[2 * span :].astype(f32) + pair[2 * span :].astype(f32)).astype(bf16)
        for ref, side in ((send_ref, 1 - near), (keep_ref, near)):
            count = (ref.shape[0] - EXTRA) // block
            for j in range(count):
                start = (j * 4 + side * 2 + core) * block
                at = j * block

                def rows(first, many):
                    part = pl.ds(pl.multiple_of(start + first, 16), many)
                    return jnp.concatenate((left[part], left_pair[part]), axis=1)

                ref[at : at + ff_rows] = mm(rows(0, ff_rows), outer_both).astype(bf16)
                ref[at + ff_rows : at + block] = mm(
                    rows(ff_rows, block - ff_rows), mixed_both
                ).astype(bf16)
            ref[count * block :] = sums

    return body


def halve_kernel(block, bit, waits):
    def body(keep_in, got, *rest):
        send_ref, keep_ref = rest[waits:]
        own = (lax.axis_index("batch") >> bit) & 1
        count = (send_ref.shape[0] - EXTRA) // block
        for ref, side in ((send_ref, 1 - own), (keep_ref, own)):
            for j in range(count):
                part = pl.ds(pl.multiple_of((2 * j + side) * block, 16), block)
                total = keep_in[part].astype(f32) + got[part].astype(f32)
                ref[j * block : (j + 1) * block] = total.astype(bf16)
            extra = slice(2 * count * block, 2 * count * block + EXTRA)
            ref[count * block :] = (keep_in[extra].astype(f32) + got[extra].astype(f32)).astype(bf16)

    return body


def attention_back_kernel(
    probs_ref,
    q_t_ref,
    k_t_ref,
    v_t_ref,
    context_ref,
    d0,
    d1,
    d2,
    d3,
    order_after,
    e0,
    e1,
    e2,
    e3,
    token_sums,
    score_grad,
    out_t,
):
    del order_after
    slots = (d0, d1, d2, d3)
    outs = (e0, e1, e2, e3)
    size = len(slots)
    width, row_len = q_t_ref.shape
    span = row_len // size
    grad_t = jnp.concatenate([slot[...] for slot in slots], axis=1)
    grad = grad_t.T
    for h in range(width // HEAD_DIM):
        cols = slice(h * HEAD_DIM, (h + 1) * HEAD_DIM)
        for s in range(size):
            part = slice(s * span, (s + 1) * span)
            grad_part = grad[part, cols]
            delta = jnp.sum(
                grad_part.astype(f32) * context_ref[part, cols], axis=-1, keepdims=True
            )
            grad_probs = mm(grad_part, v_t_ref[cols])
            score_grad[part] = (probs_ref[h, part].astype(f32) * (grad_probs - delta)).astype(bf16)
        out_t[cols] = (mm_nt(k_t_ref[cols], score_grad[...]) * HEAD_DIM ** (-0.5)).astype(bf16)
        out_t[width + h * HEAD_DIM : width + (h + 1) * HEAD_DIM] = mm(
            q_t_ref[cols], score_grad[...]
        ).astype(bf16)
        out_t[2 * width + h * HEAD_DIM : 2 * width + (h + 1) * HEAD_DIM] = mm(
            grad_t[cols], probs_ref[h]
        ).astype(bf16)
    for s in range(size):
        outs[s][...] = out_t[:, s * span : (s + 1) * span]
    token_sums[...] = mm_nt(jnp.ones((8, row_len), bf16), out_t[...])


def second_products_kernel(
    x0,
    x1,
    x2,
    x3,
    e0,
    e1,
    e2,
    e3,
    p0,
    p1,
    p2,
    p3,
    token_sums,
    order_after,
    send_ref,
    keep_ref,
    total,
):
    del order_after
    core = lax.axis_index("batch") & 1
    pieces = (p0, p1, p2, p3)
    half = p0.shape[0] // 2
    pre_t = jnp.concatenate([ref[:half] for ref in pieces], axis=1)
    inner_t = jnp.concatenate([ref[half:] for ref in pieces], axis=1)
    x_t = jnp.concatenate([ref[...].T for ref in (x0, x1, x2, x3)], axis=1)
    heads_t = jnp.concatenate([ref[...] for ref in (e0, e1, e2, e3)], axis=1)
    wide = pre_t.shape[0]
    total[:, :wide] = mm_nt(inner_t, pre_t)
    total[:, wide:] = mm_nt(x_t, heads_t)
    blocks = lax.axis_size("batch")
    rows = total.shape[0] // blocks
    padded = (send_ref.shape[0] - EXTRA) // (blocks // 2)
    for own, refs in ((0, (keep_ref, send_ref)), (1, (send_ref, keep_ref))):

        @pl.when(core == own)
        def _():
            for b in range(blocks):
                at = (b >> 1) * padded
                if padded != rows:
                    refs[b & 1][at : at + padded] = jnp.zeros((padded, total.shape[1]), bf16)
                refs[b & 1][at : at + rows] = total[b * rows : (b + 1) * rows].astype(bf16)

    for ref in (send_ref, keep_ref):
        last = (blocks // 2) * padded
        ref[last:, :wide] = jnp.zeros((EXTRA, wide), bf16)
        ref[last : last + 8, wide:] = token_sums[...].astype(bf16)
        ref[last + 8 :, wide:] = jnp.zeros((EXTRA - 8, total.shape[1] - wide), bf16)


def grad_in_kernel(
    e0, e1, e2, e3, grad_mixed, w_query, w_key, w_value, order_after, out_ref, groups, weights, sems
):
    del order_after
    slots = (e0, e1, e2, e3)
    size = len(slots)
    me = lax.axis_index("blk")
    copies = [
        pltpu.make_async_copy(weight, weights.at[k], sems.at[k])
        for k, weight in enumerate((w_query, w_key, w_value))
    ]
    for copy in copies:
        copy.start()
    for s in range(size):
        groups[ahead(me, s, size)] = slots[s][...]
    total = grad_mixed[...]
    own = e0.shape[0] // 3
    for k in range(3):
        rows = [groups[g, k * own : (k + 1) * own] for g in range(size)]
        part = jnp.concatenate(rows, axis=0).T
        copies[k].wait()
        total += mm_nt(part, weights[k])
    out_ref[...] = total.astype(bf16)


def split_columns_kernel(keep, got, order_after, own_ref, s1, s2, s3, groups):
    del order_after
    outs = (s1, s2, s3)
    size = len(outs) + 1
    me = lax.axis_index("blk")
    total = keep[...].astype(f32) + got[...].astype(f32)
    last = total.shape[0] - EXTRA
    half = last // 2
    width = total.shape[1] // size
    extra = jnp.concatenate((total[last:, : 2 * width], total[last:, 2 * width :]), axis=0)
    for g in range(size):
        cols = slice(g * width, (g + 1) * width)
        slot = behind(me, g, size)
        groups[slot, :half] = jnp.concatenate((total[:half, cols], total[half:last, cols]), axis=1)
    own_ref[:half] = groups[0]
    own_ref[half:] = extra
    for s in range(1, size):
        outs[s - 1][:half] = groups[s].astype(bf16)
        outs[s - 1][half:] = extra.astype(bf16)


def join_rows_kernel(own, r1, r2, r3, first_ref, second_ref, *rest):
    sum_refs, (rows,) = rest[:-1], rest[-1:]
    total = own[...] + r1[...].astype(f32) + r2[...].astype(f32) + r3[...].astype(f32)
    half, width = total.shape[0] - 2 * EXTRA, total.shape[1] // 2
    rows[:half] = total[:half, :width]
    rows[half:] = total[:half, width:]
    ff_rows = first_ref.shape[0]
    first_ref[...] = rows[:ff_rows]
    second_ref[...] = rows[ff_rows : ff_rows + second_ref.shape[0]]
    sums = jnp.concatenate((total[half : half + EXTRA], total[half + EXTRA :]), axis=1)
    for ref, k in zip(sum_refs[:-1], (B_OUTER, FFN_GAIN, FFN_SHIFT, ATTN_GAIN, ATTN_SHIFT, B_OUTPUT)):
        ref[...] = sums[k]
    model_width = sums.shape[1]
    for k in range(sum_refs[-1].shape[0] // model_width):
        sum_refs[-1][k * model_width : (k + 1) * model_width] = sums[B_INNER + k]


def last_sum_kernel(keep, got, inner_ref, q_ref, k_ref, v_ref, late_ref):
    total = keep[...].astype(f32) + got[...].astype(f32)
    rows, wide = inner_ref.shape
    own = q_ref.shape[1]
    inner_ref[...] = total[:rows, :wide]
    for k, ref in enumerate((q_ref, k_ref, v_ref)):
        ref[...] = total[:rows, wide + k * own : wide + (k + 1) * own]
    last = total.shape[0] - EXTRA
    late_ref[...] = total[last : last + 8, wide:]


def late_kernel(l0, l1, l2, l3, query_ref, value_ref, groups):
    slots = (l0, l1, l2, l3)
    size = len(slots)
    me = lax.axis_index("blk")
    for s in range(size):
        groups[lax.rem(me - s + size, size)] = slots[s][...]
    own = l0.shape[1] // 3
    for ref, at in ((query_ref, 0), (value_ref, 2)):
        row = [groups[g, 0:1, at * own : (at + 1) * own] for g in range(size)]
        ref[...] = jnp.concatenate(row, axis=1)[0]


def run_kernel(body, operands, outs, scratch=(), in_hbm=(), limit=8):
    vmem = pl.BlockSpec(memory_space=pltpu.VMEM)
    hbm = pl.BlockSpec(memory_space=pltpu.HBM)
    anywhere = pl.BlockSpec(memory_space=pl.ANY)

    def place(k):
        if k - len(operands) in in_hbm:
            return anywhere
        return hbm if k in in_hbm else vmem

    return pl.pallas_call(
        body,
        out_shape=[jax.ShapeDtypeStruct(shape, dtype) for shape, dtype in outs],
        in_specs=[place(k) for k in range(len(operands))],
        out_specs=[vmem] * len(outs),
        scratch_shapes=list(scratch),
        compiler_params=pltpu.CompilerParams(vmem_limit_bytes=limit * MIB),
        cost_estimate=pl.CostEstimate(flops=1, bytes_accessed=1, transcendentals=0),
    )(*operands)


def blk_shift(values, step):
    size = lax.axis_size("blk")
    return lax.ppermute(values, "blk", [(i, (i + step) % size) for i in range(size)])


def batch_swap(values, bit):
    size = lax.axis_size("batch")
    return lax.ppermute(values, "batch", [(i, i ^ (1 << bit)) for i in range(size)])


def halve(keep, got, block, bit, after=()):
    count = (keep.shape[0] - EXTRA) // block // 2
    shape = ((count * block + EXTRA, keep.shape[1]), bf16)
    return run_kernel(
        halve_kernel(block, bit, len(after)),
        [keep, got, *after],
        [shape, shape],
        in_hbm=[-1 - k for k in range(len(after))],
    )


def local(
    hidden_in,
    w_query,
    b_query,
    w_key,
    w_value,
    b_value,
    w_output,
    b_output,
    attn_gain,
    attn_shift,
    w_inner,
    b_inner,
    w_outer,
    b_outer,
    ffn_gain,
    ffn_shift,
    text_lengths,
    region_lengths,
    out_grad,
):
    _, span, width = hidden_in.shape
    hidden = w_inner.shape[1]
    size = lax.axis_size("blk")
    blocks = lax.axis_size("batch")
    bits = blocks.bit_length() - 1
    row_len = span * size
    own_heads = HEADS // size
    own_width = own_heads * HEAD_DIM
    steps = range(1, size)
    tokens_f32 = ((span, width), f32)
    tokens_bf16 = ((span, width), bf16)
    row = ((width,), f32)

    flat_in = hidden_in[0]
    x_slots = [blk_shift(flat_in, step) for step in steps]
    own_weights, own_bias, mask, vecs, x_own, grad_own = run_kernel(
        prep_kernel,
        [
            text_lengths,
            region_lengths,
            flat_in,
            out_grad[0],
            b_query,
            b_value,
            b_output,
            attn_gain,
            attn_shift,
            b_outer,
            ffn_gain,
            ffn_shift,
            b_inner,
            w_query,
            w_key,
            w_value,
        ],
        [
            ((width, 3 * own_width), bf16),
            ((8, 3 * own_width), f32),
            ((row_len, row_len), f32),
            ((EXTRA, width), f32),
            tokens_bf16,
            tokens_bf16,
        ],
        [pltpu.VMEM((3, width, 256), bf16), pltpu.SemaphoreType.DMA((3,))],
        in_hbm=(13, 14, 15),
    )
    x_slots = [x_own] + x_slots
    heads_shape = ((own_width, row_len), bf16)
    *context_slots, probs, q_t, k_t, v_t, context_own = run_kernel(
        attention_kernel,
        x_slots + [own_weights, own_bias, mask],
        [((own_width, span), bf16)] * size
        + [((own_heads, row_len, row_len), bf16)]
        + [heads_shape] * 3
        + [((row_len, own_width), f32)],
        [pltpu.VMEM((row_len, width), bf16)],
        limit=14,
    )
    context_slots = context_slots[:1] + [
        blk_shift(context_slots[step], size - step) for step in steps
    ]
    ff_rows = hidden // blocks
    rows = -(-(width // blocks) // 16) * 16
    block = ff_rows + rows

    def weight_scratch():
        return [
            pltpu.VMEM((width, width), bf16),
            pltpu.VMEM((width, hidden), bf16),
            pltpu.VMEM((hidden, width), bf16),
            pltpu.VMEM((size, own_width, span), bf16),
        ]

    layer_out, left, inner_t, outer_low, slope_t, grad_summed, attn_hat, attn_inv, sums = run_kernel(
        forward_kernel(blocks),
        [x_own] + context_slots + [vecs, grad_own, w_output, w_inner, w_outer],
        [
            tokens_bf16,
            ((blocks * block, span), bf16),
            ((width, span), bf16),
            tokens_bf16,
            ((hidden, span), bf16),
            tokens_f32,
            tokens_f32,
            ((span, 1), f32),
            ((EXTRA, width), f32),
        ],
        weight_scratch() + [pltpu.SemaphoreType.DMA((2 * (hidden // width) + 1,))],
        in_hbm=(7, 8, 9),
        limit=22,
    )
    left_pair = batch_swap(left, 0)
    pair_rows, grad_mixed, *pieces = run_kernel(
        backward_kernel,
        [
            outer_low,
            slope_t,
            grad_summed,
            attn_hat,
            attn_inv,
            inner_t,
            vecs,
            sums,
            w_output,
            w_inner,
            w_outer,
        ],
        [((2 * span + EXTRA, width), bf16), tokens_f32]
        + [((own_width, span), bf16)] * size
        + [((hidden // size + width, span), bf16)] * size,
        weight_scratch()
        + [pltpu.VMEM((EXTRA, width), f32), pltpu.SemaphoreType.DMA((2 * size + 1,))],
        in_hbm=(8, 9, 10),
        limit=22,
    )
    context_grads, pieces = pieces[:size], pieces[size:]
    context_grads = context_grads[:1] + [blk_shift(context_grads[step], step) for step in steps]
    send, keep = run_kernel(
        first_products_kernel(blocks, ff_rows),
        [left, left_pair, pair_rows, batch_swap(pair_rows, 0)],
        [((blocks // 4 * block + EXTRA, width), bf16)] * 2,
        limit=12,
    )
    got = batch_swap(send, 1)
    piece_slots = pieces[:1] + [blk_shift(pieces[step], step) for step in steps]
    *head_grads, token_sums = run_kernel(
        attention_back_kernel,
        [probs, q_t, k_t, v_t, context_own] + context_grads + [send],
        [((3 * own_width, span), bf16)] * size + [((8, 3 * own_width), f32)],
        [pltpu.VMEM((row_len, row_len), bf16), pltpu.VMEM((3 * own_width, row_len), bf16)],
        in_hbm=(-1,),
    )
    head_slots = head_grads[:1] + [blk_shift(head_grads[step], size - step) for step in steps]
    for bit in range(2, bits):
        send, keep = halve(keep, got, block, bit)
        got = batch_swap(send, bit)
    wide = hidden // size + 3 * own_width
    inner_send, inner_keep = run_kernel(
        second_products_kernel,
        x_slots + head_grads + piece_slots + [token_sums, send],
        [((blocks // 2 * rows + EXTRA, wide), bf16)] * 2,
        [pltpu.VMEM((width, wide), f32)],
        in_hbm=(-1,),
        limit=16,
    )
    inner_got = batch_swap(inner_send, 0)
    inner_send, inner_keep = halve(inner_keep, inner_got, rows, 1)
    inner_got = batch_swap(inner_send, 1)
    message = (block // 2 + 2 * EXTRA, 2 * own_width)
    own_part, *sends = run_kernel(
        split_columns_kernel,
        [keep, got, inner_send],
        [(message, f32)] + [(message, bf16)] * (size - 1),
        [pltpu.VMEM((size, block // 2, 2 * own_width), f32)],
        in_hbm=(-1,),
    )
    parts = [blk_shift(sends[step - 1], step) for step in steps]
    grad_in = run_kernel(
        grad_in_kernel,
        head_slots + [grad_mixed, w_query, w_key, w_value, sends[0]],
        [tokens_bf16],
        [
            pltpu.VMEM((size, 3 * own_width, span), bf16),
            pltpu.VMEM((3, width, width), bf16),
            pltpu.SemaphoreType.DMA((3,)),
        ],
        in_hbm=(5, 6, 7, -1),
        limit=10,
    )[0]
    for bit in range(2, bits):
        inner_send, inner_keep = halve(inner_keep, inner_got, rows, bit, [sends[0]])
        inner_got = batch_swap(inner_send, bit)
    out_rows = width // blocks
    own_cols = ((out_rows, own_width), f32)
    grad_w_inner, *grad_qkv, late = run_kernel(
        last_sum_kernel,
        [inner_keep, inner_got],
        [((out_rows, hidden // size), f32)] + [own_cols] * 3 + [((8, 3 * own_width), f32)],
    )
    grad_w_outer, grad_w_output, *sums = run_kernel(
        join_rows_kernel,
        [own_part] + parts,
        [((ff_rows, own_width), f32), own_cols] + [row] * 6 + [((hidden,), f32)],
        [pltpu.VMEM((block, own_width), f32)],
    )
    grad_b_query, grad_b_value = run_kernel(
        late_kernel,
        [late] + [blk_shift(late, step) for step in steps],
        [row] * 2,
        [pltpu.VMEM((size, 8, 3 * own_width), f32)],
    )
    return (
        layer_out[None],
        grad_in[None],
        grad_qkv[0],
        grad_b_query,
        grad_qkv[1],
        grad_qkv[2],
        grad_b_value,
        grad_w_output,
        sums[B_OUTPUT],
        sums[ATTN_GAIN],
        sums[ATTN_SHIFT],
        grad_w_inner,
        sums[6],
        grad_w_outer,
        sums[B_OUTER],
        sums[FFN_GAIN],
        sums[FFN_SHIFT],
    )


def solution(mesh):
    rows = P("batch", "blk", None)
    tile = P("batch", "blk")
    return jax.shard_map(
        local,
        mesh=mesh,
        in_specs=(rows,) + (P(),) * 15 + (P("batch", None), P("batch", None), rows),
        out_specs=(
            rows,
            rows,
            tile,
            P(),
            tile,
            tile,
            P(),
            tile,
            P(),
            P(),
            P(),
            tile,
            P(),
            tile,
            P(),
            P(),
            P(),
        ),
        check_vma=False,
    )
```

```python
import jax
import jax.numpy as jnp
from jax import lax
from jax.experimental import pallas as pl
from jax.experimental.pallas import tpu as pltpu
from jax.sharding import PartitionSpec as P

HEADS = 12
HEAD_DIM = 64
PAIRS = 4

NORM_EPS = 1e-05
MASKED_SCORE = -1e30
INV_ROOT_TWO = 0.7071067811865476
INV_ROOT_TWO_PI = 0.3989422804014327
MIB = 1024 * 1024

B_OUTER, FFN_GAIN, FFN_SHIFT, ATTN_GAIN, ATTN_SHIFT, B_OUTPUT, B_QUERY, B_VALUE, B_INNER = range(9)

EXTRA = 16

f32 = jnp.float32
bf16 = jnp.bfloat16


def mm(left, right):
    return jnp.dot(left, right, preferred_element_type=f32)


def mm_nt(left, right):
    return lax.dot_general(left, right, (((1,), (1,)), ((), ())), preferred_element_type=f32)


def norm_stats(values_in):
    row_mean = jnp.mean(values_in, axis=-1, keepdims=True)
    centred = values_in - row_mean
    inv_dev = lax.rsqrt(jnp.mean(centred * centred, axis=-1, keepdims=True) + NORM_EPS)
    return centred * inv_dev, inv_dev


def norm_back(scaled, normed, inv_dev):
    centre_term = jnp.mean(scaled, axis=-1, keepdims=True)
    slope_term = jnp.mean(scaled * normed, axis=-1, keepdims=True)
    return inv_dev * (scaled - centre_term - normed * slope_term)


def sum_rows(values):
    return jnp.sum(values, axis=0, keepdims=True)


def as_row(ref):
    return ref[...].astype(f32).reshape(1, -1)


def ahead(me, step, size):
    return lax.rem(me + step, size)


def behind(me, group, size):
    return lax.rem(group - me + size, size)


def lane_window(me, width):
    return pl.multiple_of((me * width) // 128 * 128, 128)


def prep_kernel(
    text,
    region,
    x_ref,
    grad_ref,
    b_query,
    b_value,
    b_output,
    attn_gain,
    attn_shift,
    b_outer,
    ffn_gain,
    ffn_shift,
    b_inner,
    w_query,
    w_key,
    w_value,
    w_inner,
    w_outer,
    own_weights,
    own_bias,
    mask,
    vecs,
    x_out,
    grad_out,
    inner_out,
    outer_out,
    inner_t,
    outer_t,
    windows,
    sems,
):
    me = lax.axis_index("blk")
    row_len = mask.shape[0]
    span = x_ref.shape[0]
    size = row_len // span
    width = own_weights.shape[1] // 3
    model_width = x_ref.shape[1]
    start = lane_window(me, width)
    copies = []
    for k, weight in enumerate((w_query, w_key, w_value)):
        part = weight.at[:, pl.ds(start, windows.shape[2])]
        copies.append(pltpu.make_async_copy(part, windows.at[k], sems.at[k]))
    copies.append(pltpu.make_async_copy(w_inner, inner_out, sems.at[3]))
    copies.append(pltpu.make_async_copy(w_outer, outer_out, sems.at[4]))
    for copy in copies:
        copy.start()
    x_out[...] = x_ref[...]
    grad_out[...] = grad_ref[...]
    vecs[...] = jnp.zeros(vecs.shape, f32)
    for k, ref in (
        (B_OUTER, b_outer),
        (FFN_GAIN, ffn_gain),
        (FFN_SHIFT, ffn_shift),
        (ATTN_GAIN, attn_gain),
        (ATTN_SHIFT, attn_shift),
        (B_OUTPUT, b_output),
    ):
        vecs[k : k + 1] = as_row(ref)
    hidden_row = as_row(b_inner)
    for k in range(hidden_row.shape[1] // model_width):
        part = slice(k * model_width, (k + 1) * model_width)
        vecs[B_INNER + k : B_INNER + k + 1] = hidden_row[:, part]
    own_bias[...] = jnp.zeros(own_bias.shape, f32)
    for at, ref in ((0, b_query), (2, b_value)):
        row = as_row(ref)
        out = jnp.zeros((1, width), f32)
        for g in range(size):
            out = jnp.where(me == g, row[:, g * width : (g + 1) * width], out)
        own_bias[0:1, at * width : (at + 1) * width] = out

    ends = []
    total = jnp.zeros((1, 1), jnp.int32)
    for k in range(PAIRS):
        total = total + text[:, k : k + 1] + region[:, k : k + 1]
        ends.append(total)

    def segments(dim):
        shape = [1, 1]
        shape[dim] = span
        parts = []
        for s in range(size):
            first = lax.rem(me - s + size, size) * span
            pos = lax.broadcasted_iota(jnp.int32, tuple(shape), dim) + first
            seg = jnp.zeros(tuple(shape), jnp.int32)
            for end in ends:
                seg = seg + (pos >= end).astype(jnp.int32)
            parts.append(seg)
        return jnp.concatenate(parts, axis=dim)

    seg_q = segments(0)
    seg_k = segments(1)
    diagonal = lax.broadcasted_iota(jnp.int32, (row_len, row_len), 0) == lax.broadcasted_iota(
        jnp.int32, (row_len, row_len), 1
    )
    allowed = (seg_q == seg_k) & ((seg_k < PAIRS) | diagonal)
    mask[...] = jnp.where(allowed, 0.0, MASKED_SCORE)
    off = windows.shape[2] - width
    for k in range(3):
        copies[k].wait()
        window = windows[k]
        own_weights[:, k * width : (k + 1) * width] = jnp.where(
            (me * width) % 128 == 0, window[:, :width], window[:, off:]
        )
    copies[3].wait()
    copies[4].wait()
    for k in range(hidden_row.shape[1] // model_width):
        part = slice(k * model_width, (k + 1) * model_width)
        inner_t[part] = inner_out[:, part].T
        outer_t[:, part] = outer_out[part].T


def attention_kernel(
    x0, x1, x2, x3, own_weights, own_bias, mask, c0, c1, c2, c3, probs_ref, q_t_ref, k_t_ref, v_t_ref, context_ref, x_all
):
    xs = (x0, x1, x2, x3)
    context_refs = (c0, c1, c2, c3)
    size = len(xs)
    span = x0.shape[0]
    width = own_weights.shape[1] // 3
    for s in range(size):
        x_all[s * span : (s + 1) * span] = xs[s][...]
    qkv = (mm(x_all[...], own_weights[...]) + own_bias[0:1]).astype(bf16)
    query = (qkv[:, :width] * HEAD_DIM ** (-0.5)).astype(bf16)
    key = qkv[:, width : 2 * width]
    value = qkv[:, 2 * width :]
    q_t_ref[...] = query.T
    k_t_ref[...] = key.T
    v_t_ref[...] = value.T
    for h in range(width // HEAD_DIM):
        cols = slice(h * HEAD_DIM, (h + 1) * HEAD_DIM)
        for s in range(size):
            part = slice(s * span, (s + 1) * span)
            scores = mm_nt(query[part, cols], key[:, cols]) + mask[part]
            weights = jnp.exp(scores - jnp.max(scores, axis=-1, keepdims=True))
            probs = (weights * (1.0 / jnp.sum(weights, axis=-1, keepdims=True))).astype(bf16)
            probs_ref[h, part] = probs
            context_ref[part, cols] = mm(probs, value[:, cols])
    for s in range(size):
        context_refs[s][...] = context_ref[s * span : (s + 1) * span].astype(bf16).T


def forward_kernel(blocks):
    def body(
        x_ref,
        c0,
        c1,
        c2,
        c3,
        vecs,
        grad_ref,
        w_output,
        w_inner,
        w_outer,
        out_ref,
        left_ref,
        inner_t_ref,
        outer_low_ref,
        slope_ref,
        grad_summed_ref,
        hat_ref,
        inv_ref,
        sums_ref,
        groups,
    ):
        me = lax.axis_index("blk")
        slots = (c0, c1, c2, c3)
        size = len(slots)
        width, hidden = w_inner.shape
        step = width
        count = hidden // step
        ff_rows = hidden // blocks
        block = left_ref.shape[0] // blocks

        def vec(k):
            return vecs[k : k + 1]

        for s in range(size):
            groups[ahead(me, s, size)] = slots[s][...]
        context_t = jnp.concatenate([groups[g] for g in range(size)], axis=0)
        context = context_t.T
        mixed = x_ref[...].astype(f32) + mm(context, w_output[...]) + vec(B_OUTPUT)
        hat, inv = norm_stats(mixed)
        hat_ref[...] = hat
        inv_ref[...] = inv
        attn_norm = hat * vec(ATTN_GAIN) + vec(ATTN_SHIFT)
        inner_in = attn_norm.astype(bf16)
        outer = jnp.zeros(attn_norm.shape, f32)
        cols = [slice(k * step, (k + 1) * step) for k in range(count)]
        following = mm(inner_in, w_inner[:, cols[0]])
        for k in range(count):
            pre = following + vec(B_INNER + k)
            if k + 1 < count:
                following = mm(inner_in, w_inner[:, cols[k + 1]])
            cdf = 0.5 + 0.5 * lax.erf(pre * INV_ROOT_TWO)
            act = (pre * cdf).astype(bf16)
            slope_ref[:, cols[k]] = cdf + pre * (jnp.exp(-0.5 * pre * pre) * INV_ROOT_TWO_PI)
            outer += mm(act, w_outer[cols[k]])
            act_t = act.T
            for j in range(step // ff_rows):
                at = (k * step // ff_rows + j) * block
                left_ref[at : at + ff_rows] = act_t[j * ff_rows : (j + 1) * ff_rows]
        summed = attn_norm + outer + vec(B_OUTER)
        final_hat, final_inv = norm_stats(summed)
        gain = vec(FFN_GAIN)
        upstream = grad_ref[...].astype(f32)
        grad_summed = norm_back(upstream * gain, final_hat, final_inv)
        grad_summed_ref[...] = grad_summed
        outer_low = grad_summed.astype(bf16)
        outer_low_ref[...] = outer_low
        out_ref[...] = (final_hat * gain + vec(FFN_SHIFT)).astype(bf16)
        sums_ref[...] = jnp.zeros(sums_ref.shape, f32)
        sums_ref[B_OUTER : B_OUTER + 1] = sum_rows(outer_low.astype(f32))
        sums_ref[FFN_GAIN : FFN_GAIN + 1] = sum_rows(upstream * final_hat)
        sums_ref[FFN_SHIFT : FFN_SHIFT + 1] = sum_rows(upstream)
        inner_t_ref[...] = inner_in.T
        out_rows = width // blocks
        padded = block - ff_rows
        for b in range(blocks):
            at = b * block + ff_rows
            if padded == out_rows:
                left_ref[at : at + padded] = context_t[b * out_rows : (b + 1) * out_rows]
            else:
                row = lax.broadcasted_iota(jnp.int32, (padded, width), 0)
                col = lax.broadcasted_iota(jnp.int32, (padded, width), 1)
                pick = ((row < out_rows) & (col == row + b * out_rows)).astype(f32).astype(bf16)
                left_ref[at : at + padded] = mm(pick, context_t).astype(bf16)

    return body


def backward_kernel(
    outer_low_ref,
    slope_ref,
    grad_summed_ref,
    hat_ref,
    inv_ref,
    inner_t_ref,
    vecs,
    sums_in,
    w_output,
    w_inner_t,
    w_outer_t,
    pair_ref,
    grad_mixed_ref,
    g0,
    g1,
    g2,
    g3,
    p0,
    p1,
    p2,
    p3,
    groups,
    sums,
):
    hidden, width = w_inner_t.shape
    group_refs = (g0, g1, g2, g3)
    piece_refs = (p0, p1, p2, p3)
    size = len(piece_refs)
    me = lax.axis_index("blk")
    step = hidden // size
    rows = width // size
    span = outer_low_ref.shape[0]
    where = [ahead(me, s, size) for s in range(size)]
    parts = [pl.ds(pl.multiple_of(g * step, 128), step) for g in where]
    sums[...] = sums_in[...]
    outer_low = outer_low_ref[...]
    grad_norm = grad_summed_ref[...]
    following = mm(outer_low, w_outer_t[:, parts[0]])
    for s in range(size):
        pre_low = (following * slope_ref[:, parts[s]]).astype(bf16)
        if s + 1 < size:
            following = mm(outer_low, w_outer_t[:, parts[s + 1]])
        grad_norm += mm(pre_low, w_inner_t[parts[s]])
        piece_refs[s][:step] = pre_low.T
        sums[pl.ds(B_INNER + where[s], 1)] = sum_rows(pre_low.astype(f32))
        piece_refs[s][step:] = inner_t_ref[...]
    hat = hat_ref[...]
    grad_mixed = norm_back(grad_norm * vecs[ATTN_GAIN : ATTN_GAIN + 1], hat, inv_ref[...])
    grad_mixed_ref[...] = grad_mixed
    mixed_low = grad_mixed.astype(bf16)
    pair_ref[:span] = outer_low
    pair_ref[span : 2 * span] = mixed_low
    context_grad_t = mm_nt(w_output[...], mixed_low).astype(bf16)
    for g in range(size):
        groups[behind(me, g, size)] = context_grad_t[g * rows : (g + 1) * rows]
    for s in range(size):
        group_refs[s][...] = groups[s]
    sums[ATTN_GAIN : ATTN_GAIN + 1] = sum_rows(grad_norm * hat)
    sums[ATTN_SHIFT : ATTN_SHIFT + 1] = sum_rows(grad_norm)
    sums[B_OUTPUT : B_OUTPUT + 1] = sum_rows(mixed_low.astype(f32))
    pair_ref[2 * span :] = sums[...].astype(bf16)


def first_products_kernel(blocks, ff_rows):
    def body(left, left_pair, own, pair, send_ref, keep_ref):
        span = (own.shape[0] - EXTRA) // 2
        me = lax.axis_index("batch")
        core = me & 1
        near = (me >> 1) & 1
        block = left.shape[0] // blocks
        outer_both = jnp.concatenate((own[:span], pair[:span]), axis=0)
        mixed_both = jnp.concatenate((own[span : 2 * span], pair[span : 2 * span]), axis=0)
        sums = (own[2 * span :].astype(f32) + pair[2 * span :].astype(f32)).astype(bf16)
        for ref, side in ((send_ref, 1 - near), (keep_ref, near)):
            count = (ref.shape[0] - EXTRA) // block
            for j in range(count):
                start = (j * 4 + side * 2 + core) * block
                at = j * block

                def rows(first, many):
                    part = pl.ds(pl.multiple_of(start + first, 16), many)
                    return jnp.concatenate((left[part], left_pair[part]), axis=1)

                ref[at : at + ff_rows] = mm(rows(0, ff_rows), outer_both).astype(bf16)
                ref[at + ff_rows : at + block] = mm(
                    rows(ff_rows, block - ff_rows), mixed_both
                ).astype(bf16)
            ref[count * block :] = sums

    return body


def halve_kernel(block, bit, waits):
    def body(keep_in, got, *rest):
        send_ref, keep_ref = rest[waits:]
        own = (lax.axis_index("batch") >> bit) & 1
        count = (send_ref.shape[0] - EXTRA) // block
        for ref, side in ((send_ref, 1 - own), (keep_ref, own)):
            for j in range(count):
                part = pl.ds(pl.multiple_of((2 * j + side) * block, 16), block)
                total = keep_in[part].astype(f32) + got[part].astype(f32)
                ref[j * block : (j + 1) * block] = total.astype(bf16)
            extra = slice(2 * count * block, 2 * count * block + EXTRA)
            ref[count * block :] = (keep_in[extra].astype(f32) + got[extra].astype(f32)).astype(bf16)

    return body


def attention_back_kernel(
    probs_ref,
    q_t_ref,
    k_t_ref,
    v_t_ref,
    context_ref,
    d0,
    d1,
    d2,
    d3,
    order_after,
    in1,
    in2,
    in3,
    e0,
    e1,
    e2,
    e3,
    token_sums,
    out1,
    out2,
    out3,
    score_grad,
    out_t,
):
    del order_after, in1, in2, in3, out1, out2, out3
    slots = (d0, d1, d2, d3)
    outs = (e0, e1, e2, e3)
    size = len(slots)
    width, row_len = q_t_ref.shape
    span = row_len // size
    grad_t = jnp.concatenate([slot[...] for slot in slots], axis=1)
    grad = grad_t.T
    for h in range(width // HEAD_DIM):
        cols = slice(h * HEAD_DIM, (h + 1) * HEAD_DIM)
        for s in range(size):
            part = slice(s * span, (s + 1) * span)
            grad_part = grad[part, cols]
            delta = jnp.sum(
                grad_part.astype(f32) * context_ref[part, cols], axis=-1, keepdims=True
            )
            grad_probs = mm(grad_part, v_t_ref[cols])
            score_grad[part] = (probs_ref[h, part].astype(f32) * (grad_probs - delta)).astype(bf16)
        out_t[cols] = (mm_nt(k_t_ref[cols], score_grad[...]) * HEAD_DIM ** (-0.5)).astype(bf16)
        out_t[width + h * HEAD_DIM : width + (h + 1) * HEAD_DIM] = mm(
            q_t_ref[cols], score_grad[...]
        ).astype(bf16)
        out_t[2 * width + h * HEAD_DIM : 2 * width + (h + 1) * HEAD_DIM] = mm(
            grad_t[cols], probs_ref[h]
        ).astype(bf16)
    for s in range(size):
        outs[s][...] = out_t[:, s * span : (s + 1) * span]
    token_sums[...] = mm_nt(jnp.ones((8, row_len), bf16), out_t[...])


def second_products_kernel(
    x0,
    x1,
    x2,
    x3,
    e0,
    e1,
    e2,
    e3,
    p0,
    p1,
    p2,
    p3,
    token_sums,
    order_after,
    send_ref,
    keep_ref,
    total,
):
    del order_after
    core = lax.axis_index("batch") & 1
    pieces = (p0, p1, p2, p3)
    half = p0.shape[0] // 2
    pre_t = jnp.concatenate([ref[:half] for ref in pieces], axis=1)
    inner_t = jnp.concatenate([ref[half:] for ref in pieces], axis=1)
    x_t = jnp.concatenate([ref[...].T for ref in (x0, x1, x2, x3)], axis=1)
    heads_t = jnp.concatenate([ref[...] for ref in (e0, e1, e2, e3)], axis=1)
    wide = pre_t.shape[0]
    total[:, :wide] = mm_nt(inner_t, pre_t)
    total[:, wide:] = mm_nt(x_t, heads_t)
    blocks = lax.axis_size("batch")
    rows = total.shape[0] // blocks
    padded = (send_ref.shape[0] - EXTRA) // (blocks // 2)
    for own, refs in ((0, (keep_ref, send_ref)), (1, (send_ref, keep_ref))):

        @pl.when(core == own)
        def _():
            for b in range(blocks):
                at = (b >> 1) * padded
                if padded != rows:
                    refs[b & 1][at : at + padded] = jnp.zeros((padded, total.shape[1]), bf16)
                refs[b & 1][at : at + rows] = total[b * rows : (b + 1) * rows].astype(bf16)

    for ref in (send_ref, keep_ref):
        last = (blocks // 2) * padded
        ref[last:, :wide] = jnp.zeros((EXTRA, wide), bf16)
        ref[last : last + 8, wide:] = token_sums[...].astype(bf16)
        ref[last + 8 :, wide:] = jnp.zeros((EXTRA - 8, total.shape[1] - wide), bf16)


def grad_in_kernel(
    e0, e1, e2, e3, grad_mixed, w_query, w_key, w_value, order_after, out_ref, groups, weights, sems
):
    del order_after
    slots = (e0, e1, e2, e3)
    size = len(slots)
    me = lax.axis_index("blk")
    copies = [
        pltpu.make_async_copy(weight, weights.at[k], sems.at[k])
        for k, weight in enumerate((w_query, w_key, w_value))
    ]
    for copy in copies:
        copy.start()
    for s in range(size):
        groups[ahead(me, s, size)] = slots[s][...]
    total = grad_mixed[...]
    own = e0.shape[0] // 3
    for k in range(3):
        rows = [groups[g, k * own : (k + 1) * own] for g in range(size)]
        part = jnp.concatenate(rows, axis=0).T
        copies[k].wait()
        total += mm_nt(part, weights[k])
    out_ref[...] = total.astype(bf16)


def split_columns_kernel(keep, got, w0, w1, w2, w3, own_ref, s1, s2, s3, groups):
    del w0, w1, w2, w3
    outs = (s1, s2, s3)
    size = len(outs) + 1
    me = lax.axis_index("blk")
    total = keep[...].astype(f32) + got[...].astype(f32)
    last = total.shape[0] - EXTRA
    half = last // 2
    width = total.shape[1] // size
    extra = jnp.concatenate((total[last:, : 2 * width], total[last:, 2 * width :]), axis=0)
    for g in range(size):
        cols = slice(g * width, (g + 1) * width)
        slot = behind(me, g, size)
        groups[slot, :half] = jnp.concatenate((total[:half, cols], total[half:last, cols]), axis=1)
    own_ref[:half] = groups[0]
    own_ref[half:] = extra
    for s in range(1, size):
        outs[s - 1][:half] = groups[s].astype(bf16)
        outs[s - 1][half:] = extra.astype(bf16)


def join_rows_kernel(own, r1, r2, r3, first_ref, second_ref, *rest):
    sum_refs, (rows,) = rest[:-1], rest[-1:]
    total = own[...] + r1[...].astype(f32) + r2[...].astype(f32) + r3[...].astype(f32)
    half, width = total.shape[0] - 2 * EXTRA, total.shape[1] // 2
    rows[:half] = total[:half, :width]
    rows[half:] = total[:half, width:]
    ff_rows = first_ref.shape[0]
    first_ref[...] = rows[:ff_rows]
    second_ref[...] = rows[ff_rows : ff_rows + second_ref.shape[0]]
    sums = jnp.concatenate((total[half : half + EXTRA], total[half + EXTRA :]), axis=1)
    for ref, k in zip(sum_refs[:-1], (B_OUTER, FFN_GAIN, FFN_SHIFT, ATTN_GAIN, ATTN_SHIFT, B_OUTPUT)):
        ref[...] = sums[k]
    model_width = sums.shape[1]
    for k in range(sum_refs[-1].shape[0] // model_width):
        sum_refs[-1][k * model_width : (k + 1) * model_width] = sums[B_INNER + k]


def last_sum_kernel(keep, got, inner_ref, q_ref, k_ref, v_ref, late_ref):
    total = keep[...].astype(f32) + got[...].astype(f32)
    rows, wide = inner_ref.shape
    own = q_ref.shape[1]
    inner_ref[...] = total[:rows, :wide]
    for k, ref in enumerate((q_ref, k_ref, v_ref)):
        ref[...] = total[:rows, wide + k * own : wide + (k + 1) * own]
    last = total.shape[0] - EXTRA
    late_ref[...] = total[last : last + 8, wide:]


def late_kernel(l0, l1, l2, l3, query_ref, value_ref, groups):
    slots = (l0, l1, l2, l3)
    size = len(slots)
    me = lax.axis_index("blk")
    for s in range(size):
        groups[lax.rem(me - s + size, size)] = slots[s][...]
    own = l0.shape[1] // 3
    for ref, at in ((query_ref, 0), (value_ref, 2)):
        row = [groups[g, 0:1, at * own : (at + 1) * own] for g in range(size)]
        ref[...] = jnp.concatenate(row, axis=1)[0]


def run_kernel(body, operands, outs, scratch=(), in_hbm=(), limit=8, passed=None):
    vmem = pl.BlockSpec(memory_space=pltpu.VMEM)
    hbm = pl.BlockSpec(memory_space=pltpu.HBM)
    anywhere = pl.BlockSpec(memory_space=pl.ANY)

    def place(k):
        if k - len(operands) in in_hbm:
            return anywhere
        return hbm if k in in_hbm else vmem

    return pl.pallas_call(
        body,
        out_shape=[jax.ShapeDtypeStruct(shape, dtype) for shape, dtype in outs],
        in_specs=[place(k) for k in range(len(operands))],
        out_specs=[anywhere if k in (passed or {}).values() else vmem for k in range(len(outs))],
        input_output_aliases=passed or {},
        scratch_shapes=list(scratch),
        compiler_params=pltpu.CompilerParams(vmem_limit_bytes=limit * MIB),
        cost_estimate=pl.CostEstimate(flops=1, bytes_accessed=1, transcendentals=0),
    )(*operands)


def blk_shift(values, step):
    size = lax.axis_size("blk")
    return lax.ppermute(values, "blk", [(i, (i + step) % size) for i in range(size)])


def batch_swap(values, bit):
    size = lax.axis_size("batch")
    return lax.ppermute(values, "batch", [(i, i ^ (1 << bit)) for i in range(size)])


def halve(keep, got, block, bit, after=()):
    count = (keep.shape[0] - EXTRA) // block // 2
    shape = ((count * block + EXTRA, keep.shape[1]), bf16)
    return run_kernel(
        halve_kernel(block, bit, len(after)),
        [keep, got, *after],
        [shape, shape],
        in_hbm=[-1 - k for k in range(len(after))],
    )


def local(
    hidden_in,
    w_query,
    b_query,
    w_key,
    w_value,
    b_value,
    w_output,
    b_output,
    attn_gain,
    attn_shift,
    w_inner,
    b_inner,
    w_outer,
    b_outer,
    ffn_gain,
    ffn_shift,
    text_lengths,
    region_lengths,
    out_grad,
):
    _, span, width = hidden_in.shape
    hidden = w_inner.shape[1]
    size = lax.axis_size("blk")
    blocks = lax.axis_size("batch")
    bits = blocks.bit_length() - 1
    row_len = span * size
    own_heads = HEADS // size
    own_width = own_heads * HEAD_DIM
    steps = range(1, size)
    tokens_f32 = ((span, width), f32)
    tokens_bf16 = ((span, width), bf16)
    row = ((width,), f32)

    flat_in = hidden_in[0]
    x_slots = [blk_shift(flat_in, step) for step in steps]
    own_weights, own_bias, mask, vecs, x_own, grad_own, *ffn_weights = run_kernel(
        prep_kernel,
        [
            text_lengths,
            region_lengths,
            flat_in,
            out_grad[0],
            b_query,
            b_value,
            b_output,
            attn_gain,
            attn_shift,
            b_outer,
            ffn_gain,
            ffn_shift,
            b_inner,
            w_query,
            w_key,
            w_value,
            w_inner,
            w_outer,
        ],
        [
            ((width, 3 * own_width), bf16),
            ((8, 3 * own_width), f32),
            ((row_len, row_len), f32),
            ((EXTRA, width), f32),
            tokens_bf16,
            tokens_bf16,
            ((width, hidden), bf16),
            ((hidden, width), bf16),
            ((hidden, width), bf16),
            ((width, hidden), bf16),
        ],
        [pltpu.VMEM((3, width, 256), bf16), pltpu.SemaphoreType.DMA((5,))],
        in_hbm=(13, 14, 15, 16, 17),
        limit=24,
    )
    x_slots = [x_own] + x_slots
    heads_shape = ((own_width, row_len), bf16)
    *context_slots, probs, q_t, k_t, v_t, context_own = run_kernel(
        attention_kernel,
        x_slots + [own_weights, own_bias, mask],
        [((own_width, span), bf16)] * size
        + [((own_heads, row_len, row_len), bf16)]
        + [heads_shape] * 3
        + [((row_len, own_width), f32)],
        [pltpu.VMEM((row_len, width), bf16)],
        limit=14,
    )
    context_slots = context_slots[:1] + [
        blk_shift(context_slots[step], size - step) for step in steps
    ]
    ff_rows = hidden // blocks
    rows = -(-(width // blocks) // 16) * 16
    block = ff_rows + rows

    layer_out, left, inner_t, outer_low, slope, grad_summed, attn_hat, attn_inv, sums = run_kernel(
        forward_kernel(blocks),
        [x_own] + context_slots + [vecs, grad_own, w_output] + ffn_weights[:2],
        [
            tokens_bf16,
            ((blocks * block, span), bf16),
            ((width, span), bf16),
            tokens_bf16,
            ((span, hidden), f32),
            tokens_f32,
            tokens_f32,
            ((span, 1), f32),
            ((EXTRA, width), f32),
        ],
        [pltpu.VMEM((size, own_width, span), bf16)],
        limit=20,
    )
    left_pair = batch_swap(left, 0)
    pair_rows, grad_mixed, *pieces = run_kernel(
        backward_kernel,
        [
            outer_low,
            slope,
            grad_summed,
            attn_hat,
            attn_inv,
            inner_t,
            vecs,
            sums,
            w_output,
            *ffn_weights[2:],
        ],
        [((2 * span + EXTRA, width), bf16), tokens_f32]
        + [((own_width, span), bf16)] * size
        + [((hidden // size + width, span), bf16)] * size,
        [pltpu.VMEM((size, own_width, span), bf16), pltpu.VMEM((EXTRA, width), f32)],
        limit=20,
    )
    context_grads, pieces = pieces[:size], pieces[size:]
    context_grads = context_grads[:1] + [blk_shift(context_grads[step], step) for step in steps]
    send, keep = run_kernel(
        first_products_kernel(blocks, ff_rows),
        [left, left_pair, pair_rows, batch_swap(pair_rows, 0)],
        [((blocks // 4 * block + EXTRA, width), bf16)] * 2,
        limit=12,
    )
    got = batch_swap(send, 1)
    attn_outs = run_kernel(
        attention_back_kernel,
        [probs, q_t, k_t, v_t, context_own] + context_grads + [send] + pieces[1:],
        [((3 * own_width, span), bf16)] * size
        + [((8, 3 * own_width), f32)]
        + [((hidden // size + width, span), bf16)] * (size - 1),
        [pltpu.VMEM((row_len, row_len), bf16), pltpu.VMEM((3 * own_width, row_len), bf16)],
        in_hbm=(-1, -2, -3, -4),
        passed={6 + size + k: size + 1 + k for k in range(size - 1)},
    )
    head_grads = list(attn_outs[:size])
    token_sums, pieces[1:] = attn_outs[size], attn_outs[size + 1 :]
    piece_slots = pieces[:1] + [blk_shift(pieces[step], step) for step in steps]
    head_slots = head_grads[:1] + [blk_shift(head_grads[step], size - step) for step in steps]
    for bit in range(2, bits):
        send, keep = halve(keep, got, block, bit)
        got = batch_swap(send, bit)
    wide = hidden // size + 3 * own_width
    inner_send, inner_keep = run_kernel(
        second_products_kernel,
        x_slots + head_grads + piece_slots + [token_sums, send],
        [((blocks // 2 * rows + EXTRA, wide), bf16)] * 2,
        [pltpu.VMEM((width, wide), f32)],
        in_hbm=(-1,),
        limit=16,
    )
    inner_got = batch_swap(inner_send, 0)
    inner_send, inner_keep = halve(inner_keep, inner_got, rows, 1, [got])
    inner_got = batch_swap(inner_send, 1)
    message = (block // 2 + 2 * EXTRA, 2 * own_width)
    own_part, *sends = run_kernel(
        split_columns_kernel,
        [keep, got, inner_send] + head_slots[1:],
        [(message, f32)] + [(message, bf16)] * (size - 1),
        [pltpu.VMEM((size, block // 2, 2 * own_width), f32)],
        in_hbm=(-1, -2, -3, -4),
    )
    parts = [blk_shift(sends[step - 1], step) for step in steps]
    grad_in = run_kernel(
        grad_in_kernel,
        head_slots + [grad_mixed, w_query, w_key, w_value, sends[0]],
        [tokens_bf16],
        [
            pltpu.VMEM((size, 3 * own_width, span), bf16),
            pltpu.VMEM((3, width, width), bf16),
            pltpu.SemaphoreType.DMA((3,)),
        ],
        in_hbm=(5, 6, 7, -1),
        limit=10,
    )[0]
    for bit in range(2, bits):
        inner_send, inner_keep = halve(inner_keep, inner_got, rows, bit, [sends[0]])
        inner_got = batch_swap(inner_send, bit)
    out_rows = width // blocks
    own_cols = ((out_rows, own_width), f32)
    grad_w_inner, *grad_qkv, late = run_kernel(
        last_sum_kernel,
        [inner_keep, inner_got],
        [((out_rows, hidden // size), f32)] + [own_cols] * 3 + [((8, 3 * own_width), f32)],
    )
    grad_w_outer, grad_w_output, *sums = run_kernel(
        join_rows_kernel,
        [own_part] + parts,
        [((ff_rows, own_width), f32), own_cols] + [row] * 6 + [((hidden,), f32)],
        [pltpu.VMEM((block, own_width), f32)],
    )
    grad_b_query, grad_b_value = run_kernel(
        late_kernel,
        [late] + [blk_shift(late, step) for step in steps],
        [row] * 2,
        [pltpu.VMEM((size, 8, 3 * own_width), f32)],
    )
    return (
        layer_out[None],
        grad_in[None],
        grad_qkv[0],
        grad_b_query,
        grad_qkv[1],
        grad_qkv[2],
        grad_b_value,
        grad_w_output,
        sums[B_OUTPUT],
        sums[ATTN_GAIN],
        sums[ATTN_SHIFT],
        grad_w_inner,
        sums[6],
        grad_w_outer,
        sums[B_OUTER],
        sums[FFN_GAIN],
        sums[FFN_SHIFT],
    )


def solution(mesh):
    rows = P("batch", "blk", None)
    tile = P("batch", "blk")
    return jax.shard_map(
        local,
        mesh=mesh,
        in_specs=(rows,) + (P(),) * 15 + (P("batch", None), P("batch", None), rows),
        out_specs=(
            rows,
            rows,
            tile,
            P(),
            tile,
            tile,
            P(),
            tile,
            P(),
            P(),
            P(),
            tile,
            P(),
            tile,
            P(),
            P(),
            P(),
        ),
        check_vma=False,
    )
```

```python
import jax
import jax.numpy as jnp
from jax import lax
from jax.experimental import pallas as pl
from jax.experimental.pallas import tpu as pltpu
from jax.sharding import PartitionSpec as P

HEADS = 12
HEAD_DIM = 64
PAIRS = 4

NORM_EPS = 1e-05
MASKED_SCORE = -1e30
INV_ROOT_TWO = 0.7071067811865476
INV_ROOT_TWO_PI = 0.3989422804014327
MIB = 1024 * 1024

B_OUTER, FFN_GAIN, FFN_SHIFT, ATTN_GAIN, ATTN_SHIFT, B_OUTPUT, B_QUERY, B_VALUE, B_INNER = range(9)

EXTRA = 16

f32 = jnp.float32
bf16 = jnp.bfloat16


def mm(left, right):
    return jnp.dot(left, right, preferred_element_type=f32)


def mm_nt(left, right):
    return lax.dot_general(left, right, (((1,), (1,)), ((), ())), preferred_element_type=f32)


def norm_stats(values_in):
    row_mean = jnp.mean(values_in, axis=-1, keepdims=True)
    centred = values_in - row_mean
    inv_dev = lax.rsqrt(jnp.mean(centred * centred, axis=-1, keepdims=True) + NORM_EPS)
    return centred * inv_dev, inv_dev


def norm_back(scaled, normed, inv_dev):
    centre_term = jnp.mean(scaled, axis=-1, keepdims=True)
    slope_term = jnp.mean(scaled * normed, axis=-1, keepdims=True)
    return inv_dev * (scaled - centre_term - normed * slope_term)


def sum_rows(values):
    return jnp.sum(values, axis=0, keepdims=True)


def as_row(ref):
    return ref[...].astype(f32).reshape(1, -1)


def rows_of(width, count):
    return width // 128 * count


def narrow(ref, first, values):
    count = values.shape[0]
    for k in range(values.shape[1] // 128):
        at = first + k * count
        ref[at : at + count] = values[:, k * 128 : (k + 1) * 128]


def widen(ref, first, count, width):
    return jnp.concatenate(
        [ref[first + k * count : first + (k + 1) * count] for k in range(width // 128)], axis=1
    )


def ahead(me, step, size):
    return lax.rem(me + step, size)


def behind(me, group, size):
    return lax.rem(group - me + size, size)


def lane_window(me, width):
    return pl.multiple_of((me * width) // 128 * 128, 128)


def prep_kernel(
    text,
    region,
    x_ref,
    grad_ref,
    b_query,
    b_value,
    b_output,
    attn_gain,
    attn_shift,
    b_outer,
    ffn_gain,
    ffn_shift,
    b_inner,
    w_query,
    w_key,
    w_value,
    w_inner,
    w_outer,
    own_weights,
    own_bias,
    mask,
    vecs,
    x_out,
    grad_out,
    inner_out,
    outer_out,
    windows,
    sems,
):
    me = lax.axis_index("blk")
    row_len = mask.shape[0]
    span = x_ref.shape[0]
    size = row_len // span
    width = own_weights.shape[1] // 3
    model_width = x_ref.shape[1]
    start = lane_window(me, width)
    copies = []
    for k, weight in enumerate((w_query, w_key, w_value)):
        part = weight.at[:, pl.ds(start, windows.shape[2])]
        copies.append(pltpu.make_async_copy(part, windows.at[k], sems.at[k]))
    copies.append(pltpu.make_async_copy(w_inner, inner_out, sems.at[3]))
    copies.append(pltpu.make_async_copy(w_outer, outer_out, sems.at[4]))
    for copy in copies:
        copy.start()
    x_out[...] = x_ref[...]
    grad_out[...] = grad_ref[...]
    vecs[...] = jnp.zeros(vecs.shape, f32)
    for k, ref in (
        (B_OUTER, b_outer),
        (FFN_GAIN, ffn_gain),
        (FFN_SHIFT, ffn_shift),
        (ATTN_GAIN, attn_gain),
        (ATTN_SHIFT, attn_shift),
        (B_OUTPUT, b_output),
    ):
        vecs[k : k + 1] = as_row(ref)
    hidden_row = as_row(b_inner)
    for k in range(hidden_row.shape[1] // model_width):
        part = slice(k * model_width, (k + 1) * model_width)
        vecs[B_INNER + k : B_INNER + k + 1] = hidden_row[:, part]
    own_bias[...] = jnp.zeros(own_bias.shape, f32)
    for at, ref in ((0, b_query), (2, b_value)):
        row = as_row(ref)
        out = jnp.zeros((1, width), f32)
        for g in range(size):
            out = jnp.where(me == g, row[:, g * width : (g + 1) * width], out)
        own_bias[0:1, at * width : (at + 1) * width] = out

    ends = []
    total = jnp.zeros((1, 1), jnp.int32)
    for k in range(PAIRS):
        total = total + text[:, k : k + 1] + region[:, k : k + 1]
        ends.append(total)

    def segments(dim):
        shape = [1, 1]
        shape[dim] = span
        parts = []
        for s in range(size):
            first = lax.rem(me - s + size, size) * span
            pos = lax.broadcasted_iota(jnp.int32, tuple(shape), dim) + first
            seg = jnp.zeros(tuple(shape), jnp.int32)
            for end in ends:
                seg = seg + (pos >= end).astype(jnp.int32)
            parts.append(seg)
        return jnp.concatenate(parts, axis=dim)

    seg_q = segments(0)
    seg_k = segments(1)
    diagonal = lax.broadcasted_iota(jnp.int32, (row_len, row_len), 0) == lax.broadcasted_iota(
        jnp.int32, (row_len, row_len), 1
    )
    allowed = (seg_q == seg_k) & ((seg_k < PAIRS) | diagonal)
    mask[...] = jnp.where(allowed, 0.0, MASKED_SCORE)
    off = windows.shape[2] - width
    for k in range(3):
        copies[k].wait()
        window = windows[k]
        own_weights[:, k * width : (k + 1) * width] = jnp.where(
            (me * width) % 128 == 0, window[:, :width], window[:, off:]
        )
    copies[3].wait()
    copies[4].wait()


def transpose_kernel(w_inner, w_outer, order_after, inner_t, outer_t):
    del order_after
    width, hidden = w_inner.shape
    for k in range(hidden // width):
        part = slice(k * width, (k + 1) * width)
        inner_t[part] = w_inner[:, part].T
        outer_t[:, part] = w_outer[part].T


def attention_kernel(
    x0, x1, x2, x3, own_weights, own_bias, mask, c0, c1, c2, c3, probs_ref, q_t_ref, k_t_ref, v_t_ref, context_ref, x_all
):
    xs = (x0, x1, x2, x3)
    context_refs = (c0, c1, c2, c3)
    size = len(xs)
    span = x0.shape[0]
    width = own_weights.shape[1] // 3
    for s in range(size):
        x_all[s * span : (s + 1) * span] = xs[s][...]
    qkv = (mm(x_all[...], own_weights[...]) + own_bias[0:1]).astype(bf16)
    query = (qkv[:, :width] * HEAD_DIM ** (-0.5)).astype(bf16)
    key = qkv[:, width : 2 * width]
    value = qkv[:, 2 * width :]
    q_t_ref[...] = query.T
    k_t_ref[...] = key.T
    v_t_ref[...] = value.T
    for h in range(width // HEAD_DIM):
        cols = slice(h * HEAD_DIM, (h + 1) * HEAD_DIM)
        for s in range(size):
            part = slice(s * span, (s + 1) * span)
            scores = mm_nt(query[part, cols], key[:, cols]) + mask[part]
            weights = jnp.exp(scores - jnp.max(scores, axis=-1, keepdims=True))
            probs = (weights * (1.0 / jnp.sum(weights, axis=-1, keepdims=True))).astype(bf16)
            probs_ref[h, part] = probs
            context_ref[part, cols] = mm(probs, value[:, cols])
    for s in range(size):
        context_refs[s][...] = context_ref[s * span : (s + 1) * span].astype(bf16).T


def forward_kernel(blocks):
    def body(
        x_ref,
        c0,
        c1,
        c2,
        c3,
        vecs,
        grad_ref,
        w_output,
        w_inner,
        w_outer,
        order_after,
        out_ref,
        left_own,
        left_core,
        left_x,
        inner_t_ref,
        outer_low_ref,
        slope_ref,
        grad_summed_ref,
        hat_ref,
        inv_ref,
        sums_ref,
        groups,
        left,
    ):
        del order_after
        quarter = lax.axis_index("batch") & 3
        me = lax.axis_index("blk")
        slots = (c0, c1, c2, c3)
        size = len(slots)
        width, hidden = w_inner.shape
        step = width
        count = hidden // step
        ff_rows = hidden // blocks
        many = left_own.shape[0]
        block = many // (blocks // 4)

        def left_rows(b, first, values):
            at = (b >> 2) * block + first
            left[jnp.bitwise_xor(quarter, b & 3), at : at + values.shape[0]] = values

        def vec(k):
            return vecs[k : k + 1]

        for s in range(size):
            groups[ahead(me, s, size)] = slots[s][...]
        context_t = jnp.concatenate([groups[g] for g in range(size)], axis=0)
        context = context_t.T
        mixed = x_ref[...].astype(f32) + mm(context, w_output[...]) + vec(B_OUTPUT)
        hat, inv = norm_stats(mixed)
        hat_ref[...] = hat
        inv_ref[...] = inv
        attn_norm = hat * vec(ATTN_GAIN) + vec(ATTN_SHIFT)
        inner_in = attn_norm.astype(bf16)
        outer = jnp.zeros(attn_norm.shape, f32)
        cols = [slice(k * step, (k + 1) * step) for k in range(count)]
        following = mm(inner_in, w_inner[:, cols[0]])
        for k in range(count):
            pre = following + vec(B_INNER + k)
            if k + 1 < count:
                following = mm(inner_in, w_inner[:, cols[k + 1]])
            cdf = 0.5 + 0.5 * lax.erf(pre * INV_ROOT_TWO)
            act = (pre * cdf).astype(bf16)
            slope_ref[:, cols[k]] = cdf + pre * (jnp.exp(-0.5 * pre * pre) * INV_ROOT_TWO_PI)
            outer += mm(act, w_outer[cols[k]])
            act_t = act.T
            for j in range(step // ff_rows):
                left_rows(k * step // ff_rows + j, 0, act_t[j * ff_rows : (j + 1) * ff_rows])
        summed = attn_norm + outer + vec(B_OUTER)
        final_hat, final_inv = norm_stats(summed)
        gain = vec(FFN_GAIN)
        upstream = grad_ref[...].astype(f32)
        grad_summed = norm_back(upstream * gain, final_hat, final_inv)
        grad_summed_ref[...] = grad_summed
        outer_low = grad_summed.astype(bf16)
        outer_low_ref[...] = outer_low
        out_ref[...] = (final_hat * gain + vec(FFN_SHIFT)).astype(bf16)
        sums_ref[...] = jnp.zeros(sums_ref.shape, f32)
        sums_ref[B_OUTER : B_OUTER + 1] = sum_rows(outer_low.astype(f32))
        sums_ref[FFN_GAIN : FFN_GAIN + 1] = sum_rows(upstream * final_hat)
        sums_ref[FFN_SHIFT : FFN_SHIFT + 1] = sum_rows(upstream)
        inner_t_ref[...] = inner_in.T
        out_rows = width // blocks
        padded = block - ff_rows
        for b in range(blocks):
            if padded == out_rows:
                left_rows(b, ff_rows, context_t[b * out_rows : (b + 1) * out_rows])
            else:
                row = lax.broadcasted_iota(jnp.int32, (padded, width), 0)
                col = lax.broadcasted_iota(jnp.int32, (padded, width), 1)
                pick = ((row < out_rows) & (col == row + b * out_rows)).astype(f32).astype(bf16)
                left_rows(b, ff_rows, mm(pick, context_t).astype(bf16))
        left_own[...] = left[0]
        left_core[...] = left[1]
        left_x[:many] = left[2]
        left_x[many:] = left[3]

    return body


def backward_kernel(
    outer_low_ref,
    slope_ref,
    grad_summed_ref,
    hat_ref,
    inv_ref,
    vecs,
    sums_in,
    w_output,
    w_inner_t,
    w_outer_t,
    right_ref,
    grad_mixed_ref,
    p0,
    p1,
    p2,
    p3,
    groups,
    sums,
):
    hidden, width = w_inner_t.shape
    piece_refs = (p0, p1, p2, p3)
    size = len(piece_refs)
    me = lax.axis_index("blk")
    step = hidden // size
    rows = width // size
    span = outer_low_ref.shape[0]
    where = [ahead(me, s, size) for s in range(size)]
    parts = [pl.ds(pl.multiple_of(g * step, 128), step) for g in where]
    sums[...] = sums_in[...]
    outer_low = outer_low_ref[...]
    grad_norm = grad_summed_ref[...]
    following = mm(outer_low, w_outer_t[:, parts[0]])
    for s in range(size):
        pre_low = (following * slope_ref[:, parts[s]]).astype(bf16)
        if s + 1 < size:
            following = mm(outer_low, w_outer_t[:, parts[s + 1]])
        grad_norm += mm(pre_low, w_inner_t[parts[s]])
        piece_refs[s][rows:] = pre_low.T
        sums[pl.ds(B_INNER + where[s], 1)] = sum_rows(pre_low.astype(f32))
    hat = hat_ref[...]
    grad_mixed = norm_back(grad_norm * vecs[ATTN_GAIN : ATTN_GAIN + 1], hat, inv_ref[...])
    grad_mixed_ref[...] = grad_mixed
    mixed_low = grad_mixed.astype(bf16)
    narrow(right_ref, 0, outer_low)
    narrow(right_ref, rows_of(width, span), mixed_low)
    context_grad_t = mm_nt(w_output[...], mixed_low).astype(bf16)
    for g in range(size):
        groups[behind(me, g, size)] = context_grad_t[g * rows : (g + 1) * rows]
    for s in range(size):
        piece_refs[s][:rows] = groups[s]
    sums[ATTN_GAIN : ATTN_GAIN + 1] = sum_rows(grad_norm * hat)
    sums[ATTN_SHIFT : ATTN_SHIFT + 1] = sum_rows(grad_norm)
    sums[B_OUTPUT : B_OUTPUT + 1] = sum_rows(mixed_low.astype(f32))
    narrow(right_ref, 2 * rows_of(width, span), sums[...].astype(bf16))


def pack_kernel(left_core, left_got, right, right_got, *after_and_out):
    out_ref = after_and_out[-1]
    many, size = left_core.shape[0], right.shape[0]
    out_ref[:many] = left_core[...]
    out_ref[many : 2 * many] = left_got[many:]
    out_ref[2 * many : 2 * many + size] = right[...]
    out_ref[2 * many + size :] = right_got[...]


def first_products_kernel(block, ff_rows, span):
    def body(left_own, left_got, right, right_got, packed, send_ref, keep_ref):
        many, size = left_own.shape[0], right.shape[0]
        width = send_ref.shape[1]
        tall = rows_of(width, span)
        own = (lax.axis_index("batch") >> 2) & 1
        lefts = ((left_own, 0), (left_got, 0), (packed, 0), (packed, many))
        rights = ((right, 0), (right_got, 0), (packed, 2 * many), (packed, 2 * many + size))
        outer_low = jnp.concatenate([widen(ref, at, span, width) for ref, at in rights], axis=0)
        mixed_low = jnp.concatenate(
            [widen(ref, at + tall, span, width) for ref, at in rights], axis=0
        )
        sums = widen(*rights[0][:1], 2 * tall, EXTRA, width).astype(f32)
        for ref, at in rights[1:]:
            sums += widen(ref, at + 2 * tall, EXTRA, width).astype(f32)
        for ref, side in ((send_ref, 1 - own), (keep_ref, own)):
            count = (ref.shape[0] - EXTRA) // block
            for j in range(count):

                def rows(first, number):
                    start = (2 * j + side) * block + first
                    return jnp.concatenate(
                        [
                            source[pl.ds(pl.multiple_of(start + at, 16), number)]
                            for source, at in lefts
                        ],
                        axis=1,
                    )

                at = j * block
                ref[at : at + ff_rows] = mm(rows(0, ff_rows), outer_low).astype(bf16)
                ref[at + ff_rows : at + block] = mm(
                    rows(ff_rows, block - ff_rows), mixed_low
                ).astype(bf16)
            ref[count * block :] = sums.astype(bf16)

    return body


def halve_kernel(block, bit, waits):
    def body(keep_in, got, *rest):
        send_ref, keep_ref = rest[waits:]
        own = (lax.axis_index("batch") >> bit) & 1
        count = (send_ref.shape[0] - EXTRA) // block
        for ref, side in ((send_ref, 1 - own), (keep_ref, own)):
            for j in range(count):
                part = pl.ds(pl.multiple_of((2 * j + side) * block, 16), block)
                total = keep_in[part].astype(f32) + got[part].astype(f32)
                ref[j * block : (j + 1) * block] = total.astype(bf16)
            extra = slice(2 * count * block, 2 * count * block + EXTRA)
            ref[count * block :] = (keep_in[extra].astype(f32) + got[extra].astype(f32)).astype(bf16)

    return body


def attention_back_kernel(
    probs_ref,
    q_t_ref,
    k_t_ref,
    v_t_ref,
    context_ref,
    d0,
    d1,
    d2,
    d3,
    e0,
    e1,
    e2,
    e3,
    token_sums,
    score_grad,
    out_t,
):
    slots = (d0, d1, d2, d3)
    outs = (e0, e1, e2, e3)
    size = len(slots)
    width, row_len = q_t_ref.shape
    span = row_len // size
    grad_t = jnp.concatenate([slot[:width] for slot in slots], axis=1)
    grad = grad_t.T
    for h in range(width // HEAD_DIM):
        cols = slice(h * HEAD_DIM, (h + 1) * HEAD_DIM)
        for s in range(size):
            part = slice(s * span, (s + 1) * span)
            grad_part = grad[part, cols]
            delta = jnp.sum(
                grad_part.astype(f32) * context_ref[part, cols], axis=-1, keepdims=True
            )
            grad_probs = mm(grad_part, v_t_ref[cols])
            score_grad[part] = (probs_ref[h, part].astype(f32) * (grad_probs - delta)).astype(bf16)
        out_t[cols] = (mm_nt(k_t_ref[cols], score_grad[...]) * HEAD_DIM ** (-0.5)).astype(bf16)
        out_t[width + h * HEAD_DIM : width + (h + 1) * HEAD_DIM] = mm(
            q_t_ref[cols], score_grad[...]
        ).astype(bf16)
        out_t[2 * width + h * HEAD_DIM : 2 * width + (h + 1) * HEAD_DIM] = mm(
            grad_t[cols], probs_ref[h]
        ).astype(bf16)
    for s in range(size):
        outs[s][...] = out_t[:, s * span : (s + 1) * span]
    token_sums[...] = mm_nt(jnp.ones((8, row_len), bf16), out_t[...])


def second_products_kernel(
    x0,
    x1,
    x2,
    x3,
    e0,
    e1,
    e2,
    e3,
    i0,
    i1,
    i2,
    i3,
    p0,
    p1,
    p2,
    p3,
    token_sums,
    after_first,
    after_second,
    send_ref,
    keep_ref,
    total,
):
    del after_first, after_second
    core = lax.axis_index("batch") & 1
    first = e0.shape[0] // 3
    pre_t = jnp.concatenate([ref[first:] for ref in (p0, p1, p2, p3)], axis=1)
    inner_t = jnp.concatenate([ref[...] for ref in (i0, i1, i2, i3)], axis=1)
    x_t = jnp.concatenate([ref[...].T for ref in (x0, x1, x2, x3)], axis=1)
    heads_t = jnp.concatenate([ref[...] for ref in (e0, e1, e2, e3)], axis=1)
    wide = pre_t.shape[0]
    total[:, :wide] = mm_nt(inner_t, pre_t)
    total[:, wide:] = mm_nt(x_t, heads_t)
    blocks = lax.axis_size("batch")
    rows = total.shape[0] // blocks
    padded = (send_ref.shape[0] - EXTRA) // (blocks // 2)
    for own, refs in ((0, (keep_ref, send_ref)), (1, (send_ref, keep_ref))):

        @pl.when(core == own)
        def _():
            for b in range(blocks):
                at = (b >> 1) * padded
                if padded != rows:
                    refs[b & 1][at : at + padded] = jnp.zeros((padded, total.shape[1]), bf16)
                refs[b & 1][at : at + rows] = total[b * rows : (b + 1) * rows].astype(bf16)

    for ref in (send_ref, keep_ref):
        last = (blocks // 2) * padded
        ref[last:, :wide] = jnp.zeros((EXTRA, wide), bf16)
        ref[last : last + 8, wide:] = token_sums[...].astype(bf16)
        ref[last + 8 :, wide:] = jnp.zeros((EXTRA - 8, total.shape[1] - wide), bf16)


def grad_in_kernel(
    e0, e1, e2, e3, grad_mixed, w_query, w_key, w_value, order_after, out_ref, groups, weights, sems
):
    del order_after
    slots = (e0, e1, e2, e3)
    size = len(slots)
    me = lax.axis_index("blk")
    copies = [
        pltpu.make_async_copy(weight, weights.at[k], sems.at[k])
        for k, weight in enumerate((w_query, w_key, w_value))
    ]
    for copy in copies:
        copy.start()
    for s in range(size):
        groups[ahead(me, s, size)] = slots[s][...]
    total = grad_mixed[...]
    own = e0.shape[0] // 3
    for k in range(3):
        rows = [groups[g, k * own : (k + 1) * own] for g in range(size)]
        part = jnp.concatenate(rows, axis=0).T
        copies[k].wait()
        total += mm_nt(part, weights[k])
    out_ref[...] = total.astype(bf16)


def split_columns_kernel(keep, got, w0, w1, w2, w3, own_ref, s1, s2, s3, groups):
    del w0, w1, w2, w3
    outs = (s1, s2, s3)
    size = len(outs) + 1
    me = lax.axis_index("blk")
    total = keep[...].astype(f32) + got[...].astype(f32)
    last = total.shape[0] - EXTRA
    half = last // 2
    width = total.shape[1] // size
    extra = jnp.concatenate((total[last:, : 2 * width], total[last:, 2 * width :]), axis=0)
    for g in range(size):
        cols = slice(g * width, (g + 1) * width)
        slot = behind(me, g, size)
        groups[slot, :half] = jnp.concatenate((total[:half, cols], total[half:last, cols]), axis=1)
    own_ref[:half] = groups[0]
    own_ref[half:] = extra
    for s in range(1, size):
        outs[s - 1][:half] = groups[s].astype(bf16)
        outs[s - 1][half:] = extra.astype(bf16)


def join_rows_kernel(own, r1, r2, r3, first_ref, second_ref, *rest):
    sum_refs, (rows,) = rest[:-1], rest[-1:]
    total = own[...] + r1[...].astype(f32) + r2[...].astype(f32) + r3[...].astype(f32)
    half, width = total.shape[0] - 2 * EXTRA, total.shape[1] // 2
    rows[:half] = total[:half, :width]
    rows[half:] = total[:half, width:]
    ff_rows = first_ref.shape[0]
    first_ref[...] = rows[:ff_rows]
    second_ref[...] = rows[ff_rows : ff_rows + second_ref.shape[0]]
    sums = jnp.concatenate((total[half : half + EXTRA], total[half + EXTRA :]), axis=1)
    for ref, k in zip(sum_refs[:-1], (B_OUTER, FFN_GAIN, FFN_SHIFT, ATTN_GAIN, ATTN_SHIFT, B_OUTPUT)):
        ref[...] = sums[k]
    model_width = sums.shape[1]
    for k in range(sum_refs[-1].shape[0] // model_width):
        sum_refs[-1][k * model_width : (k + 1) * model_width] = sums[B_INNER + k]


def last_sum_kernel(keep, got, inner_ref, q_ref, k_ref, v_ref, late_ref):
    total = keep[...].astype(f32) + got[...].astype(f32)
    rows, wide = inner_ref.shape
    own = q_ref.shape[1]
    inner_ref[...] = total[:rows, :wide]
    for k, ref in enumerate((q_ref, k_ref, v_ref)):
        ref[...] = total[:rows, wide + k * own : wide + (k + 1) * own]
    last = total.shape[0] - EXTRA
    late_ref[...] = total[last : last + 8, wide:]


def late_kernel(l0, l1, l2, l3, query_ref, value_ref, groups):
    slots = (l0, l1, l2, l3)
    size = len(slots)
    me = lax.axis_index("blk")
    for s in range(size):
        groups[lax.rem(me - s + size, size)] = slots[s][...]
    own = l0.shape[1] // 3
    for ref, at in ((query_ref, 0), (value_ref, 2)):
        row = [groups[g, 0:1, at * own : (at + 1) * own] for g in range(size)]
        ref[...] = jnp.concatenate(row, axis=1)[0]


def run_kernel(body, operands, outs, scratch=(), in_hbm=(), limit=8, fill=0):
    vmem = pl.BlockSpec(memory_space=pltpu.VMEM)
    hbm = pl.BlockSpec(memory_space=pltpu.HBM)
    anywhere = pl.BlockSpec(memory_space=pl.ANY)

    def place(k):
        if k - len(operands) in in_hbm:
            return anywhere
        return hbm if k in in_hbm else vmem

    return pl.pallas_call(
        body,
        out_shape=[jax.ShapeDtypeStruct(shape, dtype) for shape, dtype in outs],
        in_specs=[place(k) for k in range(len(operands))],
        out_specs=[vmem] * len(outs),
        scratch_shapes=list(scratch),
        compiler_params=pltpu.CompilerParams(vmem_limit_bytes=limit * MIB),
        cost_estimate=pl.CostEstimate(
            flops=1 + fill * 10**9, bytes_accessed=1, transcendentals=0
        ),
    )(*operands)


def blk_shift(values, step):
    size = lax.axis_size("blk")
    return lax.ppermute(values, "blk", [(i, (i + step) % size) for i in range(size)])


def batch_swap(values, bits):
    size = lax.axis_size("batch")
    return lax.ppermute(values, "batch", [(i, i ^ bits) for i in range(size)])


def halve(keep, got, block, bit, after=()):
    count = (keep.shape[0] - EXTRA) // block // 2
    shape = ((count * block + EXTRA, keep.shape[1]), bf16)
    return run_kernel(
        halve_kernel(block, bit, len(after)),
        [keep, got, *after],
        [shape, shape],
        in_hbm=[-1 - k for k in range(len(after))],
    )


def local(
    hidden_in,
    w_query,
    b_query,
    w_key,
    w_value,
    b_value,
    w_output,
    b_output,
    attn_gain,
    attn_shift,
    w_inner,
    b_inner,
    w_outer,
    b_outer,
    ffn_gain,
    ffn_shift,
    text_lengths,
    region_lengths,
    out_grad,
):
    _, span, width = hidden_in.shape
    hidden = w_inner.shape[1]
    size = lax.axis_size("blk")
    blocks = lax.axis_size("batch")
    bits = blocks.bit_length() - 1
    row_len = span * size
    own_heads = HEADS // size
    own_width = own_heads * HEAD_DIM
    steps = range(1, size)
    tokens_f32 = ((span, width), f32)
    tokens_bf16 = ((span, width), bf16)
    row = ((width,), f32)

    flat_in = hidden_in[0]
    x_slots = [blk_shift(flat_in, step) for step in steps]
    own_weights, own_bias, mask, vecs, x_own, grad_own, *ffn_weights = run_kernel(
        prep_kernel,
        [
            text_lengths,
            region_lengths,
            flat_in,
            out_grad[0],
            b_query,
            b_value,
            b_output,
            attn_gain,
            attn_shift,
            b_outer,
            ffn_gain,
            ffn_shift,
            b_inner,
            w_query,
            w_key,
            w_value,
            w_inner,
            w_outer,
        ],
        [
            ((width, 3 * own_width), bf16),
            ((8, 3 * own_width), f32),
            ((row_len, row_len), f32),
            ((EXTRA, width), f32),
            tokens_bf16,
            tokens_bf16,
            ((width, hidden), bf16),
            ((hidden, width), bf16),
        ],
        [pltpu.VMEM((3, width, 256), bf16), pltpu.SemaphoreType.DMA((5,))],
        in_hbm=(13, 14, 15, 16, 17),
        limit=24,
    )
    x_slots = [x_own] + x_slots
    heads_shape = ((own_width, row_len), bf16)
    *context_slots, probs, q_t, k_t, v_t, context_own = run_kernel(
        attention_kernel,
        x_slots + [own_weights, own_bias, mask],
        [((own_width, span), bf16)] * size
        + [((own_heads, row_len, row_len), bf16)]
        + [heads_shape] * 3
        + [((row_len, own_width), f32)],
        [pltpu.VMEM((row_len, width), bf16)],
        limit=14,
    )
    ffn_turned = run_kernel(
        transpose_kernel,
        ffn_weights + [q_t],
        [((hidden, width), bf16), ((width, hidden), bf16)],
        in_hbm=(-1,),
        limit=20,
        fill=8,
    )
    context_slots = context_slots[:1] + [
        blk_shift(context_slots[step], size - step) for step in steps
    ]
    ff_rows = hidden // blocks
    rows = -(-(width // blocks) // 16) * 16
    block = ff_rows + rows

    many = blocks // 4 * block
    (
        layer_out,
        left_own,
        left_core,
        left_x,
        inner_t,
        outer_low,
        slope,
        grad_summed,
        attn_hat,
        attn_inv,
        sums,
    ) = run_kernel(
        forward_kernel(blocks),
        [x_own]
        + context_slots
        + [vecs, grad_own, w_output]
        + ffn_weights
        + [ffn_turned[0]],
        [
            tokens_bf16,
            ((many, span), bf16),
            ((many, span), bf16),
            ((2 * many, span), bf16),
            ((width, span), bf16),
            tokens_bf16,
            ((span, hidden), f32),
            tokens_f32,
            tokens_f32,
            ((span, 1), f32),
            ((EXTRA, width), f32),
        ],
        [pltpu.VMEM((size, own_width, span), bf16), pltpu.VMEM((4, many, span), bf16)],
        in_hbm=(-1,),
        limit=20,
    )
    left_got = batch_swap(left_x, 2)
    inner_slots = [inner_t] + [blk_shift(inner_t, step) for step in steps]
    right, grad_mixed, *pieces = run_kernel(
        backward_kernel,
        [
            outer_low,
            slope,
            grad_summed,
            attn_hat,
            attn_inv,
            vecs,
            sums,
            w_output,
            *ffn_turned,
        ],
        [((2 * rows_of(width, span) + rows_of(width, EXTRA), 128), bf16), tokens_f32]
        + [((own_width + hidden // size, span), bf16)] * size,
        [pltpu.VMEM((size, own_width, span), bf16), pltpu.VMEM((EXTRA, width), f32)],
        limit=20,
    )
    right_got = batch_swap(right, 2)
    piece_slots = pieces[:1] + [blk_shift(pieces[step], step) for step in steps]
    packed = run_kernel(
        pack_kernel,
        [left_core, left_got, right, right_got] + piece_slots[1:],
        [((2 * (many + right.shape[0]), span), bf16)],
        in_hbm=(-1, -2, -3),
    )[0]
    send, keep = run_kernel(
        first_products_kernel(block, ff_rows, span),
        [left_own, left_got, right, right_got, batch_swap(packed, 1)],
        [((many // 2 + EXTRA, width), bf16)] * 2,
        limit=14,
    )
    got = batch_swap(send, 4)
    for bit in range(3, bits):
        send, keep = halve(keep, got, block, bit)
        got = batch_swap(send, 1 << bit)
    *head_grads, token_sums = run_kernel(
        attention_back_kernel,
        [probs, q_t, k_t, v_t, context_own] + piece_slots,
        [((3 * own_width, span), bf16)] * size + [((8, 3 * own_width), f32)],
        [pltpu.VMEM((row_len, row_len), bf16), pltpu.VMEM((3 * own_width, row_len), bf16)],
    )
    head_slots = head_grads[:1] + [blk_shift(head_grads[step], size - step) for step in steps]
    wide = hidden // size + 3 * own_width
    inner_send, inner_keep = run_kernel(
        second_products_kernel,
        x_slots + head_grads + inner_slots + piece_slots + [token_sums, got, head_slots[1]],
        [((blocks // 2 * rows + EXTRA, wide), bf16)] * 2,
        [pltpu.VMEM((width, wide), f32)],
        in_hbm=(-1, -2),
        limit=16,
        fill=6,
    )
    inner_got = batch_swap(inner_send, 1)
    inner_send, inner_keep = halve(inner_keep, inner_got, rows, 1)
    inner_got = batch_swap(inner_send, 2)
    message = (block // 2 + 2 * EXTRA, 2 * own_width)
    own_part, *sends = run_kernel(
        split_columns_kernel,
        [keep, got, inner_send] + head_slots[1:],
        [(message, f32)] + [(message, bf16)] * (size - 1),
        [pltpu.VMEM((size, block // 2, 2 * own_width), f32)],
        in_hbm=(-1, -2, -3, -4),
    )
    parts = [blk_shift(sends[step - 1], step) for step in steps]
    grad_in = run_kernel(
        grad_in_kernel,
        head_slots + [grad_mixed, w_query, w_key, w_value, sends[0]],
        [tokens_bf16],
        [
            pltpu.VMEM((size, 3 * own_width, span), bf16),
            pltpu.VMEM((3, width, width), bf16),
            pltpu.SemaphoreType.DMA((3,)),
        ],
        in_hbm=(5, 6, 7, -1),
        limit=10,
        fill=6,
    )[0]
    for bit in range(2, bits):
        inner_send, inner_keep = halve(inner_keep, inner_got, rows, bit, [sends[0]])
        inner_got = batch_swap(inner_send, 1 << bit)
    out_rows = width // blocks
    own_cols = ((out_rows, own_width), f32)
    grad_w_inner, *grad_qkv, late = run_kernel(
        last_sum_kernel,
        [inner_keep, inner_got],
        [((out_rows, hidden // size), f32)] + [own_cols] * 3 + [((8, 3 * own_width), f32)],
    )
    grad_w_outer, grad_w_output, *sums = run_kernel(
        join_rows_kernel,
        [own_part] + parts,
        [((ff_rows, own_width), f32), own_cols] + [row] * 6 + [((hidden,), f32)],
        [pltpu.VMEM((block, own_width), f32)],
    )
    grad_b_query, grad_b_value = run_kernel(
        late_kernel,
        [late] + [blk_shift(late, step) for step in steps],
        [row] * 2,
        [pltpu.VMEM((size, 8, 3 * own_width), f32)],
    )
    return (
        layer_out[None],
        grad_in[None],
        grad_qkv[0],
        grad_b_query,
        grad_qkv[1],
        grad_qkv[2],
        grad_b_value,
        grad_w_output,
        sums[B_OUTPUT],
        sums[ATTN_GAIN],
        sums[ATTN_SHIFT],
        grad_w_inner,
        sums[6],
        grad_w_outer,
        sums[B_OUTER],
        sums[FFN_GAIN],
        sums[FFN_SHIFT],
    )


def solution(mesh):
    rows = P("batch", "blk", None)
    tile = P("batch", "blk")
    return jax.shard_map(
        local,
        mesh=mesh,
        in_specs=(rows,) + (P(),) * 15 + (P("batch", None), P("batch", None), rows),
        out_specs=(
            rows,
            rows,
            tile,
            P(),
            tile,
            tile,
            P(),
            tile,
            P(),
            P(),
            P(),
            tile,
            P(),
            tile,
            P(),
            P(),
            P(),
        ),
        check_vma=False,
    )
```

```python
import jax
import jax.numpy as jnp
from jax import lax
from jax.experimental import pallas as pl
from jax.experimental.pallas import tpu as pltpu
from jax.sharding import PartitionSpec as P

HEADS = 12
HEAD_DIM = 64
PAIRS = 4

NORM_EPS = 1e-05
MASKED_SCORE = -1e30
INV_ROOT_TWO = 0.7071067811865476
INV_ROOT_TWO_PI = 0.3989422804014327
MIB = 1024 * 1024

B_OUTER, FFN_GAIN, FFN_SHIFT, ATTN_GAIN, ATTN_SHIFT, B_OUTPUT, B_QUERY, B_VALUE, B_INNER = range(9)

EXTRA = 16

f32 = jnp.float32
bf16 = jnp.bfloat16


def mm(left, right):
    return jnp.dot(left, right, preferred_element_type=f32)


def mm_nt(left, right):
    return lax.dot_general(left, right, (((1,), (1,)), ((), ())), preferred_element_type=f32)


def norm_stats(values_in):
    row_mean = jnp.mean(values_in, axis=-1, keepdims=True)
    centred = values_in - row_mean
    inv_dev = lax.rsqrt(jnp.mean(centred * centred, axis=-1, keepdims=True) + NORM_EPS)
    return centred * inv_dev, inv_dev


def norm_back(scaled, normed, inv_dev):
    centre_term = jnp.mean(scaled, axis=-1, keepdims=True)
    slope_term = jnp.mean(scaled * normed, axis=-1, keepdims=True)
    return inv_dev * (scaled - centre_term - normed * slope_term)


def sum_rows(values):
    return jnp.sum(values, axis=0, keepdims=True)


def as_row(ref):
    return ref[...].astype(f32).reshape(1, -1)


def rows_of(width, count):
    return width // 128 * count


def narrow(ref, first, values):
    count = values.shape[0]
    for k in range(values.shape[1] // 128):
        at = first + k * count
        ref[at : at + count] = values[:, k * 128 : (k + 1) * 128]


def widen(ref, first, count, width):
    return jnp.concatenate(
        [ref[first + k * count : first + (k + 1) * count] for k in range(width // 128)], axis=1
    )


def ahead(me, step, size):
    return lax.rem(me + step, size)


def behind(me, group, size):
    return lax.rem(group - me + size, size)


def lane_window(me, width):
    return pl.multiple_of((me * width) // 128 * 128, 128)


def prep_kernel(
    text,
    region,
    x_ref,
    grad_ref,
    b_query,
    b_value,
    b_output,
    attn_gain,
    attn_shift,
    b_outer,
    ffn_gain,
    ffn_shift,
    b_inner,
    w_query,
    w_key,
    w_value,
    own_weights,
    own_bias,
    mask,
    vecs,
    x_out,
    grad_out,
    windows,
    sems,
):
    me = lax.axis_index("blk")
    row_len = mask.shape[0]
    span = x_ref.shape[0]
    size = row_len // span
    width = own_weights.shape[1] // 3
    model_width = x_ref.shape[1]
    start = lane_window(me, width)
    copies = []
    for k, weight in enumerate((w_query, w_key, w_value)):
        part = weight.at[:, pl.ds(start, windows.shape[2])]
        copies.append(pltpu.make_async_copy(part, windows.at[k], sems.at[k]))
    for copy in copies:
        copy.start()
    x_out[...] = x_ref[...]
    grad_out[...] = grad_ref[...]
    vecs[...] = jnp.zeros(vecs.shape, f32)
    for k, ref in (
        (B_OUTER, b_outer),
        (FFN_GAIN, ffn_gain),
        (FFN_SHIFT, ffn_shift),
        (ATTN_GAIN, attn_gain),
        (ATTN_SHIFT, attn_shift),
        (B_OUTPUT, b_output),
    ):
        vecs[k : k + 1] = as_row(ref)
    hidden_row = as_row(b_inner)
    for k in range(hidden_row.shape[1] // model_width):
        part = slice(k * model_width, (k + 1) * model_width)
        vecs[B_INNER + k : B_INNER + k + 1] = hidden_row[:, part]
    own_bias[...] = jnp.zeros(own_bias.shape, f32)
    for at, ref in ((0, b_query), (2, b_value)):
        row = as_row(ref)
        out = jnp.zeros((1, width), f32)
        for g in range(size):
            out = jnp.where(me == g, row[:, g * width : (g + 1) * width], out)
        own_bias[0:1, at * width : (at + 1) * width] = out

    ends = []
    total = jnp.zeros((1, 1), jnp.int32)
    for k in range(PAIRS):
        total = total + text[:, k : k + 1] + region[:, k : k + 1]
        ends.append(total)

    def segments(dim):
        shape = [1, 1]
        shape[dim] = span
        parts = []
        for s in range(size):
            first = lax.rem(me - s + size, size) * span
            pos = lax.broadcasted_iota(jnp.int32, tuple(shape), dim) + first
            seg = jnp.zeros(tuple(shape), jnp.int32)
            for end in ends:
                seg = seg + (pos >= end).astype(jnp.int32)
            parts.append(seg)
        return jnp.concatenate(parts, axis=dim)

    seg_q = segments(0)
    seg_k = segments(1)
    diagonal = lax.broadcasted_iota(jnp.int32, (row_len, row_len), 0) == lax.broadcasted_iota(
        jnp.int32, (row_len, row_len), 1
    )
    allowed = (seg_q == seg_k) & ((seg_k < PAIRS) | diagonal)
    mask[...] = jnp.where(allowed, 0.0, MASKED_SCORE)
    off = windows.shape[2] - width
    for k in range(3):
        copies[k].wait()
        window = windows[k]
        own_weights[:, k * width : (k + 1) * width] = jnp.where(
            (me * width) % 128 == 0, window[:, :width], window[:, off:]
        )


def transpose_kernel(
    w_inner, w_outer, qkv, inner_out, outer_out, inner_t, outer_t, q_t, k_t, v_t, sems
):
    copies = [
        pltpu.make_async_copy(w_inner, inner_out, sems.at[0]),
        pltpu.make_async_copy(w_outer, outer_out, sems.at[1]),
    ]
    for copy in copies:
        copy.start()
    own = q_t.shape[0]
    for k, ref in enumerate((q_t, k_t, v_t)):
        ref[...] = qkv[:, k * own : (k + 1) * own].T
    width, hidden = inner_out.shape
    parts = [slice(k * width, (k + 1) * width) for k in range(hidden // width)]
    copies[0].wait()
    for part in parts:
        inner_t[part] = inner_out[:, part].T
    copies[1].wait()
    for part in parts:
        outer_t[:, part] = outer_out[part].T


def attention_kernel(
    x0, x1, x2, x3, own_weights, own_bias, mask, c0, c1, c2, c3, probs_ref, qkv_ref, context_ref, x_all
):
    xs = (x0, x1, x2, x3)
    context_refs = (c0, c1, c2, c3)
    size = len(xs)
    span = x0.shape[0]
    width = own_weights.shape[1] // 3
    for s in range(size):
        x_all[s * span : (s + 1) * span] = xs[s][...]
    qkv = (mm(x_all[...], own_weights[...]) + own_bias[0:1]).astype(bf16)
    query = (qkv[:, :width] * HEAD_DIM ** (-0.5)).astype(bf16)
    key = qkv[:, width : 2 * width]
    value = qkv[:, 2 * width :]
    qkv_ref[:, :width] = query
    qkv_ref[:, width:] = qkv[:, width:]
    tasks = [(h, s) for s in range(size) for h in range(width // HEAD_DIM)]

    def scores_of(task):
        h, s = task
        cols = slice(h * HEAD_DIM, (h + 1) * HEAD_DIM)
        part = slice(s * span, (s + 1) * span)
        return mm_nt(query[part, cols], key[:, cols])

    following = scores_of(tasks[0])
    done = []
    for k, (h, s) in enumerate(tasks):
        part = slice(s * span, (s + 1) * span)
        scores = following + mask[part]
        if k + 1 < len(tasks):
            following = scores_of(tasks[k + 1])
        weights = jnp.exp(scores - jnp.max(scores, axis=-1, keepdims=True))
        probs = (weights * (1.0 / jnp.sum(weights, axis=-1, keepdims=True))).astype(bf16)
        probs_ref[h, part] = probs
        done.append(mm(probs, value[:, h * HEAD_DIM : (h + 1) * HEAD_DIM]))
        if h == width // HEAD_DIM - 1:
            context = jnp.concatenate(done, axis=1)
            context_ref[part] = context
            context_refs[s][...] = context.astype(bf16).T
            done = []


def forward_kernel(blocks):
    def body(
        x_ref,
        c0,
        c1,
        c2,
        c3,
        vecs,
        grad_ref,
        w_output,
        w_inner,
        w_outer,
        order_after,
        out_ref,
        left_own,
        left_core,
        left_x,
        inner_t_ref,
        outer_low_ref,
        slope_ref,
        grad_summed_ref,
        hat_ref,
        inv_ref,
        sums_ref,
        groups,
        left,
    ):
        del order_after
        quarter = lax.axis_index("batch") & 3
        me = lax.axis_index("blk")
        slots = (c0, c1, c2, c3)
        size = len(slots)
        width, hidden = w_inner.shape
        step = width
        count = hidden // step
        ff_rows = hidden // blocks
        many = left_own.shape[0]
        block = many // (blocks // 4)

        def left_rows(b, first, values):
            at = (b >> 2) * block + first
            left[jnp.bitwise_xor(quarter, b & 3), at : at + values.shape[0]] = values

        def vec(k):
            return vecs[k : k + 1]

        for s in range(size):
            groups[ahead(me, s, size)] = slots[s][...]
        context_t = jnp.concatenate([groups[g] for g in range(size)], axis=0)
        context = context_t.T
        mixed = x_ref[...].astype(f32) + mm(context, w_output[...]) + vec(B_OUTPUT)
        hat, inv = norm_stats(mixed)
        hat_ref[...] = hat
        inv_ref[...] = inv
        attn_norm = hat * vec(ATTN_GAIN) + vec(ATTN_SHIFT)
        inner_in = attn_norm.astype(bf16)
        outer = jnp.zeros(attn_norm.shape, f32)
        cols = [slice(k * step, (k + 1) * step) for k in range(count)]
        following = mm(inner_in, w_inner[:, cols[0]])
        for k in range(count):
            pre = following + vec(B_INNER + k)
            if k + 1 < count:
                following = mm(inner_in, w_inner[:, cols[k + 1]])
            cdf = 0.5 + 0.5 * lax.erf(pre * INV_ROOT_TWO)
            act = (pre * cdf).astype(bf16)
            slope_ref[:, cols[k]] = cdf + pre * (jnp.exp(-0.5 * pre * pre) * INV_ROOT_TWO_PI)
            outer += mm(act, w_outer[cols[k]])
            act_t = act.T
            for j in range(step // ff_rows):
                left_rows(k * step // ff_rows + j, 0, act_t[j * ff_rows : (j + 1) * ff_rows])
        summed = attn_norm + outer + vec(B_OUTER)
        final_hat, final_inv = norm_stats(summed)
        gain = vec(FFN_GAIN)
        upstream = grad_ref[...].astype(f32)
        grad_summed = norm_back(upstream * gain, final_hat, final_inv)
        grad_summed_ref[...] = grad_summed
        outer_low = grad_summed.astype(bf16)
        outer_low_ref[...] = outer_low
        out_ref[...] = (final_hat * gain + vec(FFN_SHIFT)).astype(bf16)
        sums_ref[...] = jnp.zeros(sums_ref.shape, f32)
        sums_ref[B_OUTER : B_OUTER + 1] = sum_rows(outer_low.astype(f32))
        sums_ref[FFN_GAIN : FFN_GAIN + 1] = sum_rows(upstream * final_hat)
        sums_ref[FFN_SHIFT : FFN_SHIFT + 1] = sum_rows(upstream)
        inner_t_ref[...] = inner_in.T
        out_rows = width // blocks
        padded = block - ff_rows
        for b in range(blocks):
            if padded == out_rows:
                left_rows(b, ff_rows, context_t[b * out_rows : (b + 1) * out_rows])
            else:
                row = lax.broadcasted_iota(jnp.int32, (padded, width), 0)
                col = lax.broadcasted_iota(jnp.int32, (padded, width), 1)
                pick = ((row < out_rows) & (col == row + b * out_rows)).astype(f32).astype(bf16)
                left_rows(b, ff_rows, mm(pick, context_t).astype(bf16))
        left_own[...] = left[0]
        left_core[...] = left[1]
        left_x[:many] = left[2]
        left_x[many:] = left[3]

    return body


def backward_kernel(
    outer_low_ref,
    slope_ref,
    grad_summed_ref,
    hat_ref,
    inv_ref,
    vecs,
    sums_in,
    w_output,
    w_inner_t,
    w_outer_t,
    i1,
    i2,
    i3,
    right_ref,
    grad_mixed_ref,
    p0,
    p1,
    p2,
    p3,
    groups,
    sums,
):
    del i1, i2, i3
    hidden, width = w_inner_t.shape
    piece_refs = (p0, p1, p2, p3)
    size = len(piece_refs)
    me = lax.axis_index("blk")
    step = hidden // size
    rows = width // size
    span = outer_low_ref.shape[0]
    where = [ahead(me, s, size) for s in range(size)]
    parts = [pl.ds(pl.multiple_of(g * step, 128), step) for g in where]
    sums[...] = sums_in[...]
    outer_low = outer_low_ref[...]
    grad_norm = grad_summed_ref[...]
    following = mm(outer_low, w_outer_t[:, parts[0]])
    for s in range(size):
        pre_low = (following * slope_ref[:, parts[s]]).astype(bf16)
        if s + 1 < size:
            following = mm(outer_low, w_outer_t[:, parts[s + 1]])
        grad_norm += mm(pre_low, w_inner_t[parts[s]])
        piece_refs[s][rows:] = pre_low.T
        sums[pl.ds(B_INNER + where[s], 1)] = sum_rows(pre_low.astype(f32))
    hat = hat_ref[...]
    grad_mixed = norm_back(grad_norm * vecs[ATTN_GAIN : ATTN_GAIN + 1], hat, inv_ref[...])
    grad_mixed_ref[...] = grad_mixed
    mixed_low = grad_mixed.astype(bf16)
    narrow(right_ref, 0, outer_low)
    narrow(right_ref, rows_of(width, span), mixed_low)
    context_grad_t = mm_nt(w_output[...], mixed_low).astype(bf16)
    for g in range(size):
        groups[behind(me, g, size)] = context_grad_t[g * rows : (g + 1) * rows]
    for s in range(size):
        piece_refs[s][:rows] = groups[s]
    sums[ATTN_GAIN : ATTN_GAIN + 1] = sum_rows(grad_norm * hat)
    sums[ATTN_SHIFT : ATTN_SHIFT + 1] = sum_rows(grad_norm)
    sums[B_OUTPUT : B_OUTPUT + 1] = sum_rows(mixed_low.astype(f32))
    narrow(right_ref, 2 * rows_of(width, span), sums[...].astype(bf16))


def pack_kernel(left_core, left_got, right, right_got, *after_and_out):
    out_ref = after_and_out[-1]
    many, size = left_core.shape[0], right.shape[0]
    out_ref[:many] = left_core[...]
    out_ref[many : 2 * many] = left_got[many:]
    out_ref[2 * many : 2 * many + size] = right[...]
    out_ref[2 * many + size :] = right_got[...]


def first_products_kernel(block, ff_rows, span):
    def body(left_own, left_got, right, right_got, packed, send_ref, keep_ref):
        many, size = left_own.shape[0], right.shape[0]
        width = send_ref.shape[1]
        tall = rows_of(width, span)
        own = (lax.axis_index("batch") >> 2) & 1
        lefts = ((left_own, 0), (left_got, 0), (packed, 0), (packed, many))
        rights = ((right, 0), (right_got, 0), (packed, 2 * many), (packed, 2 * many + size))
        outer_low = jnp.concatenate([widen(ref, at, span, width) for ref, at in rights], axis=0)
        mixed_low = jnp.concatenate(
            [widen(ref, at + tall, span, width) for ref, at in rights], axis=0
        )
        sums = widen(*rights[0][:1], 2 * tall, EXTRA, width).astype(f32)
        for ref, at in rights[1:]:
            sums += widen(ref, at + 2 * tall, EXTRA, width).astype(f32)
        for ref, side in ((send_ref, 1 - own), (keep_ref, own)):
            count = (ref.shape[0] - EXTRA) // block
            for j in range(count):

                def rows(first, number):
                    start = (2 * j + side) * block + first
                    return jnp.concatenate(
                        [
                            source[pl.ds(pl.multiple_of(start + at, 16), number)]
                            for source, at in lefts
                        ],
                        axis=1,
                    )

                at = j * block
                ref[at : at + ff_rows] = mm(rows(0, ff_rows), outer_low).astype(bf16)
                ref[at + ff_rows : at + block] = mm(
                    rows(ff_rows, block - ff_rows), mixed_low
                ).astype(bf16)
            ref[count * block :] = sums.astype(bf16)

    return body


def halve_kernel(block, bit, parts):
    def body(keep_in, *rest):
        got, (send_ref, keep_ref) = rest[:parts], rest[-2:]
        own = (lax.axis_index("batch") >> bit) & 1
        count = (send_ref.shape[0] - EXTRA) // block

        def total(part):
            added = jnp.concatenate([ref[part] for ref in got], axis=1).astype(f32)
            return (keep_in[part].astype(f32) + added).astype(bf16)

        extra = total(slice(2 * count * block, 2 * count * block + EXTRA))
        for ref, side in ((send_ref, 1 - own), (keep_ref, own)):
            for j in range(count):
                start = pl.multiple_of((2 * j + side) * block, 16)
                ref[j * block : (j + 1) * block] = total(pl.ds(start, block))
            ref[count * block :] = extra

    return body


def attention_back_kernel(
    probs_ref,
    q_t_ref,
    k_t_ref,
    v_t_ref,
    context_ref,
    d0,
    d1,
    d2,
    d3,
    order_after,
    e0,
    e1,
    e2,
    e3,
    token_sums,
    score_grad,
    out_t,
):
    del order_after
    slots = (d0, d1, d2, d3)
    outs = (e0, e1, e2, e3)
    size = len(slots)
    width, row_len = q_t_ref.shape
    span = row_len // size
    grad_t = jnp.concatenate([slot[:width] for slot in slots], axis=1)
    grad = grad_t.T
    for h in range(width // HEAD_DIM):
        cols = slice(h * HEAD_DIM, (h + 1) * HEAD_DIM)
        for s in range(size):
            part = slice(s * span, (s + 1) * span)
            grad_part = grad[part, cols]
            delta = jnp.sum(
                grad_part.astype(f32) * context_ref[part, cols], axis=-1, keepdims=True
            )
            grad_probs = mm(grad_part, v_t_ref[cols])
            score_grad[part] = (probs_ref[h, part].astype(f32) * (grad_probs - delta)).astype(bf16)
        out_t[cols] = (mm_nt(k_t_ref[cols], score_grad[...]) * HEAD_DIM ** (-0.5)).astype(bf16)
        out_t[width + h * HEAD_DIM : width + (h + 1) * HEAD_DIM] = mm(
            q_t_ref[cols], score_grad[...]
        ).astype(bf16)
        out_t[2 * width + h * HEAD_DIM : 2 * width + (h + 1) * HEAD_DIM] = mm(
            grad_t[cols], probs_ref[h]
        ).astype(bf16)
    for s in range(size):
        outs[s][...] = out_t[:, s * span : (s + 1) * span]
    token_sums[...] = mm_nt(jnp.ones((8, row_len), bf16), out_t[...])


def second_products_kernel(
    x0,
    x1,
    x2,
    x3,
    e0,
    e1,
    e2,
    e3,
    i0,
    i1,
    i2,
    i3,
    p0,
    p1,
    p2,
    p3,
    token_sums,
    send_first,
    send_second,
    keep_ref,
    total,
    send_ref,
):
    core = lax.axis_index("batch") & 1
    first = e0.shape[0] // 3
    pre_t = jnp.concatenate([ref[first:] for ref in (p0, p1, p2, p3)], axis=1)
    inner_t = jnp.concatenate([ref[...] for ref in (i0, i1, i2, i3)], axis=1)
    x_t = jnp.concatenate([ref[...].T for ref in (x0, x1, x2, x3)], axis=1)
    heads_t = jnp.concatenate([ref[...] for ref in (e0, e1, e2, e3)], axis=1)
    wide = pre_t.shape[0]
    total[:, :wide] = mm_nt(inner_t, pre_t)
    total[:, wide:] = mm_nt(x_t, heads_t)
    blocks = lax.axis_size("batch")
    rows = total.shape[0] // blocks
    padded = (send_ref.shape[0] - EXTRA) // (blocks // 2)
    for own, refs in ((0, (keep_ref, send_ref)), (1, (send_ref, keep_ref))):

        @pl.when(core == own)
        def _():
            for b in range(blocks):
                at = (b >> 1) * padded
                if padded != rows:
                    refs[b & 1][at : at + padded] = jnp.zeros((padded, total.shape[1]), bf16)
                refs[b & 1][at : at + rows] = total[b * rows : (b + 1) * rows].astype(bf16)

    for ref in (send_ref, keep_ref):
        last = (blocks // 2) * padded
        ref[last:, :wide] = jnp.zeros((EXTRA, wide), bf16)
        ref[last : last + 8, wide:] = token_sums[...].astype(bf16)
        ref[last + 8 :, wide:] = jnp.zeros((EXTRA - 8, total.shape[1] - wide), bf16)
    send_first[...] = send_ref[:, :wide]
    send_second[...] = send_ref[:, wide:]


def grad_in_kernel(
    e0, e1, e2, e3, grad_mixed, w_query, w_key, w_value, order_after, out_ref, groups, weights, sems
):
    del order_after
    slots = (e0, e1, e2, e3)
    size = len(slots)
    me = lax.axis_index("blk")
    copies = [
        pltpu.make_async_copy(weight, weights.at[k], sems.at[k])
        for k, weight in enumerate((w_query, w_key, w_value))
    ]
    for copy in copies:
        copy.start()
    for s in range(size):
        groups[ahead(me, s, size)] = slots[s][...]
    total = grad_mixed[...]
    own = e0.shape[0] // 3
    for k in range(3):
        rows = [groups[g, k * own : (k + 1) * own] for g in range(size)]
        part = jnp.concatenate(rows, axis=0).T
        copies[k].wait()
        total += mm_nt(part, weights[k])
    out_ref[...] = total.astype(bf16)


def split_columns_kernel(keep, got, order_after, own_ref, s1, s2, s3, groups):
    del order_after
    outs = (s1, s2, s3)
    size = len(outs) + 1
    me = lax.axis_index("blk")
    total = keep[...].astype(f32) + got[...].astype(f32)
    last = total.shape[0] - EXTRA
    half = last // 2
    width = total.shape[1] // size
    extra = jnp.concatenate((total[last:, : 2 * width], total[last:, 2 * width :]), axis=0)
    for g in range(size):
        cols = slice(g * width, (g + 1) * width)
        slot = behind(me, g, size)
        groups[slot, :half] = jnp.concatenate((total[:half, cols], total[half:last, cols]), axis=1)
    own_ref[:half] = groups[0]
    own_ref[half:] = extra
    for s in range(1, size):
        outs[s - 1][:half] = groups[s].astype(bf16)
        outs[s - 1][half:] = extra.astype(bf16)


def join_rows_kernel(own, r1, r2, r3, first_ref, second_ref, *rest):
    sum_refs, (rows,) = rest[:-1], rest[-1:]
    total = own[...] + r1[...].astype(f32) + r2[...].astype(f32) + r3[...].astype(f32)
    half, width = total.shape[0] - 2 * EXTRA, total.shape[1] // 2
    rows[:half] = total[:half, :width]
    rows[half:] = total[:half, width:]
    ff_rows = first_ref.shape[0]
    first_ref[...] = rows[:ff_rows]
    second_ref[...] = rows[ff_rows : ff_rows + second_ref.shape[0]]
    sums = jnp.concatenate((total[half : half + EXTRA], total[half + EXTRA :]), axis=1)
    for ref, k in zip(sum_refs[:-1], (B_OUTER, FFN_GAIN, FFN_SHIFT, ATTN_GAIN, ATTN_SHIFT, B_OUTPUT)):
        ref[...] = sums[k]
    model_width = sums.shape[1]
    for k in range(sum_refs[-1].shape[0] // model_width):
        sum_refs[-1][k * model_width : (k + 1) * model_width] = sums[B_INNER + k]


def last_sum_kernel(keep, got, order_after, inner_ref, q_ref, k_ref, v_ref, late_ref):
    del order_after
    total = keep[...].astype(f32) + got[...].astype(f32)
    rows, wide = inner_ref.shape
    own = q_ref.shape[1]
    inner_ref[...] = total[:rows, :wide]
    for k, ref in enumerate((q_ref, k_ref, v_ref)):
        ref[...] = total[:rows, wide + k * own : wide + (k + 1) * own]
    last = total.shape[0] - EXTRA
    late_ref[...] = total[last : last + 8, wide:]


def late_kernel(l0, l1, l2, l3, query_ref, value_ref, groups):
    slots = (l0, l1, l2, l3)
    size = len(slots)
    me = lax.axis_index("blk")
    for s in range(size):
        groups[lax.rem(me - s + size, size)] = slots[s][...]
    own = l0.shape[1] // 3
    for ref, at in ((query_ref, 0), (value_ref, 2)):
        row = [groups[g, 0:1, at * own : (at + 1) * own] for g in range(size)]
        ref[...] = jnp.concatenate(row, axis=1)[0]


def run_kernel(body, operands, outs, scratch=(), in_hbm=(), limit=8, fill=0):
    vmem = pl.BlockSpec(memory_space=pltpu.VMEM)
    hbm = pl.BlockSpec(memory_space=pltpu.HBM)
    anywhere = pl.BlockSpec(memory_space=pl.ANY)

    def place(k):
        if k - len(operands) in in_hbm:
            return anywhere
        return hbm if k in in_hbm else vmem

    return pl.pallas_call(
        body,
        out_shape=[jax.ShapeDtypeStruct(shape, dtype) for shape, dtype in outs],
        in_specs=[place(k) for k in range(len(operands))],
        out_specs=[vmem] * len(outs),
        scratch_shapes=list(scratch),
        compiler_params=pltpu.CompilerParams(vmem_limit_bytes=limit * MIB),
        cost_estimate=pl.CostEstimate(
            flops=1 + fill * 10**9, bytes_accessed=1, transcendentals=0
        ),
    )(*operands)


def blk_shift(values, step):
    size = lax.axis_size("blk")
    return lax.ppermute(values, "blk", [(i, (i + step) % size) for i in range(size)])


def batch_swap(values, bits):
    size = lax.axis_size("batch")
    return lax.ppermute(values, "batch", [(i, i ^ bits) for i in range(size)])


def halve(keep, got, block, bit, after=()):
    got = got if isinstance(got, list) else [got]
    count = (keep.shape[0] - EXTRA) // block // 2
    shape = ((count * block + EXTRA, keep.shape[1]), bf16)
    return run_kernel(
        halve_kernel(block, bit, len(got)),
        [keep, *got, *after],
        [shape, shape],
        in_hbm=[-1 - k for k in range(len(after))],
    )


def local(
    hidden_in,
    w_query,
    b_query,
    w_key,
    w_value,
    b_value,
    w_output,
    b_output,
    attn_gain,
    attn_shift,
    w_inner,
    b_inner,
    w_outer,
    b_outer,
    ffn_gain,
    ffn_shift,
    text_lengths,
    region_lengths,
    out_grad,
):
    _, span, width = hidden_in.shape
    hidden = w_inner.shape[1]
    size = lax.axis_size("blk")
    blocks = lax.axis_size("batch")
    bits = blocks.bit_length() - 1
    row_len = span * size
    own_heads = HEADS // size
    own_width = own_heads * HEAD_DIM
    steps = range(1, size)
    tokens_f32 = ((span, width), f32)
    tokens_bf16 = ((span, width), bf16)
    row = ((width,), f32)

    flat_in = hidden_in[0]
    x_slots = [blk_shift(flat_in, step) for step in steps]
    own_weights, own_bias, mask, vecs, x_own, grad_own = run_kernel(
        prep_kernel,
        [
            text_lengths,
            region_lengths,
            flat_in,
            out_grad[0],
            b_query,
            b_value,
            b_output,
            attn_gain,
            attn_shift,
            b_outer,
            ffn_gain,
            ffn_shift,
            b_inner,
            w_query,
            w_key,
            w_value,
        ],
        [
            ((width, 3 * own_width), bf16),
            ((8, 3 * own_width), f32),
            ((row_len, row_len), f32),
            ((EXTRA, width), f32),
            tokens_bf16,
            tokens_bf16,
        ],
        [pltpu.VMEM((3, width, 256), bf16), pltpu.SemaphoreType.DMA((3,))],
        in_hbm=(13, 14, 15),
    )
    x_slots = [x_own] + x_slots
    *context_slots, probs, qkv, context_own = run_kernel(
        attention_kernel,
        x_slots + [own_weights, own_bias, mask],
        [((own_width, span), bf16)] * size
        + [((own_heads, row_len, row_len), bf16)]
        + [((row_len, 3 * own_width), bf16), ((row_len, own_width), f32)],
        [pltpu.VMEM((row_len, width), bf16)],
        limit=14,
    )
    turned = run_kernel(
        transpose_kernel,
        [w_inner, w_outer, qkv],
        [
            ((width, hidden), bf16),
            ((hidden, width), bf16),
            ((hidden, width), bf16),
            ((width, hidden), bf16),
        ]
        + [((own_width, row_len), bf16)] * 3,
        [pltpu.SemaphoreType.DMA((2,))],
        in_hbm=(0, 1),
        limit=24,
        fill=8,
    )
    ffn_weights, ffn_turned, (q_t, k_t, v_t) = turned[:2], turned[2:4], turned[4:]
    context_slots = context_slots[:1] + [
        blk_shift(context_slots[step], size - step) for step in steps
    ]
    ff_rows = hidden // blocks
    rows = -(-(width // blocks) // 16) * 16
    block = ff_rows + rows

    many = blocks // 4 * block
    (
        layer_out,
        left_own,
        left_core,
        left_x,
        inner_t,
        outer_low,
        slope,
        grad_summed,
        attn_hat,
        attn_inv,
        sums,
    ) = run_kernel(
        forward_kernel(blocks),
        [x_own]
        + context_slots
        + [vecs, grad_own, w_output]
        + [*ffn_weights, ffn_turned[0]],
        [
            tokens_bf16,
            ((many, span), bf16),
            ((many, span), bf16),
            ((2 * many, span), bf16),
            ((width, span), bf16),
            tokens_bf16,
            ((span, hidden), f32),
            tokens_f32,
            tokens_f32,
            ((span, 1), f32),
            ((EXTRA, width), f32),
        ],
        [pltpu.VMEM((size, own_width, span), bf16), pltpu.VMEM((4, many, span), bf16)],
        in_hbm=(-1,),
        limit=20,
    )
    left_got = batch_swap(left_x, 2)
    inner_slots = [inner_t] + [blk_shift(inner_t, step) for step in steps]
    right, grad_mixed, *pieces = run_kernel(
        backward_kernel,
        [
            outer_low,
            slope,
            grad_summed,
            attn_hat,
            attn_inv,
            vecs,
            sums,
            w_output,
            *ffn_turned,
            *inner_slots[1:],
        ],
        [((2 * rows_of(width, span) + rows_of(width, EXTRA), 128), bf16), tokens_f32]
        + [((own_width + hidden // size, span), bf16)] * size,
        [pltpu.VMEM((size, own_width, span), bf16), pltpu.VMEM((EXTRA, width), f32)],
        in_hbm=(-1, -2, -3),
        limit=20,
    )
    right_got = batch_swap(right, 2)
    piece_slots = pieces[:1] + [blk_shift(pieces[step], step) for step in steps]
    packed = run_kernel(
        pack_kernel,
        [left_core, left_got, right, right_got] + piece_slots[1:-1],
        [((2 * (many + right.shape[0]), span), bf16)],
        in_hbm=(-1, -2),
    )[0]
    send, keep = run_kernel(
        first_products_kernel(block, ff_rows, span),
        [left_own, left_got, right, right_got, batch_swap(packed, 1)],
        [((many // 2 + EXTRA, width), bf16)] * 2,
        limit=14,
    )
    got = batch_swap(send, 4)
    for bit in range(3, bits):
        send, keep = halve(keep, got, block, bit)
        got = batch_swap(send, 1 << bit)
    *head_grads, token_sums = run_kernel(
        attention_back_kernel,
        [probs, q_t, k_t, v_t, context_own] + piece_slots + [send],
        [((3 * own_width, span), bf16)] * size + [((8, 3 * own_width), f32)],
        [pltpu.VMEM((row_len, row_len), bf16), pltpu.VMEM((3 * own_width, row_len), bf16)],
        in_hbm=(-1,),
    )
    head_slots = head_grads[:1] + [blk_shift(head_grads[step], size - step) for step in steps]
    wide = hidden // size + 3 * own_width
    tall = blocks // 2 * rows + EXTRA
    first_send, second_send, inner_keep = run_kernel(
        second_products_kernel,
        x_slots + head_grads + inner_slots + piece_slots + [token_sums],
        [
            ((tall, hidden // size), bf16),
            ((tall, 3 * own_width), bf16),
            ((tall, wide), bf16),
        ],
        [pltpu.VMEM((width, wide), f32), pltpu.VMEM((tall, wide), bf16)],
        limit=16,
    )
    inner_got = [batch_swap(first_send, 1), batch_swap(second_send, 1)]
    inner_send, inner_keep = halve(inner_keep, inner_got, rows, 1, [got] + head_slots[1:-1])
    inner_got = batch_swap(inner_send, 2)
    message = (block // 2 + 2 * EXTRA, 2 * own_width)
    own_part, *sends = run_kernel(
        split_columns_kernel,
        [keep, got, inner_send],
        [(message, f32)] + [(message, bf16)] * (size - 1),
        [pltpu.VMEM((size, block // 2, 2 * own_width), f32)],
        in_hbm=(-1,),
    )
    parts = [blk_shift(sends[step - 1], step) for step in steps]
    grad_in = run_kernel(
        grad_in_kernel,
        head_slots + [grad_mixed, w_query, w_key, w_value, sends[0]],
        [tokens_bf16],
        [
            pltpu.VMEM((size, 3 * own_width, span), bf16),
            pltpu.VMEM((3, width, width), bf16),
            pltpu.SemaphoreType.DMA((3,)),
        ],
        in_hbm=(5, 6, 7, -1),
        limit=10,
        fill=6,
    )[0]
    for bit in range(2, bits):
        inner_send, inner_keep = halve(inner_keep, inner_got, rows, bit, [sends[0]])
        inner_got = batch_swap(inner_send, 1 << bit)
    out_rows = width // blocks
    own_cols = ((out_rows, own_width), f32)
    grad_w_inner, *grad_qkv, late = run_kernel(
        last_sum_kernel,
        [inner_keep, inner_got, grad_in],
        [((out_rows, hidden // size), f32)] + [own_cols] * 3 + [((8, 3 * own_width), f32)],
        in_hbm=(-1,),
    )
    grad_w_outer, grad_w_output, *sums = run_kernel(
        join_rows_kernel,
        [own_part] + parts,
        [((ff_rows, own_width), f32), own_cols] + [row] * 6 + [((hidden,), f32)],
        [pltpu.VMEM((block, own_width), f32)],
    )
    grad_b_query, grad_b_value = run_kernel(
        late_kernel,
        [late] + [blk_shift(late, step) for step in steps],
        [row] * 2,
        [pltpu.VMEM((size, 8, 3 * own_width), f32)],
    )
    return (
        layer_out[None],
        grad_in[None],
        grad_qkv[0],
        grad_b_query,
        grad_qkv[1],
        grad_qkv[2],
        grad_b_value,
        grad_w_output,
        sums[B_OUTPUT],
        sums[ATTN_GAIN],
        sums[ATTN_SHIFT],
        grad_w_inner,
        sums[6],
        grad_w_outer,
        sums[B_OUTER],
        sums[FFN_GAIN],
        sums[FFN_SHIFT],
    )


def solution(mesh):
    rows = P("batch", "blk", None)
    tile = P("batch", "blk")
    return jax.shard_map(
        local,
        mesh=mesh,
        in_specs=(rows,) + (P(),) * 15 + (P("batch", None), P("batch", None), rows),
        out_specs=(
            rows,
            rows,
            tile,
            P(),
            tile,
            tile,
            P(),
            tile,
            P(),
            P(),
            P(),
            tile,
            P(),
            tile,
            P(),
            P(),
            P(),
        ),
        check_vma=False,
    )
```

```python
import jax
import jax.numpy as jnp
from jax import lax
from jax.experimental import pallas as pl
from jax.experimental.pallas import tpu as pltpu
from jax.sharding import PartitionSpec as P

HEADS = 12
HEAD_DIM = 64
PAIRS = 4

NORM_EPS = 1e-05
MASKED_SCORE = -1e30
INV_ROOT_TWO = 0.7071067811865476
INV_ROOT_TWO_PI = 0.3989422804014327
MIB = 1024 * 1024

B_OUTER, FFN_GAIN, FFN_SHIFT, ATTN_GAIN, ATTN_SHIFT, B_OUTPUT, B_QUERY, B_VALUE, B_INNER = range(9)

EXTRA = 16

f32 = jnp.float32
bf16 = jnp.bfloat16


def mm(left, right):
    return jnp.dot(left, right, preferred_element_type=f32)


def mm_nt(left, right):
    return lax.dot_general(left, right, (((1,), (1,)), ((), ())), preferred_element_type=f32)


def norm_stats(values_in):
    row_mean = jnp.mean(values_in, axis=-1, keepdims=True)
    centred = values_in - row_mean
    inv_dev = lax.rsqrt(jnp.mean(centred * centred, axis=-1, keepdims=True) + NORM_EPS)
    return centred * inv_dev, inv_dev


def norm_back(scaled, normed, inv_dev):
    centre_term = jnp.mean(scaled, axis=-1, keepdims=True)
    slope_term = jnp.mean(scaled * normed, axis=-1, keepdims=True)
    return inv_dev * (scaled - centre_term - normed * slope_term)


def sum_rows(values):
    return jnp.sum(values, axis=0, keepdims=True)


def as_row(ref):
    return ref[...].astype(f32).reshape(1, -1)


def rows_of(width, count):
    return width // 128 * count


def narrow(ref, first, values):
    count = values.shape[0]
    for k in range(values.shape[1] // 128):
        at = first + k * count
        ref[at : at + count] = values[:, k * 128 : (k + 1) * 128]


def widen(ref, first, count, width):
    return jnp.concatenate(
        [ref[first + k * count : first + (k + 1) * count] for k in range(width // 128)], axis=1
    )


def ahead(me, step, size):
    return lax.rem(me + step, size)


def behind(me, group, size):
    return lax.rem(group - me + size, size)


def lane_window(me, width):
    return pl.multiple_of((me * width) // 128 * 128, 128)


def prep_kernel(
    text,
    region,
    x_ref,
    grad_ref,
    b_query,
    b_value,
    b_output,
    attn_gain,
    attn_shift,
    b_outer,
    ffn_gain,
    ffn_shift,
    b_inner,
    w_query,
    w_key,
    w_value,
    own_weights,
    own_bias,
    mask,
    vecs,
    x_out,
    grad_out,
    windows,
    sems,
):
    me = lax.axis_index("blk")
    row_len = mask.shape[0]
    span = x_ref.shape[0]
    size = row_len // span
    width = own_weights.shape[1] // 3
    model_width = x_ref.shape[1]
    start = lane_window(me, width)
    copies = []
    for k, weight in enumerate((w_query, w_key, w_value)):
        part = weight.at[:, pl.ds(start, windows.shape[2])]
        copies.append(pltpu.make_async_copy(part, windows.at[k], sems.at[k]))
    for copy in copies:
        copy.start()
    x_out[...] = x_ref[...]
    grad_out[...] = grad_ref[...]
    vecs[...] = jnp.zeros(vecs.shape, f32)
    for k, ref in (
        (B_OUTER, b_outer),
        (FFN_GAIN, ffn_gain),
        (FFN_SHIFT, ffn_shift),
        (ATTN_GAIN, attn_gain),
        (ATTN_SHIFT, attn_shift),
        (B_OUTPUT, b_output),
    ):
        vecs[k : k + 1] = as_row(ref)
    hidden_row = as_row(b_inner)
    for k in range(hidden_row.shape[1] // model_width):
        part = slice(k * model_width, (k + 1) * model_width)
        vecs[B_INNER + k : B_INNER + k + 1] = hidden_row[:, part]
    own_bias[...] = jnp.zeros(own_bias.shape, f32)
    for at, ref in ((0, b_query), (2, b_value)):
        row = as_row(ref)
        out = jnp.zeros((1, width), f32)
        for g in range(size):
            out = jnp.where(me == g, row[:, g * width : (g + 1) * width], out)
        own_bias[0:1, at * width : (at + 1) * width] = out

    ends = []
    total = jnp.zeros((1, 1), jnp.int32)
    for k in range(PAIRS):
        total = total + text[:, k : k + 1] + region[:, k : k + 1]
        ends.append(total)

    def segments(dim):
        shape = [1, 1]
        shape[dim] = span
        parts = []
        for s in range(size):
            first = lax.rem(me - s + size, size) * span
            pos = lax.broadcasted_iota(jnp.int32, tuple(shape), dim) + first
            seg = jnp.zeros(tuple(shape), jnp.int32)
            for end in ends:
                seg = seg + (pos >= end).astype(jnp.int32)
            parts.append(seg)
        return jnp.concatenate(parts, axis=dim)

    seg_q = segments(0)
    seg_k = segments(1)
    diagonal = lax.broadcasted_iota(jnp.int32, (row_len, row_len), 0) == lax.broadcasted_iota(
        jnp.int32, (row_len, row_len), 1
    )
    allowed = (seg_q == seg_k) & ((seg_k < PAIRS) | diagonal)
    mask[...] = jnp.where(allowed, 0.0, MASKED_SCORE)
    off = windows.shape[2] - width
    for k in range(3):
        copies[k].wait()
        window = windows[k]
        own_weights[:, k * width : (k + 1) * width] = jnp.where(
            (me * width) % 128 == 0, window[:, :width], window[:, off:]
        )


def transpose_kernel(
    w_inner, w_outer, qkv, inner_out, outer_out, inner_t, outer_t, q_t, k_t, v_t, sems
):
    copies = [
        pltpu.make_async_copy(w_inner, inner_out, sems.at[0]),
        pltpu.make_async_copy(w_outer, outer_out, sems.at[1]),
    ]
    for copy in copies:
        copy.start()
    own = q_t.shape[0]
    for k, ref in enumerate((q_t, k_t, v_t)):
        ref[...] = qkv[:, k * own : (k + 1) * own].T
    width, hidden = inner_out.shape
    parts = [slice(k * width, (k + 1) * width) for k in range(hidden // width)]
    copies[0].wait()
    for part in parts:
        inner_t[part] = inner_out[:, part].T
    copies[1].wait()
    for part in parts:
        outer_t[:, part] = outer_out[part].T


def attention_kernel(
    x0, x1, x2, x3, own_weights, own_bias, mask, c0, c1, c2, c3, probs_ref, qkv_ref, context_ref, x_all
):
    xs = (x0, x1, x2, x3)
    context_refs = (c0, c1, c2, c3)
    size = len(xs)
    span = x0.shape[0]
    width = own_weights.shape[1] // 3
    for s in range(size):
        x_all[s * span : (s + 1) * span] = xs[s][...]
    qkv = (mm(x_all[...], own_weights[...]) + own_bias[0:1]).astype(bf16)
    query = (qkv[:, :width] * HEAD_DIM ** (-0.5)).astype(bf16)
    key = qkv[:, width : 2 * width]
    value = qkv[:, 2 * width :]
    qkv_ref[:, :width] = query
    qkv_ref[:, width:] = qkv[:, width:]
    tasks = [(h, s) for s in range(size) for h in range(width // HEAD_DIM)]

    def scores_of(task):
        h, s = task
        cols = slice(h * HEAD_DIM, (h + 1) * HEAD_DIM)
        part = slice(s * span, (s + 1) * span)
        return mm_nt(query[part, cols], key[:, cols])

    following = scores_of(tasks[0])
    done = []
    for k, (h, s) in enumerate(tasks):
        part = slice(s * span, (s + 1) * span)
        scores = following + mask[part]
        if k + 1 < len(tasks):
            following = scores_of(tasks[k + 1])
        weights = jnp.exp(scores - jnp.max(scores, axis=-1, keepdims=True))
        probs = (weights * (1.0 / jnp.sum(weights, axis=-1, keepdims=True))).astype(bf16)
        probs_ref[h, part] = probs
        done.append(mm(probs, value[:, h * HEAD_DIM : (h + 1) * HEAD_DIM]))
        if h == width // HEAD_DIM - 1:
            context = jnp.concatenate(done, axis=1)
            context_ref[part] = context
            context_refs[s][...] = context.astype(bf16).T
            done = []


def forward_kernel(blocks):
    def body(
        x_ref,
        c0,
        c1,
        c2,
        c3,
        vecs,
        grad_ref,
        w_output,
        w_inner,
        w_outer,
        order_after,
        out_ref,
        left_own,
        left_core,
        left_x,
        inner_own,
        inner_core,
        inner_y,
        outer_low_ref,
        slope_ref,
        grad_summed_ref,
        hat_ref,
        inv_ref,
        sums_ref,
        groups,
        left,
        inner,
    ):
        del order_after
        batch_me = lax.axis_index("batch")
        me = lax.axis_index("blk")
        slots = (c0, c1, c2, c3)
        size = len(slots)
        width, hidden = w_inner.shape
        step = width
        count = hidden // step
        ff_rows = hidden // blocks
        many = left_own.shape[0]
        block = many // (blocks // 4)

        def left_rows(b, first, values):
            at = (b >> 2) * block + first
            left[jnp.bitwise_xor(batch_me & 3, b & 3), at : at + values.shape[0]] = values

        def vec(k):
            return vecs[k : k + 1]

        for s in range(size):
            groups[ahead(me, s, size)] = slots[s][...]
        context_t = jnp.concatenate([groups[g] for g in range(size)], axis=0)
        context = context_t.T
        mixed = x_ref[...].astype(f32) + mm(context, w_output[...]) + vec(B_OUTPUT)
        hat, inv = norm_stats(mixed)
        hat_ref[...] = hat
        inv_ref[...] = inv
        attn_norm = hat * vec(ATTN_GAIN) + vec(ATTN_SHIFT)
        inner_in = attn_norm.astype(bf16)
        outer = jnp.zeros(attn_norm.shape, f32)
        cols = [slice(k * step, (k + 1) * step) for k in range(count)]
        following = mm(inner_in, w_inner[:, cols[0]])
        for k in range(count):
            pre = following + vec(B_INNER + k)
            if k + 1 < count:
                following = mm(inner_in, w_inner[:, cols[k + 1]])
            cdf = 0.5 + 0.5 * lax.erf(pre * INV_ROOT_TWO)
            act = (pre * cdf).astype(bf16)
            slope_ref[:, cols[k]] = cdf + pre * (jnp.exp(-0.5 * pre * pre) * INV_ROOT_TWO_PI)
            outer += mm(act, w_outer[cols[k]])
            act_t = act.T
            for j in range(step // ff_rows):
                left_rows(k * step // ff_rows + j, 0, act_t[j * ff_rows : (j + 1) * ff_rows])
        summed = attn_norm + outer + vec(B_OUTER)
        final_hat, final_inv = norm_stats(summed)
        gain = vec(FFN_GAIN)
        upstream = grad_ref[...].astype(f32)
        grad_summed = norm_back(upstream * gain, final_hat, final_inv)
        grad_summed_ref[...] = grad_summed
        outer_low = grad_summed.astype(bf16)
        outer_low_ref[...] = outer_low
        out_ref[...] = (final_hat * gain + vec(FFN_SHIFT)).astype(bf16)
        sums_ref[...] = jnp.zeros(sums_ref.shape, f32)
        sums_ref[B_OUTER : B_OUTER + 1] = sum_rows(outer_low.astype(f32))
        sums_ref[FFN_GAIN : FFN_GAIN + 1] = sum_rows(upstream * final_hat)
        sums_ref[FFN_SHIFT : FFN_SHIFT + 1] = sum_rows(upstream)
        out_rows = width // blocks
        padded = block - ff_rows
        inner_t = inner_in.T

        def block_rows(values, b):
            if padded == out_rows:
                return values[b * out_rows : (b + 1) * out_rows]
            row = lax.broadcasted_iota(jnp.int32, (padded, width), 0)
            col = lax.broadcasted_iota(jnp.int32, (padded, width), 1)
            pick = ((row < out_rows) & (col == row + b * out_rows)).astype(f32).astype(bf16)
            return mm(pick, values).astype(bf16)

        for b in range(blocks):
            left_rows(b, ff_rows, block_rows(context_t, b))
            owner = jnp.bitwise_xor(batch_me & 1, b & 1) + 2 * jnp.bitwise_xor(
                (batch_me >> 2) & 1, (b >> 2) & 1
            )
            at = (((b >> 3) << 1) | ((b >> 1) & 1)) * padded
            inner[owner, at : at + padded] = block_rows(inner_t, b)
        left_own[...] = left[0]
        left_core[...] = left[1]
        left_x[:many] = left[2]
        left_x[many:] = left[3]
        few = inner_own.shape[0]
        inner_own[...] = inner[0]
        inner_core[...] = inner[1]
        inner_y[:few] = inner[2]
        inner_y[few:] = inner[3]

    return body


def backward_kernel(
    outer_low_ref,
    slope_ref,
    grad_summed_ref,
    hat_ref,
    inv_ref,
    left_x,
    inner_y,
    vecs,
    sums_in,
    w_output,
    w_inner_t,
    w_outer_t,
    x_ref,
    y_ref,
    grad_mixed_ref,
    g0,
    g1,
    g2,
    g3,
    groups,
    sums,
):
    hidden, width = w_inner_t.shape
    group_refs = (g0, g1, g2, g3)
    size = len(group_refs)
    me = lax.axis_index("blk")
    step = width
    rows = width // size
    span = outer_low_ref.shape[0]
    count = hidden // step
    parts = [slice(k * step, (k + 1) * step) for k in range(count)]
    sums[...] = sums_in[...]
    outer_low = outer_low_ref[...]
    grad_norm = grad_summed_ref[...]
    many, few = left_x.shape[0], inner_y.shape[0]
    x_ref[:many] = left_x[...]
    y_ref[:few] = inner_y[...]
    following = mm(outer_low, w_outer_t[:, parts[0]])
    for k in range(count):
        pre_low = (following * slope_ref[:, parts[k]]).astype(bf16)
        if k + 1 < count:
            following = mm(outer_low, w_outer_t[:, parts[k + 1]])
        grad_norm += mm(pre_low, w_inner_t[parts[k]])
        y_ref[few + k * step : few + (k + 1) * step] = pre_low.T
        sums[B_INNER + k : B_INNER + k + 1] = sum_rows(pre_low.astype(f32))
    hat = hat_ref[...]
    grad_mixed = norm_back(grad_norm * vecs[ATTN_GAIN : ATTN_GAIN + 1], hat, inv_ref[...])
    grad_mixed_ref[...] = grad_mixed
    mixed_low = grad_mixed.astype(bf16)
    narrow(x_ref, many, outer_low)
    narrow(x_ref, many + rows_of(width, span), mixed_low)
    context_grad_t = mm_nt(w_output[...], mixed_low).astype(bf16)
    for g in range(size):
        groups[behind(me, g, size)] = context_grad_t[g * rows : (g + 1) * rows]
    for s in range(size):
        group_refs[s][...] = groups[s]
    sums[ATTN_GAIN : ATTN_GAIN + 1] = sum_rows(grad_norm * hat)
    sums[ATTN_SHIFT : ATTN_SHIFT + 1] = sum_rows(grad_norm)
    sums[B_OUTPUT : B_OUTPUT + 1] = sum_rows(mixed_low.astype(f32))
    narrow(x_ref, many + 2 * rows_of(width, span), sums[...].astype(bf16))


def pack_kernel(core_rows, own, got, *after_and_out):
    out_ref = after_and_out[-1]
    many = core_rows.shape[0]
    size = own.shape[0] - 2 * many
    out_ref[:many] = core_rows[...]
    out_ref[many : 2 * many] = got[many : 2 * many]
    out_ref[2 * many : 2 * many + size] = own[2 * many :]
    out_ref[2 * many + size :] = got[2 * many :]


def first_products_kernel(block, ff_rows, span):
    def body(left_own, sent, received, packed, send_ref, keep_ref):
        many = left_own.shape[0]
        size = sent.shape[0] - 2 * many
        width = send_ref.shape[1]
        tall = rows_of(width, span)
        own = (lax.axis_index("batch") >> 2) & 1
        lefts = ((left_own, 0), (received, 0), (packed, 0), (packed, many))
        rights = (
            (sent, 2 * many),
            (received, 2 * many),
            (packed, 2 * many),
            (packed, 2 * many + size),
        )
        outer_low = jnp.concatenate([widen(ref, at, span, width) for ref, at in rights], axis=0)
        mixed_low = jnp.concatenate(
            [widen(ref, at + tall, span, width) for ref, at in rights], axis=0
        )
        sums = jnp.zeros((EXTRA, width), f32)
        for ref, at in rights:
            sums += widen(ref, at + 2 * tall, EXTRA, width).astype(f32)
        for ref, side in ((send_ref, 1 - own), (keep_ref, own)):
            count = (ref.shape[0] - EXTRA) // block
            for j in range(count):

                def rows(first, number):
                    start = (2 * j + side) * block + first
                    return jnp.concatenate(
                        [
                            source[pl.ds(pl.multiple_of(start + at, 16), number)]
                            for source, at in lefts
                        ],
                        axis=1,
                    )

                at = j * block
                ref[at : at + ff_rows] = mm(rows(0, ff_rows), outer_low).astype(bf16)
                ref[at + ff_rows : at + block] = mm(
                    rows(ff_rows, block - ff_rows), mixed_low
                ).astype(bf16)
            ref[count * block :] = sums.astype(bf16)

    return body


def inner_products_kernel(block):
    def body(inner_own, sent, received, packed, send_ref, keep_ref):
        few = inner_own.shape[0]
        size = sent.shape[0] - 2 * few
        own = (lax.axis_index("batch") >> 1) & 1
        lefts = ((inner_own, 0), (received, 0), (packed, 0), (packed, few))
        rights = ((sent, 2 * few), (received, 2 * few), (packed, 2 * few), (packed, 2 * few + size))
        pre_t = jnp.concatenate([ref[at : at + size] for ref, at in rights], axis=1)
        for ref, side in ((send_ref, 1 - own), (keep_ref, own)):
            pieces = []
            for j in range(ref.shape[0] // block):
                start = (2 * j + side) * block
                pieces.append(
                    jnp.concatenate(
                        [
                            source[pl.ds(pl.multiple_of(start + at, 16), block)]
                            for source, at in lefts
                        ],
                        axis=1,
                    )
                )
            ref[...] = mm_nt(jnp.concatenate(pieces, axis=0), pre_t).astype(bf16)

    return body


def halve_kernel(block, bit, parts, extra_rows):
    def body(keep_in, *rest):
        got, (send_ref, keep_ref) = rest[:parts], rest[-2:]
        own = (lax.axis_index("batch") >> bit) & 1
        count = (send_ref.shape[0] - extra_rows) // block

        def total(part):
            added = jnp.concatenate([ref[part] for ref in got], axis=1).astype(f32)
            return (keep_in[part].astype(f32) + added).astype(bf16)

        for ref, side in ((send_ref, 1 - own), (keep_ref, own)):
            for j in range(count):
                start = pl.multiple_of((2 * j + side) * block, 16)
                ref[j * block : (j + 1) * block] = total(pl.ds(start, block))
            if extra_rows:
                last = 2 * count * block
                ref[count * block :] = total(slice(last, last + extra_rows))

    return body


def attention_back_kernel(
    probs_ref,
    q_t_ref,
    k_t_ref,
    v_t_ref,
    context_ref,
    d0,
    d1,
    d2,
    d3,
    e0,
    e1,
    e2,
    e3,
    token_sums,
    score_grad,
    out_t,
):
    slots = (d0, d1, d2, d3)
    outs = (e0, e1, e2, e3)
    size = len(slots)
    width, row_len = q_t_ref.shape
    span = row_len // size
    grad_t = jnp.concatenate([slot[...] for slot in slots], axis=1)
    grad = grad_t.T
    for h in range(width // HEAD_DIM):
        cols = slice(h * HEAD_DIM, (h + 1) * HEAD_DIM)
        for s in range(size):
            part = slice(s * span, (s + 1) * span)
            grad_part = grad[part, cols]
            delta = jnp.sum(
                grad_part.astype(f32) * context_ref[part, cols], axis=-1, keepdims=True
            )
            grad_probs = mm(grad_part, v_t_ref[cols])
            score_grad[part] = (probs_ref[h, part].astype(f32) * (grad_probs - delta)).astype(bf16)
        out_t[cols] = (mm_nt(k_t_ref[cols], score_grad[...]) * HEAD_DIM ** (-0.5)).astype(bf16)
        out_t[width + h * HEAD_DIM : width + (h + 1) * HEAD_DIM] = mm(
            q_t_ref[cols], score_grad[...]
        ).astype(bf16)
        out_t[2 * width + h * HEAD_DIM : 2 * width + (h + 1) * HEAD_DIM] = mm(
            grad_t[cols], probs_ref[h]
        ).astype(bf16)
    for s in range(size):
        outs[s][...] = out_t[:, s * span : (s + 1) * span]
    token_sums[...] = mm_nt(jnp.ones((8, row_len), bf16), out_t[...])


def head_products_kernel(
    x0, x1, x2, x3, e0, e1, e2, e3, token_sums, order_after, send_ref, keep_ref, total
):
    del order_after
    core = lax.axis_index("batch") & 1
    x_t = jnp.concatenate([ref[...].T for ref in (x0, x1, x2, x3)], axis=1)
    heads_t = jnp.concatenate([ref[...] for ref in (e0, e1, e2, e3)], axis=1)
    total[...] = mm_nt(x_t, heads_t)
    blocks = lax.axis_size("batch")
    rows, width = total.shape[0] // blocks, total.shape[1]
    padded = (send_ref.shape[0] - EXTRA) // (blocks // 2)
    for own, refs in ((0, (keep_ref, send_ref)), (1, (send_ref, keep_ref))):

        @pl.when(core == own)
        def _():
            for b in range(blocks):
                at = (b >> 1) * padded
                if padded != rows:
                    refs[b & 1][at : at + padded] = jnp.zeros((padded, width), bf16)
                refs[b & 1][at : at + rows] = total[b * rows : (b + 1) * rows].astype(bf16)

    sums = jnp.concatenate((token_sums[...], jnp.zeros((EXTRA - 8, width), f32)), axis=0)
    for ref in (send_ref, keep_ref):
        ref[(blocks // 2) * padded :] = sums.astype(bf16)


def grad_in_kernel(
    e0, e1, e2, e3, grad_mixed, w_query, w_key, w_value, out_ref, groups, weights, sems
):
    slots = (e0, e1, e2, e3)
    size = len(slots)
    me = lax.axis_index("blk")
    copies = [
        pltpu.make_async_copy(weight, weights.at[k], sems.at[k])
        for k, weight in enumerate((w_query, w_key, w_value))
    ]
    for copy in copies:
        copy.start()
    for s in range(size):
        groups[ahead(me, s, size)] = slots[s][...]
    total = grad_mixed[...]
    own = e0.shape[0] // 3
    for k in range(3):
        rows = [groups[g, k * own : (k + 1) * own] for g in range(size)]
        part = jnp.concatenate(rows, axis=0).T
        copies[k].wait()
        total += mm_nt(part, weights[k])
    out_ref[...] = total.astype(bf16)


def split_inner_kernel(keep, got, own_ref, s1, s2, s3, total):
    outs = (own_ref, s1, s2, s3)
    size = len(outs)
    me = lax.axis_index("blk")
    total[...] = keep[...].astype(f32) + got[...].astype(f32)
    width = total.shape[1] // size
    for s in range(size):
        cols = pl.ds(pl.multiple_of(ahead(me, s, size) * width, 128), width)
        outs[s][...] = total[:, cols].astype(outs[s].dtype)


def join_inner_kernel(own, r1, r2, r3, out_ref):
    rows = slice(0, out_ref.shape[0])
    total = own[rows] + r1[rows].astype(f32) + r2[rows].astype(f32) + r3[rows].astype(f32)
    out_ref[...] = total


def split_columns_kernel(keep, got, late, own_ref, s1, s2, s3, groups):
    outs = (s1, s2, s3)
    size = len(outs) + 1
    me = lax.axis_index("blk")
    total = keep[...].astype(f32) + got[...].astype(f32)
    last = total.shape[0] - EXTRA
    half = last // 2
    width = total.shape[1] // size
    sums = total[last:]
    row = lax.broadcasted_iota(jnp.int32, sums.shape, 0)
    group = lax.broadcasted_iota(jnp.int32, sums.shape, 1) // width
    for k, at in ((B_QUERY, 0), (B_VALUE, 2)):
        own_row = late[0:1, at * width : (at + 1) * width]
        sums = jnp.where(
            (row == k) & (group == me), jnp.concatenate([own_row] * size, axis=1), sums
        )
    extra = jnp.concatenate((sums[:, : 2 * width], sums[:, 2 * width :]), axis=0)
    for g in range(size):
        cols = slice(g * width, (g + 1) * width)
        slot = behind(me, g, size)
        groups[slot, :half] = jnp.concatenate((total[:half, cols], total[half:last, cols]), axis=1)
    own_ref[:half] = groups[0]
    own_ref[half:] = extra
    for s in range(1, size):
        outs[s - 1][:half] = groups[s].astype(bf16)
        outs[s - 1][half:] = extra.astype(bf16)


def join_rows_kernel(own, r1, r2, r3, first_ref, second_ref, *rest):
    sum_refs, (rows,) = rest[:-1], rest[-1:]
    total = own[...] + r1[...].astype(f32) + r2[...].astype(f32) + r3[...].astype(f32)
    half, width = total.shape[0] - 2 * EXTRA, total.shape[1] // 2
    rows[:half] = total[:half, :width]
    rows[half:] = total[:half, width:]
    ff_rows = first_ref.shape[0]
    first_ref[...] = rows[:ff_rows]
    second_ref[...] = rows[ff_rows : ff_rows + second_ref.shape[0]]
    sums = jnp.concatenate((total[half : half + EXTRA], total[half + EXTRA :]), axis=1)
    for k, ref in enumerate(sum_refs[:-1]):
        ref[...] = sums[k]
    model_width = sums.shape[1]
    for k in range(sum_refs[-1].shape[0] // model_width):
        sum_refs[-1][k * model_width : (k + 1) * model_width] = sums[B_INNER + k]


def last_sum_kernel(keep, got, q_ref, k_ref, v_ref, late_ref):
    total = keep[...].astype(f32) + got[...].astype(f32)
    rows, own = q_ref.shape
    for k, ref in enumerate((q_ref, k_ref, v_ref)):
        ref[...] = total[:rows, k * own : (k + 1) * own]
    last = total.shape[0] - EXTRA
    late_ref[...] = total[last : last + 8]


def run_kernel(body, operands, outs, scratch=(), in_hbm=(), limit=8, fill=0):
    vmem = pl.BlockSpec(memory_space=pltpu.VMEM)
    hbm = pl.BlockSpec(memory_space=pltpu.HBM)
    anywhere = pl.BlockSpec(memory_space=pl.ANY)

    def place(k):
        if k - len(operands) in in_hbm:
            return anywhere
        return hbm if k in in_hbm else vmem

    return pl.pallas_call(
        body,
        out_shape=[jax.ShapeDtypeStruct(shape, dtype) for shape, dtype in outs],
        in_specs=[place(k) for k in range(len(operands))],
        out_specs=[vmem] * len(outs),
        scratch_shapes=list(scratch),
        compiler_params=pltpu.CompilerParams(vmem_limit_bytes=limit * MIB),
        cost_estimate=pl.CostEstimate(
            flops=1 + fill * 10**9, bytes_accessed=1, transcendentals=0
        ),
    )(*operands)


def blk_shift(values, step):
    size = lax.axis_size("blk")
    return lax.ppermute(values, "blk", [(i, (i + step) % size) for i in range(size)])


def batch_swap(values, bits):
    size = lax.axis_size("batch")
    return lax.ppermute(values, "batch", [(i, i ^ bits) for i in range(size)])


def halve(keep, got, block, bit, after=(), extra_rows=EXTRA):
    got = got if isinstance(got, list) else [got]
    count = (keep.shape[0] - extra_rows) // block // 2
    shape = ((count * block + extra_rows, keep.shape[1]), bf16)
    return run_kernel(
        halve_kernel(block, bit, len(got), extra_rows),
        [keep, *got, *after],
        [shape, shape],
        in_hbm=[-1 - k for k in range(len(after))],
    )


def local(
    hidden_in,
    w_query,
    b_query,
    w_key,
    w_value,
    b_value,
    w_output,
    b_output,
    attn_gain,
    attn_shift,
    w_inner,
    b_inner,
    w_outer,
    b_outer,
    ffn_gain,
    ffn_shift,
    text_lengths,
    region_lengths,
    out_grad,
):
    _, span, width = hidden_in.shape
    hidden = w_inner.shape[1]
    size = lax.axis_size("blk")
    blocks = lax.axis_size("batch")
    bits = blocks.bit_length() - 1
    row_len = span * size
    own_heads = HEADS // size
    own_width = own_heads * HEAD_DIM
    steps = range(1, size)
    tokens_f32 = ((span, width), f32)
    tokens_bf16 = ((span, width), bf16)
    row = ((width,), f32)

    flat_in = hidden_in[0]
    x_slots = [blk_shift(flat_in, step) for step in steps]
    own_weights, own_bias, mask, vecs, x_own, grad_own = run_kernel(
        prep_kernel,
        [
            text_lengths,
            region_lengths,
            flat_in,
            out_grad[0],
            b_query,
            b_value,
            b_output,
            attn_gain,
            attn_shift,
            b_outer,
            ffn_gain,
            ffn_shift,
            b_inner,
            w_query,
            w_key,
            w_value,
        ],
        [
            ((width, 3 * own_width), bf16),
            ((8, 3 * own_width), f32),
            ((row_len, row_len), f32),
            ((EXTRA, width), f32),
            tokens_bf16,
            tokens_bf16,
        ],
        [pltpu.VMEM((3, width, 256), bf16), pltpu.SemaphoreType.DMA((3,))],
        in_hbm=(13, 14, 15),
    )
    x_slots = [x_own] + x_slots
    *context_slots, probs, qkv, context_own = run_kernel(
        attention_kernel,
        x_slots + [own_weights, own_bias, mask],
        [((own_width, span), bf16)] * size
        + [((own_heads, row_len, row_len), bf16)]
        + [((row_len, 3 * own_width), bf16), ((row_len, own_width), f32)],
        [pltpu.VMEM((row_len, width), bf16)],
        limit=14,
    )
    turned = run_kernel(
        transpose_kernel,
        [w_inner, w_outer, qkv],
        [
            ((width, hidden), bf16),
            ((hidden, width), bf16),
            ((hidden, width), bf16),
            ((width, hidden), bf16),
        ]
        + [((own_width, row_len), bf16)] * 3,
        [pltpu.SemaphoreType.DMA((2,))],
        in_hbm=(0, 1),
        limit=24,
        fill=8,
    )
    ffn_weights, ffn_turned, (q_t, k_t, v_t) = turned[:2], turned[2:4], turned[4:]
    context_slots = context_slots[:1] + [
        blk_shift(context_slots[step], size - step) for step in steps
    ]
    ff_rows = hidden // blocks
    rows = -(-(width // blocks) // 16) * 16
    block = ff_rows + rows

    many = blocks // 4 * block
    few = blocks // 4 * rows
    (
        layer_out,
        left_own,
        left_core,
        left_x,
        inner_own,
        inner_core,
        inner_y,
        outer_low,
        slope,
        grad_summed,
        attn_hat,
        attn_inv,
        sums,
    ) = run_kernel(
        forward_kernel(blocks),
        [x_own]
        + context_slots
        + [vecs, grad_own, w_output]
        + [*ffn_weights, ffn_turned[0]],
        [
            tokens_bf16,
            ((many, span), bf16),
            ((many, span), bf16),
            ((2 * many, span), bf16),
            ((few, span), bf16),
            ((few, span), bf16),
            ((2 * few, span), bf16),
            tokens_bf16,
            ((span, hidden), f32),
            tokens_f32,
            tokens_f32,
            ((span, 1), f32),
            ((EXTRA, width), f32),
        ],
        [
            pltpu.VMEM((size, own_width, span), bf16),
            pltpu.VMEM((4, many, span), bf16),
            pltpu.VMEM((4, few, span), bf16),
        ],
        in_hbm=(-1,),
        limit=20,
    )
    tall = 2 * rows_of(width, span) + rows_of(width, EXTRA)
    x_sent, y_sent, grad_mixed, *context_grads = run_kernel(
        backward_kernel,
        [
            outer_low,
            slope,
            grad_summed,
            attn_hat,
            attn_inv,
            left_x,
            inner_y,
            vecs,
            sums,
            w_output,
            *ffn_turned,
        ],
        [((2 * many + tall, span), bf16), ((2 * few + hidden, span), bf16), tokens_f32]
        + [((own_width, span), bf16)] * size,
        [pltpu.VMEM((size, own_width, span), bf16), pltpu.VMEM((EXTRA, width), f32)],
        limit=20,
    )
    x_got = batch_swap(x_sent, 2)
    y_got = batch_swap(y_sent, 4)
    context_grads = context_grads[:1] + [blk_shift(context_grads[step], step) for step in steps]
    *head_grads, token_sums = run_kernel(
        attention_back_kernel,
        [probs, q_t, k_t, v_t, context_own] + context_grads,
        [((3 * own_width, span), bf16)] * size + [((8, 3 * own_width), f32)],
        [pltpu.VMEM((row_len, row_len), bf16), pltpu.VMEM((3 * own_width, row_len), bf16)],
    )
    head_slots = head_grads[:1] + [blk_shift(head_grads[step], size - step) for step in steps]
    after = [head_slots[1], head_slots[-1]]
    packed = run_kernel(
        pack_kernel,
        [inner_core, y_sent, y_got] + after,
        [((2 * (few + hidden), span), bf16)],
        in_hbm=(-1, -2),
        limit=10,
    )[0]
    inner_send, inner_keep = run_kernel(
        inner_products_kernel(rows),
        [inner_own, y_sent, y_got, batch_swap(packed, 1)],
        [((few // 2, hidden), bf16)] * 2,
        limit=14,
    )
    inner_got = batch_swap(inner_send, 2)
    for bit in range(3, bits):
        inner_send, inner_keep = halve(inner_keep, inner_got, rows, bit, extra_rows=0)
        inner_got = batch_swap(inner_send, 1 << bit)
    packed = run_kernel(
        pack_kernel,
        [left_core, x_sent, x_got] + head_slots[2:-1],
        [((2 * (many + tall), span), bf16)],
        in_hbm=(-1,),
    )[0]
    send, keep = run_kernel(
        first_products_kernel(block, ff_rows, span),
        [left_own, x_sent, x_got, batch_swap(packed, 1)],
        [((many // 2 + EXTRA, width), bf16)] * 2,
        limit=14,
    )
    got = batch_swap(send, 4)
    for bit in range(3, bits):
        send, keep = halve(keep, got, block, bit)
        got = batch_swap(send, 1 << bit)
    wide = 3 * own_width
    head_send, head_keep = run_kernel(
        head_products_kernel,
        x_slots + head_grads + [token_sums, send],
        [((blocks // 2 * rows + EXTRA, wide), bf16)] * 2,
        [pltpu.VMEM((width, wide), f32)],
        in_hbm=(-1,),
        limit=10,
    )
    head_got = batch_swap(head_send, 1)
    head_send, head_keep = halve(head_keep, head_got, rows, 1, [inner_got])
    head_got = batch_swap(head_send, 2)
    for bit in range(2, bits):
        head_send, head_keep = halve(head_keep, head_got, rows, bit, [got])
        head_got = batch_swap(head_send, 1 << bit)
    inner_part, *inner_sends = run_kernel(
        split_inner_kernel,
        [inner_keep, inner_got],
        [((rows, width), f32)] + [((rows, width), bf16)] * (size - 1),
        [pltpu.VMEM((rows, hidden), f32)],
    )
    inner_parts = [blk_shift(inner_sends[step - 1], step) for step in steps]
    grad_in = run_kernel(
        grad_in_kernel,
        head_slots + [grad_mixed, w_query, w_key, w_value],
        [tokens_bf16],
        [
            pltpu.VMEM((size, 3 * own_width, span), bf16),
            pltpu.VMEM((3, width, width), bf16),
            pltpu.SemaphoreType.DMA((3,)),
        ],
        in_hbm=(5, 6, 7),
        limit=10,
        fill=4,
    )[0]
    out_rows = width // blocks
    own_cols = ((out_rows, own_width), f32)
    *grad_qkv, late = run_kernel(
        last_sum_kernel,
        [head_keep, head_got],
        [own_cols] * 3 + [((8, wide), f32)],
    )
    message = (block // 2 + 2 * EXTRA, 2 * own_width)
    own_part, *sends = run_kernel(
        split_columns_kernel,
        [keep, got, late],
        [(message, f32)] + [(message, bf16)] * (size - 1),
        [pltpu.VMEM((size, block // 2, 2 * own_width), f32)],
    )
    parts = [blk_shift(sends[step - 1], step) for step in steps]
    grad_w_inner = run_kernel(
        join_inner_kernel, [inner_part] + inner_parts, [((out_rows, width), f32)]
    )[0]
    grad_w_outer, grad_w_output, *sums = run_kernel(
        join_rows_kernel,
        [own_part] + parts,
        [((ff_rows, own_width), f32), own_cols] + [row] * 8 + [((hidden,), f32)],
        [pltpu.VMEM((block, own_width), f32)],
    )
    return (
        layer_out[None],
        grad_in[None],
        grad_qkv[0],
        sums[B_QUERY],
        grad_qkv[1],
        grad_qkv[2],
        sums[B_VALUE],
        grad_w_output,
        sums[B_OUTPUT],
        sums[ATTN_GAIN],
        sums[ATTN_SHIFT],
        grad_w_inner,
        sums[B_INNER],
        grad_w_outer,
        sums[B_OUTER],
        sums[FFN_GAIN],
        sums[FFN_SHIFT],
    )


def solution(mesh):
    rows = P("batch", "blk", None)
    tile = P("batch", "blk")
    return jax.shard_map(
        local,
        mesh=mesh,
        in_specs=(rows,) + (P(),) * 15 + (P("batch", None), P("batch", None), rows),
        out_specs=(
            rows,
            rows,
            tile,
            P(),
            tile,
            tile,
            P(),
            tile,
            P(),
            P(),
            P(),
            tile,
            P(),
            tile,
            P(),
            P(),
            P(),
        ),
        check_vma=False,
    )
```

```python
import jax
import jax.numpy as jnp
from jax import lax
from jax.experimental import pallas as pl
from jax.experimental.pallas import tpu as pltpu
from jax.sharding import PartitionSpec as P

HEADS = 12
HEAD_DIM = 64
PAIRS = 4

NORM_EPS = 1e-05
MASKED_SCORE = -1e30
INV_ROOT_TWO = 0.7071067811865476
INV_ROOT_TWO_PI = 0.3989422804014327
MIB = 1024 * 1024

B_OUTER, FFN_GAIN, FFN_SHIFT, ATTN_GAIN, ATTN_SHIFT, B_OUTPUT, B_QUERY, B_VALUE, B_INNER = range(9)

EXTRA = 16

f32 = jnp.float32
bf16 = jnp.bfloat16


def mm(left, right):
    return jnp.dot(left, right, preferred_element_type=f32)


def mm_nt(left, right):
    return lax.dot_general(left, right, (((1,), (1,)), ((), ())), preferred_element_type=f32)


def norm_stats(values_in):
    row_mean = jnp.mean(values_in, axis=-1, keepdims=True)
    centred = values_in - row_mean
    inv_dev = lax.rsqrt(jnp.mean(centred * centred, axis=-1, keepdims=True) + NORM_EPS)
    return centred * inv_dev, inv_dev


def norm_back(scaled, normed, inv_dev):
    centre_term = jnp.mean(scaled, axis=-1, keepdims=True)
    slope_term = jnp.mean(scaled * normed, axis=-1, keepdims=True)
    return inv_dev * (scaled - centre_term - normed * slope_term)


def sum_rows(values):
    return jnp.sum(values, axis=0, keepdims=True)


def as_row(ref):
    return ref[...].astype(f32).reshape(1, -1)


def rows_of(width, count):
    return width // 128 * count


def narrow(ref, first, values):
    count = values.shape[0]
    for k in range(values.shape[1] // 128):
        at = first + k * count
        ref[at : at + count] = values[:, k * 128 : (k + 1) * 128]


def widen(ref, first, count, width):
    return jnp.concatenate(
        [ref[first + k * count : first + (k + 1) * count] for k in range(width // 128)], axis=1
    )


def ahead(me, step, size):
    return lax.rem(me + step, size)


def behind(me, group, size):
    return lax.rem(group - me + size, size)


def lane_window(me, width):
    return pl.multiple_of((me * width) // 128 * 128, 128)


def prep_kernel(
    text,
    region,
    x_ref,
    grad_ref,
    stacked,
    b_inner,
    w_query,
    w_key,
    w_value,
    w_outer,
    own_weights,
    own_bias,
    mask,
    vecs,
    x_out,
    grad_out,
    outer_out,
    windows,
    sems,
):
    me = lax.axis_index("blk")
    row_len = mask.shape[0]
    span = x_ref.shape[0]
    size = row_len // span
    width = own_weights.shape[1] // 3
    model_width = x_ref.shape[1]
    start = lane_window(me, width)
    copies = []
    for k, weight in enumerate((w_query, w_key, w_value)):
        part = weight.at[:, pl.ds(start, windows.shape[2])]
        copies.append(pltpu.make_async_copy(part, windows.at[k], sems.at[k]))
    copies.append(pltpu.make_async_copy(w_outer, outer_out, sems.at[3]))
    for copy in copies:
        copy.start()
    x_out[...] = x_ref[...]
    grad_out[...] = grad_ref[...]
    vecs[...] = stacked[...].astype(f32)
    hidden_row = as_row(b_inner)
    for k in range(hidden_row.shape[1] // model_width):
        part = slice(k * model_width, (k + 1) * model_width)
        vecs[B_INNER + k : B_INNER + k + 1] = hidden_row[:, part]
    own_bias[...] = jnp.zeros(own_bias.shape, f32)
    for at, k in ((0, B_QUERY), (2, B_VALUE)):
        row = vecs[k : k + 1]
        out = jnp.zeros((1, width), f32)
        for g in range(size):
            out = jnp.where(me == g, row[:, g * width : (g + 1) * width], out)
        own_bias[0:1, at * width : (at + 1) * width] = out

    ends = []
    total = jnp.zeros((1, 1), jnp.int32)
    for k in range(PAIRS):
        total = total + text[:, k : k + 1] + region[:, k : k + 1]
        ends.append(total)

    def segments(dim):
        shape = [1, 1]
        shape[dim] = span
        parts = []
        for s in range(size):
            first = lax.rem(me - s + size, size) * span
            pos = lax.broadcasted_iota(jnp.int32, tuple(shape), dim) + first
            seg = jnp.zeros(tuple(shape), jnp.int32)
            for end in ends:
                seg = seg + (pos >= end).astype(jnp.int32)
            parts.append(seg)
        return jnp.concatenate(parts, axis=dim)

    seg_q = segments(0)
    seg_k = segments(1)
    diagonal = lax.broadcasted_iota(jnp.int32, (row_len, row_len), 0) == lax.broadcasted_iota(
        jnp.int32, (row_len, row_len), 1
    )
    allowed = (seg_q == seg_k) & ((seg_k < PAIRS) | diagonal)
    mask[...] = jnp.where(allowed, 0.0, MASKED_SCORE)
    off = windows.shape[2] - width
    for k in range(3):
        copies[k].wait()
        window = windows[k]
        own_weights[:, k * width : (k + 1) * width] = jnp.where(
            (me * width) % 128 == 0, window[:, :width], window[:, off:]
        )
    copies[3].wait()


def transpose_kernel(
    w_inner, w_outer, qkv, inner_out, inner_t, outer_t, q_t, k_t, v_t, sems
):
    copy = pltpu.make_async_copy(w_inner, inner_out, sems.at[0])
    copy.start()
    own = q_t.shape[0]
    for k, ref in enumerate((q_t, k_t, v_t)):
        ref[...] = qkv[:, k * own : (k + 1) * own].T
    width, hidden = inner_out.shape
    parts = [slice(k * width, (k + 1) * width) for k in range(hidden // width)]
    for part in parts:
        outer_t[:, part] = w_outer[part].T
    copy.wait()
    for part in parts:
        inner_t[part] = inner_out[:, part].T


def attention_kernel(
    x0, x1, x2, x3, own_weights, own_bias, mask, c0, c1, c2, c3, probs_ref, qkv_ref, context_ref, x_all
):
    xs = (x0, x1, x2, x3)
    context_refs = (c0, c1, c2, c3)
    size = len(xs)
    span = x0.shape[0]
    width = own_weights.shape[1] // 3
    for s in range(size):
        x_all[s * span : (s + 1) * span] = xs[s][...]
    qkv = (mm(x_all[...], own_weights[...]) + own_bias[0:1]).astype(bf16)
    query = (qkv[:, :width] * HEAD_DIM ** (-0.5)).astype(bf16)
    key = qkv[:, width : 2 * width]
    value = qkv[:, 2 * width :]
    qkv_ref[:, :width] = query
    qkv_ref[:, width:] = qkv[:, width:]
    tasks = [(h, s) for s in range(size) for h in range(width // HEAD_DIM)]

    def scores_of(task):
        h, s = task
        cols = slice(h * HEAD_DIM, (h + 1) * HEAD_DIM)
        part = slice(s * span, (s + 1) * span)
        return mm_nt(query[part, cols], key[:, cols])

    following = scores_of(tasks[0])
    done = []
    for k, (h, s) in enumerate(tasks):
        part = slice(s * span, (s + 1) * span)
        scores = following + mask[part]
        if k + 1 < len(tasks):
            following = scores_of(tasks[k + 1])
        weights = jnp.exp(scores - jnp.max(scores, axis=-1, keepdims=True))
        probs = (weights * (1.0 / jnp.sum(weights, axis=-1, keepdims=True))).astype(bf16)
        probs_ref[h, part] = probs
        done.append(mm(probs, value[:, h * HEAD_DIM : (h + 1) * HEAD_DIM]))
        if h == width // HEAD_DIM - 1:
            context = jnp.concatenate(done, axis=1)
            context_ref[part] = context
            context_refs[s][...] = context.astype(bf16).T
            done = []


def forward_kernel(blocks):
    def body(
        x_ref,
        c0,
        c1,
        c2,
        c3,
        vecs,
        grad_ref,
        w_output,
        w_inner,
        w_outer,
        order_after,
        out_ref,
        left_own,
        left_core,
        left_x,
        inner_own,
        inner_core,
        inner_y,
        outer_low_ref,
        slope_ref,
        grad_summed_ref,
        hat_ref,
        inv_ref,
        sums_ref,
        groups,
        left,
        inner,
    ):
        del order_after
        batch_me = lax.axis_index("batch")
        me = lax.axis_index("blk")
        slots = (c0, c1, c2, c3)
        size = len(slots)
        width, hidden = w_inner.shape
        step = width
        count = hidden // step
        ff_rows = hidden // blocks
        many = left_own.shape[0]
        block = many // (blocks // 4)

        def left_rows(b, first, values):
            at = (b >> 2) * block + first
            left[jnp.bitwise_xor(batch_me & 3, b & 3), at : at + values.shape[0]] = values

        def vec(k):
            return vecs[k : k + 1]

        for s in range(size):
            groups[ahead(me, s, size)] = slots[s][...]
        context_t = jnp.concatenate([groups[g] for g in range(size)], axis=0)
        context = context_t.T
        mixed = x_ref[...].astype(f32) + mm(context, w_output[...]) + vec(B_OUTPUT)
        hat, inv = norm_stats(mixed)
        hat_ref[...] = hat
        inv_ref[...] = inv
        attn_norm = hat * vec(ATTN_GAIN) + vec(ATTN_SHIFT)
        inner_in = attn_norm.astype(bf16)
        outer = jnp.zeros(attn_norm.shape, f32)
        cols = [slice(k * step, (k + 1) * step) for k in range(count)]
        following = mm(inner_in, w_inner[:, cols[0]])
        for k in range(count):
            pre = following + vec(B_INNER + k)
            if k + 1 < count:
                following = mm(inner_in, w_inner[:, cols[k + 1]])
            cdf = 0.5 + 0.5 * lax.erf(pre * INV_ROOT_TWO)
            act = (pre * cdf).astype(bf16)
            slope_ref[:, cols[k]] = cdf + pre * (jnp.exp(-0.5 * pre * pre) * INV_ROOT_TWO_PI)
            outer += mm(act, w_outer[cols[k]])
            act_t = act.T
            for j in range(step // ff_rows):
                left_rows(k * step // ff_rows + j, 0, act_t[j * ff_rows : (j + 1) * ff_rows])
        summed = attn_norm + outer + vec(B_OUTER)
        final_hat, final_inv = norm_stats(summed)
        gain = vec(FFN_GAIN)
        upstream = grad_ref[...].astype(f32)
        grad_summed = norm_back(upstream * gain, final_hat, final_inv)
        grad_summed_ref[...] = grad_summed
        outer_low = grad_summed.astype(bf16)
        outer_low_ref[...] = outer_low
        out_ref[...] = (final_hat * gain + vec(FFN_SHIFT)).astype(bf16)
        sums_ref[...] = jnp.zeros(sums_ref.shape, f32)
        sums_ref[B_OUTER : B_OUTER + 1] = sum_rows(outer_low.astype(f32))
        sums_ref[FFN_GAIN : FFN_GAIN + 1] = sum_rows(upstream * final_hat)
        sums_ref[FFN_SHIFT : FFN_SHIFT + 1] = sum_rows(upstream)
        out_rows = width // blocks
        padded = block - ff_rows
        inner_t = inner_in.T

        def block_rows(values, b):
            if padded == out_rows:
                return values[b * out_rows : (b + 1) * out_rows]
            row = lax.broadcasted_iota(jnp.int32, (padded, width), 0)
            col = lax.broadcasted_iota(jnp.int32, (padded, width), 1)
            pick = ((row < out_rows) & (col == row + b * out_rows)).astype(f32).astype(bf16)
            return mm(pick, values).astype(bf16)

        for b in range(blocks):
            left_rows(b, ff_rows, block_rows(context_t, b))
            owner = jnp.bitwise_xor(batch_me & 1, b & 1) + 2 * jnp.bitwise_xor(
                (batch_me >> 2) & 1, (b >> 2) & 1
            )
            at = (((b >> 3) << 1) | ((b >> 1) & 1)) * padded
            inner[owner, at : at + padded] = block_rows(inner_t, b)
        left_own[...] = left[0]
        left_core[...] = left[1]
        left_x[:many] = left[2]
        left_x[many:] = left[3]
        few = inner_own.shape[0]
        inner_own[...] = inner[0]
        inner_core[...] = inner[1]
        inner_y[:few] = inner[2]
        inner_y[few:] = inner[3]

    return body


def backward_kernel(
    outer_low_ref,
    slope_ref,
    grad_summed_ref,
    hat_ref,
    inv_ref,
    left_x,
    inner_y,
    vecs,
    sums_in,
    w_output,
    w_inner_t,
    w_outer_t,
    x_ref,
    y_ref,
    grad_mixed_ref,
    g0,
    g1,
    g2,
    g3,
    groups,
    sums,
):
    hidden, width = w_inner_t.shape
    group_refs = (g0, g1, g2, g3)
    size = len(group_refs)
    me = lax.axis_index("blk")
    step = width
    rows = width // size
    span = outer_low_ref.shape[0]
    count = hidden // step
    parts = [slice(k * step, (k + 1) * step) for k in range(count)]
    sums[...] = sums_in[...]
    outer_low = outer_low_ref[...]
    grad_norm = grad_summed_ref[...]
    many, few = left_x.shape[0], inner_y.shape[0]
    x_ref[:many] = left_x[...]
    y_ref[:few] = inner_y[...]
    following = mm(outer_low, w_outer_t[:, parts[0]])
    for k in range(count):
        pre_low = (following * slope_ref[:, parts[k]]).astype(bf16)
        if k + 1 < count:
            following = mm(outer_low, w_outer_t[:, parts[k + 1]])
        grad_norm += mm(pre_low, w_inner_t[parts[k]])
        y_ref[few + k * step : few + (k + 1) * step] = pre_low.T
        sums[B_INNER + k : B_INNER + k + 1] = sum_rows(pre_low.astype(f32))
    hat = hat_ref[...]
    grad_mixed = norm_back(grad_norm * vecs[ATTN_GAIN : ATTN_GAIN + 1], hat, inv_ref[...])
    grad_mixed_ref[...] = grad_mixed
    mixed_low = grad_mixed.astype(bf16)
    narrow(x_ref, many, outer_low)
    narrow(x_ref, many + rows_of(width, span), mixed_low)
    context_grad_t = mm_nt(w_output[...], mixed_low).astype(bf16)
    for g in range(size):
        groups[behind(me, g, size)] = context_grad_t[g * rows : (g + 1) * rows]
    for s in range(size):
        group_refs[s][...] = groups[s]
    sums[ATTN_GAIN : ATTN_GAIN + 1] = sum_rows(grad_norm * hat)
    sums[ATTN_SHIFT : ATTN_SHIFT + 1] = sum_rows(grad_norm)
    sums[B_OUTPUT : B_OUTPUT + 1] = sum_rows(mixed_low.astype(f32))
    narrow(x_ref, many + 2 * rows_of(width, span), sums[...].astype(bf16))


def pack_kernel(core_rows, own, got, *after_and_out):
    out_ref = after_and_out[-1]
    many = core_rows.shape[0]
    size = own.shape[0] - 2 * many
    out_ref[:many] = core_rows[...]
    out_ref[many : 2 * many] = got[many : 2 * many]
    out_ref[2 * many : 2 * many + size] = own[2 * many :]
    out_ref[2 * many + size :] = got[2 * many :]


def first_products_kernel(block, ff_rows, span):
    def body(left_own, sent, received, packed, send_ref, keep_ref):
        many = left_own.shape[0]
        size = sent.shape[0] - 2 * many
        width = send_ref.shape[1]
        tall = rows_of(width, span)
        own = (lax.axis_index("batch") >> 2) & 1
        lefts = ((left_own, 0), (received, 0), (packed, 0), (packed, many))
        rights = (
            (sent, 2 * many),
            (received, 2 * many),
            (packed, 2 * many),
            (packed, 2 * many + size),
        )
        outer_low = jnp.concatenate([widen(ref, at, span, width) for ref, at in rights], axis=0)
        mixed_low = jnp.concatenate(
            [widen(ref, at + tall, span, width) for ref, at in rights], axis=0
        )
        sums = jnp.zeros((EXTRA, width), f32)
        for ref, at in rights:
            sums += widen(ref, at + 2 * tall, EXTRA, width).astype(f32)
        for ref, side in ((send_ref, 1 - own), (keep_ref, own)):
            count = (ref.shape[0] - EXTRA) // block
            for j in range(count):

                def rows(first, number):
                    start = (2 * j + side) * block + first
                    return jnp.concatenate(
                        [
                            source[pl.ds(pl.multiple_of(start + at, 16), number)]
                            for source, at in lefts
                        ],
                        axis=1,
                    )

                at = j * block
                ref[at : at + ff_rows] = mm(rows(0, ff_rows), outer_low).astype(bf16)
                ref[at + ff_rows : at + block] = mm(
                    rows(ff_rows, block - ff_rows), mixed_low
                ).astype(bf16)
            ref[count * block :] = sums.astype(bf16)

    return body


def inner_products_kernel(block):
    def body(inner_own, sent, received, packed, send_ref, keep_ref):
        few = inner_own.shape[0]
        size = sent.shape[0] - 2 * few
        own = (lax.axis_index("batch") >> 1) & 1
        lefts = ((inner_own, 0), (received, 0), (packed, 0), (packed, few))
        rights = ((sent, 2 * few), (received, 2 * few), (packed, 2 * few), (packed, 2 * few + size))
        pre_t = jnp.concatenate([ref[at : at + size] for ref, at in rights], axis=1)
        for ref, side in ((send_ref, 1 - own), (keep_ref, own)):
            pieces = []
            for j in range(ref.shape[0] // block):
                start = (2 * j + side) * block
                pieces.append(
                    jnp.concatenate(
                        [
                            source[pl.ds(pl.multiple_of(start + at, 16), block)]
                            for source, at in lefts
                        ],
                        axis=1,
                    )
                )
            ref[...] = mm_nt(jnp.concatenate(pieces, axis=0), pre_t).astype(bf16)

    return body


def halve_kernel(block, bit, parts, extra_rows):
    def body(keep_in, *rest):
        got, (send_ref, keep_ref) = rest[:parts], rest[-2:]
        own = (lax.axis_index("batch") >> bit) & 1
        count = (send_ref.shape[0] - extra_rows) // block

        def total(part):
            added = jnp.concatenate([ref[part] for ref in got], axis=1).astype(f32)
            return (keep_in[part].astype(f32) + added).astype(bf16)

        for ref, side in ((send_ref, 1 - own), (keep_ref, own)):
            for j in range(count):
                start = pl.multiple_of((2 * j + side) * block, 16)
                ref[j * block : (j + 1) * block] = total(pl.ds(start, block))
            if extra_rows:
                last = 2 * count * block
                ref[count * block :] = total(slice(last, last + extra_rows))

    return body


def attention_back_kernel(
    probs_ref,
    q_t_ref,
    k_t_ref,
    v_t_ref,
    context_ref,
    d0,
    d1,
    d2,
    d3,
    e0,
    e1,
    e2,
    e3,
    token_sums,
    score_grad,
    out_t,
):
    slots = (d0, d1, d2, d3)
    outs = (e0, e1, e2, e3)
    size = len(slots)
    width, row_len = q_t_ref.shape
    span = row_len // size
    grad_t = jnp.concatenate([slot[...] for slot in slots], axis=1)
    grad = grad_t.T
    for h in range(width // HEAD_DIM):
        cols = slice(h * HEAD_DIM, (h + 1) * HEAD_DIM)
        for s in range(size):
            part = slice(s * span, (s + 1) * span)
            grad_part = grad[part, cols]
            delta = jnp.sum(
                grad_part.astype(f32) * context_ref[part, cols], axis=-1, keepdims=True
            )
            grad_probs = mm(grad_part, v_t_ref[cols])
            score_grad[part] = (probs_ref[h, part].astype(f32) * (grad_probs - delta)).astype(bf16)
        out_t[cols] = (mm_nt(k_t_ref[cols], score_grad[...]) * HEAD_DIM ** (-0.5)).astype(bf16)
        out_t[width + h * HEAD_DIM : width + (h + 1) * HEAD_DIM] = mm(
            q_t_ref[cols], score_grad[...]
        ).astype(bf16)
        out_t[2 * width + h * HEAD_DIM : 2 * width + (h + 1) * HEAD_DIM] = mm(
            grad_t[cols], probs_ref[h]
        ).astype(bf16)
    for s in range(size):
        outs[s][...] = out_t[:, s * span : (s + 1) * span]
    token_sums[...] = mm_nt(jnp.ones((8, row_len), bf16), out_t[...])


def head_products_kernel(
    x0, x1, x2, x3, e0, e1, e2, e3, token_sums, order_after, send_ref, keep_ref, total
):
    del order_after
    core = lax.axis_index("batch") & 1
    x_t = jnp.concatenate([ref[...].T for ref in (x0, x1, x2, x3)], axis=1)
    heads_t = jnp.concatenate([ref[...] for ref in (e0, e1, e2, e3)], axis=1)
    total[...] = mm_nt(x_t, heads_t)
    blocks = lax.axis_size("batch")
    rows, width = total.shape[0] // blocks, total.shape[1]
    padded = (send_ref.shape[0] - EXTRA) // (blocks // 2)
    for own, refs in ((0, (keep_ref, send_ref)), (1, (send_ref, keep_ref))):

        @pl.when(core == own)
        def _():
            for b in range(blocks):
                at = (b >> 1) * padded
                if padded != rows:
                    refs[b & 1][at : at + padded] = jnp.zeros((padded, width), bf16)
                refs[b & 1][at : at + rows] = total[b * rows : (b + 1) * rows].astype(bf16)

    sums = jnp.concatenate((token_sums[...], jnp.zeros((EXTRA - 8, width), f32)), axis=0)
    for ref in (send_ref, keep_ref):
        ref[(blocks // 2) * padded :] = sums.astype(bf16)


def grad_in_kernel(
    e0, e1, e2, e3, grad_mixed, w_query, w_key, w_value, out_ref, groups, weights, sems
):
    slots = (e0, e1, e2, e3)
    size = len(slots)
    me = lax.axis_index("blk")
    copies = [
        pltpu.make_async_copy(weight, weights.at[k], sems.at[k])
        for k, weight in enumerate((w_query, w_key, w_value))
    ]
    for copy in copies:
        copy.start()
    for s in range(size):
        groups[ahead(me, s, size)] = slots[s][...]
    total = grad_mixed[...]
    own = e0.shape[0] // 3
    for k in range(3):
        rows = [groups[g, k * own : (k + 1) * own] for g in range(size)]
        part = jnp.concatenate(rows, axis=0).T
        copies[k].wait()
        total += mm_nt(part, weights[k])
    out_ref[...] = total.astype(bf16)


def split_inner_kernel(keep, got, own_ref, s1, s2, s3, total):
    outs = (own_ref, s1, s2, s3)
    size = len(outs)
    me = lax.axis_index("blk")
    total[...] = keep[...].astype(f32) + got[...].astype(f32)
    width = total.shape[1] // size
    for s in range(size):
        cols = pl.ds(pl.multiple_of(ahead(me, s, size) * width, 128), width)
        outs[s][...] = total[:, cols].astype(outs[s].dtype)


def join_inner_kernel(own, r1, r2, r3, out_ref):
    rows = slice(0, out_ref.shape[0])
    total = own[rows] + r1[rows].astype(f32) + r2[rows].astype(f32) + r3[rows].astype(f32)
    out_ref[...] = total


def split_columns_kernel(keep, got, late, own_ref, s1, s2, s3, groups):
    outs = (s1, s2, s3)
    size = len(outs) + 1
    me = lax.axis_index("blk")
    total = keep[...].astype(f32) + got[...].astype(f32)
    last = total.shape[0] - EXTRA
    half = last // 2
    width = total.shape[1] // size
    sums = total[last:]
    row = lax.broadcasted_iota(jnp.int32, sums.shape, 0)
    group = lax.broadcasted_iota(jnp.int32, sums.shape, 1) // width
    for k, at in ((B_QUERY, 0), (B_VALUE, 2)):
        own_row = late[0:1, at * width : (at + 1) * width]
        sums = jnp.where(
            (row == k) & (group == me), jnp.concatenate([own_row] * size, axis=1), sums
        )
    extra = jnp.concatenate((sums[:, : 2 * width], sums[:, 2 * width :]), axis=0)
    for g in range(size):
        cols = slice(g * width, (g + 1) * width)
        slot = behind(me, g, size)
        groups[slot, :half] = jnp.concatenate((total[:half, cols], total[half:last, cols]), axis=1)
    own_ref[:half] = groups[0]
    own_ref[half:] = extra
    for s in range(1, size):
        outs[s - 1][:half] = groups[s].astype(bf16)
        outs[s - 1][half:] = extra.astype(bf16)


def join_rows_kernel(own, r1, r2, r3, first_ref, second_ref, *rest):
    sum_refs, (rows,) = rest[:-1], rest[-1:]
    total = own[...] + r1[...].astype(f32) + r2[...].astype(f32) + r3[...].astype(f32)
    half, width = total.shape[0] - 2 * EXTRA, total.shape[1] // 2
    rows[:half] = total[:half, :width]
    rows[half:] = total[:half, width:]
    ff_rows = first_ref.shape[0]
    first_ref[...] = rows[:ff_rows]
    second_ref[...] = rows[ff_rows : ff_rows + second_ref.shape[0]]
    sums = jnp.concatenate((total[half : half + EXTRA], total[half + EXTRA :]), axis=1)
    for k, ref in enumerate(sum_refs[:-1]):
        ref[...] = sums[k]
    model_width = sums.shape[1]
    for k in range(sum_refs[-1].shape[0] // model_width):
        sum_refs[-1][k * model_width : (k + 1) * model_width] = sums[B_INNER + k]


def last_sum_kernel(keep, got, q_ref, k_ref, v_ref, late_ref):
    total = keep[...].astype(f32) + got[...].astype(f32)
    rows, own = q_ref.shape
    for k, ref in enumerate((q_ref, k_ref, v_ref)):
        ref[...] = total[:rows, k * own : (k + 1) * own]
    last = total.shape[0] - EXTRA
    late_ref[...] = total[last : last + 8]


def run_kernel(body, operands, outs, scratch=(), in_hbm=(), limit=8, fill=0):
    vmem = pl.BlockSpec(memory_space=pltpu.VMEM)
    hbm = pl.BlockSpec(memory_space=pltpu.HBM)
    anywhere = pl.BlockSpec(memory_space=pl.ANY)

    def place(k):
        if k - len(operands) in in_hbm:
            return anywhere
        return hbm if k in in_hbm else vmem

    return pl.pallas_call(
        body,
        out_shape=[jax.ShapeDtypeStruct(shape, dtype) for shape, dtype in outs],
        in_specs=[place(k) for k in range(len(operands))],
        out_specs=[vmem] * len(outs),
        scratch_shapes=list(scratch),
        compiler_params=pltpu.CompilerParams(vmem_limit_bytes=limit * MIB),
        cost_estimate=pl.CostEstimate(
            flops=1 + fill * 10**9, bytes_accessed=1, transcendentals=0
        ),
    )(*operands)


def blk_shift(values, step):
    size = lax.axis_size("blk")
    return lax.ppermute(values, "blk", [(i, (i + step) % size) for i in range(size)])


def batch_swap(values, bits):
    size = lax.axis_size("batch")
    return lax.ppermute(values, "batch", [(i, i ^ bits) for i in range(size)])


def halve(keep, got, block, bit, after=(), extra_rows=EXTRA):
    got = got if isinstance(got, list) else [got]
    count = (keep.shape[0] - extra_rows) // block // 2
    shape = ((count * block + extra_rows, keep.shape[1]), bf16)
    return run_kernel(
        halve_kernel(block, bit, len(got), extra_rows),
        [keep, *got, *after],
        [shape, shape],
        in_hbm=[-1 - k for k in range(len(after))],
    )


def local(
    hidden_in,
    w_query,
    b_query,
    w_key,
    w_value,
    b_value,
    w_output,
    b_output,
    attn_gain,
    attn_shift,
    w_inner,
    b_inner,
    w_outer,
    b_outer,
    ffn_gain,
    ffn_shift,
    text_lengths,
    region_lengths,
    out_grad,
):
    _, span, width = hidden_in.shape
    hidden = w_inner.shape[1]
    size = lax.axis_size("blk")
    blocks = lax.axis_size("batch")
    bits = blocks.bit_length() - 1
    row_len = span * size
    own_heads = HEADS // size
    own_width = own_heads * HEAD_DIM
    steps = range(1, size)
    tokens_f32 = ((span, width), f32)
    tokens_bf16 = ((span, width), bf16)
    row = ((width,), f32)

    flat_in = hidden_in[0]
    x_slots = [blk_shift(flat_in, step) for step in steps]
    stacked = jnp.zeros((EXTRA, width), bf16)
    number = lax.broadcasted_iota(jnp.int32, stacked.shape, 0)
    for k, vector in (
        (B_OUTER, b_outer),
        (FFN_GAIN, ffn_gain),
        (FFN_SHIFT, ffn_shift),
        (ATTN_GAIN, attn_gain),
        (ATTN_SHIFT, attn_shift),
        (B_OUTPUT, b_output),
        (B_QUERY, b_query),
        (B_VALUE, b_value),
    ):
        stacked = jnp.where(number == k, vector[None, :], stacked)
    own_weights, own_bias, mask, vecs, x_own, grad_own, outer_copy = run_kernel(
        prep_kernel,
        [
            text_lengths,
            region_lengths,
            flat_in,
            out_grad[0],
            stacked,
            b_inner,
            w_query,
            w_key,
            w_value,
            w_outer,
        ],
        [
            ((width, 3 * own_width), bf16),
            ((8, 3 * own_width), f32),
            ((row_len, row_len), f32),
            ((EXTRA, width), f32),
            tokens_bf16,
            tokens_bf16,
            ((hidden, width), bf16),
        ],
        [pltpu.VMEM((3, width, 256), bf16), pltpu.SemaphoreType.DMA((4,))],
        in_hbm=(6, 7, 8, 9),
        limit=14,
    )
    x_slots = [x_own] + x_slots
    *context_slots, probs, qkv, context_own = run_kernel(
        attention_kernel,
        x_slots + [own_weights, own_bias, mask],
        [((own_width, span), bf16)] * size
        + [((own_heads, row_len, row_len), bf16)]
        + [((row_len, 3 * own_width), bf16), ((row_len, own_width), f32)],
        [pltpu.VMEM((row_len, width), bf16)],
        limit=14,
    )
    turned = run_kernel(
        transpose_kernel,
        [w_inner, outer_copy, qkv],
        [
            ((width, hidden), bf16),
            ((hidden, width), bf16),
            ((width, hidden), bf16),
        ]
        + [((own_width, row_len), bf16)] * 3,
        [pltpu.SemaphoreType.DMA((1,))],
        in_hbm=(0,),
        limit=20,
        fill=8,
    )
    ffn_weights, ffn_turned = (turned[0], outer_copy), turned[1:3]
    q_t, k_t, v_t = turned[3:]
    context_slots = context_slots[:1] + [
        blk_shift(context_slots[step], size - step) for step in steps
    ]
    ff_rows = hidden // blocks
    rows = -(-(width // blocks) // 16) * 16
    block = ff_rows + rows

    many = blocks // 4 * block
    few = blocks // 4 * rows
    (
        layer_out,
        left_own,
        left_core,
        left_x,
        inner_own,
        inner_core,
        inner_y,
        outer_low,
        slope,
        grad_summed,
        attn_hat,
        attn_inv,
        sums,
    ) = run_kernel(
        forward_kernel(blocks),
        [x_own]
        + context_slots
        + [vecs, grad_own, w_output]
        + [*ffn_weights, ffn_turned[0]],
        [
            tokens_bf16,
            ((many, span), bf16),
            ((many, span), bf16),
            ((2 * many, span), bf16),
            ((few, span), bf16),
            ((few, span), bf16),
            ((2 * few, span), bf16),
            tokens_bf16,
            ((span, hidden), f32),
            tokens_f32,
            tokens_f32,
            ((span, 1), f32),
            ((EXTRA, width), f32),
        ],
        [
            pltpu.VMEM((size, own_width, span), bf16),
            pltpu.VMEM((4, many, span), bf16),
            pltpu.VMEM((4, few, span), bf16),
        ],
        in_hbm=(-1,),
        limit=20,
    )
    tall = 2 * rows_of(width, span) + rows_of(width, EXTRA)
    x_sent, y_sent, grad_mixed, *context_grads = run_kernel(
        backward_kernel,
        [
            outer_low,
            slope,
            grad_summed,
            attn_hat,
            attn_inv,
            left_x,
            inner_y,
            vecs,
            sums,
            w_output,
            *ffn_turned,
        ],
        [((2 * many + tall, span), bf16), ((2 * few + hidden, span), bf16), tokens_f32]
        + [((own_width, span), bf16)] * size,
        [pltpu.VMEM((size, own_width, span), bf16), pltpu.VMEM((EXTRA, width), f32)],
        limit=20,
    )
    x_got = batch_swap(x_sent, 2)
    y_got = batch_swap(y_sent, 4)
    context_grads = context_grads[:1] + [blk_shift(context_grads[step], step) for step in steps]
    *head_grads, token_sums = run_kernel(
        attention_back_kernel,
        [probs, q_t, k_t, v_t, context_own] + context_grads,
        [((3 * own_width, span), bf16)] * size + [((8, 3 * own_width), f32)],
        [pltpu.VMEM((row_len, row_len), bf16), pltpu.VMEM((3 * own_width, row_len), bf16)],
    )
    head_slots = head_grads[:1] + [blk_shift(head_grads[step], size - step) for step in steps]
    packed = run_kernel(
        pack_kernel,
        [inner_core, y_sent, y_got, token_sums],
        [((2 * (few + hidden), span), bf16)],
        in_hbm=(-1,),
        limit=10,
    )[0]
    inner_send, inner_keep = run_kernel(
        inner_products_kernel(rows),
        [inner_own, y_sent, y_got, batch_swap(packed, 1)],
        [((few // 2, hidden), bf16)] * 2,
        limit=14,
    )
    inner_got = batch_swap(inner_send, 2)
    for bit in range(3, bits):
        inner_send, inner_keep = halve(inner_keep, inner_got, rows, bit, extra_rows=0)
        inner_got = batch_swap(inner_send, 1 << bit)
    packed = run_kernel(
        pack_kernel,
        [left_core, x_sent, x_got],
        [((2 * (many + tall), span), bf16)],
    )[0]
    send, keep = run_kernel(
        first_products_kernel(block, ff_rows, span),
        [left_own, x_sent, x_got, batch_swap(packed, 1)],
        [((many // 2 + EXTRA, width), bf16)] * 2,
        limit=14,
    )
    got = batch_swap(send, 4)
    for bit in range(3, bits):
        send, keep = halve(keep, got, block, bit)
        got = batch_swap(send, 1 << bit)
    wide = 3 * own_width
    head_send, head_keep = run_kernel(
        head_products_kernel,
        x_slots + head_grads + [token_sums, send],
        [((blocks // 2 * rows + EXTRA, wide), bf16)] * 2,
        [pltpu.VMEM((width, wide), f32)],
        in_hbm=(-1,),
        limit=10,
    )
    head_got = batch_swap(head_send, 1)
    head_send, head_keep = halve(head_keep, head_got, rows, 1, [inner_got] + head_slots[1:-1])
    head_got = batch_swap(head_send, 2)
    for bit in range(2, bits):
        head_send, head_keep = halve(head_keep, head_got, rows, bit, [got])
        head_got = batch_swap(head_send, 1 << bit)
    inner_part, *inner_sends = run_kernel(
        split_inner_kernel,
        [inner_keep, inner_got],
        [((rows, width), f32)] + [((rows, width), bf16)] * (size - 1),
        [pltpu.VMEM((rows, hidden), f32)],
    )
    inner_parts = [blk_shift(inner_sends[step - 1], step) for step in steps]
    grad_in = run_kernel(
        grad_in_kernel,
        head_slots + [grad_mixed, w_query, w_key, w_value],
        [tokens_bf16],
        [
            pltpu.VMEM((size, 3 * own_width, span), bf16),
            pltpu.VMEM((3, width, width), bf16),
            pltpu.SemaphoreType.DMA((3,)),
        ],
        in_hbm=(5, 6, 7),
        limit=10,
        fill=4,
    )[0]
    out_rows = width // blocks
    own_cols = ((out_rows, own_width), f32)
    *grad_qkv, late = run_kernel(
        last_sum_kernel,
        [head_keep, head_got],
        [own_cols] * 3 + [((8, wide), f32)],
    )
    message = (block // 2 + 2 * EXTRA, 2 * own_width)
    own_part, *sends = run_kernel(
        split_columns_kernel,
        [keep, got, late],
        [(message, f32)] + [(message, bf16)] * (size - 1),
        [pltpu.VMEM((size, block // 2, 2 * own_width), f32)],
    )
    parts = [blk_shift(sends[step - 1], step) for step in steps]
    grad_w_inner = run_kernel(
        join_inner_kernel, [inner_part] + inner_parts, [((out_rows, width), f32)]
    )[0]
    grad_w_outer, grad_w_output, *sums = run_kernel(
        join_rows_kernel,
        [own_part] + parts,
        [((ff_rows, own_width), f32), own_cols] + [row] * 8 + [((hidden,), f32)],
        [pltpu.VMEM((block, own_width), f32)],
    )
    return (
        layer_out[None],
        grad_in[None],
        grad_qkv[0],
        sums[B_QUERY],
        grad_qkv[1],
        grad_qkv[2],
        sums[B_VALUE],
        grad_w_output,
        sums[B_OUTPUT],
        sums[ATTN_GAIN],
        sums[ATTN_SHIFT],
        grad_w_inner,
        sums[B_INNER],
        grad_w_outer,
        sums[B_OUTER],
        sums[FFN_GAIN],
        sums[FFN_SHIFT],
    )


def solution(mesh):
    rows = P("batch", "blk", None)
    tile = P("batch", "blk")
    return jax.shard_map(
        local,
        mesh=mesh,
        in_specs=(rows,) + (P(),) * 15 + (P("batch", None), P("batch", None), rows),
        out_specs=(
            rows,
            rows,
            tile,
            P(),
            tile,
            tile,
            P(),
            tile,
            P(),
            P(),
            P(),
            tile,
            P(),
            tile,
            P(),
            P(),
            P(),
        ),
        check_vma=False,
    )
```

```python
import jax
import jax.numpy as jnp
from jax import lax
from jax.experimental import pallas as pl
from jax.experimental.pallas import tpu as pltpu
from jax.sharding import PartitionSpec as P

HEADS = 12
HEAD_DIM = 64
PAIRS = 4

NORM_EPS = 1e-05
MASKED_SCORE = -1e30
INV_ROOT_TWO = 0.7071067811865476
INV_ROOT_TWO_PI = 0.3989422804014327
MIB = 1024 * 1024

B_OUTER, FFN_GAIN, FFN_SHIFT, ATTN_GAIN, ATTN_SHIFT, B_OUTPUT, B_QUERY, B_VALUE, B_INNER = range(9)

EXTRA = 16

f32 = jnp.float32
bf16 = jnp.bfloat16


def mm(left, right):
    return jnp.dot(left, right, preferred_element_type=f32)


def mm_nt(left, right):
    return lax.dot_general(left, right, (((1,), (1,)), ((), ())), preferred_element_type=f32)


def norm_stats(values_in):
    row_mean = jnp.mean(values_in, axis=-1, keepdims=True)
    centred = values_in - row_mean
    inv_dev = lax.rsqrt(jnp.mean(centred * centred, axis=-1, keepdims=True) + NORM_EPS)
    return centred * inv_dev, inv_dev


def norm_back(scaled, normed, inv_dev):
    centre_term = jnp.mean(scaled, axis=-1, keepdims=True)
    slope_term = jnp.mean(scaled * normed, axis=-1, keepdims=True)
    return inv_dev * (scaled - centre_term - normed * slope_term)


def sum_rows(values):
    return jnp.sum(values, axis=0, keepdims=True)


def as_row(ref):
    return ref[...].astype(f32).reshape(1, -1)


def rows_of(width, count):
    return width // 128 * count


def narrow(ref, first, values):
    count = values.shape[0]
    for k in range(values.shape[1] // 128):
        at = first + k * count
        ref[at : at + count] = values[:, k * 128 : (k + 1) * 128]


def widen(ref, first, count, width):
    return jnp.concatenate(
        [ref[first + k * count : first + (k + 1) * count] for k in range(width // 128)], axis=1
    )


def ahead(me, step, size):
    return lax.rem(me + step, size)


def behind(me, group, size):
    return lax.rem(group - me + size, size)


def lane_window(me, width):
    return pl.multiple_of((me * width) // 128 * 128, 128)


def prep_kernel(
    text,
    region,
    x_ref,
    grad_ref,
    stacked,
    b_inner,
    w_query,
    w_key,
    w_value,
    w_outer,
    own_weights,
    own_bias,
    mask,
    vecs,
    x_out,
    grad_out,
    outer_out,
    windows,
    sems,
):
    me = lax.axis_index("blk")
    row_len = mask.shape[0]
    span = x_ref.shape[0]
    size = row_len // span
    width = own_weights.shape[1] // 3
    model_width = x_ref.shape[1]
    start = lane_window(me, width)
    copies = []
    for k, weight in enumerate((w_query, w_key, w_value)):
        part = weight.at[:, pl.ds(start, windows.shape[2])]
        copies.append(pltpu.make_async_copy(part, windows.at[k], sems.at[k]))
    copies.append(pltpu.make_async_copy(w_outer, outer_out, sems.at[3]))
    for copy in copies:
        copy.start()
    x_out[...] = x_ref[...]
    grad_out[...] = grad_ref[...]
    vecs[...] = stacked[...].astype(f32)
    hidden_row = as_row(b_inner)
    for k in range(hidden_row.shape[1] // model_width):
        part = slice(k * model_width, (k + 1) * model_width)
        vecs[B_INNER + k : B_INNER + k + 1] = hidden_row[:, part]
    own_bias[...] = jnp.zeros(own_bias.shape, f32)
    for at, k in ((0, B_QUERY), (2, B_VALUE)):
        row = vecs[k : k + 1]
        out = jnp.zeros((1, width), f32)
        for g in range(size):
            out = jnp.where(me == g, row[:, g * width : (g + 1) * width], out)
        own_bias[0:1, at * width : (at + 1) * width] = out

    ends = []
    total = jnp.zeros((1, 1), jnp.int32)
    for k in range(PAIRS):
        total = total + text[:, k : k + 1] + region[:, k : k + 1]
        ends.append(total)

    def segments(dim):
        shape = [1, 1]
        shape[dim] = span
        parts = []
        for s in range(size):
            first = lax.rem(me - s + size, size) * span
            pos = lax.broadcasted_iota(jnp.int32, tuple(shape), dim) + first
            seg = jnp.zeros(tuple(shape), jnp.int32)
            for end in ends:
                seg = seg + (pos >= end).astype(jnp.int32)
            parts.append(seg)
        return jnp.concatenate(parts, axis=dim)

    seg_q = segments(0)
    seg_k = segments(1)
    diagonal = lax.broadcasted_iota(jnp.int32, (row_len, row_len), 0) == lax.broadcasted_iota(
        jnp.int32, (row_len, row_len), 1
    )
    allowed = (seg_q == seg_k) & ((seg_k < PAIRS) | diagonal)
    mask[...] = jnp.where(allowed, 0.0, MASKED_SCORE)
    off = windows.shape[2] - width
    for k in range(3):
        copies[k].wait()
        window = windows[k]
        own_weights[:, k * width : (k + 1) * width] = jnp.where(
            (me * width) % 128 == 0, window[:, :width], window[:, off:]
        )
    copies[3].wait()


def transpose_kernel(
    w_inner, w_outer, qkv, inner_out, inner_t, outer_t, q_t, k_t, v_t, sems
):
    copy = pltpu.make_async_copy(w_inner, inner_out, sems.at[0])
    copy.start()
    own = q_t.shape[0]
    for k, ref in enumerate((q_t, k_t, v_t)):
        ref[...] = qkv[:, k * own : (k + 1) * own].T
    width, hidden = inner_out.shape
    parts = [slice(k * width, (k + 1) * width) for k in range(hidden // width)]
    for part in parts:
        outer_t[:, part] = w_outer[part].T
    copy.wait()
    for part in parts:
        inner_t[part] = inner_out[:, part].T


def attention_kernel(
    x0, x1, x2, x3, own_weights, own_bias, mask, c0, c1, c2, c3, probs_ref, qkv_ref, context_ref, x_all
):
    xs = (x0, x1, x2, x3)
    context_refs = (c0, c1, c2, c3)
    size = len(xs)
    span = x0.shape[0]
    width = own_weights.shape[1] // 3
    for s in range(size):
        x_all[s * span : (s + 1) * span] = xs[s][...]
    qkv = (mm(x_all[...], own_weights[...]) + own_bias[0:1]).astype(bf16)
    query = (qkv[:, :width] * HEAD_DIM ** (-0.5)).astype(bf16)
    key = qkv[:, width : 2 * width]
    value = qkv[:, 2 * width :]
    qkv_ref[:, :width] = query
    qkv_ref[:, width:] = qkv[:, width:]
    tasks = [(h, s) for s in range(size) for h in range(width // HEAD_DIM)]

    def scores_of(task):
        h, s = task
        cols = slice(h * HEAD_DIM, (h + 1) * HEAD_DIM)
        part = slice(s * span, (s + 1) * span)
        return mm_nt(query[part, cols], key[:, cols])

    following = scores_of(tasks[0])
    done = []
    for k, (h, s) in enumerate(tasks):
        part = slice(s * span, (s + 1) * span)
        scores = following + mask[part]
        if k + 1 < len(tasks):
            following = scores_of(tasks[k + 1])
        weights = jnp.exp(scores - jnp.max(scores, axis=-1, keepdims=True))
        probs = (weights * (1.0 / jnp.sum(weights, axis=-1, keepdims=True))).astype(bf16)
        probs_ref[h, part] = probs
        done.append(mm(probs, value[:, h * HEAD_DIM : (h + 1) * HEAD_DIM]))
        if h == width // HEAD_DIM - 1:
            context = jnp.concatenate(done, axis=1)
            context_ref[part] = context
            context_refs[s][...] = context.astype(bf16).T
            done = []


def forward_kernel(blocks):
    def body(
        x_ref,
        c0,
        c1,
        c2,
        c3,
        vecs,
        grad_ref,
        w_output,
        w_inner,
        w_outer,
        order_after,
        out_ref,
        left_own,
        left_core,
        left_x,
        inner_own,
        inner_core,
        inner_y,
        outer_low_ref,
        slope_ref,
        grad_summed_ref,
        hat_ref,
        inv_ref,
        sums_ref,
        groups,
        left,
        inner,
    ):
        del order_after
        batch_me = lax.axis_index("batch")
        me = lax.axis_index("blk")
        slots = (c0, c1, c2, c3)
        size = len(slots)
        width, hidden = w_inner.shape
        step = width
        count = hidden // step
        ff_rows = hidden // blocks
        many = left_own.shape[0]
        block = many // (blocks // 4)

        def left_rows(b, first, values):
            at = (b >> 2) * block + first
            left[jnp.bitwise_xor(batch_me & 3, b & 3), at : at + values.shape[0]] = values

        def vec(k):
            return vecs[k : k + 1]

        for s in range(size):
            groups[ahead(me, s, size)] = slots[s][...]
        context_t = jnp.concatenate([groups[g] for g in range(size)], axis=0)
        context = context_t.T
        mixed = x_ref[...].astype(f32) + mm(context, w_output[...]) + vec(B_OUTPUT)
        hat, inv = norm_stats(mixed)
        hat_ref[...] = hat
        inv_ref[...] = inv
        attn_norm = hat * vec(ATTN_GAIN) + vec(ATTN_SHIFT)
        inner_in = attn_norm.astype(bf16)
        outer = jnp.zeros(attn_norm.shape, f32)
        cols = [slice(k * step, (k + 1) * step) for k in range(count)]
        following = mm(inner_in, w_inner[:, cols[0]])
        for k in range(count):
            pre = following + vec(B_INNER + k)
            if k + 1 < count:
                following = mm(inner_in, w_inner[:, cols[k + 1]])
            cdf = 0.5 + 0.5 * lax.erf(pre * INV_ROOT_TWO)
            act = (pre * cdf).astype(bf16)
            slope_ref[:, cols[k]] = cdf + pre * (jnp.exp(-0.5 * pre * pre) * INV_ROOT_TWO_PI)
            outer += mm(act, w_outer[cols[k]])
            act_t = act.T
            for j in range(step // ff_rows):
                left_rows(k * step // ff_rows + j, 0, act_t[j * ff_rows : (j + 1) * ff_rows])
        summed = attn_norm + outer + vec(B_OUTER)
        final_hat, final_inv = norm_stats(summed)
        gain = vec(FFN_GAIN)
        upstream = grad_ref[...].astype(f32)
        grad_summed = norm_back(upstream * gain, final_hat, final_inv)
        grad_summed_ref[...] = grad_summed
        outer_low = grad_summed.astype(bf16)
        outer_low_ref[...] = outer_low
        out_ref[...] = (final_hat * gain + vec(FFN_SHIFT)).astype(bf16)
        sums_ref[...] = jnp.zeros(sums_ref.shape, f32)
        sums_ref[B_OUTER : B_OUTER + 1] = sum_rows(outer_low.astype(f32))
        sums_ref[FFN_GAIN : FFN_GAIN + 1] = sum_rows(upstream * final_hat)
        sums_ref[FFN_SHIFT : FFN_SHIFT + 1] = sum_rows(upstream)
        out_rows = width // blocks
        padded = block - ff_rows
        inner_t = inner_in.T

        def block_rows(values, b):
            if padded == out_rows:
                return values[b * out_rows : (b + 1) * out_rows]
            row = lax.broadcasted_iota(jnp.int32, (padded, width), 0)
            col = lax.broadcasted_iota(jnp.int32, (padded, width), 1)
            pick = ((row < out_rows) & (col == row + b * out_rows)).astype(f32).astype(bf16)
            return mm(pick, values).astype(bf16)

        for b in range(blocks):
            left_rows(b, ff_rows, block_rows(context_t, b))
            owner = jnp.bitwise_xor(batch_me & 1, b & 1) + 2 * jnp.bitwise_xor(
                (batch_me >> 2) & 1, (b >> 2) & 1
            )
            at = (((b >> 3) << 1) | ((b >> 1) & 1)) * padded
            inner[owner, at : at + padded] = block_rows(inner_t, b)
        left_own[...] = left[0]
        left_core[...] = left[1]
        left_x[:many] = left[2]
        left_x[many:] = left[3]
        few = inner_own.shape[0]
        inner_own[...] = inner[0]
        inner_core[...] = inner[1]
        inner_y[:few] = inner[2]
        inner_y[few:] = inner[3]

    return body


def backward_kernel(
    outer_low_ref,
    slope_ref,
    grad_summed_ref,
    hat_ref,
    inv_ref,
    left_x,
    inner_y,
    vecs,
    sums_in,
    w_output,
    w_inner_t,
    w_outer_t,
    x_ref,
    y_ref,
    grad_mixed_ref,
    g0,
    g1,
    g2,
    g3,
    groups,
    sums,
):
    hidden, width = w_inner_t.shape
    group_refs = (g0, g1, g2, g3)
    size = len(group_refs)
    me = lax.axis_index("blk")
    step = width
    rows = width // size
    span = outer_low_ref.shape[0]
    count = hidden // step
    parts = [slice(k * step, (k + 1) * step) for k in range(count)]
    sums[...] = sums_in[...]
    outer_low = outer_low_ref[...]
    grad_norm = grad_summed_ref[...]
    many, few = left_x.shape[0], inner_y.shape[0]
    x_ref[:many] = left_x[...]
    y_ref[:few] = inner_y[...]
    following = mm(outer_low, w_outer_t[:, parts[0]])
    for k in range(count):
        pre_low = (following * slope_ref[:, parts[k]]).astype(bf16)
        if k + 1 < count:
            following = mm(outer_low, w_outer_t[:, parts[k + 1]])
        grad_norm += mm(pre_low, w_inner_t[parts[k]])
        y_ref[few + k * step : few + (k + 1) * step] = pre_low.T
        sums[B_INNER + k : B_INNER + k + 1] = sum_rows(pre_low.astype(f32))
    hat = hat_ref[...]
    grad_mixed = norm_back(grad_norm * vecs[ATTN_GAIN : ATTN_GAIN + 1], hat, inv_ref[...])
    grad_mixed_ref[...] = grad_mixed
    mixed_low = grad_mixed.astype(bf16)
    narrow(x_ref, many, outer_low)
    narrow(x_ref, many + rows_of(width, span), mixed_low)
    context_grad_t = mm_nt(w_output[...], mixed_low).astype(bf16)
    for g in range(size):
        groups[behind(me, g, size)] = context_grad_t[g * rows : (g + 1) * rows]
    for s in range(size):
        group_refs[s][...] = groups[s]
    sums[ATTN_GAIN : ATTN_GAIN + 1] = sum_rows(grad_norm * hat)
    sums[ATTN_SHIFT : ATTN_SHIFT + 1] = sum_rows(grad_norm)
    sums[B_OUTPUT : B_OUTPUT + 1] = sum_rows(mixed_low.astype(f32))
    narrow(x_ref, many + 2 * rows_of(width, span), sums[...].astype(bf16))


def pack_kernel(core_rows, own, got, *after_and_out):
    out_ref = after_and_out[-1]
    many = core_rows.shape[0]
    size = own.shape[0] - 2 * many
    out_ref[:many] = core_rows[...]
    out_ref[many : 2 * many] = got[many : 2 * many]
    out_ref[2 * many : 2 * many + size] = own[2 * many :]
    out_ref[2 * many + size :] = got[2 * many :]


def first_products_kernel(block, ff_rows, span):
    def body(left_own, sent, received, packed, send_ref, keep_ref):
        many = left_own.shape[0]
        size = sent.shape[0] - 2 * many
        width = send_ref.shape[1]
        tall = rows_of(width, span)
        own = (lax.axis_index("batch") >> 2) & 1
        lefts = ((left_own, 0), (received, 0), (packed, 0), (packed, many))
        rights = (
            (sent, 2 * many),
            (received, 2 * many),
            (packed, 2 * many),
            (packed, 2 * many + size),
        )
        outer_low = jnp.concatenate([widen(ref, at, span, width) for ref, at in rights], axis=0)
        mixed_low = jnp.concatenate(
            [widen(ref, at + tall, span, width) for ref, at in rights], axis=0
        )
        sums = jnp.zeros((EXTRA, width), f32)
        for ref, at in rights:
            sums += widen(ref, at + 2 * tall, EXTRA, width).astype(f32)
        for ref, side in ((send_ref, 1 - own), (keep_ref, own)):
            count = (ref.shape[0] - EXTRA) // block
            for j in range(count):

                def rows(first, number):
                    start = (2 * j + side) * block + first
                    return jnp.concatenate(
                        [
                            source[pl.ds(pl.multiple_of(start + at, 16), number)]
                            for source, at in lefts
                        ],
                        axis=1,
                    )

                at = j * block
                ref[at : at + ff_rows] = mm(rows(0, ff_rows), outer_low).astype(bf16)
                ref[at + ff_rows : at + block] = mm(
                    rows(ff_rows, block - ff_rows), mixed_low
                ).astype(bf16)
            ref[count * block :] = sums.astype(bf16)

    return body


def inner_products_kernel(block):
    def body(inner_own, sent, received, packed, send_ref, keep_ref):
        few = inner_own.shape[0]
        size = sent.shape[0] - 2 * few
        own = (lax.axis_index("batch") >> 1) & 1
        lefts = ((inner_own, 0), (received, 0), (packed, 0), (packed, few))
        rights = ((sent, 2 * few), (received, 2 * few), (packed, 2 * few), (packed, 2 * few + size))
        pre_t = jnp.concatenate([ref[at : at + size] for ref, at in rights], axis=1)
        for ref, side in ((send_ref, 1 - own), (keep_ref, own)):
            pieces = []
            for j in range(ref.shape[0] // block):
                start = (2 * j + side) * block
                pieces.append(
                    jnp.concatenate(
                        [
                            source[pl.ds(pl.multiple_of(start + at, 16), block)]
                            for source, at in lefts
                        ],
                        axis=1,
                    )
                )
            ref[...] = mm_nt(jnp.concatenate(pieces, axis=0), pre_t).astype(bf16)

    return body


def halve_kernel(block, bit, parts, extra_rows):
    def body(keep_in, *rest):
        got, (send_ref, keep_ref) = rest[:parts], rest[-2:]
        own = (lax.axis_index("batch") >> bit) & 1
        count = (send_ref.shape[0] - extra_rows) // block

        def total(part):
            added = jnp.concatenate([ref[part] for ref in got], axis=1).astype(f32)
            return (keep_in[part].astype(f32) + added).astype(bf16)

        for ref, side in ((send_ref, 1 - own), (keep_ref, own)):
            for j in range(count):
                start = pl.multiple_of((2 * j + side) * block, 16)
                ref[j * block : (j + 1) * block] = total(pl.ds(start, block))
            if extra_rows:
                last = 2 * count * block
                ref[count * block :] = total(slice(last, last + extra_rows))

    return body


def attention_back_kernel(
    probs_ref,
    q_t_ref,
    k_t_ref,
    v_t_ref,
    context_ref,
    d0,
    d1,
    d2,
    d3,
    e0,
    e1,
    e2,
    e3,
    token_sums,
    score_grad,
    out_t,
):
    slots = (d0, d1, d2, d3)
    outs = (e0, e1, e2, e3)
    size = len(slots)
    width, row_len = q_t_ref.shape
    span = row_len // size
    grad_t = jnp.concatenate([slot[...] for slot in slots], axis=1)
    grad = grad_t.T
    for h in range(width // HEAD_DIM):
        cols = slice(h * HEAD_DIM, (h + 1) * HEAD_DIM)
        for s in range(size):
            part = slice(s * span, (s + 1) * span)
            grad_part = grad[part, cols]
            delta = jnp.sum(
                grad_part.astype(f32) * context_ref[part, cols], axis=-1, keepdims=True
            )
            grad_probs = mm(grad_part, v_t_ref[cols])
            score_grad[part] = (probs_ref[h, part].astype(f32) * (grad_probs - delta)).astype(bf16)
        out_t[cols] = (mm_nt(k_t_ref[cols], score_grad[...]) * HEAD_DIM ** (-0.5)).astype(bf16)
        out_t[width + h * HEAD_DIM : width + (h + 1) * HEAD_DIM] = mm(
            q_t_ref[cols], score_grad[...]
        ).astype(bf16)
        out_t[2 * width + h * HEAD_DIM : 2 * width + (h + 1) * HEAD_DIM] = mm(
            grad_t[cols], probs_ref[h]
        ).astype(bf16)
    for s in range(size):
        outs[s][...] = out_t[:, s * span : (s + 1) * span]
    token_sums[...] = mm_nt(jnp.ones((8, row_len), bf16), out_t[...])


def head_products_kernel(
    x0, x1, x2, x3, e0, e1, e2, e3, token_sums, order_after, send_ref, keep_ref, total
):
    del order_after
    core = lax.axis_index("batch") & 1
    x_t = jnp.concatenate([ref[...].T for ref in (x0, x1, x2, x3)], axis=1)
    heads_t = jnp.concatenate([ref[...] for ref in (e0, e1, e2, e3)], axis=1)
    total[...] = mm_nt(x_t, heads_t)
    blocks = lax.axis_size("batch")
    rows, width = total.shape[0] // blocks, total.shape[1]
    padded = (send_ref.shape[0] - EXTRA) // (blocks // 2)
    for own, refs in ((0, (keep_ref, send_ref)), (1, (send_ref, keep_ref))):

        @pl.when(core == own)
        def _():
            for b in range(blocks):
                at = (b >> 1) * padded
                if padded != rows:
                    refs[b & 1][at : at + padded] = jnp.zeros((padded, width), bf16)
                refs[b & 1][at : at + rows] = total[b * rows : (b + 1) * rows].astype(bf16)

    sums = jnp.concatenate((token_sums[...], jnp.zeros((EXTRA - 8, width), f32)), axis=0)
    for ref in (send_ref, keep_ref):
        ref[(blocks // 2) * padded :] = sums.astype(bf16)


def grad_in_kernel(
    e0, e1, e2, e3, grad_mixed, w_query, w_key, w_value, out_ref, groups, weights, sems
):
    slots = (e0, e1, e2, e3)
    size = len(slots)
    me = lax.axis_index("blk")
    copies = [
        pltpu.make_async_copy(weight, weights.at[k], sems.at[k])
        for k, weight in enumerate((w_query, w_key, w_value))
    ]
    for copy in copies:
        copy.start()
    for s in range(size):
        groups[ahead(me, s, size)] = slots[s][...]
    total = grad_mixed[...]
    own = e0.shape[0] // 3
    for k in range(3):
        rows = [groups[g, k * own : (k + 1) * own] for g in range(size)]
        part = jnp.concatenate(rows, axis=0).T
        copies[k].wait()
        total += mm_nt(part, weights[k])
    out_ref[...] = total.astype(bf16)


def split_inner_kernel(keep, got, own_ref, s1, s2, s3, total):
    outs = (own_ref, s1, s2, s3)
    size = len(outs)
    me = lax.axis_index("blk")
    total[...] = keep[...].astype(f32) + got[...].astype(f32)
    width = total.shape[1] // size
    for s in range(size):
        cols = pl.ds(pl.multiple_of(ahead(me, s, size) * width, 128), width)
        outs[s][...] = total[:, cols].astype(outs[s].dtype)


def join_inner_kernel(own, r1, r2, r3, out_ref):
    rows = slice(0, out_ref.shape[0])
    total = own[rows] + r1[rows].astype(f32) + r2[rows].astype(f32) + r3[rows].astype(f32)
    out_ref[...] = total


def split_columns_kernel(keep, got, late, own_ref, s1, s2, s3, groups):
    outs = (s1, s2, s3)
    size = len(outs) + 1
    me = lax.axis_index("blk")
    total = keep[...].astype(f32) + got[...].astype(f32)
    last = total.shape[0] - EXTRA
    half = last // 2
    width = total.shape[1] // size
    sums = total[last:]
    row = lax.broadcasted_iota(jnp.int32, sums.shape, 0)
    group = lax.broadcasted_iota(jnp.int32, sums.shape, 1) // width
    for k, at in ((B_QUERY, 0), (B_VALUE, 2)):
        own_row = late[0:1, at * width : (at + 1) * width]
        sums = jnp.where(
            (row == k) & (group == me), jnp.concatenate([own_row] * size, axis=1), sums
        )
    extra = jnp.concatenate((sums[:, : 2 * width], sums[:, 2 * width :]), axis=0)
    for g in range(size):
        cols = slice(g * width, (g + 1) * width)
        slot = behind(me, g, size)
        groups[slot, :half] = jnp.concatenate((total[:half, cols], total[half:last, cols]), axis=1)
    own_ref[:half] = groups[0]
    own_ref[half:] = extra
    for s in range(1, size):
        outs[s - 1][:half] = groups[s].astype(bf16)
        outs[s - 1][half:] = extra.astype(bf16)


def join_rows_kernel(own, r1, r2, r3, first_ref, second_ref, *rest):
    sum_refs, (rows,) = rest[:-1], rest[-1:]
    total = own[...] + r1[...].astype(f32) + r2[...].astype(f32) + r3[...].astype(f32)
    half, width = total.shape[0] - 2 * EXTRA, total.shape[1] // 2
    rows[:half] = total[:half, :width]
    rows[half:] = total[:half, width:]
    ff_rows = first_ref.shape[0]
    first_ref[...] = rows[:ff_rows]
    second_ref[...] = rows[ff_rows : ff_rows + second_ref.shape[0]]
    sums = jnp.concatenate((total[half : half + EXTRA], total[half + EXTRA :]), axis=1)
    for k, ref in enumerate(sum_refs[:-1]):
        ref[...] = sums[k]
    model_width = sums.shape[1]
    for k in range(sum_refs[-1].shape[0] // model_width):
        sum_refs[-1][k * model_width : (k + 1) * model_width] = sums[B_INNER + k]


def last_sum_kernel(keep, got, order_after, q_ref, k_ref, v_ref, late_ref):
    del order_after
    total = keep[...].astype(f32) + got[...].astype(f32)
    rows, own = q_ref.shape
    for k, ref in enumerate((q_ref, k_ref, v_ref)):
        ref[...] = total[:rows, k * own : (k + 1) * own]
    last = total.shape[0] - EXTRA
    late_ref[...] = total[last : last + 8]


def run_kernel(body, operands, outs, scratch=(), in_hbm=(), limit=8, fill=0):
    vmem = pl.BlockSpec(memory_space=pltpu.VMEM)
    hbm = pl.BlockSpec(memory_space=pltpu.HBM)
    anywhere = pl.BlockSpec(memory_space=pl.ANY)

    def place(k):
        if k - len(operands) in in_hbm:
            return anywhere
        return hbm if k in in_hbm else vmem

    return pl.pallas_call(
        body,
        out_shape=[jax.ShapeDtypeStruct(shape, dtype) for shape, dtype in outs],
        in_specs=[place(k) for k in range(len(operands))],
        out_specs=[vmem] * len(outs),
        scratch_shapes=list(scratch),
        compiler_params=pltpu.CompilerParams(vmem_limit_bytes=limit * MIB),
        cost_estimate=pl.CostEstimate(
            flops=1 + fill * 10**9, bytes_accessed=1, transcendentals=0
        ),
    )(*operands)


def blk_shift(values, step):
    size = lax.axis_size("blk")
    return lax.ppermute(values, "blk", [(i, (i + step) % size) for i in range(size)])


def batch_swap(values, bits):
    size = lax.axis_size("batch")
    return lax.ppermute(values, "batch", [(i, i ^ bits) for i in range(size)])


def halve(keep, got, block, bit, after=(), extra_rows=EXTRA):
    got = got if isinstance(got, list) else [got]
    count = (keep.shape[0] - extra_rows) // block // 2
    shape = ((count * block + extra_rows, keep.shape[1]), bf16)
    return run_kernel(
        halve_kernel(block, bit, len(got), extra_rows),
        [keep, *got, *after],
        [shape, shape],
        in_hbm=[-1 - k for k in range(len(after))],
    )


def local(
    hidden_in,
    w_query,
    b_query,
    w_key,
    w_value,
    b_value,
    w_output,
    b_output,
    attn_gain,
    attn_shift,
    w_inner,
    b_inner,
    w_outer,
    b_outer,
    ffn_gain,
    ffn_shift,
    text_lengths,
    region_lengths,
    out_grad,
):
    _, span, width = hidden_in.shape
    hidden = w_inner.shape[1]
    size = lax.axis_size("blk")
    blocks = lax.axis_size("batch")
    bits = blocks.bit_length() - 1
    row_len = span * size
    own_heads = HEADS // size
    own_width = own_heads * HEAD_DIM
    steps = range(1, size)
    tokens_f32 = ((span, width), f32)
    tokens_bf16 = ((span, width), bf16)
    row = ((width,), f32)

    flat_in = hidden_in[0]
    x_slots = [blk_shift(flat_in, step) for step in steps]
    stacked = jnp.zeros((EXTRA, width), bf16)
    number = lax.broadcasted_iota(jnp.int32, stacked.shape, 0)
    for k, vector in (
        (B_OUTER, b_outer),
        (FFN_GAIN, ffn_gain),
        (FFN_SHIFT, ffn_shift),
        (ATTN_GAIN, attn_gain),
        (ATTN_SHIFT, attn_shift),
        (B_OUTPUT, b_output),
        (B_QUERY, b_query),
        (B_VALUE, b_value),
    ):
        stacked = jnp.where(number == k, vector[None, :], stacked)
    own_weights, own_bias, mask, vecs, x_own, grad_own, outer_copy = run_kernel(
        prep_kernel,
        [
            text_lengths,
            region_lengths,
            flat_in,
            out_grad[0],
            stacked,
            b_inner,
            w_query,
            w_key,
            w_value,
            w_outer,
        ],
        [
            ((width, 3 * own_width), bf16),
            ((8, 3 * own_width), f32),
            ((row_len, row_len), f32),
            ((EXTRA, width), f32),
            tokens_bf16,
            tokens_bf16,
            ((hidden, width), bf16),
        ],
        [pltpu.VMEM((3, width, 256), bf16), pltpu.SemaphoreType.DMA((4,))],
        in_hbm=(6, 7, 8, 9),
        limit=14,
    )
    x_slots = [x_own] + x_slots
    *context_slots, probs, qkv, context_own = run_kernel(
        attention_kernel,
        x_slots + [own_weights, own_bias, mask],
        [((own_width, span), bf16)] * size
        + [((own_heads, row_len, row_len), bf16)]
        + [((row_len, 3 * own_width), bf16), ((row_len, own_width), f32)],
        [pltpu.VMEM((row_len, width), bf16)],
        limit=14,
    )
    turned = run_kernel(
        transpose_kernel,
        [w_inner, outer_copy, qkv],
        [
            ((width, hidden), bf16),
            ((hidden, width), bf16),
            ((width, hidden), bf16),
        ]
        + [((own_width, row_len), bf16)] * 3,
        [pltpu.SemaphoreType.DMA((1,))],
        in_hbm=(0,),
        limit=20,
        fill=8,
    )
    ffn_weights, ffn_turned = (turned[0], outer_copy), turned[1:3]
    q_t, k_t, v_t = turned[3:]
    context_slots = context_slots[:1] + [
        blk_shift(context_slots[step], size - step) for step in steps
    ]
    ff_rows = hidden // blocks
    rows = -(-(width // blocks) // 16) * 16
    block = ff_rows + rows

    many = blocks // 4 * block
    few = blocks // 4 * rows
    (
        layer_out,
        left_own,
        left_core,
        left_x,
        inner_own,
        inner_core,
        inner_y,
        outer_low,
        slope,
        grad_summed,
        attn_hat,
        attn_inv,
        sums,
    ) = run_kernel(
        forward_kernel(blocks),
        [x_own]
        + context_slots
        + [vecs, grad_own, w_output]
        + [*ffn_weights, ffn_turned[0]],
        [
            tokens_bf16,
            ((many, span), bf16),
            ((many, span), bf16),
            ((2 * many, span), bf16),
            ((few, span), bf16),
            ((few, span), bf16),
            ((2 * few, span), bf16),
            tokens_bf16,
            ((span, hidden), f32),
            tokens_f32,
            tokens_f32,
            ((span, 1), f32),
            ((EXTRA, width), f32),
        ],
        [
            pltpu.VMEM((size, own_width, span), bf16),
            pltpu.VMEM((4, many, span), bf16),
            pltpu.VMEM((4, few, span), bf16),
        ],
        in_hbm=(-1,),
        limit=20,
    )
    tall = 2 * rows_of(width, span) + rows_of(width, EXTRA)
    x_sent, y_sent, grad_mixed, *context_grads = run_kernel(
        backward_kernel,
        [
            outer_low,
            slope,
            grad_summed,
            attn_hat,
            attn_inv,
            left_x,
            inner_y,
            vecs,
            sums,
            w_output,
            *ffn_turned,
        ],
        [((2 * many + tall, span), bf16), ((2 * few + hidden, span), bf16), tokens_f32]
        + [((own_width, span), bf16)] * size,
        [pltpu.VMEM((size, own_width, span), bf16), pltpu.VMEM((EXTRA, width), f32)],
        limit=20,
    )
    x_got = batch_swap(x_sent, 2)
    y_got = batch_swap(y_sent, 4)
    context_grads = context_grads[:1] + [blk_shift(context_grads[step], step) for step in steps]
    *head_grads, token_sums = run_kernel(
        attention_back_kernel,
        [probs, q_t, k_t, v_t, context_own] + context_grads,
        [((3 * own_width, span), bf16)] * size + [((8, 3 * own_width), f32)],
        [pltpu.VMEM((row_len, row_len), bf16), pltpu.VMEM((3 * own_width, row_len), bf16)],
    )
    head_slots = head_grads[:1] + [blk_shift(head_grads[step], size - step) for step in steps]
    packed = run_kernel(
        pack_kernel,
        [inner_core, y_sent, y_got, head_slots[1], head_slots[-1]],
        [((2 * (few + hidden), span), bf16)],
        in_hbm=(-1, -2),
        limit=10,
    )[0]
    inner_send, inner_keep = run_kernel(
        inner_products_kernel(rows),
        [inner_own, y_sent, y_got, batch_swap(packed, 1)],
        [((few // 2, hidden), bf16)] * 2,
        limit=14,
    )
    inner_got = batch_swap(inner_send, 2)
    for bit in range(3, bits):
        inner_send, inner_keep = halve(inner_keep, inner_got, rows, bit, extra_rows=0)
        inner_got = batch_swap(inner_send, 1 << bit)
    packed = run_kernel(
        pack_kernel,
        [left_core, x_sent, x_got],
        [((2 * (many + tall), span), bf16)],
    )[0]
    send, keep = run_kernel(
        first_products_kernel(block, ff_rows, span),
        [left_own, x_sent, x_got, batch_swap(packed, 1)],
        [((many // 2 + EXTRA, width), bf16)] * 2,
        limit=14,
    )
    got = batch_swap(send, 4)
    for bit in range(3, bits):
        send, keep = halve(keep, got, block, bit)
        got = batch_swap(send, 1 << bit)
    wide = 3 * own_width
    head_send, head_keep = run_kernel(
        head_products_kernel,
        x_slots + head_grads + [token_sums, send],
        [((blocks // 2 * rows + EXTRA, wide), bf16)] * 2,
        [pltpu.VMEM((width, wide), f32)],
        in_hbm=(-1,),
        limit=10,
    )
    head_got = batch_swap(head_send, 1)
    head_send, head_keep = halve(head_keep, head_got, rows, 1, [inner_got] + head_slots[2:-1])
    head_got = batch_swap(head_send, 2)
    for bit in range(2, bits):
        head_send, head_keep = halve(head_keep, head_got, rows, bit, [got])
        head_got = batch_swap(head_send, 1 << bit)
    inner_part, *inner_sends = run_kernel(
        split_inner_kernel,
        [inner_keep, inner_got],
        [((rows, width), f32)] + [((rows, width), bf16)] * (size - 1),
        [pltpu.VMEM((rows, hidden), f32)],
    )
    inner_parts = [blk_shift(inner_sends[step - 1], step) for step in steps]
    grad_in = run_kernel(
        grad_in_kernel,
        head_slots + [grad_mixed, w_query, w_key, w_value],
        [tokens_bf16],
        [
            pltpu.VMEM((size, 3 * own_width, span), bf16),
            pltpu.VMEM((3, width, width), bf16),
            pltpu.SemaphoreType.DMA((3,)),
        ],
        in_hbm=(5, 6, 7),
        limit=10,
        fill=4,
    )[0]
    out_rows = width // blocks
    own_cols = ((out_rows, own_width), f32)
    *grad_qkv, late = run_kernel(
        last_sum_kernel,
        [head_keep, head_got, inner_parts[1]],
        [own_cols] * 3 + [((8, wide), f32)],
        in_hbm=(-1,),
    )
    message = (block // 2 + 2 * EXTRA, 2 * own_width)
    own_part, *sends = run_kernel(
        split_columns_kernel,
        [keep, got, late],
        [(message, f32)] + [(message, bf16)] * (size - 1),
        [pltpu.VMEM((size, block // 2, 2 * own_width), f32)],
    )
    parts = [blk_shift(sends[step - 1], step) for step in steps]
    grad_w_inner = run_kernel(
        join_inner_kernel, [inner_part] + inner_parts, [((out_rows, width), f32)]
    )[0]
    grad_w_outer, grad_w_output, *sums = run_kernel(
        join_rows_kernel,
        [own_part] + parts,
        [((ff_rows, own_width), f32), own_cols] + [row] * 8 + [((hidden,), f32)],
        [pltpu.VMEM((block, own_width), f32)],
    )
    return (
        layer_out[None],
        grad_in[None],
        grad_qkv[0],
        sums[B_QUERY],
        grad_qkv[1],
        grad_qkv[2],
        sums[B_VALUE],
        grad_w_output,
        sums[B_OUTPUT],
        sums[ATTN_GAIN],
        sums[ATTN_SHIFT],
        grad_w_inner,
        sums[B_INNER],
        grad_w_outer,
        sums[B_OUTER],
        sums[FFN_GAIN],
        sums[FFN_SHIFT],
    )


def solution(mesh):
    rows = P("batch", "blk", None)
    tile = P("batch", "blk")
    return jax.shard_map(
        local,
        mesh=mesh,
        in_specs=(rows,) + (P(),) * 15 + (P("batch", None), P("batch", None), rows),
        out_specs=(
            rows,
            rows,
            tile,
            P(),
            tile,
            tile,
            P(),
            tile,
            P(),
            P(),
            P(),
            tile,
            P(),
            tile,
            P(),
            P(),
            P(),
        ),
        check_vma=False,
    )
```

```python
import jax
import jax.numpy as jnp
from jax import lax
from jax.experimental import pallas as pl
from jax.experimental.pallas import tpu as pltpu
from jax.sharding import PartitionSpec as P

HEADS = 12
HEAD_DIM = 64
PAIRS = 4

NORM_EPS = 1e-05
MASKED_SCORE = -1e30
INV_ROOT_TWO = 0.7071067811865476
INV_ROOT_TWO_PI = 0.3989422804014327
MIB = 1024 * 1024

B_OUTER, FFN_GAIN, FFN_SHIFT, ATTN_GAIN, ATTN_SHIFT, B_OUTPUT, B_QUERY, B_VALUE, B_INNER = range(9)

EXTRA = 16

f32 = jnp.float32
bf16 = jnp.bfloat16


def mm(left, right):
    return jnp.dot(left, right, preferred_element_type=f32)


def mm_nt(left, right):
    return lax.dot_general(left, right, (((1,), (1,)), ((), ())), preferred_element_type=f32)


def norm_stats(values_in):
    row_mean = jnp.mean(values_in, axis=-1, keepdims=True)
    centred = values_in - row_mean
    inv_dev = lax.rsqrt(jnp.mean(centred * centred, axis=-1, keepdims=True) + NORM_EPS)
    return centred * inv_dev, inv_dev


def norm_back(scaled, normed, inv_dev):
    centre_term = jnp.mean(scaled, axis=-1, keepdims=True)
    slope_term = jnp.mean(scaled * normed, axis=-1, keepdims=True)
    return inv_dev * (scaled - centre_term - normed * slope_term)


def sum_rows(values):
    return jnp.sum(values, axis=0, keepdims=True)


def as_row(ref):
    return ref[...].astype(f32).reshape(1, -1)


def rows_of(width, count):
    return width // 128 * count


def narrow(ref, first, values):
    count = values.shape[0]
    for k in range(values.shape[1] // 128):
        at = first + k * count
        ref[at : at + count] = values[:, k * 128 : (k + 1) * 128]


def widen(ref, first, count, width):
    return jnp.concatenate(
        [ref[first + k * count : first + (k + 1) * count] for k in range(width // 128)], axis=1
    )


def ahead(me, step, size):
    return lax.rem(me + step, size)


def behind(me, group, size):
    return lax.rem(group - me + size, size)


def prep_kernel(
    text,
    region,
    x_ref,
    grad_ref,
    stacked,
    b_inner,
    w_query,
    w_key,
    w_value,
    w_outer,
    mask,
    vecs,
    x_out,
    grad_out,
    query_out,
    key_out,
    value_out,
    outer_out,
    sems,
):
    me = lax.axis_index("blk")
    row_len = mask.shape[0]
    span = x_ref.shape[0]
    size = row_len // span
    model_width = x_ref.shape[1]
    copies = [
        pltpu.make_async_copy(weight, out, sems.at[k])
        for k, (weight, out) in enumerate(
            (
                (w_query, query_out),
                (w_key, key_out),
                (w_value, value_out),
                (w_outer, outer_out),
            )
        )
    ]
    for copy in copies:
        copy.start()
    x_out[...] = x_ref[...]
    grad_out[...] = grad_ref[...]
    vecs[...] = stacked[...].astype(f32)
    hidden_row = as_row(b_inner)
    for k in range(hidden_row.shape[1] // model_width):
        part = slice(k * model_width, (k + 1) * model_width)
        vecs[B_INNER + k : B_INNER + k + 1] = hidden_row[:, part]

    ends = []
    total = jnp.zeros((1, 1), jnp.int32)
    for k in range(PAIRS):
        total = total + text[:, k : k + 1] + region[:, k : k + 1]
        ends.append(total)

    def segments(dim):
        shape = [1, 1]
        shape[dim] = span
        parts = []
        for s in range(size):
            first = lax.rem(me - s + size, size) * span
            pos = lax.broadcasted_iota(jnp.int32, tuple(shape), dim) + first
            seg = jnp.zeros(tuple(shape), jnp.int32)
            for end in ends:
                seg = seg + (pos >= end).astype(jnp.int32)
            parts.append(seg)
        return jnp.concatenate(parts, axis=dim)

    seg_q = segments(0)
    seg_k = segments(1)
    diagonal = lax.broadcasted_iota(jnp.int32, (row_len, row_len), 0) == lax.broadcasted_iota(
        jnp.int32, (row_len, row_len), 1
    )
    allowed = (seg_q == seg_k) & ((seg_k < PAIRS) | diagonal)
    mask[...] = jnp.where(allowed, 0.0, MASKED_SCORE)
    for copy in copies:
        copy.wait()


def transpose_kernel(w_inner, w_outer, inner_out, inner_t, outer_t, sems):
    copy = pltpu.make_async_copy(w_inner, inner_out, sems.at[0])
    copy.start()
    width, hidden = inner_out.shape
    parts = [slice(k * width, (k + 1) * width) for k in range(hidden // width)]
    for part in parts:
        outer_t[:, part] = w_outer[part].T
    copy.wait()
    for part in parts:
        inner_t[part] = inner_out[:, part].T


def attend(query, key, value, mask_of, tasks, store):
    def scores_of(task):
        part, cols = task
        return mm_nt(query[part, cols], key[:, cols])

    following = scores_of(tasks[0])
    for k, (part, cols) in enumerate(tasks):
        scores = following + mask_of(part)
        if k + 1 < len(tasks):
            following = scores_of(tasks[k + 1])
        weights = jnp.exp(scores - jnp.max(scores, axis=-1, keepdims=True))
        probs = (weights * (1.0 / jnp.sum(weights, axis=-1, keepdims=True))).astype(bf16)
        store(part, cols, probs, mm(probs, value[:, cols]))


def own_attention_kernel(
    x0, x1, x2, x3, w_query, w_key, w_value, vecs, mask, context_ref, x_all
):
    span, width = x0.shape
    for s, ref in enumerate((x0, x1, x2, x3)):
        x_all[s * span : (s + 1) * span] = ref[...]
    query = (mm(x0[...], w_query[...]) + vecs[B_QUERY : B_QUERY + 1]).astype(bf16)
    query = (query * HEAD_DIM ** (-0.5)).astype(bf16)
    key = mm(x_all[...], w_key[...]).astype(bf16)
    value = (mm(x_all[...], w_value[...]) + vecs[B_VALUE : B_VALUE + 1]).astype(bf16)
    rows = slice(0, span)
    tasks = [(rows, slice(h * HEAD_DIM, (h + 1) * HEAD_DIM)) for h in range(width // HEAD_DIM)]
    done = []
    attend(
        query,
        key,
        value,
        lambda part: mask[part],
        tasks,
        lambda part, cols, probs, context: done.append(context),
    )
    context_ref[...] = jnp.concatenate(done, axis=1).astype(bf16)


def head_attention_kernel(
    x0,
    x1,
    x2,
    x3,
    w_query,
    w_key,
    w_value,
    vecs,
    mask,
    order_after,
    probs_ref,
    q_t_ref,
    k_t_ref,
    v_t_ref,
    context_ref,
    x_all,
):
    del order_after
    me = lax.axis_index("blk")
    span = x0.shape[0]
    size = x_all.shape[0] // span
    width = context_ref.shape[1]
    for s, ref in enumerate((x0, x1, x2, x3)):
        x_all[s * span : (s + 1) * span] = ref[...]

    def own_row(k):
        row = vecs[k : k + 1]
        out = jnp.zeros((1, width), f32)
        for g in range(size):
            out = jnp.where(me == g, row[:, g * width : (g + 1) * width], out)
        return out

    def own_cols(ref):
        first = pl.multiple_of((me * width) // 128 * 128, 128)
        window = ref[:, pl.ds(first, 256)]
        return jnp.where((me * width) % 128 == 0, window[:, :width], window[:, 256 - width :])

    query = (mm(x_all[...], own_cols(w_query)) + own_row(B_QUERY)).astype(bf16)
    query = (query * HEAD_DIM ** (-0.5)).astype(bf16)
    key = mm(x_all[...], own_cols(w_key)).astype(bf16)
    value = (mm(x_all[...], own_cols(w_value)) + own_row(B_VALUE)).astype(bf16)
    q_t_ref[...] = query.T
    k_t_ref[...] = key.T
    v_t_ref[...] = value.T
    tasks = [
        (slice(s * span, (s + 1) * span), slice(h * HEAD_DIM, (h + 1) * HEAD_DIM))
        for s in range(size)
        for h in range(width // HEAD_DIM)
    ]

    def store(part, cols, probs, context):
        probs_ref[cols.start // HEAD_DIM, part] = probs
        context_ref[part, cols] = context

    attend(query, key, value, lambda part: mask[part], tasks, store)


def forward_kernel(blocks):
    def body(
        x_ref,
        context_ref,
        vecs,
        grad_ref,
        w_output,
        w_inner,
        w_outer,
        order_after,
        out_ref,
        left_own,
        left_core,
        left_x,
        inner_own,
        inner_core,
        inner_y,
        outer_low_ref,
        slope_ref,
        grad_summed_ref,
        hat_ref,
        inv_ref,
        sums_ref,
        left,
        inner,
    ):
        del order_after
        batch_me = lax.axis_index("batch")
        width, hidden = w_inner.shape
        step = width
        count = hidden // step
        ff_rows = hidden // blocks
        many = left_own.shape[0]
        block = many // (blocks // 4)

        def left_rows(b, first, values):
            at = (b >> 2) * block + first
            left[jnp.bitwise_xor(batch_me & 3, b & 3), at : at + values.shape[0]] = values

        def vec(k):
            return vecs[k : k + 1]

        context = context_ref[...]
        mixed = x_ref[...].astype(f32) + mm(context, w_output[...]) + vec(B_OUTPUT)
        hat, inv = norm_stats(mixed)
        hat_ref[...] = hat
        inv_ref[...] = inv
        attn_norm = hat * vec(ATTN_GAIN) + vec(ATTN_SHIFT)
        inner_in = attn_norm.astype(bf16)
        outer = jnp.zeros(attn_norm.shape, f32)
        cols = [slice(k * step, (k + 1) * step) for k in range(count)]
        following = mm(inner_in, w_inner[:, cols[0]])
        for k in range(count):
            pre = following + vec(B_INNER + k)
            if k + 1 < count:
                following = mm(inner_in, w_inner[:, cols[k + 1]])
            cdf = 0.5 + 0.5 * lax.erf(pre * INV_ROOT_TWO)
            act = (pre * cdf).astype(bf16)
            slope_ref[:, cols[k]] = cdf + pre * (jnp.exp(-0.5 * pre * pre) * INV_ROOT_TWO_PI)
            outer += mm(act, w_outer[cols[k]])
            act_t = act.T
            for j in range(step // ff_rows):
                left_rows(k * step // ff_rows + j, 0, act_t[j * ff_rows : (j + 1) * ff_rows])
        summed = attn_norm + outer + vec(B_OUTER)
        final_hat, final_inv = norm_stats(summed)
        gain = vec(FFN_GAIN)
        upstream = grad_ref[...].astype(f32)
        grad_summed = norm_back(upstream * gain, final_hat, final_inv)
        grad_summed_ref[...] = grad_summed
        outer_low = grad_summed.astype(bf16)
        outer_low_ref[...] = outer_low
        out_ref[...] = (final_hat * gain + vec(FFN_SHIFT)).astype(bf16)
        sums_ref[...] = jnp.zeros(sums_ref.shape, f32)
        sums_ref[B_OUTER : B_OUTER + 1] = sum_rows(outer_low.astype(f32))
        sums_ref[FFN_GAIN : FFN_GAIN + 1] = sum_rows(upstream * final_hat)
        sums_ref[FFN_SHIFT : FFN_SHIFT + 1] = sum_rows(upstream)
        out_rows = width // blocks
        padded = block - ff_rows
        inner_t = inner_in.T
        context_t = context.T

        def block_rows(values, b):
            if padded == out_rows:
                return values[b * out_rows : (b + 1) * out_rows]
            row = lax.broadcasted_iota(jnp.int32, (padded, width), 0)
            col = lax.broadcasted_iota(jnp.int32, (padded, width), 1)
            pick = ((row < out_rows) & (col == row + b * out_rows)).astype(f32).astype(bf16)
            return mm(pick, values).astype(bf16)

        for b in range(blocks):
            left_rows(b, ff_rows, block_rows(context_t, b))
            owner = jnp.bitwise_xor(batch_me & 1, b & 1) + 2 * jnp.bitwise_xor(
                (batch_me >> 2) & 1, (b >> 2) & 1
            )
            at = (((b >> 3) << 1) | ((b >> 1) & 1)) * padded
            inner[owner, at : at + padded] = block_rows(inner_t, b)
        left_own[...] = left[0]
        left_core[...] = left[1]
        left_x[:many] = left[2]
        left_x[many:] = left[3]
        few = inner_own.shape[0]
        inner_own[...] = inner[0]
        inner_core[...] = inner[1]
        inner_y[:few] = inner[2]
        inner_y[few:] = inner[3]

    return body


def backward_kernel(
    outer_low_ref,
    slope_ref,
    grad_summed_ref,
    hat_ref,
    inv_ref,
    left_x,
    inner_y,
    vecs,
    sums_in,
    w_output,
    w_inner_t,
    w_outer_t,
    x_ref,
    y_ref,
    grad_mixed_ref,
    g0,
    g1,
    g2,
    g3,
    groups,
    sums,
):
    hidden, width = w_inner_t.shape
    group_refs = (g0, g1, g2, g3)
    size = len(group_refs)
    me = lax.axis_index("blk")
    step = width
    rows = width // size
    span = outer_low_ref.shape[0]
    count = hidden // step
    parts = [slice(k * step, (k + 1) * step) for k in range(count)]
    sums[...] = sums_in[...]
    outer_low = outer_low_ref[...]
    grad_norm = grad_summed_ref[...]
    many, few = left_x.shape[0], inner_y.shape[0]
    x_ref[:many] = left_x[...]
    y_ref[:few] = inner_y[...]
    following = mm(outer_low, w_outer_t[:, parts[0]])
    for k in range(count):
        pre_low = (following * slope_ref[:, parts[k]]).astype(bf16)
        if k + 1 < count:
            following = mm(outer_low, w_outer_t[:, parts[k + 1]])
        grad_norm += mm(pre_low, w_inner_t[parts[k]])
        y_ref[few + k * step : few + (k + 1) * step] = pre_low.T
        sums[B_INNER + k : B_INNER + k + 1] = sum_rows(pre_low.astype(f32))
    hat = hat_ref[...]
    grad_mixed = norm_back(grad_norm * vecs[ATTN_GAIN : ATTN_GAIN + 1], hat, inv_ref[...])
    grad_mixed_ref[...] = grad_mixed
    mixed_low = grad_mixed.astype(bf16)
    narrow(x_ref, many, outer_low)
    narrow(x_ref, many + rows_of(width, span), mixed_low)
    context_grad_t = mm_nt(w_output[...], mixed_low).astype(bf16)
    for g in range(size):
        groups[behind(me, g, size)] = context_grad_t[g * rows : (g + 1) * rows]
    for s in range(size):
        group_refs[s][...] = groups[s]
    sums[ATTN_GAIN : ATTN_GAIN + 1] = sum_rows(grad_norm * hat)
    sums[ATTN_SHIFT : ATTN_SHIFT + 1] = sum_rows(grad_norm)
    sums[B_OUTPUT : B_OUTPUT + 1] = sum_rows(mixed_low.astype(f32))
    narrow(x_ref, many + 2 * rows_of(width, span), sums[...].astype(bf16))


def pack_kernel(core_rows, own, got, *after_and_out):
    out_ref = after_and_out[-1]
    many = core_rows.shape[0]
    size = own.shape[0] - 2 * many
    out_ref[:many] = core_rows[...]
    out_ref[many : 2 * many] = got[many : 2 * many]
    out_ref[2 * many : 2 * many + size] = own[2 * many :]
    out_ref[2 * many + size :] = got[2 * many :]


def first_products_kernel(block, ff_rows, span):
    def body(left_own, sent, received, packed, send_ref, keep_ref):
        many = left_own.shape[0]
        size = sent.shape[0] - 2 * many
        width = send_ref.shape[1]
        tall = rows_of(width, span)
        own = (lax.axis_index("batch") >> 2) & 1
        lefts = ((left_own, 0), (received, 0), (packed, 0), (packed, many))
        rights = (
            (sent, 2 * many),
            (received, 2 * many),
            (packed, 2 * many),
            (packed, 2 * many + size),
        )
        outer_low = jnp.concatenate([widen(ref, at, span, width) for ref, at in rights], axis=0)
        mixed_low = jnp.concatenate(
            [widen(ref, at + tall, span, width) for ref, at in rights], axis=0
        )
        sums = jnp.zeros((EXTRA, width), f32)
        for ref, at in rights:
            sums += widen(ref, at + 2 * tall, EXTRA, width).astype(f32)
        for ref, side in ((send_ref, 1 - own), (keep_ref, own)):
            count = (ref.shape[0] - EXTRA) // block
            for j in range(count):

                def rows(first, number):
                    start = (2 * j + side) * block + first
                    return jnp.concatenate(
                        [
                            source[pl.ds(pl.multiple_of(start + at, 16), number)]
                            for source, at in lefts
                        ],
                        axis=1,
                    )

                at = j * block
                ref[at : at + ff_rows] = mm(rows(0, ff_rows), outer_low).astype(bf16)
                ref[at + ff_rows : at + block] = mm(
                    rows(ff_rows, block - ff_rows), mixed_low
                ).astype(bf16)
            ref[count * block :] = sums.astype(bf16)

    return body


def inner_products_kernel(block):
    def body(inner_own, sent, received, packed, send_ref, keep_ref):
        few = inner_own.shape[0]
        size = sent.shape[0] - 2 * few
        own = (lax.axis_index("batch") >> 1) & 1
        lefts = ((inner_own, 0), (received, 0), (packed, 0), (packed, few))
        rights = ((sent, 2 * few), (received, 2 * few), (packed, 2 * few), (packed, 2 * few + size))
        pre_t = jnp.concatenate([ref[at : at + size] for ref, at in rights], axis=1)
        many = send_ref.shape[0]
        pieces = []
        for side in (1 - own, own):
            for j in range(many // block):
                start = (2 * j + side) * block
                pieces.append(
                    jnp.concatenate(
                        [
                            source[pl.ds(pl.multiple_of(start + at, 16), block)]
                            for source, at in lefts
                        ],
                        axis=1,
                    )
                )
        total = mm_nt(jnp.concatenate(pieces, axis=0), pre_t).astype(bf16)
        send_ref[...] = total[:many]
        keep_ref[...] = total[many:]

    return body


def halve_kernel(block, bit, parts, extra_rows):
    def body(keep_in, *rest):
        got, (send_ref, keep_ref) = rest[:parts], rest[-2:]
        own = (lax.axis_index("batch") >> bit) & 1
        count = (send_ref.shape[0] - extra_rows) // block

        def total(part):
            added = jnp.concatenate([ref[part] for ref in got], axis=1).astype(f32)
            return (keep_in[part].astype(f32) + added).astype(bf16)

        for ref, side in ((send_ref, 1 - own), (keep_ref, own)):
            for j in range(count):
                start = pl.multiple_of((2 * j + side) * block, 16)
                ref[j * block : (j + 1) * block] = total(pl.ds(start, block))
            if extra_rows:
                last = 2 * count * block
                ref[count * block :] = total(slice(last, last + extra_rows))

    return body


def attention_back_kernel(
    probs_ref,
    q_t_ref,
    k_t_ref,
    v_t_ref,
    context_ref,
    d0,
    d1,
    d2,
    d3,
    e0,
    e1,
    e2,
    e3,
    token_sums,
    score_grad,
    out_t,
):
    slots = (d0, d1, d2, d3)
    outs = (e0, e1, e2, e3)
    size = len(slots)
    width, row_len = q_t_ref.shape
    span = row_len // size
    grad_t = jnp.concatenate([slot[...] for slot in slots], axis=1)
    grad = grad_t.T
    for h in range(width // HEAD_DIM):
        cols = slice(h * HEAD_DIM, (h + 1) * HEAD_DIM)
        for s in range(size):
            part = slice(s * span, (s + 1) * span)
            grad_part = grad[part, cols]
            delta = jnp.sum(
                grad_part.astype(f32) * context_ref[part, cols], axis=-1, keepdims=True
            )
            grad_probs = mm(grad_part, v_t_ref[cols])
            score_grad[part] = (probs_ref[h, part].astype(f32) * (grad_probs - delta)).astype(bf16)
        out_t[cols] = (mm_nt(k_t_ref[cols], score_grad[...]) * HEAD_DIM ** (-0.5)).astype(bf16)
        out_t[width + h * HEAD_DIM : width + (h + 1) * HEAD_DIM] = mm(
            q_t_ref[cols], score_grad[...]
        ).astype(bf16)
        out_t[2 * width + h * HEAD_DIM : 2 * width + (h + 1) * HEAD_DIM] = mm(
            grad_t[cols], probs_ref[h]
        ).astype(bf16)
    for s in range(size):
        outs[s][...] = out_t[:, s * span : (s + 1) * span]
    token_sums[...] = mm_nt(jnp.ones((8, row_len), bf16), out_t[...])


def head_products_kernel(
    x0, x1, x2, x3, e0, e1, e2, e3, token_sums, order_after, send_ref, keep_ref, total
):
    del order_after
    core = lax.axis_index("batch") & 1
    x_t = jnp.concatenate([ref[...].T for ref in (x0, x1, x2, x3)], axis=1)
    heads_t = jnp.concatenate([ref[...] for ref in (e0, e1, e2, e3)], axis=1)
    total[...] = mm_nt(x_t, heads_t)
    blocks = lax.axis_size("batch")
    rows, width = total.shape[0] // blocks, total.shape[1]
    padded = (send_ref.shape[0] - EXTRA) // (blocks // 2)
    for own, refs in ((0, (keep_ref, send_ref)), (1, (send_ref, keep_ref))):

        @pl.when(core == own)
        def _():
            for b in range(blocks):
                at = (b >> 1) * padded
                if padded != rows:
                    refs[b & 1][at : at + padded] = jnp.zeros((padded, width), bf16)
                refs[b & 1][at : at + rows] = total[b * rows : (b + 1) * rows].astype(bf16)

    sums = jnp.concatenate((token_sums[...], jnp.zeros((EXTRA - 8, width), f32)), axis=0)
    for ref in (send_ref, keep_ref):
        ref[(blocks // 2) * padded :] = sums.astype(bf16)


def grad_in_kernel(
    e0, e1, e2, e3, grad_mixed, w_query, w_key, w_value, out_ref, groups, weights, sems
):
    slots = (e0, e1, e2, e3)
    size = len(slots)
    me = lax.axis_index("blk")
    copies = [
        pltpu.make_async_copy(weight, weights.at[k], sems.at[k])
        for k, weight in enumerate((w_query, w_key, w_value))
    ]
    for copy in copies:
        copy.start()
    for s in range(size):
        groups[ahead(me, s, size)] = slots[s][...]
    total = grad_mixed[...]
    own = e0.shape[0] // 3
    for k in range(3):
        rows = [groups[g, k * own : (k + 1) * own] for g in range(size)]
        part = jnp.concatenate(rows, axis=0).T
        copies[k].wait()
        total += mm_nt(part, weights[k])
    out_ref[...] = total.astype(bf16)


def split_inner_kernel(keep, got, own_ref, s1, s2, s3, total):
    outs = (own_ref, s1, s2, s3)
    size = len(outs)
    me = lax.axis_index("blk")
    total[...] = keep[...].astype(f32) + got[...].astype(f32)
    width = total.shape[1] // size
    for s in range(size):
        cols = pl.ds(pl.multiple_of(ahead(me, s, size) * width, 128), width)
        outs[s][...] = total[:, cols].astype(outs[s].dtype)


def join_inner_kernel(own, r1, r2, r3, out_ref):
    rows = slice(0, out_ref.shape[0])
    total = own[rows] + r1[rows].astype(f32) + r2[rows].astype(f32) + r3[rows].astype(f32)
    out_ref[...] = total


def split_columns_kernel(keep, got, late, own_ref, s1, s2, s3, groups):
    outs = (s1, s2, s3)
    size = len(outs) + 1
    me = lax.axis_index("blk")
    total = keep[...].astype(f32) + got[...].astype(f32)
    last = total.shape[0] - EXTRA
    half = last // 2
    width = total.shape[1] // size
    sums = total[last:]
    row = lax.broadcasted_iota(jnp.int32, sums.shape, 0)
    group = lax.broadcasted_iota(jnp.int32, sums.shape, 1) // width
    for k, at in ((B_QUERY, 0), (B_VALUE, 2)):
        own_row = late[0:1, at * width : (at + 1) * width]
        sums = jnp.where(
            (row == k) & (group == me), jnp.concatenate([own_row] * size, axis=1), sums
        )
    extra = jnp.concatenate((sums[:, : 2 * width], sums[:, 2 * width :]), axis=0)
    for g in range(size):
        cols = slice(g * width, (g + 1) * width)
        slot = behind(me, g, size)
        groups[slot, :half] = jnp.concatenate((total[:half, cols], total[half:last, cols]), axis=1)
    own_ref[:half] = groups[0]
    own_ref[half:] = extra
    for s in range(1, size):
        outs[s - 1][:half] = groups[s].astype(bf16)
        outs[s - 1][half:] = extra.astype(bf16)


def join_rows_kernel(own, r1, r2, r3, first_ref, second_ref, *rest):
    sum_refs, (rows,) = rest[:-1], rest[-1:]
    total = own[...] + r1[...].astype(f32) + r2[...].astype(f32) + r3[...].astype(f32)
    half, width = total.shape[0] - 2 * EXTRA, total.shape[1] // 2
    rows[:half] = total[:half, :width]
    rows[half:] = total[:half, width:]
    ff_rows = first_ref.shape[0]
    first_ref[...] = rows[:ff_rows]
    second_ref[...] = rows[ff_rows : ff_rows + second_ref.shape[0]]
    sums = jnp.concatenate((total[half : half + EXTRA], total[half + EXTRA :]), axis=1)
    for k, ref in enumerate(sum_refs[:-1]):
        ref[...] = sums[k]
    model_width = sums.shape[1]
    for k in range(sum_refs[-1].shape[0] // model_width):
        sum_refs[-1][k * model_width : (k + 1) * model_width] = sums[B_INNER + k]


def last_sum_kernel(keep, got, order_after, q_ref, k_ref, v_ref, late_ref):
    del order_after
    total = keep[...].astype(f32) + got[...].astype(f32)
    rows, own = q_ref.shape
    for k, ref in enumerate((q_ref, k_ref, v_ref)):
        ref[...] = total[:rows, k * own : (k + 1) * own]
    last = total.shape[0] - EXTRA
    late_ref[...] = total[last : last + 8]


def run_kernel(body, operands, outs, scratch=(), in_hbm=(), limit=8, fill=0):
    vmem = pl.BlockSpec(memory_space=pltpu.VMEM)
    hbm = pl.BlockSpec(memory_space=pltpu.HBM)
    anywhere = pl.BlockSpec(memory_space=pl.ANY)

    def place(k):
        if k - len(operands) in in_hbm:
            return anywhere
        return hbm if k in in_hbm else vmem

    return pl.pallas_call(
        body,
        out_shape=[jax.ShapeDtypeStruct(shape, dtype) for shape, dtype in outs],
        in_specs=[place(k) for k in range(len(operands))],
        out_specs=[vmem] * len(outs),
        scratch_shapes=list(scratch),
        compiler_params=pltpu.CompilerParams(vmem_limit_bytes=limit * MIB),
        cost_estimate=pl.CostEstimate(
            flops=1 + fill * 10**9, bytes_accessed=1, transcendentals=0
        ),
    )(*operands)


def blk_shift(values, step):
    size = lax.axis_size("blk")
    return lax.ppermute(values, "blk", [(i, (i + step) % size) for i in range(size)])


def batch_swap(values, bits):
    size = lax.axis_size("batch")
    return lax.ppermute(values, "batch", [(i, i ^ bits) for i in range(size)])


def halve(keep, got, block, bit, after=(), extra_rows=EXTRA):
    got = got if isinstance(got, list) else [got]
    count = (keep.shape[0] - extra_rows) // block // 2
    shape = ((count * block + extra_rows, keep.shape[1]), bf16)
    return run_kernel(
        halve_kernel(block, bit, len(got), extra_rows),
        [keep, *got, *after],
        [shape, shape],
        in_hbm=[-1 - k for k in range(len(after))],
    )


def local(
    hidden_in,
    w_query,
    b_query,
    w_key,
    w_value,
    b_value,
    w_output,
    b_output,
    attn_gain,
    attn_shift,
    w_inner,
    b_inner,
    w_outer,
    b_outer,
    ffn_gain,
    ffn_shift,
    text_lengths,
    region_lengths,
    out_grad,
):
    _, span, width = hidden_in.shape
    hidden = w_inner.shape[1]
    size = lax.axis_size("blk")
    blocks = lax.axis_size("batch")
    bits = blocks.bit_length() - 1
    row_len = span * size
    own_heads = HEADS // size
    own_width = own_heads * HEAD_DIM
    steps = range(1, size)
    tokens_f32 = ((span, width), f32)
    tokens_bf16 = ((span, width), bf16)
    row = ((width,), f32)

    flat_in = hidden_in[0]
    x_slots = [blk_shift(flat_in, step) for step in steps]
    stacked = jnp.zeros((EXTRA, width), bf16)
    number = lax.broadcasted_iota(jnp.int32, stacked.shape, 0)
    for k, vector in (
        (B_OUTER, b_outer),
        (FFN_GAIN, ffn_gain),
        (FFN_SHIFT, ffn_shift),
        (ATTN_GAIN, attn_gain),
        (ATTN_SHIFT, attn_shift),
        (B_OUTPUT, b_output),
        (B_QUERY, b_query),
        (B_VALUE, b_value),
    ):
        stacked = jnp.where(number == k, vector[None, :], stacked)
    square = ((width, width), bf16)
    mask, vecs, x_own, grad_own, *attn_weights, outer_copy = run_kernel(
        prep_kernel,
        [
            text_lengths,
            region_lengths,
            flat_in,
            out_grad[0],
            stacked,
            b_inner,
            w_query,
            w_key,
            w_value,
            w_outer,
        ],
        [
            ((row_len, row_len), f32),
            ((EXTRA, width), f32),
            tokens_bf16,
            tokens_bf16,
            square,
            square,
            square,
            ((hidden, width), bf16),
        ],
        [pltpu.SemaphoreType.DMA((4,))],
        in_hbm=(6, 7, 8, 9),
        limit=16,
    )
    inner_copy, *ffn_turned = run_kernel(
        transpose_kernel,
        [w_inner, outer_copy],
        [((width, hidden), bf16), ((hidden, width), bf16), ((width, hidden), bf16)],
        [pltpu.SemaphoreType.DMA((1,))],
        in_hbm=(0,),
        limit=20,
        fill=4,
    )
    ffn_weights = (inner_copy, outer_copy)
    x_slots = [x_own] + x_slots
    context = run_kernel(
        own_attention_kernel,
        x_slots + attn_weights + [vecs, mask],
        [tokens_bf16],
        [pltpu.VMEM((row_len, width), bf16)],
        limit=20,
    )[0]
    ff_rows = hidden // blocks
    rows = -(-(width // blocks) // 16) * 16
    block = ff_rows + rows

    many = blocks // 4 * block
    few = blocks // 4 * rows
    (
        layer_out,
        left_own,
        left_core,
        left_x,
        inner_own,
        inner_core,
        inner_y,
        outer_low,
        slope,
        grad_summed,
        attn_hat,
        attn_inv,
        sums,
    ) = run_kernel(
        forward_kernel(blocks),
        [x_own, context, vecs, grad_own, w_output]
        + [*ffn_weights, ffn_turned[0]],
        [
            tokens_bf16,
            ((many, span), bf16),
            ((many, span), bf16),
            ((2 * many, span), bf16),
            ((few, span), bf16),
            ((few, span), bf16),
            ((2 * few, span), bf16),
            tokens_bf16,
            ((span, hidden), f32),
            tokens_f32,
            tokens_f32,
            ((span, 1), f32),
            ((EXTRA, width), f32),
        ],
        [
            pltpu.VMEM((4, many, span), bf16),
            pltpu.VMEM((4, few, span), bf16),
        ],
        in_hbm=(-1,),
        limit=20,
    )
    tall = 2 * rows_of(width, span) + rows_of(width, EXTRA)
    x_sent, y_sent, grad_mixed, *context_grads = run_kernel(
        backward_kernel,
        [
            outer_low,
            slope,
            grad_summed,
            attn_hat,
            attn_inv,
            left_x,
            inner_y,
            vecs,
            sums,
            w_output,
            *ffn_turned,
        ],
        [((2 * many + tall, span), bf16), ((2 * few + hidden, span), bf16), tokens_f32]
        + [((own_width, span), bf16)] * size,
        [pltpu.VMEM((size, own_width, span), bf16), pltpu.VMEM((EXTRA, width), f32)],
        limit=20,
    )
    x_got = batch_swap(x_sent, 2)
    y_got = batch_swap(y_sent, 4)
    context_grads = context_grads[:1] + [blk_shift(context_grads[step], step) for step in steps]
    heads_shape = ((own_width, row_len), bf16)
    probs, q_t, k_t, v_t, context_own = run_kernel(
        head_attention_kernel,
        x_slots + attn_weights + [vecs, mask, grad_mixed],
        [((own_heads, row_len, row_len), bf16)]
        + [heads_shape] * 3
        + [((row_len, own_width), f32)],
        [pltpu.VMEM((row_len, width), bf16)],
        in_hbm=(-1,),
        limit=16,
        fill=4,
    )
    *head_grads, token_sums = run_kernel(
        attention_back_kernel,
        [probs, q_t, k_t, v_t, context_own] + context_grads,
        [((3 * own_width, span), bf16)] * size + [((8, 3 * own_width), f32)],
        [pltpu.VMEM((row_len, row_len), bf16), pltpu.VMEM((3 * own_width, row_len), bf16)],
    )
    head_slots = head_grads[:1] + [blk_shift(head_grads[step], size - step) for step in steps]
    packed = run_kernel(
        pack_kernel,
        [inner_core, y_sent, y_got, head_slots[1], head_slots[-1]],
        [((2 * (few + hidden), span), bf16)],
        in_hbm=(-1, -2),
        limit=10,
    )[0]
    inner_send, inner_keep = run_kernel(
        inner_products_kernel(rows),
        [inner_own, y_sent, y_got, batch_swap(packed, 1)],
        [((few // 2, hidden), bf16)] * 2,
        limit=14,
    )
    inner_got = batch_swap(inner_send, 2)
    for bit in range(3, bits):
        inner_send, inner_keep = halve(inner_keep, inner_got, rows, bit, extra_rows=0)
        inner_got = batch_swap(inner_send, 1 << bit)
    packed = run_kernel(
        pack_kernel,
        [left_core, x_sent, x_got],
        [((2 * (many + tall), span), bf16)],
    )[0]
    send, keep = run_kernel(
        first_products_kernel(block, ff_rows, span),
        [left_own, x_sent, x_got, batch_swap(packed, 1)],
        [((many // 2 + EXTRA, width), bf16)] * 2,
        limit=14,
    )
    got = batch_swap(send, 4)
    for bit in range(3, bits):
        send, keep = halve(keep, got, block, bit)
        got = batch_swap(send, 1 << bit)
    wide = 3 * own_width
    head_send, head_keep = run_kernel(
        head_products_kernel,
        x_slots + head_grads + [token_sums, send],
        [((blocks // 2 * rows + EXTRA, wide), bf16)] * 2,
        [pltpu.VMEM((width, wide), f32)],
        in_hbm=(-1,),
        limit=10,
    )
    head_got = batch_swap(head_send, 1)
    head_send, head_keep = halve(head_keep, head_got, rows, 1, [inner_got] + head_slots[2:-1])
    head_got = batch_swap(head_send, 2)
    for bit in range(2, bits):
        head_send, head_keep = halve(head_keep, head_got, rows, bit, [got])
        head_got = batch_swap(head_send, 1 << bit)
    inner_part, *inner_sends = run_kernel(
        split_inner_kernel,
        [inner_keep, inner_got],
        [((rows, width), f32)] + [((rows, width), bf16)] * (size - 1),
        [pltpu.VMEM((rows, hidden), f32)],
    )
    inner_parts = [blk_shift(inner_sends[step - 1], step) for step in steps]
    grad_in = run_kernel(
        grad_in_kernel,
        head_slots + [grad_mixed, w_query, w_key, w_value],
        [tokens_bf16],
        [
            pltpu.VMEM((size, 3 * own_width, span), bf16),
            pltpu.VMEM((3, width, width), bf16),
            pltpu.SemaphoreType.DMA((3,)),
        ],
        in_hbm=(5, 6, 7),
        limit=10,
        fill=4,
    )[0]
    out_rows = width // blocks
    own_cols = ((out_rows, own_width), f32)
    *grad_qkv, late = run_kernel(
        last_sum_kernel,
        [head_keep, head_got, inner_parts[1]],
        [own_cols] * 3 + [((8, wide), f32)],
        in_hbm=(-1,),
    )
    message = (block // 2 + 2 * EXTRA, 2 * own_width)
    own_part, *sends = run_kernel(
        split_columns_kernel,
        [keep, got, late],
        [(message, f32)] + [(message, bf16)] * (size - 1),
        [pltpu.VMEM((size, block // 2, 2 * own_width), f32)],
    )
    parts = [blk_shift(sends[step - 1], step) for step in steps]
    grad_w_inner = run_kernel(
        join_inner_kernel, [inner_part] + inner_parts, [((out_rows, width), f32)]
    )[0]
    grad_w_outer, grad_w_output, *sums = run_kernel(
        join_rows_kernel,
        [own_part] + parts,
        [((ff_rows, own_width), f32), own_cols] + [row] * 8 + [((hidden,), f32)],
        [pltpu.VMEM((block, own_width), f32)],
    )
    return (
        layer_out[None],
        grad_in[None],
        grad_qkv[0],
        sums[B_QUERY],
        grad_qkv[1],
        grad_qkv[2],
        sums[B_VALUE],
        grad_w_output,
        sums[B_OUTPUT],
        sums[ATTN_GAIN],
        sums[ATTN_SHIFT],
        grad_w_inner,
        sums[B_INNER],
        grad_w_outer,
        sums[B_OUTER],
        sums[FFN_GAIN],
        sums[FFN_SHIFT],
    )


def solution(mesh):
    rows = P("batch", "blk", None)
    tile = P("batch", "blk")
    return jax.shard_map(
        local,
        mesh=mesh,
        in_specs=(rows,) + (P(),) * 15 + (P("batch", None), P("batch", None), rows),
        out_specs=(
            rows,
            rows,
            tile,
            P(),
            tile,
            tile,
            P(),
            tile,
            P(),
            P(),
            P(),
            tile,
            P(),
            tile,
            P(),
            P(),
            P(),
        ),
        check_vma=False,
    )
```

```python
import jax
import jax.numpy as jnp
from jax import lax
from jax.experimental import pallas as pl
from jax.experimental.pallas import tpu as pltpu
from jax.sharding import PartitionSpec as P

HEADS = 12
HEAD_DIM = 64
PAIRS = 4

NORM_EPS = 1e-05
MASKED_SCORE = -1e30
INV_ROOT_TWO = 0.7071067811865476
INV_ROOT_TWO_PI = 0.3989422804014327
MIB = 1024 * 1024

B_OUTER, FFN_GAIN, FFN_SHIFT, ATTN_GAIN, ATTN_SHIFT, B_OUTPUT, B_QUERY, B_VALUE, B_INNER = range(9)

EXTRA = 16

f32 = jnp.float32
bf16 = jnp.bfloat16


def mm(left, right):
    return jnp.dot(left, right, preferred_element_type=f32)


def mm_nt(left, right):
    return lax.dot_general(left, right, (((1,), (1,)), ((), ())), preferred_element_type=f32)


def norm_stats(values_in):
    row_mean = jnp.mean(values_in, axis=-1, keepdims=True)
    centred = values_in - row_mean
    inv_dev = lax.rsqrt(jnp.mean(centred * centred, axis=-1, keepdims=True) + NORM_EPS)
    return centred * inv_dev, inv_dev


def norm_back(scaled, normed, inv_dev):
    centre_term = jnp.mean(scaled, axis=-1, keepdims=True)
    slope_term = jnp.mean(scaled * normed, axis=-1, keepdims=True)
    return inv_dev * (scaled - centre_term - normed * slope_term)


def sum_rows(values):
    return jnp.sum(values, axis=0, keepdims=True)


def as_row(ref):
    return ref[...].astype(f32).reshape(1, -1)


def rows_of(width, count):
    return width // 128 * count


def narrow(ref, first, values):
    count = values.shape[0]
    for k in range(values.shape[1] // 128):
        at = first + k * count
        ref[at : at + count] = values[:, k * 128 : (k + 1) * 128]


def widen(ref, first, count, width):
    return jnp.concatenate(
        [ref[first + k * count : first + (k + 1) * count] for k in range(width // 128)], axis=1
    )


def ahead(me, step, size):
    return lax.rem(me + step, size)


def behind(me, group, size):
    return lax.rem(group - me + size, size)


def prep_kernel(
    text,
    region,
    x_ref,
    grad_ref,
    stacked,
    b_inner,
    w_query,
    w_key,
    w_value,
    w_outer,
    mask,
    vecs,
    x_out,
    grad_out,
    query_out,
    key_out,
    value_out,
    outer_out,
    sems,
):
    me = lax.axis_index("blk")
    row_len = mask.shape[0]
    span = x_ref.shape[0]
    size = row_len // span
    model_width = x_ref.shape[1]
    copies = [
        pltpu.make_async_copy(weight, out, sems.at[k])
        for k, (weight, out) in enumerate(
            (
                (w_query, query_out),
                (w_key, key_out),
                (w_value, value_out),
                (w_outer, outer_out),
            )
        )
    ]
    for copy in copies:
        copy.start()
    x_out[...] = x_ref[...]
    grad_out[...] = grad_ref[...]
    vecs[...] = stacked[...].astype(f32)
    hidden_row = as_row(b_inner)
    for k in range(hidden_row.shape[1] // model_width):
        part = slice(k * model_width, (k + 1) * model_width)
        vecs[B_INNER + k : B_INNER + k + 1] = hidden_row[:, part]

    ends = []
    total = jnp.zeros((1, 1), jnp.int32)
    for k in range(PAIRS):
        total = total + text[:, k : k + 1] + region[:, k : k + 1]
        ends.append(total)

    def segments(dim):
        shape = [1, 1]
        shape[dim] = span
        parts = []
        for s in range(size):
            first = lax.rem(me - s + size, size) * span
            pos = lax.broadcasted_iota(jnp.int32, tuple(shape), dim) + first
            seg = jnp.zeros(tuple(shape), jnp.int32)
            for end in ends:
                seg = seg + (pos >= end).astype(jnp.int32)
            parts.append(seg)
        return jnp.concatenate(parts, axis=dim)

    seg_q = segments(0)
    seg_k = segments(1)
    diagonal = lax.broadcasted_iota(jnp.int32, (row_len, row_len), 0) == lax.broadcasted_iota(
        jnp.int32, (row_len, row_len), 1
    )
    allowed = (seg_q == seg_k) & ((seg_k < PAIRS) | diagonal)
    mask[...] = jnp.where(allowed, 0.0, MASKED_SCORE)
    for copy in copies:
        copy.wait()


def transpose_kernel(w_inner, w_outer, inner_out, inner_t, outer_t, sems):
    copy = pltpu.make_async_copy(w_inner, inner_out, sems.at[0])
    copy.start()
    width, hidden = inner_out.shape
    parts = [slice(k * width, (k + 1) * width) for k in range(hidden // width)]
    for part in parts:
        outer_t[:, part] = w_outer[part].T
    copy.wait()
    for part in parts:
        inner_t[part] = inner_out[:, part].T


def attend(query, key, value, mask_of, tasks, store):
    def scores_of(task):
        part, cols = task
        return mm_nt(query[part, cols], key[:, cols])

    following = scores_of(tasks[0])
    for k, (part, cols) in enumerate(tasks):
        scores = following + mask_of(part)
        if k + 1 < len(tasks):
            following = scores_of(tasks[k + 1])
        weights = jnp.exp(scores - jnp.max(scores, axis=-1, keepdims=True))
        probs = (weights * (1.0 / jnp.sum(weights, axis=-1, keepdims=True))).astype(bf16)
        store(part, cols, probs, mm(probs, value[:, cols]))


def own_attention_kernel(
    x0, x1, x2, x3, w_query, w_key, w_value, vecs, mask, context_ref, x_all
):
    span, width = x0.shape
    for s, ref in enumerate((x0, x1, x2, x3)):
        x_all[s * span : (s + 1) * span] = ref[...]
    query = (mm(x0[...], w_query[...]) + vecs[B_QUERY : B_QUERY + 1]).astype(bf16)
    query = (query * HEAD_DIM ** (-0.5)).astype(bf16)
    key = mm(x_all[...], w_key[...]).astype(bf16)
    value = (mm(x_all[...], w_value[...]) + vecs[B_VALUE : B_VALUE + 1]).astype(bf16)
    rows = slice(0, span)
    tasks = [(rows, slice(h * HEAD_DIM, (h + 1) * HEAD_DIM)) for h in range(width // HEAD_DIM)]
    done = []
    attend(
        query,
        key,
        value,
        lambda part: mask[part],
        tasks,
        lambda part, cols, probs, context: done.append(context),
    )
    context_ref[...] = jnp.concatenate(done, axis=1).astype(bf16)


def head_attention_kernel(
    x0,
    x1,
    x2,
    x3,
    w_query,
    w_key,
    w_value,
    vecs,
    mask,
    order_after,
    probs_ref,
    q_t_ref,
    k_t_ref,
    v_t_ref,
    context_ref,
    x_all,
):
    del order_after
    me = lax.axis_index("blk")
    span = x0.shape[0]
    size = x_all.shape[0] // span
    width = context_ref.shape[1]
    for s, ref in enumerate((x0, x1, x2, x3)):
        x_all[s * span : (s + 1) * span] = ref[...]

    def own_row(k):
        row = vecs[k : k + 1]
        out = jnp.zeros((1, width), f32)
        for g in range(size):
            out = jnp.where(me == g, row[:, g * width : (g + 1) * width], out)
        return out

    def own_cols(ref):
        first = pl.multiple_of((me * width) // 128 * 128, 128)
        window = ref[:, pl.ds(first, 256)]
        return jnp.where((me * width) % 128 == 0, window[:, :width], window[:, 256 - width :])

    query = (mm(x_all[...], own_cols(w_query)) + own_row(B_QUERY)).astype(bf16)
    query = (query * HEAD_DIM ** (-0.5)).astype(bf16)
    key = mm(x_all[...], own_cols(w_key)).astype(bf16)
    value = (mm(x_all[...], own_cols(w_value)) + own_row(B_VALUE)).astype(bf16)
    q_t_ref[...] = query.T
    k_t_ref[...] = key.T
    v_t_ref[...] = value.T
    tasks = [
        (slice(s * span, (s + 1) * span), slice(h * HEAD_DIM, (h + 1) * HEAD_DIM))
        for s in range(size)
        for h in range(width // HEAD_DIM)
    ]

    def store(part, cols, probs, context):
        probs_ref[cols.start // HEAD_DIM, part] = probs
        context_ref[part, cols] = context

    attend(query, key, value, lambda part: mask[part], tasks, store)


def forward_kernel(blocks):
    def body(
        x_ref,
        context_ref,
        vecs,
        grad_ref,
        w_output,
        w_inner,
        w_outer,
        order_after,
        out_ref,
        left_own,
        left_core,
        left_x,
        inner_own,
        inner_core,
        inner_y,
        outer_low_ref,
        slope_ref,
        grad_summed_ref,
        hat_ref,
        inv_ref,
        sums_ref,
        left,
        inner,
    ):
        del order_after
        batch_me = lax.axis_index("batch")
        width, hidden = w_inner.shape
        step = width
        count = hidden // step
        ff_rows = hidden // blocks
        many = left_own.shape[0]
        block = many // (blocks // 4)

        def left_rows(b, first, values):
            at = (b >> 2) * block + first
            left[jnp.bitwise_xor(batch_me & 3, b & 3), at : at + values.shape[0]] = values

        def vec(k):
            return vecs[k : k + 1]

        context = context_ref[...]
        mixed = x_ref[...].astype(f32) + mm(context, w_output[...]) + vec(B_OUTPUT)
        hat, inv = norm_stats(mixed)
        hat_ref[...] = hat
        inv_ref[...] = inv
        attn_norm = hat * vec(ATTN_GAIN) + vec(ATTN_SHIFT)
        inner_in = attn_norm.astype(bf16)
        outer = jnp.zeros(attn_norm.shape, f32)
        cols = [slice(k * step, (k + 1) * step) for k in range(count)]
        following = mm(inner_in, w_inner[:, cols[0]])
        for k in range(count):
            pre = following + vec(B_INNER + k)
            if k + 1 < count:
                following = mm(inner_in, w_inner[:, cols[k + 1]])
            cdf = 0.5 + 0.5 * lax.erf(pre * INV_ROOT_TWO)
            act = (pre * cdf).astype(bf16)
            slope_ref[:, cols[k]] = cdf + pre * (jnp.exp(-0.5 * pre * pre) * INV_ROOT_TWO_PI)
            outer += mm(act, w_outer[cols[k]])
            act_t = act.T
            for j in range(step // ff_rows):
                left_rows(k * step // ff_rows + j, 0, act_t[j * ff_rows : (j + 1) * ff_rows])
        summed = attn_norm + outer + vec(B_OUTER)
        final_hat, final_inv = norm_stats(summed)
        gain = vec(FFN_GAIN)
        upstream = grad_ref[...].astype(f32)
        grad_summed = norm_back(upstream * gain, final_hat, final_inv)
        grad_summed_ref[...] = grad_summed
        outer_low = grad_summed.astype(bf16)
        outer_low_ref[...] = outer_low
        out_ref[...] = (final_hat * gain + vec(FFN_SHIFT)).astype(bf16)
        sums_ref[...] = jnp.zeros(sums_ref.shape, f32)
        sums_ref[B_OUTER : B_OUTER + 1] = sum_rows(outer_low.astype(f32))
        sums_ref[FFN_GAIN : FFN_GAIN + 1] = sum_rows(upstream * final_hat)
        sums_ref[FFN_SHIFT : FFN_SHIFT + 1] = sum_rows(upstream)
        out_rows = width // blocks
        padded = block - ff_rows
        inner_t = inner_in.T
        context_t = context.T

        def block_rows(values, b):
            if padded == out_rows:
                return values[b * out_rows : (b + 1) * out_rows]
            row = lax.broadcasted_iota(jnp.int32, (padded, width), 0)
            col = lax.broadcasted_iota(jnp.int32, (padded, width), 1)
            pick = ((row < out_rows) & (col == row + b * out_rows)).astype(f32).astype(bf16)
            return mm(pick, values).astype(bf16)

        for b in range(blocks):
            left_rows(b, ff_rows, block_rows(context_t, b))
            owner = jnp.bitwise_xor(batch_me & 1, b & 1) + 2 * jnp.bitwise_xor(
                (batch_me >> 2) & 1, (b >> 2) & 1
            )
            at = (((b >> 3) << 1) | ((b >> 1) & 1)) * padded
            inner[owner, at : at + padded] = block_rows(inner_t, b)
        left_own[...] = left[0]
        left_core[...] = left[1]
        left_x[:many] = left[2]
        left_x[many:] = left[3]
        few = inner_own.shape[0]
        inner_own[...] = inner[0]
        inner_core[...] = inner[1]
        inner_y[:few] = inner[2]
        inner_y[few:] = inner[3]

    return body


def backward_kernel(
    outer_low_ref,
    slope_ref,
    grad_summed_ref,
    hat_ref,
    inv_ref,
    left_x,
    inner_y,
    vecs,
    sums_in,
    w_output,
    w_inner_t,
    w_outer_t,
    x_ref,
    y_ref,
    grad_mixed_ref,
    g0,
    g1,
    g2,
    g3,
    groups,
    sums,
):
    hidden, width = w_inner_t.shape
    group_refs = (g0, g1, g2, g3)
    size = len(group_refs)
    me = lax.axis_index("blk")
    step = width
    rows = width // size
    span = outer_low_ref.shape[0]
    count = hidden // step
    parts = [slice(k * step, (k + 1) * step) for k in range(count)]
    sums[...] = sums_in[...]
    outer_low = outer_low_ref[...]
    grad_norm = grad_summed_ref[...]
    many, few = left_x.shape[0], inner_y.shape[0]
    x_ref[:many] = left_x[...]
    y_ref[:few] = inner_y[...]
    following = mm(outer_low, w_outer_t[:, parts[0]])
    for k in range(count):
        pre_low = (following * slope_ref[:, parts[k]]).astype(bf16)
        if k + 1 < count:
            following = mm(outer_low, w_outer_t[:, parts[k + 1]])
        grad_norm += mm(pre_low, w_inner_t[parts[k]])
        y_ref[few + k * step : few + (k + 1) * step] = pre_low.T
        sums[B_INNER + k : B_INNER + k + 1] = sum_rows(pre_low.astype(f32))
    hat = hat_ref[...]
    grad_mixed = norm_back(grad_norm * vecs[ATTN_GAIN : ATTN_GAIN + 1], hat, inv_ref[...])
    grad_mixed_ref[...] = grad_mixed
    mixed_low = grad_mixed.astype(bf16)
    narrow(x_ref, many, outer_low)
    narrow(x_ref, many + rows_of(width, span), mixed_low)
    context_grad_t = mm_nt(w_output[...], mixed_low).astype(bf16)
    for g in range(size):
        groups[behind(me, g, size)] = context_grad_t[g * rows : (g + 1) * rows]
    for s in range(size):
        group_refs[s][...] = groups[s]
    sums[ATTN_GAIN : ATTN_GAIN + 1] = sum_rows(grad_norm * hat)
    sums[ATTN_SHIFT : ATTN_SHIFT + 1] = sum_rows(grad_norm)
    sums[B_OUTPUT : B_OUTPUT + 1] = sum_rows(mixed_low.astype(f32))
    narrow(x_ref, many + 2 * rows_of(width, span), sums[...].astype(bf16))


def pack_kernel(core_rows, own, got, *after_and_out):
    out_ref = after_and_out[-1]
    many = core_rows.shape[0]
    size = own.shape[0] - 2 * many
    out_ref[:many] = core_rows[...]
    out_ref[many : 2 * many] = got[many : 2 * many]
    out_ref[2 * many : 2 * many + size] = own[2 * many :]
    out_ref[2 * many + size :] = got[2 * many :]


def first_products_kernel(block, ff_rows, span):
    def body(left_own, sent, received, packed, send_ref, keep_ref):
        many = left_own.shape[0]
        size = sent.shape[0] - 2 * many
        width = send_ref.shape[1]
        tall = rows_of(width, span)
        own = (lax.axis_index("batch") >> 2) & 1
        lefts = ((left_own, 0), (received, 0), (packed, 0), (packed, many))
        rights = (
            (sent, 2 * many),
            (received, 2 * many),
            (packed, 2 * many),
            (packed, 2 * many + size),
        )
        outer_low = jnp.concatenate([widen(ref, at, span, width) for ref, at in rights], axis=0)
        mixed_low = jnp.concatenate(
            [widen(ref, at + tall, span, width) for ref, at in rights], axis=0
        )
        sums = jnp.zeros((EXTRA, width), f32)
        for ref, at in rights:
            sums += widen(ref, at + 2 * tall, EXTRA, width).astype(f32)
        for ref, side in ((send_ref, 1 - own), (keep_ref, own)):
            count = (ref.shape[0] - EXTRA) // block
            for j in range(count):

                def rows(first, number):
                    start = (2 * j + side) * block + first
                    return jnp.concatenate(
                        [
                            source[pl.ds(pl.multiple_of(start + at, 16), number)]
                            for source, at in lefts
                        ],
                        axis=1,
                    )

                at = j * block
                ref[at : at + ff_rows] = mm(rows(0, ff_rows), outer_low).astype(bf16)
                ref[at + ff_rows : at + block] = mm(
                    rows(ff_rows, block - ff_rows), mixed_low
                ).astype(bf16)
            ref[count * block :] = sums.astype(bf16)

    return body


def inner_products_kernel(block):
    def body(inner_own, sent, received, packed, send_ref, keep_ref):
        few = inner_own.shape[0]
        size = sent.shape[0] - 2 * few
        own = (lax.axis_index("batch") >> 1) & 1
        lefts = ((inner_own, 0), (received, 0), (packed, 0), (packed, few))
        rights = ((sent, 2 * few), (received, 2 * few), (packed, 2 * few), (packed, 2 * few + size))
        pre_t = jnp.concatenate([ref[at : at + size] for ref, at in rights], axis=1)
        many = send_ref.shape[0]
        pieces = []
        for side in (1 - own, own):
            for j in range(many // block):
                start = (2 * j + side) * block
                pieces.append(
                    jnp.concatenate(
                        [
                            source[pl.ds(pl.multiple_of(start + at, 16), block)]
                            for source, at in lefts
                        ],
                        axis=1,
                    )
                )
        total = mm_nt(jnp.concatenate(pieces, axis=0), pre_t).astype(bf16)
        send_ref[...] = total[:many]
        keep_ref[...] = total[many:]

    return body


def halve_kernel(block, bit, parts, extra_rows):
    def body(keep_in, *rest):
        got, (send_ref, keep_ref) = rest[:parts], rest[-2:]
        own = (lax.axis_index("batch") >> bit) & 1
        count = (send_ref.shape[0] - extra_rows) // block

        def total(part):
            added = jnp.concatenate([ref[part] for ref in got], axis=1).astype(f32)
            return (keep_in[part].astype(f32) + added).astype(bf16)

        for ref, side in ((send_ref, 1 - own), (keep_ref, own)):
            for j in range(count):
                start = pl.multiple_of((2 * j + side) * block, 16)
                ref[j * block : (j + 1) * block] = total(pl.ds(start, block))
            if extra_rows:
                last = 2 * count * block
                ref[count * block :] = total(slice(last, last + extra_rows))

    return body


def attention_back_kernel(
    probs_ref,
    q_t_ref,
    k_t_ref,
    v_t_ref,
    context_ref,
    d0,
    d1,
    d2,
    d3,
    e0,
    e1,
    e2,
    e3,
    token_sums,
    score_grad,
    out_t,
):
    slots = (d0, d1, d2, d3)
    outs = (e0, e1, e2, e3)
    size = len(slots)
    width, row_len = q_t_ref.shape
    span = row_len // size
    grad_t = jnp.concatenate([slot[...] for slot in slots], axis=1)
    grad = grad_t.T
    for h in range(width // HEAD_DIM):
        cols = slice(h * HEAD_DIM, (h + 1) * HEAD_DIM)
        for s in range(size):
            part = slice(s * span, (s + 1) * span)
            grad_part = grad[part, cols]
            delta = jnp.sum(
                grad_part.astype(f32) * context_ref[part, cols], axis=-1, keepdims=True
            )
            grad_probs = mm(grad_part, v_t_ref[cols])
            score_grad[part] = (probs_ref[h, part].astype(f32) * (grad_probs - delta)).astype(bf16)
        out_t[cols] = (mm_nt(k_t_ref[cols], score_grad[...]) * HEAD_DIM ** (-0.5)).astype(bf16)
        out_t[width + h * HEAD_DIM : width + (h + 1) * HEAD_DIM] = mm(
            q_t_ref[cols], score_grad[...]
        ).astype(bf16)
        out_t[2 * width + h * HEAD_DIM : 2 * width + (h + 1) * HEAD_DIM] = mm(
            grad_t[cols], probs_ref[h]
        ).astype(bf16)
    for s in range(size):
        outs[s][...] = out_t[:, s * span : (s + 1) * span]
    token_sums[...] = mm_nt(jnp.ones((8, row_len), bf16), out_t[...])


def head_products_kernel(
    x0, x1, x2, x3, e0, e1, e2, e3, token_sums, order_after, send_ref, keep_ref, total
):
    del order_after
    core = lax.axis_index("batch") & 1
    x_t = jnp.concatenate([ref[...].T for ref in (x0, x1, x2, x3)], axis=1)
    heads_t = jnp.concatenate([ref[...] for ref in (e0, e1, e2, e3)], axis=1)
    total[...] = mm_nt(x_t, heads_t)
    blocks = lax.axis_size("batch")
    rows, width = total.shape[0] // blocks, total.shape[1]
    padded = (send_ref.shape[0] - EXTRA) // (blocks // 2)
    for own, refs in ((0, (keep_ref, send_ref)), (1, (send_ref, keep_ref))):

        @pl.when(core == own)
        def _():
            for b in range(blocks):
                at = (b >> 1) * padded
                if padded != rows:
                    refs[b & 1][at : at + padded] = jnp.zeros((padded, width), bf16)
                refs[b & 1][at : at + rows] = total[b * rows : (b + 1) * rows].astype(bf16)

    sums = jnp.concatenate((token_sums[...], jnp.zeros((EXTRA - 8, width), f32)), axis=0)
    for ref in (send_ref, keep_ref):
        ref[(blocks // 2) * padded :] = sums.astype(bf16)


def grad_in_kernel(
    e0, e1, e2, e3, grad_mixed, w_query, w_key, w_value, out_ref, groups, weights, sems
):
    slots = (e0, e1, e2, e3)
    size = len(slots)
    me = lax.axis_index("blk")
    copies = [
        pltpu.make_async_copy(weight, weights.at[k], sems.at[k])
        for k, weight in enumerate((w_query, w_key, w_value))
    ]
    for copy in copies:
        copy.start()
    for s in range(size):
        groups[ahead(me, s, size)] = slots[s][...]
    total = grad_mixed[...]
    own = e0.shape[0] // 3
    for k in range(3):
        rows = [groups[g, k * own : (k + 1) * own] for g in range(size)]
        part = jnp.concatenate(rows, axis=0).T
        copies[k].wait()
        total += mm_nt(part, weights[k])
    out_ref[...] = total.astype(bf16)


def split_inner_kernel(keep, got, own_ref, s1, s2, s3, total):
    outs = (own_ref, s1, s2, s3)
    size = len(outs)
    me = lax.axis_index("blk")
    total[...] = keep[...].astype(f32) + got[...].astype(f32)
    width = total.shape[1] // size
    for s in range(size):
        cols = pl.ds(pl.multiple_of(ahead(me, s, size) * width, 128), width)
        outs[s][...] = total[:, cols].astype(outs[s].dtype)


def join_inner_kernel(own, r1, r2, r3, out_ref):
    rows = slice(0, out_ref.shape[0])
    total = own[rows] + r1[rows].astype(f32) + r2[rows].astype(f32) + r3[rows].astype(f32)
    out_ref[...] = total


def split_columns_kernel(keep, got, late, own_ref, s1, s2, s3, groups):
    outs = (s1, s2, s3)
    size = len(outs) + 1
    me = lax.axis_index("blk")
    total = keep[...].astype(f32) + got[...].astype(f32)
    last = total.shape[0] - EXTRA
    half = last // 2
    width = total.shape[1] // size
    sums = total[last:]
    row = lax.broadcasted_iota(jnp.int32, sums.shape, 0)
    group = lax.broadcasted_iota(jnp.int32, sums.shape, 1) // width
    for k, at in ((B_QUERY, 0), (B_VALUE, 2)):
        own_row = late[0:1, at * width : (at + 1) * width]
        sums = jnp.where(
            (row == k) & (group == me), jnp.concatenate([own_row] * size, axis=1), sums
        )
    extra = jnp.concatenate((sums[:, : 2 * width], sums[:, 2 * width :]), axis=0)
    for g in range(size):
        cols = slice(g * width, (g + 1) * width)
        slot = behind(me, g, size)
        groups[slot, :half] = jnp.concatenate((total[:half, cols], total[half:last, cols]), axis=1)
    own_ref[:half] = groups[0]
    own_ref[half:] = extra
    for s in range(1, size):
        outs[s - 1][:half] = groups[s].astype(bf16)
        outs[s - 1][half:] = extra.astype(bf16)


def join_rows_kernel(own, r1, r2, r3, first_ref, second_ref, *rest):
    sum_refs, (rows,) = rest[:-1], rest[-1:]
    total = own[...] + r1[...].astype(f32) + r2[...].astype(f32) + r3[...].astype(f32)
    half, width = total.shape[0] - 2 * EXTRA, total.shape[1] // 2
    rows[:half] = total[:half, :width]
    rows[half:] = total[:half, width:]
    ff_rows = first_ref.shape[0]
    first_ref[...] = rows[:ff_rows]
    second_ref[...] = rows[ff_rows : ff_rows + second_ref.shape[0]]
    sums = jnp.concatenate((total[half : half + EXTRA], total[half + EXTRA :]), axis=1)
    for k, ref in enumerate(sum_refs[:-1]):
        ref[...] = sums[k]
    model_width = sums.shape[1]
    for k in range(sum_refs[-1].shape[0] // model_width):
        sum_refs[-1][k * model_width : (k + 1) * model_width] = sums[B_INNER + k]


def last_sum_kernel(keep, got, order_after, q_ref, k_ref, v_ref, late_ref):
    del order_after
    total = keep[...].astype(f32) + got[...].astype(f32)
    rows, own = q_ref.shape
    for k, ref in enumerate((q_ref, k_ref, v_ref)):
        ref[...] = total[:rows, k * own : (k + 1) * own]
    last = total.shape[0] - EXTRA
    late_ref[...] = total[last : last + 8]


def run_kernel(body, operands, outs, scratch=(), in_hbm=(), limit=8, fill=0):
    vmem = pl.BlockSpec(memory_space=pltpu.VMEM)
    hbm = pl.BlockSpec(memory_space=pltpu.HBM)
    anywhere = pl.BlockSpec(memory_space=pl.ANY)

    def place(k):
        if k - len(operands) in in_hbm:
            return anywhere
        return hbm if k in in_hbm else vmem

    return pl.pallas_call(
        body,
        out_shape=[jax.ShapeDtypeStruct(shape, dtype) for shape, dtype in outs],
        in_specs=[place(k) for k in range(len(operands))],
        out_specs=[vmem] * len(outs),
        scratch_shapes=list(scratch),
        compiler_params=pltpu.CompilerParams(vmem_limit_bytes=limit * MIB),
        cost_estimate=pl.CostEstimate(
            flops=1 + fill * 10**9, bytes_accessed=1, transcendentals=0
        ),
    )(*operands)


def blk_shift(values, step):
    size = lax.axis_size("blk")
    return lax.ppermute(values, "blk", [(i, (i + step) % size) for i in range(size)])


def batch_swap(values, bits):
    size = lax.axis_size("batch")
    return lax.ppermute(values, "batch", [(i, i ^ bits) for i in range(size)])


def halve(keep, got, block, bit, after=(), extra_rows=EXTRA):
    got = got if isinstance(got, list) else [got]
    count = (keep.shape[0] - extra_rows) // block // 2
    shape = ((count * block + extra_rows, keep.shape[1]), bf16)
    return run_kernel(
        halve_kernel(block, bit, len(got), extra_rows),
        [keep, *got, *after],
        [shape, shape],
        in_hbm=[-1 - k for k in range(len(after))],
    )


def local(
    hidden_in,
    w_query,
    b_query,
    w_key,
    w_value,
    b_value,
    w_output,
    b_output,
    attn_gain,
    attn_shift,
    w_inner,
    b_inner,
    w_outer,
    b_outer,
    ffn_gain,
    ffn_shift,
    text_lengths,
    region_lengths,
    out_grad,
):
    _, span, width = hidden_in.shape
    hidden = w_inner.shape[1]
    size = lax.axis_size("blk")
    blocks = lax.axis_size("batch")
    bits = blocks.bit_length() - 1
    row_len = span * size
    own_heads = HEADS // size
    own_width = own_heads * HEAD_DIM
    steps = range(1, size)
    tokens_f32 = ((span, width), f32)
    tokens_bf16 = ((span, width), bf16)
    row = ((width,), f32)

    flat_in = hidden_in[0]
    x_slots = [blk_shift(flat_in, step) for step in steps]
    stacked = jnp.zeros((EXTRA, width), bf16)
    number = lax.broadcasted_iota(jnp.int32, stacked.shape, 0)
    for k, vector in (
        (B_OUTER, b_outer),
        (FFN_GAIN, ffn_gain),
        (FFN_SHIFT, ffn_shift),
        (ATTN_GAIN, attn_gain),
        (ATTN_SHIFT, attn_shift),
        (B_OUTPUT, b_output),
        (B_QUERY, b_query),
        (B_VALUE, b_value),
    ):
        stacked = jnp.where(number == k, vector[None, :], stacked)
    square = ((width, width), bf16)
    mask, vecs, x_own, grad_own, *attn_weights, outer_copy = run_kernel(
        prep_kernel,
        [
            text_lengths,
            region_lengths,
            flat_in,
            out_grad[0],
            stacked,
            b_inner,
            w_query,
            w_key,
            w_value,
            w_outer,
        ],
        [
            ((row_len, row_len), f32),
            ((EXTRA, width), f32),
            tokens_bf16,
            tokens_bf16,
            square,
            square,
            square,
            ((hidden, width), bf16),
        ],
        [pltpu.SemaphoreType.DMA((4,))],
        in_hbm=(6, 7, 8, 9),
        limit=16,
    )
    inner_copy, *ffn_turned = run_kernel(
        transpose_kernel,
        [w_inner, outer_copy],
        [((width, hidden), bf16), ((hidden, width), bf16), ((width, hidden), bf16)],
        [pltpu.SemaphoreType.DMA((1,))],
        in_hbm=(0,),
        limit=20,
        fill=4,
    )
    ffn_weights = (inner_copy, outer_copy)
    x_slots = [x_own] + x_slots
    context = run_kernel(
        own_attention_kernel,
        x_slots + attn_weights + [vecs, mask],
        [tokens_bf16],
        [pltpu.VMEM((row_len, width), bf16)],
        limit=20,
    )[0]
    ff_rows = hidden // blocks
    rows = -(-(width // blocks) // 16) * 16
    block = ff_rows + rows

    many = blocks // 4 * block
    few = blocks // 4 * rows
    (
        layer_out,
        left_own,
        left_core,
        left_x,
        inner_own,
        inner_core,
        inner_y,
        outer_low,
        slope,
        grad_summed,
        attn_hat,
        attn_inv,
        sums,
    ) = run_kernel(
        forward_kernel(blocks),
        [x_own, context, vecs, grad_own, w_output]
        + [*ffn_weights, ffn_turned[0]],
        [
            tokens_bf16,
            ((many, span), bf16),
            ((many, span), bf16),
            ((2 * many, span), bf16),
            ((few, span), bf16),
            ((few, span), bf16),
            ((2 * few, span), bf16),
            tokens_bf16,
            ((span, hidden), f32),
            tokens_f32,
            tokens_f32,
            ((span, 1), f32),
            ((EXTRA, width), f32),
        ],
        [
            pltpu.VMEM((4, many, span), bf16),
            pltpu.VMEM((4, few, span), bf16),
        ],
        in_hbm=(-1,),
        limit=20,
    )
    tall = 2 * rows_of(width, span) + rows_of(width, EXTRA)
    x_sent, y_sent, grad_mixed, *context_grads = run_kernel(
        backward_kernel,
        [
            outer_low,
            slope,
            grad_summed,
            attn_hat,
            attn_inv,
            left_x,
            inner_y,
            vecs,
            sums,
            w_output,
            *ffn_turned,
        ],
        [((2 * many + tall, span), bf16), ((2 * few + hidden, span), bf16), tokens_f32]
        + [((own_width, span), bf16)] * size,
        [pltpu.VMEM((size, own_width, span), bf16), pltpu.VMEM((EXTRA, width), f32)],
        limit=20,
    )
    x_got = batch_swap(x_sent, 2)
    y_got = batch_swap(y_sent, 4)
    context_grads = context_grads[:1] + [blk_shift(context_grads[step], step) for step in steps]
    heads_shape = ((own_width, row_len), bf16)
    probs, q_t, k_t, v_t, context_own = run_kernel(
        head_attention_kernel,
        x_slots + attn_weights + [vecs, mask, grad_mixed],
        [((own_heads, row_len, row_len), bf16)]
        + [heads_shape] * 3
        + [((row_len, own_width), f32)],
        [pltpu.VMEM((row_len, width), bf16)],
        in_hbm=(-1,),
        limit=16,
    )
    *head_grads, token_sums = run_kernel(
        attention_back_kernel,
        [probs, q_t, k_t, v_t, context_own] + context_grads,
        [((3 * own_width, span), bf16)] * size + [((8, 3 * own_width), f32)],
        [pltpu.VMEM((row_len, row_len), bf16), pltpu.VMEM((3 * own_width, row_len), bf16)],
    )
    head_slots = head_grads[:1] + [blk_shift(head_grads[step], size - step) for step in steps]
    packed = run_kernel(
        pack_kernel,
        [inner_core, y_sent, y_got, head_slots[1]],
        [((2 * (few + hidden), span), bf16)],
        in_hbm=(-1,),
        limit=10,
    )[0]
    inner_send, inner_keep = run_kernel(
        inner_products_kernel(rows),
        [inner_own, y_sent, y_got, batch_swap(packed, 1)],
        [((few // 2, hidden), bf16)] * 2,
        limit=14,
    )
    inner_got = batch_swap(inner_send, 2)
    for bit in range(3, bits):
        inner_send, inner_keep = halve(inner_keep, inner_got, rows, bit, extra_rows=0)
        inner_got = batch_swap(inner_send, 1 << bit)
    packed = run_kernel(
        pack_kernel,
        [left_core, x_sent, x_got],
        [((2 * (many + tall), span), bf16)],
    )[0]
    send, keep = run_kernel(
        first_products_kernel(block, ff_rows, span),
        [left_own, x_sent, x_got, batch_swap(packed, 1)],
        [((many // 2 + EXTRA, width), bf16)] * 2,
        limit=14,
    )
    got = batch_swap(send, 4)
    for bit in range(3, bits):
        send, keep = halve(keep, got, block, bit)
        got = batch_swap(send, 1 << bit)
    wide = 3 * own_width
    head_send, head_keep = run_kernel(
        head_products_kernel,
        x_slots + head_grads + [token_sums, send],
        [((blocks // 2 * rows + EXTRA, wide), bf16)] * 2,
        [pltpu.VMEM((width, wide), f32)],
        in_hbm=(-1,),
        limit=10,
    )
    head_got = batch_swap(head_send, 1)
    head_send, head_keep = halve(head_keep, head_got, rows, 1, [inner_got] + head_slots[2:])
    head_got = batch_swap(head_send, 2)
    for bit in range(2, bits):
        head_send, head_keep = halve(head_keep, head_got, rows, bit, [got])
        head_got = batch_swap(head_send, 1 << bit)
    inner_part, *inner_sends = run_kernel(
        split_inner_kernel,
        [inner_keep, inner_got],
        [((rows, width), f32)] + [((rows, width), bf16)] * (size - 1),
        [pltpu.VMEM((rows, hidden), f32)],
    )
    inner_parts = [blk_shift(inner_sends[step - 1], step) for step in steps]
    grad_in = run_kernel(
        grad_in_kernel,
        head_slots + [grad_mixed, w_query, w_key, w_value],
        [tokens_bf16],
        [
            pltpu.VMEM((size, 3 * own_width, span), bf16),
            pltpu.VMEM((3, width, width), bf16),
            pltpu.SemaphoreType.DMA((3,)),
        ],
        in_hbm=(5, 6, 7),
        limit=10,
        fill=4,
    )[0]
    out_rows = width // blocks
    own_cols = ((out_rows, own_width), f32)
    *grad_qkv, late = run_kernel(
        last_sum_kernel,
        [head_keep, head_got, inner_parts[1]],
        [own_cols] * 3 + [((8, wide), f32)],
        in_hbm=(-1,),
    )
    message = (block // 2 + 2 * EXTRA, 2 * own_width)
    own_part, *sends = run_kernel(
        split_columns_kernel,
        [keep, got, late],
        [(message, f32)] + [(message, bf16)] * (size - 1),
        [pltpu.VMEM((size, block // 2, 2 * own_width), f32)],
    )
    parts = [blk_shift(sends[step - 1], step) for step in steps]
    grad_w_inner = run_kernel(
        join_inner_kernel, [inner_part] + inner_parts, [((out_rows, width), f32)]
    )[0]
    grad_w_outer, grad_w_output, *sums = run_kernel(
        join_rows_kernel,
        [own_part] + parts,
        [((ff_rows, own_width), f32), own_cols] + [row] * 8 + [((hidden,), f32)],
        [pltpu.VMEM((block, own_width), f32)],
    )
    return (
        layer_out[None],
        grad_in[None],
        grad_qkv[0],
        sums[B_QUERY],
        grad_qkv[1],
        grad_qkv[2],
        sums[B_VALUE],
        grad_w_output,
        sums[B_OUTPUT],
        sums[ATTN_GAIN],
        sums[ATTN_SHIFT],
        grad_w_inner,
        sums[B_INNER],
        grad_w_outer,
        sums[B_OUTER],
        sums[FFN_GAIN],
        sums[FFN_SHIFT],
    )


def solution(mesh):
    rows = P("batch", "blk", None)
    tile = P("batch", "blk")
    return jax.shard_map(
        local,
        mesh=mesh,
        in_specs=(rows,) + (P(),) * 15 + (P("batch", None), P("batch", None), rows),
        out_specs=(
            rows,
            rows,
            tile,
            P(),
            tile,
            tile,
            P(),
            tile,
            P(),
            P(),
            P(),
            tile,
            P(),
            tile,
            P(),
            P(),
            P(),
        ),
        check_vma=False,
    )
```

```python
import jax
import jax.numpy as jnp
from jax import lax
from jax.experimental import pallas as pl
from jax.experimental.pallas import tpu as pltpu
from jax.sharding import PartitionSpec as P

HEADS = 12
HEAD_DIM = 64
PAIRS = 4

NORM_EPS = 1e-05
MASKED_SCORE = -1e30
INV_ROOT_TWO = 0.7071067811865476
INV_ROOT_TWO_PI = 0.3989422804014327
MIB = 1024 * 1024

B_OUTER, FFN_GAIN, FFN_SHIFT, ATTN_GAIN, ATTN_SHIFT, B_OUTPUT, B_QUERY, B_VALUE, B_INNER = range(9)

EXTRA = 16

f32 = jnp.float32
bf16 = jnp.bfloat16


def mm(left, right):
    return jnp.dot(left, right, preferred_element_type=f32)


def mm_nt(left, right):
    return lax.dot_general(left, right, (((1,), (1,)), ((), ())), preferred_element_type=f32)


def norm_stats(values_in):
    row_mean = jnp.mean(values_in, axis=-1, keepdims=True)
    centred = values_in - row_mean
    inv_dev = lax.rsqrt(jnp.mean(centred * centred, axis=-1, keepdims=True) + NORM_EPS)
    return centred * inv_dev, inv_dev


def norm_back(scaled, normed, inv_dev):
    centre_term = jnp.mean(scaled, axis=-1, keepdims=True)
    slope_term = jnp.mean(scaled * normed, axis=-1, keepdims=True)
    return inv_dev * (scaled - centre_term - normed * slope_term)


def sum_rows(values):
    return jnp.sum(values, axis=0, keepdims=True)


def as_row(ref):
    return ref[...].astype(f32).reshape(1, -1)


def rows_of(width, count):
    return width // 128 * count


def narrow(ref, first, values):
    count = values.shape[0]
    for k in range(values.shape[1] // 128):
        at = first + k * count
        ref[at : at + count] = values[:, k * 128 : (k + 1) * 128]


def widen(ref, first, count, width):
    return jnp.concatenate(
        [ref[first + k * count : first + (k + 1) * count] for k in range(width // 128)], axis=1
    )


def ahead(me, step, size):
    return lax.rem(me + step, size)


def behind(me, group, size):
    return lax.rem(group - me + size, size)


def prep_kernel(
    text,
    region,
    x_ref,
    grad_ref,
    stacked,
    b_inner,
    w_query,
    w_key,
    w_value,
    w_outer,
    mask,
    vecs,
    x_out,
    grad_out,
    query_out,
    key_out,
    value_out,
    outer_out,
    sems,
):
    me = lax.axis_index("blk")
    row_len = mask.shape[0]
    span = x_ref.shape[0]
    size = row_len // span
    model_width = x_ref.shape[1]
    copies = [
        pltpu.make_async_copy(weight, out, sems.at[k])
        for k, (weight, out) in enumerate(
            (
                (w_query, query_out),
                (w_key, key_out),
                (w_value, value_out),
                (w_outer, outer_out),
            )
        )
    ]
    for copy in copies:
        copy.start()
    x_out[...] = x_ref[...]
    grad_out[...] = grad_ref[...]
    vecs[...] = stacked[...].astype(f32)
    hidden_row = as_row(b_inner)
    for k in range(hidden_row.shape[1] // model_width):
        part = slice(k * model_width, (k + 1) * model_width)
        vecs[B_INNER + k : B_INNER + k + 1] = hidden_row[:, part]

    ends = []
    total = jnp.zeros((1, 1), jnp.int32)
    for k in range(PAIRS):
        total = total + text[:, k : k + 1] + region[:, k : k + 1]
        ends.append(total)

    def segments(dim):
        shape = [1, 1]
        shape[dim] = span
        parts = []
        for s in range(size):
            first = lax.rem(me - s + size, size) * span
            pos = lax.broadcasted_iota(jnp.int32, tuple(shape), dim) + first
            seg = jnp.zeros(tuple(shape), jnp.int32)
            for end in ends:
                seg = seg + (pos >= end).astype(jnp.int32)
            parts.append(seg)
        return jnp.concatenate(parts, axis=dim)

    seg_q = segments(0)
    seg_k = segments(1)
    diagonal = lax.broadcasted_iota(jnp.int32, (row_len, row_len), 0) == lax.broadcasted_iota(
        jnp.int32, (row_len, row_len), 1
    )
    allowed = (seg_q == seg_k) & ((seg_k < PAIRS) | diagonal)
    mask[...] = jnp.where(allowed, 0.0, MASKED_SCORE)
    for copy in copies:
        copy.wait()


def transpose_kernel(w_inner, w_outer, inner_out, inner_t, outer_t, sems):
    copy = pltpu.make_async_copy(w_inner, inner_out, sems.at[0])
    copy.start()
    width, hidden = inner_out.shape
    parts = [slice(k * width, (k + 1) * width) for k in range(hidden // width)]
    for part in parts:
        outer_t[:, part] = w_outer[part].T
    copy.wait()
    for part in parts:
        inner_t[part] = inner_out[:, part].T


def attend(query, key, value, mask_of, tasks, store):
    def scores_of(task):
        part, cols = task
        return mm_nt(query[part, cols], key[:, cols])

    following = scores_of(tasks[0])
    for k, (part, cols) in enumerate(tasks):
        scores = following + mask_of(part)
        if k + 1 < len(tasks):
            following = scores_of(tasks[k + 1])
        weights = jnp.exp(scores - jnp.max(scores, axis=-1, keepdims=True))
        probs = (weights * (1.0 / jnp.sum(weights, axis=-1, keepdims=True))).astype(bf16)
        store(part, cols, probs, mm(probs, value[:, cols]))


def own_attention_kernel(
    x0, x1, x2, x3, w_query, w_key, w_value, vecs, mask, context_ref, x_all
):
    span, width = x0.shape
    for s, ref in enumerate((x0, x1, x2, x3)):
        x_all[s * span : (s + 1) * span] = ref[...]
    query = (mm(x0[...], w_query[...]) + vecs[B_QUERY : B_QUERY + 1]).astype(bf16)
    query = (query * HEAD_DIM ** (-0.5)).astype(bf16)
    key = mm(x_all[...], w_key[...]).astype(bf16)
    value = (mm(x_all[...], w_value[...]) + vecs[B_VALUE : B_VALUE + 1]).astype(bf16)
    rows = slice(0, span)
    tasks = [(rows, slice(h * HEAD_DIM, (h + 1) * HEAD_DIM)) for h in range(width // HEAD_DIM)]
    done = []
    attend(
        query,
        key,
        value,
        lambda part: mask[part],
        tasks,
        lambda part, cols, probs, context: done.append(context),
    )
    context_ref[...] = jnp.concatenate(done, axis=1).astype(bf16)


def head_attention_kernel(
    x0,
    x1,
    x2,
    x3,
    w_query,
    w_key,
    w_value,
    vecs,
    mask,
    order_after,
    probs_ref,
    q_t_ref,
    k_t_ref,
    v_t_ref,
    context_ref,
    x_all,
):
    del order_after
    me = lax.axis_index("blk")
    span = x0.shape[0]
    size = x_all.shape[0] // span
    width = context_ref.shape[1]
    for s, ref in enumerate((x0, x1, x2, x3)):
        x_all[s * span : (s + 1) * span] = ref[...]

    def own_row(k):
        row = vecs[k : k + 1]
        out = jnp.zeros((1, width), f32)
        for g in range(size):
            out = jnp.where(me == g, row[:, g * width : (g + 1) * width], out)
        return out

    def own_cols(ref):
        first = pl.multiple_of((me * width) // 128 * 128, 128)
        window = ref[:, pl.ds(first, 256)]
        return jnp.where((me * width) % 128 == 0, window[:, :width], window[:, 256 - width :])

    query = (mm(x_all[...], own_cols(w_query)) + own_row(B_QUERY)).astype(bf16)
    query = (query * HEAD_DIM ** (-0.5)).astype(bf16)
    key = mm(x_all[...], own_cols(w_key)).astype(bf16)
    value = (mm(x_all[...], own_cols(w_value)) + own_row(B_VALUE)).astype(bf16)
    q_t_ref[...] = query.T
    k_t_ref[...] = key.T
    v_t_ref[...] = value.T
    tasks = [
        (slice(s * span, (s + 1) * span), slice(h * HEAD_DIM, (h + 1) * HEAD_DIM))
        for s in range(size)
        for h in range(width // HEAD_DIM)
    ]

    def store(part, cols, probs, context):
        probs_ref[cols.start // HEAD_DIM, part] = probs
        context_ref[part, cols] = context

    attend(query, key, value, lambda part: mask[part], tasks, store)


def forward_kernel(blocks):
    def body(
        x_ref,
        context_ref,
        vecs,
        grad_ref,
        w_output,
        w_inner,
        w_outer,
        order_after,
        out_ref,
        left_own,
        left_core,
        left_x,
        inner_own,
        inner_core,
        inner_y,
        outer_low_ref,
        slope_ref,
        grad_summed_ref,
        hat_ref,
        inv_ref,
        sums_ref,
        left,
        inner,
    ):
        del order_after
        batch_me = lax.axis_index("batch")
        width, hidden = w_inner.shape
        step = width
        count = hidden // step
        ff_rows = hidden // blocks
        many = left_own.shape[0]
        block = many // (blocks // 4)

        def left_rows(b, first, values):
            at = (b >> 2) * block + first
            left[jnp.bitwise_xor(batch_me & 3, b & 3), at : at + values.shape[0]] = values

        def vec(k):
            return vecs[k : k + 1]

        context = context_ref[...]
        mixed = x_ref[...].astype(f32) + mm(context, w_output[...]) + vec(B_OUTPUT)
        hat, inv = norm_stats(mixed)
        hat_ref[...] = hat
        inv_ref[...] = inv
        attn_norm = hat * vec(ATTN_GAIN) + vec(ATTN_SHIFT)
        inner_in = attn_norm.astype(bf16)
        outer = jnp.zeros(attn_norm.shape, f32)
        cols = [slice(k * step, (k + 1) * step) for k in range(count)]
        following = mm(inner_in, w_inner[:, cols[0]])
        for k in range(count):
            pre = following + vec(B_INNER + k)
            if k + 1 < count:
                following = mm(inner_in, w_inner[:, cols[k + 1]])
            cdf = 0.5 + 0.5 * lax.erf(pre * INV_ROOT_TWO)
            act = (pre * cdf).astype(bf16)
            slope_ref[:, cols[k]] = cdf + pre * (jnp.exp(-0.5 * pre * pre) * INV_ROOT_TWO_PI)
            outer += mm(act, w_outer[cols[k]])
            act_t = act.T
            for j in range(step // ff_rows):
                left_rows(k * step // ff_rows + j, 0, act_t[j * ff_rows : (j + 1) * ff_rows])
        summed = attn_norm + outer + vec(B_OUTER)
        final_hat, final_inv = norm_stats(summed)
        gain = vec(FFN_GAIN)
        upstream = grad_ref[...].astype(f32)
        grad_summed = norm_back(upstream * gain, final_hat, final_inv)
        grad_summed_ref[...] = grad_summed
        outer_low = grad_summed.astype(bf16)
        outer_low_ref[...] = outer_low
        out_ref[...] = (final_hat * gain + vec(FFN_SHIFT)).astype(bf16)
        sums_ref[...] = jnp.zeros(sums_ref.shape, f32)
        sums_ref[B_OUTER : B_OUTER + 1] = sum_rows(outer_low.astype(f32))
        sums_ref[FFN_GAIN : FFN_GAIN + 1] = sum_rows(upstream * final_hat)
        sums_ref[FFN_SHIFT : FFN_SHIFT + 1] = sum_rows(upstream)
        out_rows = width // blocks
        padded = block - ff_rows
        inner_t = inner_in.T
        context_t = context.T

        def block_rows(values, b):
            if padded == out_rows:
                return values[b * out_rows : (b + 1) * out_rows]
            row = lax.broadcasted_iota(jnp.int32, (padded, width), 0)
            col = lax.broadcasted_iota(jnp.int32, (padded, width), 1)
            pick = ((row < out_rows) & (col == row + b * out_rows)).astype(f32).astype(bf16)
            return mm(pick, values).astype(bf16)

        for b in range(blocks):
            left_rows(b, ff_rows, block_rows(context_t, b))
            owner = jnp.bitwise_xor(batch_me & 1, b & 1) + 2 * jnp.bitwise_xor(
                (batch_me >> 2) & 1, (b >> 2) & 1
            )
            at = (((b >> 3) << 1) | ((b >> 1) & 1)) * padded
            inner[owner, at : at + padded] = block_rows(inner_t, b)
        left_own[...] = left[0]
        left_core[...] = left[1]
        left_x[:many] = left[2]
        left_x[many:] = left[3]
        few = inner_own.shape[0]
        inner_own[...] = inner[0]
        inner_core[...] = inner[1]
        inner_y[:few] = inner[2]
        inner_y[few:] = inner[3]

    return body


def backward_kernel(
    outer_low_ref,
    slope_ref,
    grad_summed_ref,
    hat_ref,
    inv_ref,
    left_x,
    inner_y,
    vecs,
    sums_in,
    w_output,
    w_inner_t,
    w_outer_t,
    x_ref,
    y_ref,
    grad_mixed_ref,
    g0,
    g1,
    g2,
    g3,
    groups,
    sums,
):
    hidden, width = w_inner_t.shape
    group_refs = (g0, g1, g2, g3)
    size = len(group_refs)
    me = lax.axis_index("blk")
    step = width
    rows = width // size
    span = outer_low_ref.shape[0]
    count = hidden // step
    parts = [slice(k * step, (k + 1) * step) for k in range(count)]
    sums[...] = sums_in[...]
    outer_low = outer_low_ref[...]
    grad_norm = grad_summed_ref[...]
    many, few = left_x.shape[0], inner_y.shape[0]
    x_ref[:many] = left_x[...]
    y_ref[:few] = inner_y[...]
    following = mm(outer_low, w_outer_t[:, parts[0]])
    for k in range(count):
        pre_low = (following * slope_ref[:, parts[k]]).astype(bf16)
        if k + 1 < count:
            following = mm(outer_low, w_outer_t[:, parts[k + 1]])
        grad_norm += mm(pre_low, w_inner_t[parts[k]])
        y_ref[few + k * step : few + (k + 1) * step] = pre_low.T
        sums[B_INNER + k : B_INNER + k + 1] = sum_rows(pre_low.astype(f32))
    hat = hat_ref[...]
    grad_mixed = norm_back(grad_norm * vecs[ATTN_GAIN : ATTN_GAIN + 1], hat, inv_ref[...])
    grad_mixed_ref[...] = grad_mixed
    mixed_low = grad_mixed.astype(bf16)
    narrow(x_ref, many, outer_low)
    narrow(x_ref, many + rows_of(width, span), mixed_low)
    context_grad_t = mm_nt(w_output[...], mixed_low).astype(bf16)
    for g in range(size):
        groups[behind(me, g, size)] = context_grad_t[g * rows : (g + 1) * rows]
    for s in range(size):
        group_refs[s][...] = groups[s]
    sums[ATTN_GAIN : ATTN_GAIN + 1] = sum_rows(grad_norm * hat)
    sums[ATTN_SHIFT : ATTN_SHIFT + 1] = sum_rows(grad_norm)
    sums[B_OUTPUT : B_OUTPUT + 1] = sum_rows(mixed_low.astype(f32))
    narrow(x_ref, many + 2 * rows_of(width, span), sums[...].astype(bf16))


def pack_kernel(core_rows, own, got, *after_and_out):
    out_ref = after_and_out[-1]
    many = core_rows.shape[0]
    size = own.shape[0] - 2 * many
    out_ref[:many] = core_rows[...]
    out_ref[many : 2 * many] = got[many : 2 * many]
    out_ref[2 * many : 2 * many + size] = own[2 * many :]
    out_ref[2 * many + size :] = got[2 * many :]


def first_products_kernel(block, ff_rows, span):
    def body(left_own, sent, received, packed, *after_and_outs):
        send_ref, keep_ref = after_and_outs[-2:]
        many = left_own.shape[0]
        size = sent.shape[0] - 2 * many
        width = send_ref.shape[1]
        tall = rows_of(width, span)
        own = (lax.axis_index("batch") >> 2) & 1
        lefts = ((left_own, 0), (received, 0), (packed, 0), (packed, many))
        rights = (
            (sent, 2 * many),
            (received, 2 * many),
            (packed, 2 * many),
            (packed, 2 * many + size),
        )
        outer_low = jnp.concatenate([widen(ref, at, span, width) for ref, at in rights], axis=0)
        mixed_low = jnp.concatenate(
            [widen(ref, at + tall, span, width) for ref, at in rights], axis=0
        )
        sums = jnp.zeros((EXTRA, width), f32)
        for ref, at in rights:
            sums += widen(ref, at + 2 * tall, EXTRA, width).astype(f32)
        for ref, side in ((send_ref, 1 - own), (keep_ref, own)):
            count = (ref.shape[0] - EXTRA) // block
            for j in range(count):

                def rows(first, number):
                    start = (2 * j + side) * block + first
                    return jnp.concatenate(
                        [
                            source[pl.ds(pl.multiple_of(start + at, 16), number)]
                            for source, at in lefts
                        ],
                        axis=1,
                    )

                at = j * block
                ref[at : at + ff_rows] = mm(rows(0, ff_rows), outer_low).astype(bf16)
                ref[at + ff_rows : at + block] = mm(
                    rows(ff_rows, block - ff_rows), mixed_low
                ).astype(bf16)
            ref[count * block :] = sums.astype(bf16)

    return body


def inner_products_kernel(block):
    def body(inner_own, sent, received, packed, send_ref, keep_ref):
        few = inner_own.shape[0]
        size = sent.shape[0] - 2 * few
        own = (lax.axis_index("batch") >> 1) & 1
        lefts = ((inner_own, 0), (received, 0), (packed, 0), (packed, few))
        rights = ((sent, 2 * few), (received, 2 * few), (packed, 2 * few), (packed, 2 * few + size))
        pre_t = jnp.concatenate([ref[at : at + size] for ref, at in rights], axis=1)
        many = send_ref.shape[0]
        pieces = []
        for side in (1 - own, own):
            for j in range(many // block):
                start = (2 * j + side) * block
                pieces.append(
                    jnp.concatenate(
                        [
                            source[pl.ds(pl.multiple_of(start + at, 16), block)]
                            for source, at in lefts
                        ],
                        axis=1,
                    )
                )
        total = mm_nt(jnp.concatenate(pieces, axis=0), pre_t).astype(bf16)
        send_ref[...] = total[:many]
        keep_ref[...] = total[many:]

    return body


def halve_kernel(block, bit, parts, extra_rows):
    def body(keep_in, *rest):
        got, (send_ref, keep_ref) = rest[:parts], rest[-2:]
        own = (lax.axis_index("batch") >> bit) & 1
        count = (send_ref.shape[0] - extra_rows) // block

        def total(part):
            added = jnp.concatenate([ref[part] for ref in got], axis=1).astype(f32)
            return (keep_in[part].astype(f32) + added).astype(bf16)

        for ref, side in ((send_ref, 1 - own), (keep_ref, own)):
            for j in range(count):
                start = pl.multiple_of((2 * j + side) * block, 16)
                ref[j * block : (j + 1) * block] = total(pl.ds(start, block))
            if extra_rows:
                last = 2 * count * block
                ref[count * block :] = total(slice(last, last + extra_rows))

    return body


def attention_back_kernel(
    probs_ref,
    q_t_ref,
    k_t_ref,
    v_t_ref,
    context_ref,
    d0,
    d1,
    d2,
    d3,
    e0,
    e1,
    e2,
    e3,
    token_sums,
    score_grad,
    out_t,
):
    slots = (d0, d1, d2, d3)
    outs = (e0, e1, e2, e3)
    size = len(slots)
    width, row_len = q_t_ref.shape
    span = row_len // size
    grad_t = jnp.concatenate([slot[...] for slot in slots], axis=1)
    grad = grad_t.T
    for h in range(width // HEAD_DIM):
        cols = slice(h * HEAD_DIM, (h + 1) * HEAD_DIM)
        for s in range(size):
            part = slice(s * span, (s + 1) * span)
            grad_part = grad[part, cols]
            delta = jnp.sum(
                grad_part.astype(f32) * context_ref[part, cols], axis=-1, keepdims=True
            )
            grad_probs = mm(grad_part, v_t_ref[cols])
            score_grad[part] = (probs_ref[h, part].astype(f32) * (grad_probs - delta)).astype(bf16)
        out_t[cols] = (mm_nt(k_t_ref[cols], score_grad[...]) * HEAD_DIM ** (-0.5)).astype(bf16)
        out_t[width + h * HEAD_DIM : width + (h + 1) * HEAD_DIM] = mm(
            q_t_ref[cols], score_grad[...]
        ).astype(bf16)
        out_t[2 * width + h * HEAD_DIM : 2 * width + (h + 1) * HEAD_DIM] = mm(
            grad_t[cols], probs_ref[h]
        ).astype(bf16)
    for s in range(size):
        outs[s][...] = out_t[:, s * span : (s + 1) * span]
    token_sums[...] = mm_nt(jnp.ones((8, row_len), bf16), out_t[...])


def head_products_kernel(
    x0, x1, x2, x3, e0, e1, e2, e3, token_sums, send_ref, keep_ref, total
):
    core = lax.axis_index("batch") & 1
    x_t = jnp.concatenate([ref[...].T for ref in (x0, x1, x2, x3)], axis=1)
    heads_t = jnp.concatenate([ref[...] for ref in (e0, e1, e2, e3)], axis=1)
    total[...] = mm_nt(x_t, heads_t)
    blocks = lax.axis_size("batch")
    rows, width = total.shape[0] // blocks, total.shape[1]
    padded = (send_ref.shape[0] - EXTRA) // (blocks // 2)
    for own, refs in ((0, (keep_ref, send_ref)), (1, (send_ref, keep_ref))):

        @pl.when(core == own)
        def _():
            for b in range(blocks):
                at = (b >> 1) * padded
                if padded != rows:
                    refs[b & 1][at : at + padded] = jnp.zeros((padded, width), bf16)
                refs[b & 1][at : at + rows] = total[b * rows : (b + 1) * rows].astype(bf16)

    sums = jnp.concatenate((token_sums[...], jnp.zeros((EXTRA - 8, width), f32)), axis=0)
    for ref in (send_ref, keep_ref):
        ref[(blocks // 2) * padded :] = sums.astype(bf16)


def grad_in_kernel(
    e0, e1, e2, e3, grad_mixed, w_query, w_key, w_value, out_ref, groups, weights, sems
):
    slots = (e0, e1, e2, e3)
    size = len(slots)
    me = lax.axis_index("blk")
    copies = [
        pltpu.make_async_copy(weight, weights.at[k], sems.at[k])
        for k, weight in enumerate((w_query, w_key, w_value))
    ]
    for copy in copies:
        copy.start()
    for s in range(size):
        groups[ahead(me, s, size)] = slots[s][...]
    total = grad_mixed[...]
    own = e0.shape[0] // 3
    for k in range(3):
        rows = [groups[g, k * own : (k + 1) * own] for g in range(size)]
        part = jnp.concatenate(rows, axis=0).T
        copies[k].wait()
        total += mm_nt(part, weights[k])
    out_ref[...] = total.astype(bf16)


def split_inner_kernel(keep, got, order_after, own_ref, s1, s2, s3, total):
    del order_after
    outs = (own_ref, s1, s2, s3)
    size = len(outs)
    me = lax.axis_index("blk")
    total[...] = keep[...].astype(f32) + got[...].astype(f32)
    width = total.shape[1] // size
    for s in range(size):
        cols = pl.ds(pl.multiple_of(ahead(me, s, size) * width, 128), width)
        outs[s][...] = total[:, cols].astype(outs[s].dtype)


def join_inner_kernel(own, r1, r2, r3, out_ref):
    rows = slice(0, out_ref.shape[0])
    total = own[rows] + r1[rows].astype(f32) + r2[rows].astype(f32) + r3[rows].astype(f32)
    out_ref[...] = total


def split_columns_kernel(keep, got, late, own_ref, s1, s2, s3, groups):
    outs = (s1, s2, s3)
    size = len(outs) + 1
    me = lax.axis_index("blk")
    total = keep[...].astype(f32) + got[...].astype(f32)
    last = total.shape[0] - EXTRA
    half = last // 2
    width = total.shape[1] // size
    sums = total[last:]
    row = lax.broadcasted_iota(jnp.int32, sums.shape, 0)
    group = lax.broadcasted_iota(jnp.int32, sums.shape, 1) // width
    for k, at in ((B_QUERY, 0), (B_VALUE, 2)):
        own_row = late[0:1, at * width : (at + 1) * width]
        sums = jnp.where(
            (row == k) & (group == me), jnp.concatenate([own_row] * size, axis=1), sums
        )
    extra = jnp.concatenate((sums[:, : 2 * width], sums[:, 2 * width :]), axis=0)
    for g in range(size):
        cols = slice(g * width, (g + 1) * width)
        slot = behind(me, g, size)
        groups[slot, :half] = jnp.concatenate((total[:half, cols], total[half:last, cols]), axis=1)
    own_ref[:half] = groups[0]
    own_ref[half:] = extra
    for s in range(1, size):
        outs[s - 1][:half] = groups[s].astype(bf16)
        outs[s - 1][half:] = extra.astype(bf16)


def join_rows_kernel(own, r1, r2, r3, first_ref, second_ref, *rest):
    sum_refs, (rows,) = rest[:-1], rest[-1:]
    total = own[...] + r1[...].astype(f32) + r2[...].astype(f32) + r3[...].astype(f32)
    half, width = total.shape[0] - 2 * EXTRA, total.shape[1] // 2
    rows[:half] = total[:half, :width]
    rows[half:] = total[:half, width:]
    ff_rows = first_ref.shape[0]
    first_ref[...] = rows[:ff_rows]
    second_ref[...] = rows[ff_rows : ff_rows + second_ref.shape[0]]
    sums = jnp.concatenate((total[half : half + EXTRA], total[half + EXTRA :]), axis=1)
    for k, ref in enumerate(sum_refs[:-1]):
        ref[...] = sums[k]
    model_width = sums.shape[1]
    for k in range(sum_refs[-1].shape[0] // model_width):
        sum_refs[-1][k * model_width : (k + 1) * model_width] = sums[B_INNER + k]


def last_sum_kernel(keep, got, *after_and_outs):
    q_ref, k_ref, v_ref, late_ref = after_and_outs[-4:]
    total = keep[...].astype(f32) + got[...].astype(f32)
    rows, own = q_ref.shape
    for k, ref in enumerate((q_ref, k_ref, v_ref)):
        ref[...] = total[:rows, k * own : (k + 1) * own]
    last = total.shape[0] - EXTRA
    late_ref[...] = total[last : last + 8]


def run_kernel(body, operands, outs, scratch=(), in_hbm=(), limit=8, fill=0):
    vmem = pl.BlockSpec(memory_space=pltpu.VMEM)
    hbm = pl.BlockSpec(memory_space=pltpu.HBM)
    anywhere = pl.BlockSpec(memory_space=pl.ANY)

    def place(k):
        if k - len(operands) in in_hbm:
            return anywhere
        return hbm if k in in_hbm else vmem

    return pl.pallas_call(
        body,
        out_shape=[jax.ShapeDtypeStruct(shape, dtype) for shape, dtype in outs],
        in_specs=[place(k) for k in range(len(operands))],
        out_specs=[vmem] * len(outs),
        scratch_shapes=list(scratch),
        compiler_params=pltpu.CompilerParams(vmem_limit_bytes=limit * MIB),
        cost_estimate=pl.CostEstimate(
            flops=1 + fill * 10**9, bytes_accessed=1, transcendentals=0
        ),
    )(*operands)


def blk_shift(values, step):
    size = lax.axis_size("blk")
    return lax.ppermute(values, "blk", [(i, (i + step) % size) for i in range(size)])


def batch_swap(values, bits):
    size = lax.axis_size("batch")
    return lax.ppermute(values, "batch", [(i, i ^ bits) for i in range(size)])


def halve(keep, got, block, bit, after=(), extra_rows=EXTRA):
    got = got if isinstance(got, list) else [got]
    count = (keep.shape[0] - extra_rows) // block // 2
    shape = ((count * block + extra_rows, keep.shape[1]), bf16)
    return run_kernel(
        halve_kernel(block, bit, len(got), extra_rows),
        [keep, *got, *after],
        [shape, shape],
        in_hbm=[-1 - k for k in range(len(after))],
    )


def local(
    hidden_in,
    w_query,
    b_query,
    w_key,
    w_value,
    b_value,
    w_output,
    b_output,
    attn_gain,
    attn_shift,
    w_inner,
    b_inner,
    w_outer,
    b_outer,
    ffn_gain,
    ffn_shift,
    text_lengths,
    region_lengths,
    out_grad,
):
    _, span, width = hidden_in.shape
    hidden = w_inner.shape[1]
    size = lax.axis_size("blk")
    blocks = lax.axis_size("batch")
    bits = blocks.bit_length() - 1
    row_len = span * size
    own_heads = HEADS // size
    own_width = own_heads * HEAD_DIM
    steps = range(1, size)
    tokens_f32 = ((span, width), f32)
    tokens_bf16 = ((span, width), bf16)
    row = ((width,), f32)

    flat_in = hidden_in[0]
    x_slots = [blk_shift(flat_in, step) for step in steps]
    stacked = jnp.zeros((EXTRA, width), bf16)
    number = lax.broadcasted_iota(jnp.int32, stacked.shape, 0)
    for k, vector in (
        (B_OUTER, b_outer),
        (FFN_GAIN, ffn_gain),
        (FFN_SHIFT, ffn_shift),
        (ATTN_GAIN, attn_gain),
        (ATTN_SHIFT, attn_shift),
        (B_OUTPUT, b_output),
        (B_QUERY, b_query),
        (B_VALUE, b_value),
    ):
        stacked = jnp.where(number == k, vector[None, :], stacked)
    square = ((width, width), bf16)
    mask, vecs, x_own, grad_own, *attn_weights, outer_copy = run_kernel(
        prep_kernel,
        [
            text_lengths,
            region_lengths,
            flat_in,
            out_grad[0],
            stacked,
            b_inner,
            w_query,
            w_key,
            w_value,
            w_outer,
        ],
        [
            ((row_len, row_len), f32),
            ((EXTRA, width), f32),
            tokens_bf16,
            tokens_bf16,
            square,
            square,
            square,
            ((hidden, width), bf16),
        ],
        [pltpu.SemaphoreType.DMA((4,))],
        in_hbm=(6, 7, 8, 9),
        limit=16,
    )
    inner_copy, *ffn_turned = run_kernel(
        transpose_kernel,
        [w_inner, outer_copy],
        [((width, hidden), bf16), ((hidden, width), bf16), ((width, hidden), bf16)],
        [pltpu.SemaphoreType.DMA((1,))],
        in_hbm=(0,),
        limit=20,
        fill=4,
    )
    ffn_weights = (inner_copy, outer_copy)
    x_slots = [x_own] + x_slots
    context = run_kernel(
        own_attention_kernel,
        x_slots + attn_weights + [vecs, mask],
        [tokens_bf16],
        [pltpu.VMEM((row_len, width), bf16)],
        limit=20,
    )[0]
    ff_rows = hidden // blocks
    rows = -(-(width // blocks) // 16) * 16
    block = ff_rows + rows

    many = blocks // 4 * block
    few = blocks // 4 * rows
    (
        layer_out,
        left_own,
        left_core,
        left_x,
        inner_own,
        inner_core,
        inner_y,
        outer_low,
        slope,
        grad_summed,
        attn_hat,
        attn_inv,
        sums,
    ) = run_kernel(
        forward_kernel(blocks),
        [x_own, context, vecs, grad_own, w_output]
        + [*ffn_weights, ffn_turned[0]],
        [
            tokens_bf16,
            ((many, span), bf16),
            ((many, span), bf16),
            ((2 * many, span), bf16),
            ((few, span), bf16),
            ((few, span), bf16),
            ((2 * few, span), bf16),
            tokens_bf16,
            ((span, hidden), f32),
            tokens_f32,
            tokens_f32,
            ((span, 1), f32),
            ((EXTRA, width), f32),
        ],
        [
            pltpu.VMEM((4, many, span), bf16),
            pltpu.VMEM((4, few, span), bf16),
        ],
        in_hbm=(-1,),
        limit=20,
    )
    tall = 2 * rows_of(width, span) + rows_of(width, EXTRA)
    x_sent, y_sent, grad_mixed, *context_grads = run_kernel(
        backward_kernel,
        [
            outer_low,
            slope,
            grad_summed,
            attn_hat,
            attn_inv,
            left_x,
            inner_y,
            vecs,
            sums,
            w_output,
            *ffn_turned,
        ],
        [((2 * many + tall, span), bf16), ((2 * few + hidden, span), bf16), tokens_f32]
        + [((own_width, span), bf16)] * size,
        [pltpu.VMEM((size, own_width, span), bf16), pltpu.VMEM((EXTRA, width), f32)],
        limit=20,
    )
    x_got = batch_swap(x_sent, 2)
    y_got = batch_swap(y_sent, 4)
    context_grads = context_grads[:1] + [blk_shift(context_grads[step], step) for step in steps]
    heads_shape = ((own_width, row_len), bf16)
    probs, q_t, k_t, v_t, context_own = run_kernel(
        head_attention_kernel,
        x_slots + attn_weights + [vecs, mask, grad_mixed],
        [((own_heads, row_len, row_len), bf16)]
        + [heads_shape] * 3
        + [((row_len, own_width), f32)],
        [pltpu.VMEM((row_len, width), bf16)],
        in_hbm=(-1,),
        limit=16,
    )
    *head_grads, token_sums = run_kernel(
        attention_back_kernel,
        [probs, q_t, k_t, v_t, context_own] + context_grads,
        [((3 * own_width, span), bf16)] * size + [((8, 3 * own_width), f32)],
        [pltpu.VMEM((row_len, row_len), bf16), pltpu.VMEM((3 * own_width, row_len), bf16)],
    )
    head_slots = head_grads[:1] + [blk_shift(head_grads[step], size - step) for step in steps]
    wide = 3 * own_width
    head_send, head_keep = run_kernel(
        head_products_kernel,
        x_slots + head_grads + [token_sums],
        [((blocks // 2 * rows + EXTRA, wide), bf16)] * 2,
        [pltpu.VMEM((width, wide), f32)],
        limit=10,
    )
    head_got = batch_swap(head_send, 1)
    head_send, head_keep = halve(head_keep, head_got, rows, 1)
    head_got = batch_swap(head_send, 2)
    packed = run_kernel(
        pack_kernel,
        [inner_core, y_sent, y_got, head_send, head_slots[1], x_got],
        [((2 * (few + hidden), span), bf16)],
        in_hbm=(-1, -2, -3),
        limit=10,
    )[0]
    inner_send, inner_keep = run_kernel(
        inner_products_kernel(rows),
        [inner_own, y_sent, y_got, batch_swap(packed, 1)],
        [((few // 2, hidden), bf16)] * 2,
        limit=14,
    )
    inner_got = batch_swap(inner_send, 2)
    for bit in range(3, bits):
        inner_send, inner_keep = halve(inner_keep, inner_got, rows, bit, extra_rows=0)
        inner_got = batch_swap(inner_send, 1 << bit)
    packed = run_kernel(
        pack_kernel,
        [left_core, x_sent, x_got],
        [((2 * (many + tall), span), bf16)],
    )[0]
    for bit in range(2, bits):
        head_send, head_keep = halve(head_keep, head_got, rows, bit)
        head_got = batch_swap(head_send, 1 << bit)
    send, keep = run_kernel(
        first_products_kernel(block, ff_rows, span),
        [left_own, x_sent, x_got, batch_swap(packed, 1), head_send, head_slots[-1]],
        [((many // 2 + EXTRA, width), bf16)] * 2,
        in_hbm=(-1, -2),
        limit=14,
    )
    got = batch_swap(send, 4)
    for bit in range(3, bits):
        send, keep = halve(keep, got, block, bit)
        got = batch_swap(send, 1 << bit)
    inner_part, *inner_sends = run_kernel(
        split_inner_kernel,
        [inner_keep, inner_got, head_slots[2]],
        [((rows, width), f32)] + [((rows, width), bf16)] * (size - 1),
        [pltpu.VMEM((rows, hidden), f32)],
        in_hbm=(-1,),
    )
    inner_parts = [blk_shift(inner_sends[step - 1], step) for step in steps]
    grad_in = run_kernel(
        grad_in_kernel,
        head_slots + [grad_mixed, w_query, w_key, w_value],
        [tokens_bf16],
        [
            pltpu.VMEM((size, 3 * own_width, span), bf16),
            pltpu.VMEM((3, width, width), bf16),
            pltpu.SemaphoreType.DMA((3,)),
        ],
        in_hbm=(5, 6, 7),
        limit=10,
        fill=4,
    )[0]
    out_rows = width // blocks
    own_cols = ((out_rows, own_width), f32)
    *grad_qkv, late = run_kernel(
        last_sum_kernel,
        [head_keep, head_got, grad_in] + inner_parts,
        [own_cols] * 3 + [((8, wide), f32)],
        in_hbm=(-1, -2, -3, -4),
    )
    message = (block // 2 + 2 * EXTRA, 2 * own_width)
    own_part, *sends = run_kernel(
        split_columns_kernel,
        [keep, got, late],
        [(message, f32)] + [(message, bf16)] * (size - 1),
        [pltpu.VMEM((size, block // 2, 2 * own_width), f32)],
    )
    parts = [blk_shift(sends[step - 1], step) for step in steps]
    grad_w_inner = run_kernel(
        join_inner_kernel, [inner_part] + inner_parts, [((out_rows, width), f32)]
    )[0]
    grad_w_outer, grad_w_output, *sums = run_kernel(
        join_rows_kernel,
        [own_part] + parts,
        [((ff_rows, own_width), f32), own_cols] + [row] * 8 + [((hidden,), f32)],
        [pltpu.VMEM((block, own_width), f32)],
    )
    return (
        layer_out[None],
        grad_in[None],
        grad_qkv[0],
        sums[B_QUERY],
        grad_qkv[1],
        grad_qkv[2],
        sums[B_VALUE],
        grad_w_output,
        sums[B_OUTPUT],
        sums[ATTN_GAIN],
        sums[ATTN_SHIFT],
        grad_w_inner,
        sums[B_INNER],
        grad_w_outer,
        sums[B_OUTER],
        sums[FFN_GAIN],
        sums[FFN_SHIFT],
    )


def solution(mesh):
    rows = P("batch", "blk", None)
    tile = P("batch", "blk")
    return jax.shard_map(
        local,
        mesh=mesh,
        in_specs=(rows,) + (P(),) * 15 + (P("batch", None), P("batch", None), rows),
        out_specs=(
            rows,
            rows,
            tile,
            P(),
            tile,
            tile,
            P(),
            tile,
            P(),
            P(),
            P(),
            tile,
            P(),
            tile,
            P(),
            P(),
            P(),
        ),
        check_vma=False,
    )
```

```python
import jax
import jax.numpy as jnp
from jax import lax
from jax.experimental import pallas as pl
from jax.experimental.pallas import tpu as pltpu
from jax.sharding import PartitionSpec as P

HEADS = 12
HEAD_DIM = 64
PAIRS = 4

NORM_EPS = 1e-05
MASKED_SCORE = -1e30
INV_ROOT_TWO = 0.7071067811865476
INV_ROOT_TWO_PI = 0.3989422804014327
MIB = 1024 * 1024

B_OUTER, FFN_GAIN, FFN_SHIFT, ATTN_GAIN, ATTN_SHIFT, B_OUTPUT, B_QUERY, B_VALUE, B_INNER = range(9)

EXTRA = 16

f32 = jnp.float32
bf16 = jnp.bfloat16


def mm(left, right):
    return jnp.dot(left, right, preferred_element_type=f32)


def mm_nt(left, right):
    return lax.dot_general(left, right, (((1,), (1,)), ((), ())), preferred_element_type=f32)


def norm_stats(values_in):
    row_mean = jnp.mean(values_in, axis=-1, keepdims=True)
    centred = values_in - row_mean
    inv_dev = lax.rsqrt(jnp.mean(centred * centred, axis=-1, keepdims=True) + NORM_EPS)
    return centred * inv_dev, inv_dev


def norm_back(scaled, normed, inv_dev):
    centre_term = jnp.mean(scaled, axis=-1, keepdims=True)
    slope_term = jnp.mean(scaled * normed, axis=-1, keepdims=True)
    return inv_dev * (scaled - centre_term - normed * slope_term)


def sum_rows(values):
    return jnp.sum(values, axis=0, keepdims=True)


def as_row(ref):
    return ref[...].astype(f32).reshape(1, -1)


def rows_of(width, count):
    return width // 128 * count


def narrow(ref, first, values):
    count = values.shape[0]
    for k in range(values.shape[1] // 128):
        at = first + k * count
        ref[at : at + count] = values[:, k * 128 : (k + 1) * 128]


def widen(ref, first, count, width):
    return jnp.concatenate(
        [ref[first + k * count : first + (k + 1) * count] for k in range(width // 128)], axis=1
    )


def ahead(me, step, size):
    return lax.rem(me + step, size)


def behind(me, group, size):
    return lax.rem(group - me + size, size)


def prep_kernel(
    text,
    region,
    x_ref,
    grad_ref,
    stacked,
    b_inner,
    w_query,
    w_key,
    w_value,
    w_outer,
    mask,
    vecs,
    x_out,
    grad_out,
    query_out,
    key_out,
    value_out,
    outer_out,
    sems,
):
    me = lax.axis_index("blk")
    row_len = mask.shape[0]
    span = x_ref.shape[0]
    size = row_len // span
    model_width = x_ref.shape[1]
    copies = [
        pltpu.make_async_copy(weight, out, sems.at[k])
        for k, (weight, out) in enumerate(
            (
                (w_query, query_out),
                (w_key, key_out),
                (w_value, value_out),
                (w_outer, outer_out),
            )
        )
    ]
    for copy in copies:
        copy.start()
    x_out[...] = x_ref[...]
    grad_out[...] = grad_ref[...]
    vecs[...] = stacked[...].astype(f32)
    hidden_row = as_row(b_inner)
    for k in range(hidden_row.shape[1] // model_width):
        part = slice(k * model_width, (k + 1) * model_width)
        vecs[B_INNER + k : B_INNER + k + 1] = hidden_row[:, part]

    ends = []
    total = jnp.zeros((1, 1), jnp.int32)
    for k in range(PAIRS):
        total = total + text[:, k : k + 1] + region[:, k : k + 1]
        ends.append(total)

    def segments(dim):
        shape = [1, 1]
        shape[dim] = span
        parts = []
        for s in range(size):
            first = lax.rem(me - s + size, size) * span
            pos = lax.broadcasted_iota(jnp.int32, tuple(shape), dim) + first
            seg = jnp.zeros(tuple(shape), jnp.int32)
            for end in ends:
                seg = seg + (pos >= end).astype(jnp.int32)
            parts.append(seg)
        return jnp.concatenate(parts, axis=dim)

    seg_q = segments(0)
    seg_k = segments(1)
    diagonal = lax.broadcasted_iota(jnp.int32, (row_len, row_len), 0) == lax.broadcasted_iota(
        jnp.int32, (row_len, row_len), 1
    )
    allowed = (seg_q == seg_k) & ((seg_k < PAIRS) | diagonal)
    mask[...] = jnp.where(allowed, 0.0, MASKED_SCORE)
    for copy in copies:
        copy.wait()


def transpose_kernel(w_inner, w_outer, inner_out, inner_t, outer_t, sems):
    copy = pltpu.make_async_copy(w_inner, inner_out, sems.at[0])
    copy.start()
    width, hidden = inner_out.shape
    parts = [slice(k * width, (k + 1) * width) for k in range(hidden // width)]
    for part in parts:
        outer_t[:, part] = w_outer[part].T
    copy.wait()
    for part in parts:
        inner_t[part] = inner_out[:, part].T


def attend(query, key, value, mask_of, tasks, store):
    def scores_of(task):
        part, cols = task
        return mm_nt(query[part, cols], key[:, cols])

    following = scores_of(tasks[0])
    for k, (part, cols) in enumerate(tasks):
        scores = following + mask_of(part)
        if k + 1 < len(tasks):
            following = scores_of(tasks[k + 1])
        weights = jnp.exp(scores - jnp.max(scores, axis=-1, keepdims=True))
        probs = (weights * (1.0 / jnp.sum(weights, axis=-1, keepdims=True))).astype(bf16)
        store(part, cols, probs, mm(probs, value[:, cols]))


def own_attention_kernel(
    x0, x1, x2, x3, w_query, w_key, w_value, vecs, mask, context_ref, x_all
):
    span, width = x0.shape
    for s, ref in enumerate((x0, x1, x2, x3)):
        x_all[s * span : (s + 1) * span] = ref[...]
    query = (mm(x0[...], w_query[...]) + vecs[B_QUERY : B_QUERY + 1]).astype(bf16)
    query = (query * HEAD_DIM ** (-0.5)).astype(bf16)
    key = mm(x_all[...], w_key[...]).astype(bf16)
    value = (mm(x_all[...], w_value[...]) + vecs[B_VALUE : B_VALUE + 1]).astype(bf16)
    rows = slice(0, span)
    tasks = [(rows, slice(h * HEAD_DIM, (h + 1) * HEAD_DIM)) for h in range(width // HEAD_DIM)]
    done = []
    attend(
        query,
        key,
        value,
        lambda part: mask[part],
        tasks,
        lambda part, cols, probs, context: done.append(context),
    )
    context_ref[...] = jnp.concatenate(done, axis=1).astype(bf16)


def head_attention_kernel(
    x0,
    x1,
    x2,
    x3,
    w_query,
    w_key,
    w_value,
    vecs,
    mask,
    order_after,
    probs_ref,
    q_t_ref,
    k_t_ref,
    v_t_ref,
    context_ref,
    x_all,
):
    del order_after
    me = lax.axis_index("blk")
    span = x0.shape[0]
    size = x_all.shape[0] // span
    width = context_ref.shape[1]
    for s, ref in enumerate((x0, x1, x2, x3)):
        x_all[s * span : (s + 1) * span] = ref[...]

    def own_row(k):
        row = vecs[k : k + 1]
        out = jnp.zeros((1, width), f32)
        for g in range(size):
            out = jnp.where(me == g, row[:, g * width : (g + 1) * width], out)
        return out

    def own_cols(ref):
        first = pl.multiple_of((me * width) // 128 * 128, 128)
        window = ref[:, pl.ds(first, 256)]
        return jnp.where((me * width) % 128 == 0, window[:, :width], window[:, 256 - width :])

    query = (mm(x_all[...], own_cols(w_query)) + own_row(B_QUERY)).astype(bf16)
    query = (query * HEAD_DIM ** (-0.5)).astype(bf16)
    key = mm(x_all[...], own_cols(w_key)).astype(bf16)
    value = (mm(x_all[...], own_cols(w_value)) + own_row(B_VALUE)).astype(bf16)
    q_t_ref[...] = query.T
    k_t_ref[...] = key.T
    v_t_ref[...] = value.T
    tasks = [
        (slice(s * span, (s + 1) * span), slice(h * HEAD_DIM, (h + 1) * HEAD_DIM))
        for s in range(size)
        for h in range(width // HEAD_DIM)
    ]

    def store(part, cols, probs, context):
        probs_ref[cols.start // HEAD_DIM, part] = probs
        context_ref[part, cols] = context

    attend(query, key, value, lambda part: mask[part], tasks, store)


def forward_kernel(blocks):
    def body(
        x_ref,
        context_ref,
        vecs,
        grad_ref,
        w_output,
        w_inner,
        w_outer,
        order_after,
        out_ref,
        left_own,
        left_core,
        left_x,
        inner_own,
        inner_core,
        inner_y,
        outer_low_ref,
        slope_ref,
        grad_summed_ref,
        hat_ref,
        inv_ref,
        sums_ref,
        left,
        inner,
    ):
        del order_after
        batch_me = lax.axis_index("batch")
        width, hidden = w_inner.shape
        step = width
        count = hidden // step
        ff_rows = hidden // blocks
        many = left_own.shape[0]
        block = many // (blocks // 4)

        def left_rows(b, first, values):
            at = (b >> 2) * block + first
            left[jnp.bitwise_xor(batch_me & 3, b & 3), at : at + values.shape[0]] = values

        def vec(k):
            return vecs[k : k + 1]

        context = context_ref[...]
        mixed = x_ref[...].astype(f32) + mm(context, w_output[...]) + vec(B_OUTPUT)
        hat, inv = norm_stats(mixed)
        hat_ref[...] = hat
        inv_ref[...] = inv
        attn_norm = hat * vec(ATTN_GAIN) + vec(ATTN_SHIFT)
        inner_in = attn_norm.astype(bf16)
        outer = jnp.zeros(attn_norm.shape, f32)
        cols = [slice(k * step, (k + 1) * step) for k in range(count)]
        following = mm(inner_in, w_inner[:, cols[0]])
        for k in range(count):
            pre = following + vec(B_INNER + k)
            if k + 1 < count:
                following = mm(inner_in, w_inner[:, cols[k + 1]])
            cdf = 0.5 + 0.5 * lax.erf(pre * INV_ROOT_TWO)
            act = (pre * cdf).astype(bf16)
            slope_ref[:, cols[k]] = cdf + pre * (jnp.exp(-0.5 * pre * pre) * INV_ROOT_TWO_PI)
            outer += mm(act, w_outer[cols[k]])
            act_t = act.T
            for j in range(step // ff_rows):
                left_rows(k * step // ff_rows + j, 0, act_t[j * ff_rows : (j + 1) * ff_rows])
        summed = attn_norm + outer + vec(B_OUTER)
        final_hat, final_inv = norm_stats(summed)
        gain = vec(FFN_GAIN)
        upstream = grad_ref[...].astype(f32)
        grad_summed = norm_back(upstream * gain, final_hat, final_inv)
        grad_summed_ref[...] = grad_summed
        outer_low = grad_summed.astype(bf16)
        outer_low_ref[...] = outer_low
        out_ref[...] = (final_hat * gain + vec(FFN_SHIFT)).astype(bf16)
        sums_ref[...] = jnp.zeros(sums_ref.shape, f32)
        sums_ref[B_OUTER : B_OUTER + 1] = sum_rows(outer_low.astype(f32))
        sums_ref[FFN_GAIN : FFN_GAIN + 1] = sum_rows(upstream * final_hat)
        sums_ref[FFN_SHIFT : FFN_SHIFT + 1] = sum_rows(upstream)
        out_rows = width // blocks
        padded = block - ff_rows
        inner_t = inner_in.T
        context_t = context.T

        def block_rows(values, b):
            if padded == out_rows:
                return values[b * out_rows : (b + 1) * out_rows]
            row = lax.broadcasted_iota(jnp.int32, (padded, width), 0)
            col = lax.broadcasted_iota(jnp.int32, (padded, width), 1)
            pick = ((row < out_rows) & (col == row + b * out_rows)).astype(f32).astype(bf16)
            return mm(pick, values).astype(bf16)

        for b in range(blocks):
            left_rows(b, ff_rows, block_rows(context_t, b))
            owner = jnp.bitwise_xor(batch_me & 1, b & 1) + 2 * jnp.bitwise_xor(
                (batch_me >> 2) & 1, (b >> 2) & 1
            )
            at = (((b >> 3) << 1) | ((b >> 1) & 1)) * padded
            inner[owner, at : at + padded] = block_rows(inner_t, b)
        left_own[...] = left[0]
        left_core[...] = left[1]
        left_x[:many] = left[2]
        left_x[many:] = left[3]
        few = inner_own.shape[0]
        inner_own[...] = inner[0]
        inner_core[...] = inner[1]
        inner_y[:few] = inner[2]
        inner_y[few:] = inner[3]

    return body


def backward_kernel(
    outer_low_ref,
    slope_ref,
    grad_summed_ref,
    hat_ref,
    inv_ref,
    left_x,
    inner_y,
    vecs,
    sums_in,
    w_output,
    w_inner_t,
    w_outer_t,
    x_ref,
    y_ref,
    grad_mixed_ref,
    g0,
    g1,
    g2,
    g3,
    groups,
    sums,
):
    hidden, width = w_inner_t.shape
    group_refs = (g0, g1, g2, g3)
    size = len(group_refs)
    me = lax.axis_index("blk")
    step = width
    rows = width // size
    span = outer_low_ref.shape[0]
    count = hidden // step
    parts = [slice(k * step, (k + 1) * step) for k in range(count)]
    sums[...] = sums_in[...]
    outer_low = outer_low_ref[...]
    grad_norm = grad_summed_ref[...]
    many, few = left_x.shape[0], inner_y.shape[0]
    x_ref[:many] = left_x[...]
    y_ref[:few] = inner_y[...]
    following = mm(outer_low, w_outer_t[:, parts[0]])
    for k in range(count):
        pre_low = (following * slope_ref[:, parts[k]]).astype(bf16)
        if k + 1 < count:
            following = mm(outer_low, w_outer_t[:, parts[k + 1]])
        grad_norm += mm(pre_low, w_inner_t[parts[k]])
        y_ref[few + k * step : few + (k + 1) * step] = pre_low.T
        sums[B_INNER + k : B_INNER + k + 1] = sum_rows(pre_low.astype(f32))
    hat = hat_ref[...]
    grad_mixed = norm_back(grad_norm * vecs[ATTN_GAIN : ATTN_GAIN + 1], hat, inv_ref[...])
    grad_mixed_ref[...] = grad_mixed
    mixed_low = grad_mixed.astype(bf16)
    narrow(x_ref, many, outer_low)
    narrow(x_ref, many + rows_of(width, span), mixed_low)
    context_grad_t = mm_nt(w_output[...], mixed_low).astype(bf16)
    for g in range(size):
        groups[behind(me, g, size)] = context_grad_t[g * rows : (g + 1) * rows]
    for s in range(size):
        group_refs[s][...] = groups[s]
    sums[ATTN_GAIN : ATTN_GAIN + 1] = sum_rows(grad_norm * hat)
    sums[ATTN_SHIFT : ATTN_SHIFT + 1] = sum_rows(grad_norm)
    sums[B_OUTPUT : B_OUTPUT + 1] = sum_rows(mixed_low.astype(f32))
    narrow(x_ref, many + 2 * rows_of(width, span), sums[...].astype(bf16))


def pack_kernel(core_rows, own, got, *after_and_out):
    out_ref = after_and_out[-1]
    many = core_rows.shape[0]
    size = own.shape[0] - 2 * many
    out_ref[:many] = core_rows[...]
    out_ref[many : 2 * many] = got[many : 2 * many]
    out_ref[2 * many : 2 * many + size] = own[2 * many :]
    out_ref[2 * many + size :] = got[2 * many :]


def first_products_kernel(block, ff_rows, span):
    def body(left_own, sent, received, packed, *after_and_outs):
        send_ref, keep_ref = after_and_outs[-2:]
        many = left_own.shape[0]
        size = sent.shape[0] - 2 * many
        width = send_ref.shape[1]
        tall = rows_of(width, span)
        own = (lax.axis_index("batch") >> 2) & 1
        lefts = ((left_own, 0), (received, 0), (packed, 0), (packed, many))
        rights = (
            (sent, 2 * many),
            (received, 2 * many),
            (packed, 2 * many),
            (packed, 2 * many + size),
        )
        outer_low = jnp.concatenate([widen(ref, at, span, width) for ref, at in rights], axis=0)
        mixed_low = jnp.concatenate(
            [widen(ref, at + tall, span, width) for ref, at in rights], axis=0
        )
        sums = jnp.zeros((EXTRA, width), f32)
        for ref, at in rights:
            sums += widen(ref, at + 2 * tall, EXTRA, width).astype(f32)
        for ref, side in ((send_ref, 1 - own), (keep_ref, own)):
            count = (ref.shape[0] - EXTRA) // block
            for j in range(count):

                def rows(first, number):
                    start = (2 * j + side) * block + first
                    return jnp.concatenate(
                        [
                            source[pl.ds(pl.multiple_of(start + at, 16), number)]
                            for source, at in lefts
                        ],
                        axis=1,
                    )

                at = j * block
                ref[at : at + ff_rows] = mm(rows(0, ff_rows), outer_low).astype(bf16)
                ref[at + ff_rows : at + block] = mm(
                    rows(ff_rows, block - ff_rows), mixed_low
                ).astype(bf16)
            ref[count * block :] = sums.astype(bf16)

    return body


def inner_products_kernel(block):
    def body(inner_own, sent, received, packed, send_ref, keep_ref):
        few = inner_own.shape[0]
        size = sent.shape[0] - 2 * few
        own = (lax.axis_index("batch") >> 1) & 1
        lefts = ((inner_own, 0), (received, 0), (packed, 0), (packed, few))
        rights = ((sent, 2 * few), (received, 2 * few), (packed, 2 * few), (packed, 2 * few + size))
        pre_t = jnp.concatenate([ref[at : at + size] for ref, at in rights], axis=1)
        many = send_ref.shape[0]
        pieces = []
        for side in (1 - own, own):
            for j in range(many // block):
                start = (2 * j + side) * block
                pieces.append(
                    jnp.concatenate(
                        [
                            source[pl.ds(pl.multiple_of(start + at, 16), block)]
                            for source, at in lefts
                        ],
                        axis=1,
                    )
                )
        total = mm_nt(jnp.concatenate(pieces, axis=0), pre_t).astype(bf16)
        send_ref[...] = total[:many]
        keep_ref[...] = total[many:]

    return body


def halve_kernel(block, bit, parts, extra_rows):
    def body(keep_in, *rest):
        got, (send_ref, keep_ref) = rest[:parts], rest[-2:]
        own = (lax.axis_index("batch") >> bit) & 1
        count = (send_ref.shape[0] - extra_rows) // block

        def total(part):
            added = jnp.concatenate([ref[part] for ref in got], axis=1).astype(f32)
            return (keep_in[part].astype(f32) + added).astype(bf16)

        for ref, side in ((send_ref, 1 - own), (keep_ref, own)):
            for j in range(count):
                start = pl.multiple_of((2 * j + side) * block, 16)
                ref[j * block : (j + 1) * block] = total(pl.ds(start, block))
            if extra_rows:
                last = 2 * count * block
                ref[count * block :] = total(slice(last, last + extra_rows))

    return body


def attention_back_kernel(
    probs_ref,
    q_t_ref,
    k_t_ref,
    v_t_ref,
    context_ref,
    d0,
    d1,
    d2,
    d3,
    e0,
    e1,
    e2,
    e3,
    token_sums,
    score_grad,
    out_t,
):
    slots = (d0, d1, d2, d3)
    outs = (e0, e1, e2, e3)
    size = len(slots)
    width, row_len = q_t_ref.shape
    span = row_len // size
    grad_t = jnp.concatenate([slot[...] for slot in slots], axis=1)
    grad = grad_t.T
    for h in range(width // HEAD_DIM):
        cols = slice(h * HEAD_DIM, (h + 1) * HEAD_DIM)
        for s in range(size):
            part = slice(s * span, (s + 1) * span)
            grad_part = grad[part, cols]
            delta = jnp.sum(
                grad_part.astype(f32) * context_ref[part, cols], axis=-1, keepdims=True
            )
            grad_probs = mm(grad_part, v_t_ref[cols])
            score_grad[part] = (probs_ref[h, part].astype(f32) * (grad_probs - delta)).astype(bf16)
        out_t[cols] = (mm_nt(k_t_ref[cols], score_grad[...]) * HEAD_DIM ** (-0.5)).astype(bf16)
        out_t[width + h * HEAD_DIM : width + (h + 1) * HEAD_DIM] = mm(
            q_t_ref[cols], score_grad[...]
        ).astype(bf16)
        out_t[2 * width + h * HEAD_DIM : 2 * width + (h + 1) * HEAD_DIM] = mm(
            grad_t[cols], probs_ref[h]
        ).astype(bf16)
    for s in range(size):
        outs[s][...] = out_t[:, s * span : (s + 1) * span]
    token_sums[...] = mm_nt(jnp.ones((8, row_len), bf16), out_t[...])


def head_products_kernel(
    x0, x1, x2, x3, e0, e1, e2, e3, token_sums, send_ref, keep_ref, total
):
    core = lax.axis_index("batch") & 1
    x_t = jnp.concatenate([ref[...].T for ref in (x0, x1, x2, x3)], axis=1)
    heads_t = jnp.concatenate([ref[...] for ref in (e0, e1, e2, e3)], axis=1)
    total[...] = mm_nt(x_t, heads_t)
    blocks = lax.axis_size("batch")
    rows, width = total.shape[0] // blocks, total.shape[1]
    padded = (send_ref.shape[0] - EXTRA) // (blocks // 2)
    for own, refs in ((0, (keep_ref, send_ref)), (1, (send_ref, keep_ref))):

        @pl.when(core == own)
        def _():
            for b in range(blocks):
                at = (b >> 1) * padded
                if padded != rows:
                    refs[b & 1][at : at + padded] = jnp.zeros((padded, width), bf16)
                refs[b & 1][at : at + rows] = total[b * rows : (b + 1) * rows].astype(bf16)

    sums = jnp.concatenate((token_sums[...], jnp.zeros((EXTRA - 8, width), f32)), axis=0)
    for ref in (send_ref, keep_ref):
        ref[(blocks // 2) * padded :] = sums.astype(bf16)


def grad_in_kernel(
    e0, e1, e2, e3, grad_mixed, w_query, w_key, w_value, out_ref, done_ref, groups, weights, sems
):
    slots = (e0, e1, e2, e3)
    size = len(slots)
    me = lax.axis_index("blk")
    copies = [
        pltpu.make_async_copy(weight, weights.at[k], sems.at[k])
        for k, weight in enumerate((w_query, w_key, w_value))
    ]
    for copy in copies:
        copy.start()
    for s in range(size):
        groups[ahead(me, s, size)] = slots[s][...]
    total = grad_mixed[...]
    own = e0.shape[0] // 3
    for k in range(3):
        rows = [groups[g, k * own : (k + 1) * own] for g in range(size)]
        part = jnp.concatenate(rows, axis=0).T
        copies[k].wait()
        total += mm_nt(part, weights[k])
    out_ref[...] = total.astype(bf16)
    done_ref[...] = jnp.zeros(done_ref.shape, f32)


def split_inner_kernel(keep, got, order_after, own_ref, s1, s2, s3, total):
    del order_after
    outs = (own_ref, s1, s2, s3)
    size = len(outs)
    me = lax.axis_index("blk")
    total[...] = keep[...].astype(f32) + got[...].astype(f32)
    width = total.shape[1] // size
    for s in range(size):
        cols = pl.ds(pl.multiple_of(ahead(me, s, size) * width, 128), width)
        outs[s][...] = total[:, cols].astype(outs[s].dtype)


def join_inner_kernel(own, r1, r2, r3, out_ref):
    rows = slice(0, out_ref.shape[0])
    total = own[rows] + r1[rows].astype(f32) + r2[rows].astype(f32) + r3[rows].astype(f32)
    out_ref[...] = total


def split_columns_kernel(keep, got, late, own_ref, s1, s2, s3, groups):
    outs = (s1, s2, s3)
    size = len(outs) + 1
    me = lax.axis_index("blk")
    total = keep[...].astype(f32) + got[...].astype(f32)
    last = total.shape[0] - EXTRA
    half = last // 2
    width = total.shape[1] // size
    sums = total[last:]
    row = lax.broadcasted_iota(jnp.int32, sums.shape, 0)
    group = lax.broadcasted_iota(jnp.int32, sums.shape, 1) // width
    for k, at in ((B_QUERY, 0), (B_VALUE, 2)):
        own_row = late[0:1, at * width : (at + 1) * width]
        sums = jnp.where(
            (row == k) & (group == me), jnp.concatenate([own_row] * size, axis=1), sums
        )
    extra = jnp.concatenate((sums[:, : 2 * width], sums[:, 2 * width :]), axis=0)
    for g in range(size):
        cols = slice(g * width, (g + 1) * width)
        slot = behind(me, g, size)
        groups[slot, :half] = jnp.concatenate((total[:half, cols], total[half:last, cols]), axis=1)
    own_ref[:half] = groups[0]
    own_ref[half:] = extra
    for s in range(1, size):
        outs[s - 1][:half] = groups[s].astype(bf16)
        outs[s - 1][half:] = extra.astype(bf16)


def join_rows_kernel(own, r1, r2, r3, first_ref, second_ref, *rest):
    sum_refs, (rows,) = rest[:-1], rest[-1:]
    total = own[...] + r1[...].astype(f32) + r2[...].astype(f32) + r3[...].astype(f32)
    half, width = total.shape[0] - 2 * EXTRA, total.shape[1] // 2
    rows[:half] = total[:half, :width]
    rows[half:] = total[:half, width:]
    ff_rows = first_ref.shape[0]
    first_ref[...] = rows[:ff_rows]
    second_ref[...] = rows[ff_rows : ff_rows + second_ref.shape[0]]
    sums = jnp.concatenate((total[half : half + EXTRA], total[half + EXTRA :]), axis=1)
    for k, ref in enumerate(sum_refs[:-1]):
        ref[...] = sums[k]
    model_width = sums.shape[1]
    for k in range(sum_refs[-1].shape[0] // model_width):
        sum_refs[-1][k * model_width : (k + 1) * model_width] = sums[B_INNER + k]


def last_sum_kernel(keep, got, *after_and_outs):
    q_ref, k_ref, v_ref, late_ref = after_and_outs[-4:]
    total = keep[...].astype(f32) + got[...].astype(f32)
    rows, own = q_ref.shape
    for k, ref in enumerate((q_ref, k_ref, v_ref)):
        ref[...] = total[:rows, k * own : (k + 1) * own]
    last = total.shape[0] - EXTRA
    late_ref[...] = total[last : last + 8]


def run_kernel(body, operands, outs, scratch=(), in_hbm=(), limit=8, fill=0):
    vmem = pl.BlockSpec(memory_space=pltpu.VMEM)
    hbm = pl.BlockSpec(memory_space=pltpu.HBM)
    anywhere = pl.BlockSpec(memory_space=pl.ANY)

    def place(k):
        if k - len(operands) in in_hbm:
            return anywhere
        return hbm if k in in_hbm else vmem

    return pl.pallas_call(
        body,
        out_shape=[jax.ShapeDtypeStruct(shape, dtype) for shape, dtype in outs],
        in_specs=[place(k) for k in range(len(operands))],
        out_specs=[vmem] * len(outs),
        scratch_shapes=list(scratch),
        compiler_params=pltpu.CompilerParams(vmem_limit_bytes=limit * MIB),
        cost_estimate=pl.CostEstimate(
            flops=1 + fill * 10**9, bytes_accessed=1, transcendentals=0
        ),
    )(*operands)


def blk_shift(values, step):
    size = lax.axis_size("blk")
    return lax.ppermute(values, "blk", [(i, (i + step) % size) for i in range(size)])


def batch_swap(values, bits):
    size = lax.axis_size("batch")
    return lax.ppermute(values, "batch", [(i, i ^ bits) for i in range(size)])


def halve(keep, got, block, bit, after=(), extra_rows=EXTRA):
    got = got if isinstance(got, list) else [got]
    count = (keep.shape[0] - extra_rows) // block // 2
    shape = ((count * block + extra_rows, keep.shape[1]), bf16)
    return run_kernel(
        halve_kernel(block, bit, len(got), extra_rows),
        [keep, *got, *after],
        [shape, shape],
        in_hbm=[-1 - k for k in range(len(after))],
    )


def local(
    hidden_in,
    w_query,
    b_query,
    w_key,
    w_value,
    b_value,
    w_output,
    b_output,
    attn_gain,
    attn_shift,
    w_inner,
    b_inner,
    w_outer,
    b_outer,
    ffn_gain,
    ffn_shift,
    text_lengths,
    region_lengths,
    out_grad,
):
    _, span, width = hidden_in.shape
    hidden = w_inner.shape[1]
    size = lax.axis_size("blk")
    blocks = lax.axis_size("batch")
    bits = blocks.bit_length() - 1
    row_len = span * size
    own_heads = HEADS // size
    own_width = own_heads * HEAD_DIM
    steps = range(1, size)
    tokens_f32 = ((span, width), f32)
    tokens_bf16 = ((span, width), bf16)
    row = ((width,), f32)

    flat_in = hidden_in[0]
    x_slots = [blk_shift(flat_in, step) for step in steps]
    stacked = jnp.zeros((EXTRA, width), bf16)
    number = lax.broadcasted_iota(jnp.int32, stacked.shape, 0)
    for k, vector in (
        (B_OUTER, b_outer),
        (FFN_GAIN, ffn_gain),
        (FFN_SHIFT, ffn_shift),
        (ATTN_GAIN, attn_gain),
        (ATTN_SHIFT, attn_shift),
        (B_OUTPUT, b_output),
        (B_QUERY, b_query),
        (B_VALUE, b_value),
    ):
        stacked = jnp.where(number == k, vector[None, :], stacked)
    square = ((width, width), bf16)
    mask, vecs, x_own, grad_own, *attn_weights, outer_copy = run_kernel(
        prep_kernel,
        [
            text_lengths,
            region_lengths,
            flat_in,
            out_grad[0],
            stacked,
            b_inner,
            w_query,
            w_key,
            w_value,
            w_outer,
        ],
        [
            ((row_len, row_len), f32),
            ((EXTRA, width), f32),
            tokens_bf16,
            tokens_bf16,
            square,
            square,
            square,
            ((hidden, width), bf16),
        ],
        [pltpu.SemaphoreType.DMA((4,))],
        in_hbm=(6, 7, 8, 9),
        limit=16,
    )
    inner_copy, *ffn_turned = run_kernel(
        transpose_kernel,
        [w_inner, outer_copy],
        [((width, hidden), bf16), ((hidden, width), bf16), ((width, hidden), bf16)],
        [pltpu.SemaphoreType.DMA((1,))],
        in_hbm=(0,),
        limit=20,
        fill=4,
    )
    ffn_weights = (inner_copy, outer_copy)
    x_slots = [x_own] + x_slots
    context = run_kernel(
        own_attention_kernel,
        x_slots + attn_weights + [vecs, mask],
        [tokens_bf16],
        [pltpu.VMEM((row_len, width), bf16)],
        limit=20,
    )[0]
    ff_rows = hidden // blocks
    rows = -(-(width // blocks) // 16) * 16
    block = ff_rows + rows

    many = blocks // 4 * block
    few = blocks // 4 * rows
    (
        layer_out,
        left_own,
        left_core,
        left_x,
        inner_own,
        inner_core,
        inner_y,
        outer_low,
        slope,
        grad_summed,
        attn_hat,
        attn_inv,
        sums,
    ) = run_kernel(
        forward_kernel(blocks),
        [x_own, context, vecs, grad_own, w_output]
        + [*ffn_weights, ffn_turned[0]],
        [
            tokens_bf16,
            ((many, span), bf16),
            ((many, span), bf16),
            ((2 * many, span), bf16),
            ((few, span), bf16),
            ((few, span), bf16),
            ((2 * few, span), bf16),
            tokens_bf16,
            ((span, hidden), f32),
            tokens_f32,
            tokens_f32,
            ((span, 1), f32),
            ((EXTRA, width), f32),
        ],
        [
            pltpu.VMEM((4, many, span), bf16),
            pltpu.VMEM((4, few, span), bf16),
        ],
        in_hbm=(-1,),
        limit=20,
    )
    tall = 2 * rows_of(width, span) + rows_of(width, EXTRA)
    x_sent, y_sent, grad_mixed, *context_grads = run_kernel(
        backward_kernel,
        [
            outer_low,
            slope,
            grad_summed,
            attn_hat,
            attn_inv,
            left_x,
            inner_y,
            vecs,
            sums,
            w_output,
            *ffn_turned,
        ],
        [((2 * many + tall, span), bf16), ((2 * few + hidden, span), bf16), tokens_f32]
        + [((own_width, span), bf16)] * size,
        [pltpu.VMEM((size, own_width, span), bf16), pltpu.VMEM((EXTRA, width), f32)],
        limit=20,
    )
    x_got = batch_swap(x_sent, 2)
    y_got = batch_swap(y_sent, 4)
    context_grads = context_grads[:1] + [blk_shift(context_grads[step], step) for step in steps]
    heads_shape = ((own_width, row_len), bf16)
    probs, q_t, k_t, v_t, context_own = run_kernel(
        head_attention_kernel,
        x_slots + attn_weights + [vecs, mask, grad_mixed],
        [((own_heads, row_len, row_len), bf16)]
        + [heads_shape] * 3
        + [((row_len, own_width), f32)],
        [pltpu.VMEM((row_len, width), bf16)],
        in_hbm=(-1,),
        limit=16,
    )
    *head_grads, token_sums = run_kernel(
        attention_back_kernel,
        [probs, q_t, k_t, v_t, context_own] + context_grads,
        [((3 * own_width, span), bf16)] * size + [((8, 3 * own_width), f32)],
        [pltpu.VMEM((row_len, row_len), bf16), pltpu.VMEM((3 * own_width, row_len), bf16)],
    )
    head_slots = head_grads[:1] + [blk_shift(head_grads[step], size - step) for step in steps]
    wide = 3 * own_width
    head_send, head_keep = run_kernel(
        head_products_kernel,
        x_slots + head_grads + [token_sums],
        [((blocks // 2 * rows + EXTRA, wide), bf16)] * 2,
        [pltpu.VMEM((width, wide), f32)],
        limit=10,
    )
    head_got = batch_swap(head_send, 1)
    head_send, head_keep = halve(head_keep, head_got, rows, 1)
    head_got = batch_swap(head_send, 2)
    packed = run_kernel(
        pack_kernel,
        [inner_core, y_sent, y_got, head_send, head_slots[1], head_slots[-1], x_got],
        [((2 * (few + hidden), span), bf16)],
        in_hbm=(-1, -2, -3, -4),
        limit=10,
    )[0]
    inner_send, inner_keep = run_kernel(
        inner_products_kernel(rows),
        [inner_own, y_sent, y_got, batch_swap(packed, 1)],
        [((few // 2, hidden), bf16)] * 2,
        limit=14,
    )
    inner_got = batch_swap(inner_send, 2)
    for bit in range(3, bits):
        inner_send, inner_keep = halve(inner_keep, inner_got, rows, bit, extra_rows=0)
        inner_got = batch_swap(inner_send, 1 << bit)
    packed = run_kernel(
        pack_kernel,
        [left_core, x_sent, x_got],
        [((2 * (many + tall), span), bf16)],
    )[0]
    send, keep = run_kernel(
        first_products_kernel(block, ff_rows, span),
        [left_own, x_sent, x_got, batch_swap(packed, 1)],
        [((many // 2 + EXTRA, width), bf16)] * 2,
        limit=14,
    )
    got = batch_swap(send, 4)
    for bit in range(3, bits):
        send, keep = halve(keep, got, block, bit)
        got = batch_swap(send, 1 << bit)
    inner_part, *inner_sends = run_kernel(
        split_inner_kernel,
        [inner_keep, inner_got, head_slots[2]],
        [((rows, width), f32)] + [((rows, width), bf16)] * (size - 1),
        [pltpu.VMEM((rows, hidden), f32)],
        in_hbm=(-1,),
    )
    inner_parts = [blk_shift(inner_sends[step - 1], step) for step in steps]
    for bit in range(2, bits):
        head_send, head_keep = halve(head_keep, head_got, rows, bit, [inner_sends[0]])
        head_got = batch_swap(head_send, 1 << bit)
    grad_in, grad_in_done = run_kernel(
        grad_in_kernel,
        head_slots + [grad_mixed, w_query, w_key, w_value],
        [tokens_bf16, ((8, 128), f32)],
        [
            pltpu.VMEM((size, 3 * own_width, span), bf16),
            pltpu.VMEM((3, width, width), bf16),
            pltpu.SemaphoreType.DMA((3,)),
        ],
        in_hbm=(5, 6, 7),
        limit=10,
        fill=4,
    )
    out_rows = width // blocks
    own_cols = ((out_rows, own_width), f32)
    *grad_qkv, late = run_kernel(
        last_sum_kernel,
        [head_keep, head_got, grad_in_done] + inner_parts[:-1],
        [own_cols] * 3 + [((8, wide), f32)],
        in_hbm=(-1, -2, -3),
    )
    message = (block // 2 + 2 * EXTRA, 2 * own_width)
    own_part, *sends = run_kernel(
        split_columns_kernel,
        [keep, got, late],
        [(message, f32)] + [(message, bf16)] * (size - 1),
        [pltpu.VMEM((size, block // 2, 2 * own_width), f32)],
    )
    parts = [blk_shift(sends[step - 1], step) for step in steps]
    grad_w_inner = run_kernel(
        join_inner_kernel, [inner_part] + inner_parts, [((out_rows, width), f32)]
    )[0]
    grad_w_outer, grad_w_output, *sums = run_kernel(
        join_rows_kernel,
        [own_part] + parts,
        [((ff_rows, own_width), f32), own_cols] + [row] * 8 + [((hidden,), f32)],
        [pltpu.VMEM((block, own_width), f32)],
    )
    return (
        layer_out[None],
        grad_in[None],
        grad_qkv[0],
        sums[B_QUERY],
        grad_qkv[1],
        grad_qkv[2],
        sums[B_VALUE],
        grad_w_output,
        sums[B_OUTPUT],
        sums[ATTN_GAIN],
        sums[ATTN_SHIFT],
        grad_w_inner,
        sums[B_INNER],
        grad_w_outer,
        sums[B_OUTER],
        sums[FFN_GAIN],
        sums[FFN_SHIFT],
    )


def solution(mesh):
    rows = P("batch", "blk", None)
    tile = P("batch", "blk")
    return jax.shard_map(
        local,
        mesh=mesh,
        in_specs=(rows,) + (P(),) * 15 + (P("batch", None), P("batch", None), rows),
        out_specs=(
            rows,
            rows,
            tile,
            P(),
            tile,
            tile,
            P(),
            tile,
            P(),
            P(),
            P(),
            tile,
            P(),
            tile,
            P(),
            P(),
            P(),
        ),
        check_vma=False,
    )
```
